32 devices in a mesh: dp: 4 (over x, core), ctx: 2 (over y), fsdp: 4 (over z).
Axes of the slice: x: 2, y: 2, z: 4, core: 2. Of those that a mesh axis runs over, the one named last changes fastest.
Arguments:
- tokens: bfloat16 [4, 1536, 960], P('dp', ('ctx', 'fsdp')), may hold values from -6 to 6
- block_order: int32 [4, 4], P('dp'), may hold values from 0 to 3, each once within a row
- attention_gain: bfloat16 [960], P('fsdp'), may hold values from 0.5 to 1.5
- query_weight: bfloat16 [960, 960], P('fsdp'), may hold values from -0.1875 to 0.1875
- key_weight: bfloat16 [960, 320], P('fsdp'), may hold values from -0.1875 to 0.1875
- value_weight: bfloat16 [960, 320], P('fsdp'), may hold values from -0.1875 to 0.1875
- output_weight: bfloat16 [960, 960], P('fsdp'), may hold values from -1.5 to 1.5
- feedforward_gain: bfloat16 [960], P('fsdp'), may hold values from 0.5 to 1.5
- gate_weight: bfloat16 [960, 2560], P('fsdp'), may hold values from -0.1875 to 0.1875
- up_weight: bfloat16 [960, 2560], P('fsdp'), may hold values from -0.1875 to 0.1875
- down_weight: bfloat16 [2560, 960], P('fsdp'), may hold values from -0.125 to 0.125
- cotangent: bfloat16 [4, 1536, 960], P('dp', ('ctx', 'fsdp')), may hold values from -6 to 6
Outputs:
- result: float32 [4, 1536, 960], P('dp', ('ctx', 'fsdp'))
- input_grad: float32 [4, 1536, 960], P('dp', ('ctx', 'fsdp'))
- attention_gain_grad: float32 [960], P('fsdp')
- query_weight_grad: float32 [960, 960], P('fsdp')
- key_weight_grad: float32 [960, 320], P('fsdp')
- value_weight_grad: float32 [960, 320], P('fsdp')
- output_weight_grad: float32 [960, 960], P('fsdp')
- feedforward_gain_grad: float32 [960], P('fsdp')
- gate_weight_grad: float32 [960, 2560], P('fsdp')
- up_weight_grad: float32 [960, 2560], P('fsdp')
- down_weight_grad: float32 [2560, 960], P('fsdp')
The draws below stay inside these ranges and needn't reach their ends.
Inputs may be any that keep to these rules, and one draw needn't show every extreme that they name: Each row is a permutation of the 4 blocks: stored block j of a sequence holds the tokens from block_order[j] * 384 on, in order.
All inputs are finite; a program needn't handle non-finite values.
Results may differ from the reference program's by a relative error of at most 0.02.
Values may be sent and summed in bfloat16 or wider, within the bound.
No kernel may reach another device: no remote copies, remote signals or barrier semaphores. Data moves between devices by JAX's collectives and lax.ppermute only.
A program may use at most 192 MiB of HBM per device.

```python
import math
import jax
import jax.numpy as jnp
from jax import lax

D = 960
HEADS = 15
KV_HEADS = 5
HEAD_DIM = 64
FF = 2560
BATCH = 4
LENGTH = 1536
BLOCKS = 4
BLOCK_LENGTH = 384


def block_scale(rng, shape, shards, low, top_value):
    loudness = 1.0
    for axis_at, parts in shards:
        heights = jax.random.uniform(jax.random.fold_in(jax.random.fold_in(rng, 6), axis_at), (parts,), jnp.float32, low / len(shards), top_value / len(shards))
        loudness = loudness * jnp.repeat(jnp.exp(heights), shape[axis_at] // parts).reshape((-1,) + (1,) * (len(shape) - 1 - axis_at))
    return loudness


def scatter_about(stream_key, dims, deviation, most, split=(), kind=jnp.bfloat16):
    drawn = jax.random.normal(stream_key, dims, jnp.float32) * deviation
    if len(split) > 0:
        drawn = block_scale(stream_key, dims, split, -0.22, 0.18) * drawn
    return jnp.clip(drawn, min=-most, max=most).astype(kind)


def setup_inputs(seed: int = 0) -> dict:
    arg_keys = jax.random.split(jax.random.key(seed), 13)
    tokens = scatter_about(arg_keys[0], (BATCH, LENGTH, D), 1.0, 6.0, ((0, 4), (1, 8)))
    block_order = jax.vmap(lambda own: jax.random.permutation(own, BLOCKS))(jax.random.split(arg_keys[1], BATCH)).reshape((BATCH, BLOCKS)).astype(jnp.int32)
    attention_gain = jnp.clip(1.0 + 0.1 * jax.random.normal(arg_keys[2], (D,), jnp.float32), 0.5, 1.5).astype(jnp.bfloat16)
    query_weight = scatter_about(arg_keys[3], (D, HEADS * HEAD_DIM), D ** -0.5, 0.1875, ((0, 4),))
    key_weight = scatter_about(arg_keys[4], (D, KV_HEADS * HEAD_DIM), D ** -0.5, 0.1875, ((0, 4),))
    value_weight = scatter_about(arg_keys[5], (D, KV_HEADS * HEAD_DIM), D ** -0.5, 0.1875, ((0, 4),))
    output_weight = scatter_about(arg_keys[6], (HEADS * HEAD_DIM, D), (max(1, HEADS * HEAD_DIM * 24 // LENGTH)) ** -0.5, 1.5, ((0, 4),))
    feedforward_gain = jnp.clip(1.0 + 0.1 * jax.random.normal(arg_keys[7], (D,), jnp.float32), 0.5, 1.5).astype(jnp.bfloat16)
    gate_weight = scatter_about(arg_keys[8], (D, FF), D ** -0.5, 0.1875, ((0, 4),))
    up_weight = scatter_about(arg_keys[9], (D, FF), D ** -0.5, 0.1875, ((0, 4),))
    down_weight = scatter_about(arg_keys[10], (FF, D), FF ** -0.5, 0.125, ((0, 4),))
    cotangent = scatter_about(arg_keys[11], (BATCH, LENGTH, D), 1.0, 6.0, ((0, 4), (1, 8)))
    return {"tokens": tokens, "block_order": block_order, "attention_gain": attention_gain, "query_weight": query_weight, "key_weight": key_weight, "value_weight": value_weight, "output_weight": output_weight, "feedforward_gain": feedforward_gain, "gate_weight": gate_weight, "up_weight": up_weight, "down_weight": down_weight, "cotangent": cotangent}


EPSILON = 1e-05
ROPE_BASE = 100000.0
MASKED = -1e+30

@jax.custom_vjp
def low(v):
    return lax.optimization_barrier(v.astype(jnp.bfloat16)).astype(jnp.float32)

@jax.custom_vjp
def low_back(v):
    return v

def low_keep(v):
    return (low(v), None)

def low_pass(kept, grad):
    return (grad,)

def back_keep(v):
    return (v, None)

def back_low(kept, grad):
    return (low(grad),)
low.defvjp(low_keep, low_pass)
low_back.defvjp(back_keep, back_low)

def widen(values):
    return values.astype(jnp.float32)

def project(left, right):
    return jnp.dot(left, right, precision=lax.Precision.HIGHEST, preferred_element_type=jnp.float32)

def norm_rows(values, gain):
    return values * lax.rsqrt(lax.optimization_barrier(jnp.mean(values * values, axis=-1, keepdims=True)) + EPSILON) * gain

def rotation(positions):
    half_dim = HEAD_DIM // 2
    exponent = -(jnp.arange(half_dim, dtype=jnp.float32) * 2.0) / HEAD_DIM
    frequency = jnp.power(jnp.float32(ROPE_BASE), exponent)
    angles = positions.astype(jnp.float32)[..., None] * frequency
    cosine_half = jnp.cos(angles)
    sine_half = jnp.sin(angles)
    return (jnp.concatenate([cosine_half, cosine_half], axis=-1), jnp.concatenate([sine_half, sine_half], axis=-1))

def rotate(values, cosine_table, sine_table):
    half_dim = values.shape[-1] // 2
    turned = jnp.concatenate([-values[..., half_dim:], values[..., :half_dim]], axis=-1)
    return values * cosine_table + turned * sine_table

def attention(queries, local_keys, local_values, positions):
    length = queries.shape[0]
    block_size = math.gcd(length, 512)
    groups = HEADS // KV_HEADS
    grouped = queries.reshape(length // block_size, block_size, KV_HEADS, groups, HEAD_DIM)
    spots = positions.reshape(length // block_size, block_size)
    score_scale = 1.0 / math.sqrt(HEAD_DIM)

    def one_block(block_pair):
        query_block, query_pos = block_pair
        scores = low_back(jnp.einsum('rkgd,ukd->kgru', query_block, local_keys, precision=lax.Precision.HIGHEST) * score_scale)
        allowed = query_pos[:, None] >= positions[None, :]
        scores = jnp.where(allowed, scores, MASKED)
        largest = lax.optimization_barrier(jnp.max(scores, axis=-1, keepdims=True))
        weights = jnp.exp(scores - largest)
        weights = weights / lax.optimization_barrier(jnp.sum(weights, axis=-1, keepdims=True))
        return jnp.einsum('kgru,ukd->rkgd', low(weights), local_values, precision=lax.Precision.HIGHEST)
    blocks_out = lax.map(jax.checkpoint(one_block), (grouped, spots))
    return blocks_out.reshape(length, HEADS * HEAD_DIM)

def layer(inputs, block_row, attention_gain, query_weight, key_weight, value_weight, output_weight, feedforward_gain, gate_weight, up_weight, down_weight):
    length = inputs.shape[0]
    positions = (block_row[:, None] * BLOCK_LENGTH + jnp.arange(BLOCK_LENGTH, dtype=jnp.int32)[None, :]).reshape(-1)
    cosine_table, sine_table = rotation(positions)
    cosine_table = cosine_table[:, None, :]
    sine_table = sine_table[:, None, :]
    normed_one = low(norm_rows(inputs, attention_gain))
    queries = low_back(project(normed_one, query_weight)).reshape(length, HEADS, HEAD_DIM)
    queries = low(rotate(queries, cosine_table, sine_table))
    local_keys = low_back(project(normed_one, key_weight)).reshape(length, KV_HEADS, HEAD_DIM)
    local_keys = low(rotate(local_keys, cosine_table, sine_table))
    local_values = low(low_back(project(normed_one, value_weight))).reshape(length, KV_HEADS, HEAD_DIM)
    attended = low(low_back(attention(queries, local_keys, local_values, positions)))
    residual = inputs + low_back(project(attended, output_weight))
    normed_two = low(norm_rows(residual, feedforward_gain))
    gate_value = low_back(project(normed_two, gate_weight))
    upward = low_back(project(normed_two, up_weight))
    activated = low(jax.nn.silu(gate_value) * upward)
    return residual + project(activated, down_weight)

def reference(tokens, block_order, attention_gain, query_weight, key_weight, value_weight, output_weight, feedforward_gain, gate_weight, up_weight, down_weight, cotangent):

    def run(inputs, first_gain, query_wide, key_wide, value_wide, output_wide, second_gain, gate_wide, up_wide, down_wide):

        def one_sequence(sequence_pair):
            return layer(sequence_pair[0], sequence_pair[1], first_gain, query_wide, key_wide, value_wide, output_wide, second_gain, gate_wide, up_wide, down_wide)
        return lax.map(one_sequence, (inputs, block_order))
    result, pullback = jax.vjp(run, widen(tokens), widen(attention_gain), widen(query_weight), widen(key_weight), widen(value_weight), widen(output_weight), widen(feedforward_gain), widen(gate_weight), widen(up_weight), widen(down_weight))
    gradients = pullback(widen(cotangent))
    return (result, gradients[0], gradients[1], gradients[2], gradients[3], gradients[4], gradients[5], gradients[6], gradients[7], gradients[8], gradients[9])
```

```python
import functools
import math

import jax
import jax.numpy as jnp
from jax import lax
from jax.experimental import pallas as pl
from jax.experimental.pallas import tpu as pltpu
from jax.sharding import PartitionSpec as P

HEADS = 15
KV_HEADS = 5
HEAD_DIM = 64
GROUPS = HEADS // KV_HEADS
LANES = 128

EPSILON = 1e-05
ROPE_BASE = 100000.0
MASKED = -1e30

F32 = jnp.float32
BF16 = jnp.bfloat16
VMEM_LIMIT = 56 * 1024 * 1024


def dot_plain(left, right):
    return jnp.dot(left, right, preferred_element_type=F32)


def dot_last(left, right):
    return lax.dot_general(left, right, (((1,), (1,)), ((), ())), preferred_element_type=F32)


def dot_first(left, right):
    return lax.dot_general(left, right, (((0,), (0,)), ((), ())), preferred_element_type=F32)


def swap(x, axis, mask):
    count = lax.axis_size(axis)
    return lax.ppermute(x, axis, [(i, i ^ mask) for i in range(count)])


def swap_plane(x, dp_mask, ctx_mask):
    ctx_count = lax.axis_size("ctx")
    pairs = []
    for d in range(lax.axis_size("dp")):
        for c in range(ctx_count):
            pairs.append((d * ctx_count + c, (d ^ dp_mask) * ctx_count + (c ^ ctx_mask)))
    return lax.ppermute(x, ("dp", "ctx"), pairs)


def swap_core(x):
    return swap_plane(x, 1, 0)


CHIP_MASKS = ((2, 0), (0, 1), (2, 1))


def plane_group_count():
    return lax.axis_size("dp") * 2


def own_and_chips(x):
    return [x] + [swap_plane(x, a, b) for a, b in CHIP_MASKS]


def gather_fsdp(x):
    count = lax.axis_size("fsdp")
    index = lax.axis_index("fsdp")
    out = jnp.zeros((count,) + x.shape, x.dtype)
    for r in range(count):
        piece = x if r == 0 else swap(x, "fsdp", r)
        out = lax.dynamic_update_slice_in_dim(out, piece[None], index ^ r, 0)
    return out


def scatter_fsdp(parts):
    count = lax.axis_size("fsdp")
    index = lax.axis_index("fsdp")
    total = lax.dynamic_index_in_dim(parts, index, 0, keepdims=False).astype(F32)
    for r in range(1, count):
        piece = lax.dynamic_index_in_dim(parts, index ^ r, 0, keepdims=False)
        total = total + swap(piece, "fsdp", r).astype(F32)
    return total


def sum_chips(x):
    own, across, along, diagonal = own_and_chips(x)
    return (own.astype(F32) + across.astype(F32)) + (along.astype(F32) + diagonal.astype(F32))


def sum_far(x):
    count = lax.axis_size("ctx")
    if count == 2:
        return x
    groups = [list(range(0, count, 2)), list(range(1, count, 2))]
    return lax.psum(x.astype(F32), "ctx", axis_index_groups=groups).astype(x.dtype)


def whole(shape, memory_space=pltpu.VMEM):
    return pl.BlockSpec(memory_space=memory_space)


def call(kernel, out_shapes, *args, scratch=(), flops=0, name=None):
    specs = [pl.BlockSpec(memory_space=pltpu.VMEM) for _ in args]
    outs = tuple(jax.ShapeDtypeStruct(s, d) for s, d in out_shapes)
    bytes_all = sum(a.size * a.dtype.itemsize for a in args) + sum(
        math.prod(s) * jnp.dtype(d).itemsize for s, d in out_shapes
    )
    return pl.pallas_call(
        kernel,
        out_shape=outs,
        in_specs=specs,
        out_specs=tuple(pl.BlockSpec(memory_space=pltpu.VMEM) for _ in outs),
        scratch_shapes=list(scratch),
        compiler_params=pltpu.CompilerParams(vmem_limit_bytes=VMEM_LIMIT),
        cost_estimate=pl.CostEstimate(flops=flops, bytes_accessed=bytes_all, transcendentals=0),
        name=name,
    )(*args)


def rope_lanes(values, cosine, sine):
    rows, width = values.shape
    lane = lax.broadcasted_iota(jnp.int32, (rows, LANES), 1)
    first_half = (lane % HEAD_DIM) < (HEAD_DIM // 2)
    out = []
    for start in range(0, width, LANES):
        piece = values[:, start : min(start + LANES, width)]
        size = piece.shape[1]
        if size < LANES:
            piece = jnp.concatenate([piece, jnp.zeros((rows, LANES - size), piece.dtype)], axis=1)
        ahead = pltpu.roll(piece, LANES - HEAD_DIM // 2, 1)
        behind = pltpu.roll(piece, HEAD_DIM // 2, 1)
        partner = jnp.where(first_half, ahead, behind)
        out.append((piece * cosine + partner * sine)[:, :size])
    return jnp.concatenate(out, axis=1)


def heads_of(ref, first, count, rows=None):
    out = []
    for h in range(first, first + count):
        start = (h * HEAD_DIM) // LANES * LANES
        stop = min(start + LANES, ref.shape[-1])
        pair = ref[:, start:stop] if rows is None else ref[rows, start:stop]
        at = h * HEAD_DIM - start
        out.append(pair[:, at : at + HEAD_DIM])
    return out[0] if count == 1 else jnp.concatenate(out, axis=0)


def kv_kernel(normed_ref, mine_ref, other_ref, core_ref, cos_ref, sin_ref, kv_ref):
    normed = normed_ref[...]
    mine = dot_plain(normed, mine_ref[...])
    other = dot_plain(normed, other_ref[...])
    first_core = core_ref[...] == 0
    keys = jnp.where(first_core, mine, other)
    values = jnp.where(first_core, other, mine)
    keys = rope_lanes(keys, cos_ref[...], sin_ref[...])
    kv_ref[...] = jnp.concatenate([keys, values], axis=1).astype(BF16)


def forward_kernel(
    chunk, query_ref, kv_ref, key_pos_ref, query_pos_ref, cos_ref, sin_ref,
    attended_ref, queries_ref, turned_ref, log_ref
):
    key_count = kv_ref.shape[0]
    rows = query_ref.shape[0]
    columns = GROUPS * rows
    roped = rope_lanes(query_ref[...], cos_ref[...], sin_ref[...]).astype(BF16)
    queries_ref[...] = roped * jnp.asarray(1.0 / math.sqrt(HEAD_DIM), BF16)
    query_pos = query_pos_ref[...]
    outs = []
    for kv_head in range(KV_HEADS):
        stacked = heads_of(queries_ref, kv_head * GROUPS, GROUPS)

        def step(j, state, kv_head=kv_head, stacked=stacked):
            largest, total, weighted = state
            at = pl.ds(pl.multiple_of(j * chunk, chunk), chunk)
            keys = heads_of(kv_ref, kv_head, 1, at)
            values = heads_of(kv_ref, KV_HEADS + kv_head, 1, at)
            scores = dot_last(keys, stacked)
            scores = jnp.where(key_pos_ref[at, :] <= query_pos, scores, MASKED)
            new_largest = jnp.maximum(largest, jnp.max(scores, axis=0, keepdims=True))
            weights = jnp.exp(scores - new_largest)
            factor = jnp.exp(largest - new_largest)
            total = total * factor + jnp.sum(weights, axis=0, keepdims=True)
            weighted = weighted * factor + dot_first(values, weights.astype(BF16))
            return new_largest, total, weighted

        start = (
            jnp.full((1, columns), MASKED, F32),
            jnp.zeros((1, columns), F32),
            jnp.zeros((HEAD_DIM, columns), F32),
        )
        largest, total, weighted = lax.fori_loop(0, key_count // chunk, step, start)
        turned = weighted / total
        turned_ref[kv_head] = turned
        log_ref[kv_head : kv_head + 1, :] = largest + jnp.log(total)
        straight = turned.T
        for g in range(GROUPS):
            outs.append(straight[g * rows : (g + 1) * rows, :])
    attended_ref[...] = jnp.concatenate(outs, axis=1).astype(BF16)


def backward_kernel(
    chunk, queries_ref, kv_ref, key_pos_ref, query_pos_ref, cos_ref, sin_ref, turned_ref,
    log_ref, grad_ref, query_grad_ref, kv_grad_ref
):
    key_count = kv_ref.shape[0]
    rows = queries_ref.shape[0]
    columns = GROUPS * rows
    query_pos = query_pos_ref[...]
    outs = []
    for kv_head in range(KV_HEADS):
        stacked = heads_of(queries_ref, kv_head * GROUPS, GROUPS)
        upstream = heads_of(grad_ref, kv_head * GROUPS, GROUPS)
        delta = jnp.sum(
            upstream.astype(F32).T * turned_ref[kv_head], axis=0, keepdims=True
        )
        log_total = log_ref[kv_head : kv_head + 1, :]
        lanes_at = kv_head * HEAD_DIM
        values_at = (KV_HEADS + kv_head) * HEAD_DIM

        def step(j, query_grad, kv_head=kv_head, stacked=stacked, upstream=upstream,
                 delta=delta, log_total=log_total, lanes_at=lanes_at, values_at=values_at):
            at = pl.ds(pl.multiple_of(j * chunk, chunk), chunk)
            keys = heads_of(kv_ref, kv_head, 1, at)
            values = heads_of(kv_ref, KV_HEADS + kv_head, 1, at)
            scores = dot_last(keys, stacked)
            scores = jnp.where(key_pos_ref[at, :] <= query_pos, scores, MASKED)
            weights = jnp.exp(scores - log_total)
            weight_grad = dot_last(values, upstream)
            score_grad = (weights * (weight_grad - delta)).astype(BF16)
            value_grad = dot_plain(weights.astype(BF16), upstream)
            key_grad = dot_plain(score_grad, stacked)
            kv_grad_ref[at, lanes_at : lanes_at + HEAD_DIM] = key_grad.astype(BF16)
            kv_grad_ref[at, values_at : values_at + HEAD_DIM] = value_grad.astype(BF16)
            return query_grad + dot_first(keys, score_grad)

        query_grad = lax.fori_loop(
            0, key_count // chunk, step, jnp.zeros((HEAD_DIM, columns), F32)
        )
        straight = query_grad.T * (1.0 / math.sqrt(HEAD_DIM))
        for g in range(GROUPS):
            outs.append(straight[g * rows : (g + 1) * rows, :])
    query_grad_ref[...] = rope_lanes(
        jnp.concatenate(outs, axis=1), cos_ref[...], -sin_ref[...]
    ).astype(BF16)


def kv_back_kernel(own_ref, one_ref, two_ref, three_ref, cos_ref, sin_ref, out_ref):
    total = (own_ref[...].astype(F32) + one_ref[...].astype(F32)) + (
        two_ref[...].astype(F32) + three_ref[...].astype(F32)
    )
    width = KV_HEADS * HEAD_DIM
    keys = rope_lanes(total[:, :width], cos_ref[...], -sin_ref[...])
    out_ref[...] = jnp.concatenate([keys, total[:, width:]], axis=1).astype(BF16)


def norm_rows(values, gain):
    inverse = lax.rsqrt(jnp.mean(values * values, axis=-1, keepdims=True) + EPSILON)
    return (values * inverse * gain, inverse)


def norm_back(gradient, values, inverse, gain):
    scaled = gradient * gain
    inner_mean = jnp.mean(scaled * values, axis=-1, keepdims=True)
    return inverse * scaled - values * (inverse * inverse * inverse) * inner_mean


def base_of(block_order, stored, block_length):
    which = stored // block_length
    count = block_order.shape[1]
    matches = (which[:, None] == jnp.arange(count, dtype=jnp.int32)[None, :]).astype(jnp.int32)
    return jnp.sum(block_order[0][None, :] * matches, axis=-1) * block_length + stored % block_length


def tables(positions):
    half_dim = HEAD_DIM // 2
    exponent = -(jnp.arange(half_dim, dtype=F32) * 2.0) / HEAD_DIM
    frequency = jnp.power(F32(ROPE_BASE), exponent)
    angles = positions.astype(F32)[:, None] * frequency
    cosine, sine = jnp.cos(angles), jnp.sin(angles)
    return (
        jnp.concatenate([cosine] * 4, axis=-1),
        jnp.concatenate([-sine, sine, -sine, sine], axis=-1),
    )


def on_device(
    tokens,
    block_order,
    attention_gain,
    query_weight,
    key_weight,
    value_weight,
    output_weight,
    feedforward_gain,
    gate_weight,
    up_weight,
    down_weight,
    cotangent,
):
    rows, width = tokens.shape[1], tokens.shape[2]
    shard_count = lax.axis_size("fsdp")
    ctx_count = lax.axis_size("ctx")
    block_length = rows * shard_count * ctx_count // block_order.shape[1]
    shard = lax.axis_index("fsdp")
    ctx = lax.axis_index("ctx")
    dp = lax.axis_index("dp")
    core = dp & 1
    member = dp * 2 + (ctx & 1)
    members = plane_group_count()
    weight_rows = query_weight.shape[0]
    query_width = HEADS * HEAD_DIM
    kv_width = KV_HEADS * HEAD_DIM

    gains = gather_fsdp(jnp.stack([attention_gain, feedforward_gain]))
    gains = jnp.transpose(gains, (1, 0, 2)).reshape(2, width).astype(F32)
    first_gain, second_gain = gains[0], gains[1]
    inputs = tokens[0].astype(F32)
    normed_one, inverse_one = norm_rows(inputs, first_gain)
    normed_one = normed_one.astype(BF16)

    kv_mine = gather_fsdp(jnp.where(core == 0, key_weight, value_weight)).reshape(width, kv_width)
    kv_other = swap_core(kv_mine)

    mine = lax.all_gather(
        jnp.where(core == 0, query_weight, output_weight), "fsdp", axis=0, tiled=True
    )
    other = swap_core(mine)
    query_full = jnp.where(core == 0, mine, other)
    output_full = jnp.where(core == 0, other, mine)

    hidden = gate_weight.shape[1]
    shard_hidden = hidden // shard_count
    piece = shard_hidden // members

    def columns_of(weight):
        grid = weight.reshape(weight_rows, shard_count, members, piece)
        return lax.dynamic_index_in_dim(grid, member, 2, keepdims=False).reshape(
            weight_rows, shard_count * piece
        )

    part_hidden = shard_count * piece
    gate_up = lax.all_gather(
        jnp.concatenate([columns_of(gate_weight), columns_of(up_weight)], axis=1),
        "fsdp", axis=0, tiled=True,
    )
    down_part = lax.all_gather(
        lax.dynamic_slice_in_dim(down_weight, member * piece, piece, 0), "fsdp", axis=0, tiled=True
    )

    my_start = (ctx * shard_count + shard) * rows
    my_base = base_of(block_order, my_start[None], block_length)
    offsets = jnp.arange(rows, dtype=jnp.int32)
    positions = my_base + offsets
    cosine, sine = tables(positions)
    query_pos = jnp.concatenate([positions] * GROUPS)[None, :]
    starts = jnp.stack(
        [((ctx ^ d) * shard_count + (shard ^ r)) * rows
         for d in range(ctx_count) for r in range(shard_count)]
    )
    key_pos = (base_of(block_order, starts, block_length)[:, None] + offsets[None, :]).reshape(-1, 1)

    (kv_own,) = call(
        kv_kernel, [((rows, 2 * kv_width), BF16)], normed_one, kv_mine, kv_other,
        jnp.full((1, kv_width), core, jnp.int32), cosine, sine,
        flops=4 * rows * width * kv_width, name="keys_values",
    )
    near = [kv_own] + [swap(kv_own, "fsdp", r) for r in range(1, shard_count)]
    rest = jnp.concatenate(near[1:], axis=0)
    blocks = list(near)
    for d in range(1, ctx_count):
        blocks += [swap(kv_own, "ctx", d), swap(rest, "ctx", d)]
    kv_all = jnp.concatenate(blocks, axis=0)

    query_raw = dot_plain(normed_one, query_full)
    key_count = kv_all.shape[0]
    chunk = rows * 2
    attention_flops = 2 * HEADS * rows * key_count * HEAD_DIM
    attended_low, queries, attended_turned, log_total = call(
        functools.partial(forward_kernel, chunk),
        [
            ((rows, query_width), BF16),
            ((rows, query_width), BF16),
            ((KV_HEADS, HEAD_DIM, GROUPS * rows), F32),
            ((KV_HEADS, GROUPS * rows), F32),
        ],
        query_raw, kv_all, key_pos, query_pos, cosine, sine,
        flops=8 * attention_flops, name="attention_forward",
    )

    residual = inputs + dot_plain(attended_low, output_full)
    normed_two, inverse_two = norm_rows(residual, second_gain)
    normed_two = normed_two.astype(BF16)

    cot_a = jnp.concatenate(own_and_chips(cotangent[0]), axis=0)
    cot_b = swap_core(cot_a)
    normed_a = jnp.concatenate(own_and_chips(normed_two), axis=0)
    normed_b = swap_core(normed_a)

    def feed_forward(normed, cot):
        gate_value_up = dot_plain(normed, gate_up)
        gate_value, upward = gate_value_up[:, :part_hidden], gate_value_up[:, part_hidden:]
        sigmoid_gate = jax.nn.sigmoid(gate_value)
        activated = (gate_value * sigmoid_gate * upward).astype(BF16)
        act_grad = dot_last(cot, down_part)
        gate_grad = act_grad * upward * sigmoid_gate * (1.0 + gate_value * (1.0 - sigmoid_gate))
        up_grad = act_grad * gate_value * sigmoid_gate
        both = jnp.concatenate([gate_grad.astype(BF16), up_grad.astype(BF16)], axis=1)
        return activated, both

    act_b, both_b = feed_forward(normed_b, cot_b)
    act_a, both_a = feed_forward(normed_a, cot_a)

    def sum_plane(part_b, part_a):
        from_core = swap_core(part_b.astype(BF16))
        chips = (part_a + from_core.astype(F32)).reshape(4, rows, width)
        low = chips.astype(BF16)
        total = chips[0]
        for k, (a, b) in enumerate(CHIP_MASKS):
            total = total + swap_plane(low[k + 1], a, b).astype(F32)
        return total

    normed_two_grad = sum_plane(dot_last(both_b, gate_up), dot_last(both_a, gate_up))
    result = residual + sum_plane(dot_plain(act_b, down_part), dot_plain(act_a, down_part))
    normed_ab = jnp.concatenate([normed_a, normed_b], axis=0)
    both_ab = jnp.concatenate([both_a, both_b], axis=0)
    act_ab = jnp.concatenate([act_a, act_b], axis=0)
    cot_ab = jnp.concatenate([cot_a, cot_b], axis=0)
    gate_up_grad = dot_first(normed_ab, both_ab).astype(BF16)
    down_grad = dot_first(act_ab, cot_ab).astype(BF16)
    gate_up_share = sum_far(lax.psum_scatter(gate_up_grad, "fsdp", scatter_dimension=0, tiled=True))
    down_share = sum_far(lax.psum_scatter(down_grad, "fsdp", scatter_dimension=0, tiled=True))
    group_axes = ("dp", "ctx")
    groups = [
        [d * ctx_count + c for d in range(lax.axis_size("dp")) for c in (first, first + 1)]
        for first in range(0, ctx_count, 2)
    ]
    extra = {} if ctx_count == 2 else {"axis_index_groups": groups}
    gate_up_all = lax.all_gather(gate_up_share, group_axes, axis=0, tiled=False, **extra)
    down_all = lax.all_gather(down_share, group_axes, axis=0, tiled=True, **extra)
    gate_up_all = gate_up_all.reshape(members, weight_rows, 2, shard_count, piece)
    gate_up_all = jnp.transpose(gate_up_all, (2, 1, 3, 0, 4)).reshape(2, weight_rows, hidden)
    gate_weight_grad = gate_up_all[0].astype(F32)
    up_weight_grad = gate_up_all[1].astype(F32)
    down_weight_grad = down_all.astype(F32)

    second_gain_grad = jnp.sum(normed_two_grad * residual * inverse_two, axis=0)
    residual_grad = cotangent[0].astype(F32) + norm_back(
        normed_two_grad, residual, inverse_two, second_gain
    )
    residual_low = residual_grad.astype(BF16)
    attended_grad = dot_last(residual_low, output_full).astype(BF16)
    output_grad = dot_first(attended_low, residual_low).astype(BF16)

    query_low, kv_grad = call(
        functools.partial(backward_kernel, chunk),
        [((rows, query_width), BF16), ((key_count, 2 * kv_width), BF16)],
        queries, kv_all, key_pos, query_pos, cosine, sine, attended_turned, log_total,
        attended_grad,
        flops=20 * attention_flops, name="attention_backward",
    )
    blocks = kv_grad.reshape(ctx_count, shard_count, rows, 2 * kv_width)
    near = blocks[0].astype(F32)
    for d in range(1, ctx_count):
        near = near + swap(blocks[d], "ctx", d).astype(F32)
    near = near.astype(BF16)
    (kv_low,) = call(
        kv_back_kernel, [((rows, 2 * kv_width), BF16)],
        near[0], *[swap(near[r], "fsdp", r) for r in range(1, shard_count)], cosine, sine,
        name="keys_values_back",
    )
    key_low, value_low = kv_low[:, :kv_width], kv_low[:, kv_width:]

    def sum_halves(grad):
        n = grad.shape[1]
        half = weight_rows // 2
        grid = grad.reshape(shard_count, 2, half, n)
        keep = lax.dynamic_index_in_dim(grid, core, 1, keepdims=False)
        send = lax.dynamic_index_in_dim(grid, 1 - core, 1, keepdims=False)
        both = (keep.astype(F32) + swap_core(send).astype(F32)).astype(BF16)
        low = sum_chips(scatter_fsdp(both).astype(BF16))
        low = sum_far(low).astype(BF16)
        away = swap_core(low)
        top = jnp.where(core == 0, low, away)
        bottom = jnp.where(core == 0, away, low)
        return jnp.concatenate([top, bottom], axis=0).astype(F32)

    output_weight_grad = sum_halves(output_grad)
    query_weight_grad = sum_halves(dot_first(normed_one, query_low).astype(BF16))

    kv_low_mine = jnp.where(core == 0, key_low, value_low)
    kv_low_other = jnp.where(core == 0, value_low, key_low)
    normed_one_grad = (
        dot_last(query_low, query_full)
        + dot_last(kv_low_mine, kv_mine)
        + dot_last(kv_low_other, kv_other)
    )
    first_gain_grad = jnp.sum(normed_one_grad * inputs * inverse_one, axis=0)
    input_grad = residual_grad + norm_back(normed_one_grad, inputs, inverse_one, first_gain)

    extra_rows = 8

    def packed(low, gain_grad):
        grid = dot_first(normed_one, low).reshape(shard_count, weight_rows, kv_width)
        gain = gain_grad.reshape(shard_count, 1, weight_rows)
        gain = jnp.pad(gain, ((0, 0), (0, extra_rows - 1), (0, kv_width - weight_rows)))
        return jnp.concatenate([grid.astype(BF16), gain.astype(BF16)], axis=1)

    keep = packed(kv_low_mine, jnp.where(core == 0, first_gain_grad, second_gain_grad))
    send = packed(kv_low_other, jnp.where(core == 0, second_gain_grad, first_gain_grad))
    both = (keep.astype(F32) + swap_core(send).astype(F32)).astype(BF16)
    low = sum_chips(scatter_fsdp(both).astype(BF16))
    low = sum_far(low).astype(BF16)
    away = swap_core(low)
    first = jnp.where(core == 0, low, away).astype(F32)
    second = jnp.where(core == 0, away, low).astype(F32)

    return (
        result[None],
        input_grad[None],
        first[weight_rows, :weight_rows],
        query_weight_grad,
        first[:weight_rows],
        second[:weight_rows],
        output_weight_grad,
        second[weight_rows, :weight_rows],
        gate_weight_grad,
        up_weight_grad,
        down_weight_grad,
    )


def solution(mesh):
    row = P("fsdp", None)
    token = P("dp", ("ctx", "fsdp"), None)
    return jax.shard_map(
        on_device,
        mesh=mesh,
        in_specs=(
            token, P("dp", None), P("fsdp"), row, row, row, row, P("fsdp"), row, row, row, token,
        ),
        out_specs=(
            token, token, P("fsdp"), row, row, row, row, P("fsdp"), row, row, row,
        ),
        check_vma=False,
    )
```

```python
import functools
import math

import jax
import jax.numpy as jnp
from jax import lax
from jax.experimental import pallas as pl
from jax.experimental.pallas import tpu as pltpu
from jax.sharding import PartitionSpec as P

HEADS = 15
KV_HEADS = 5
HEAD_DIM = 64
GROUPS = HEADS // KV_HEADS
LANES = 128

EPSILON = 1e-05
ROPE_BASE = 100000.0
MASKED = -1e30

F32 = jnp.float32
BF16 = jnp.bfloat16
VMEM_LIMIT = 56 * 1024 * 1024


def dot_plain(left, right):
    return jnp.dot(left, right, preferred_element_type=F32)


def dot_last(left, right):
    return lax.dot_general(left, right, (((1,), (1,)), ((), ())), preferred_element_type=F32)


def dot_first(left, right):
    return lax.dot_general(left, right, (((0,), (0,)), ((), ())), preferred_element_type=F32)


def swap(x, axis, mask):
    count = lax.axis_size(axis)
    return lax.ppermute(x, axis, [(i, i ^ mask) for i in range(count)])


def swap_plane(x, dp_mask, ctx_mask):
    ctx_count = lax.axis_size("ctx")
    pairs = []
    for d in range(lax.axis_size("dp")):
        for c in range(ctx_count):
            pairs.append((d * ctx_count + c, (d ^ dp_mask) * ctx_count + (c ^ ctx_mask)))
    return lax.ppermute(x, ("dp", "ctx"), pairs)


def swap_core(x):
    return swap_plane(x, 1, 0)


CHIP_MASKS = ((2, 0), (0, 1), (2, 1))


def plane_pieces(x):
    mine = [x] + [swap_plane(x, a, b) for a, b in CHIP_MASKS]
    return mine, [swap_core(piece) for piece in mine]


def sum_far(x):
    count = lax.axis_size("ctx")
    if count == 2:
        return x
    groups = [list(range(0, count, 2)), list(range(1, count, 2))]
    return lax.psum(x.astype(F32), "ctx", axis_index_groups=groups).astype(x.dtype)


def call(kernel, spots, args, out_shapes, scratch=(), flops=0, name=None):
    specs = [pl.BlockSpec(memory_space=pltpu.SMEM)]
    specs += [pl.BlockSpec(memory_space=pltpu.VMEM) for _ in args]
    outs = tuple(jax.ShapeDtypeStruct(s, d) for s, d in out_shapes)
    bytes_all = sum(a.size * a.dtype.itemsize for a in args) + sum(
        math.prod(s) * jnp.dtype(d).itemsize for s, d in out_shapes
    )
    return pl.pallas_call(
        kernel,
        out_shape=outs,
        in_specs=specs,
        out_specs=tuple(pl.BlockSpec(memory_space=pltpu.VMEM) for _ in outs),
        scratch_shapes=[pltpu.VMEM(s, d) for s, d in scratch],
        compiler_params=pltpu.CompilerParams(vmem_limit_bytes=VMEM_LIMIT),
        cost_estimate=pl.CostEstimate(flops=flops, bytes_accessed=bytes_all, transcendentals=0),
        name=name,
    )(spots, *args)


def split_refs(refs, *counts):
    out, at = [], 0
    for n in counts:
        out.append(refs[at : at + n])
        at += n
    assert at == len(refs)
    return out


def lane_blocks(values, count):
    size = values.shape[1] // count
    return [values[:, i * size : (i + 1) * size] for i in range(count)]


def join_lanes(ref):
    return jnp.concatenate([ref[i] for i in range(ref.shape[0])], axis=1)


def rope_lanes(values, cosine, sine):
    rows, width = values.shape
    lane = lax.broadcasted_iota(jnp.int32, (rows, LANES), 1)
    first_half = (lane % HEAD_DIM) < (HEAD_DIM // 2)
    out = []
    for start in range(0, width, LANES):
        piece = values[:, start : min(start + LANES, width)]
        size = piece.shape[1]
        if size < LANES:
            piece = jnp.concatenate([piece, jnp.zeros((rows, LANES - size), piece.dtype)], axis=1)
        ahead = pltpu.roll(piece, LANES - HEAD_DIM // 2, 1)
        behind = pltpu.roll(piece, HEAD_DIM // 2, 1)
        partner = jnp.where(first_half, ahead, behind)
        out.append((piece * cosine + partner * sine)[:, :size])
    return jnp.concatenate(out, axis=1)


def heads_of(ref, first, count, rows=None):
    out = []
    for h in range(first, first + count):
        start = (h * HEAD_DIM) // LANES * LANES
        stop = min(start + LANES, ref.shape[-1])
        pair = ref[:, start:stop] if rows is None else ref[rows, start:stop]
        at = h * HEAD_DIM - start
        out.append(pair[:, at : at + HEAD_DIM])
    return out[0] if count == 1 else jnp.concatenate(out, axis=0)


def stack_rows(scratch, pieces):
    rows = pieces[0].shape[0]
    for i, piece in enumerate(pieces):
        scratch[i * rows : (i + 1) * rows, :] = piece[...]


def norm_rows(values, gain):
    inverse = lax.rsqrt(jnp.mean(values * values, axis=-1, keepdims=True) + EPSILON)
    return (values * inverse * gain, inverse)


def norm_back(gradient, values, inverse, gain):
    scaled = gradient * gain
    inner_mean = jnp.mean(scaled * values, axis=-1, keepdims=True)
    return inverse * scaled - values * (inverse * inverse * inverse) * inner_mean


EXTRA_ROWS = 16


def pack_kernel(shards, members, spots, gate_ref, up_ref, down_ref, out_ref):
    member = spots[3]
    span = gate_ref.shape[1] // shards
    piece = span // members
    rows = gate_ref.shape[0]
    pick = (
        lax.broadcasted_iota(jnp.int32, (span, piece), 0)
        == lax.broadcasted_iota(jnp.int32, (span, piece), 1) + member * piece
    ).astype(BF16)
    out = []
    for ref in (gate_ref, up_ref):
        for z in range(shards):
            out.append(dot_plain(ref[:, z * span : (z + 1) * span], pick))
    own = down_ref[pl.ds(pl.multiple_of(member * piece, piece), piece), :]
    folds = rows // piece
    down = jnp.concatenate(lane_blocks(own, folds), axis=0)
    both = jnp.concatenate(out, axis=1).astype(BF16)
    out_ref[...] = jnp.concatenate([both, down], axis=1)


def begin_kernel(shards, spots, *refs):
    ins, outs, scratch = split_refs(refs, 7 + 2 * (shards - 1), 4, 3)
    tokens_ref, gain_one, gain_two, key_ref, value_ref, cos_ref, sin_ref = ins[:7]
    mine, other = split_refs(ins[7:], shards - 1, shards - 1)
    kv_ref, normed_ref, inverse_ref, gains_ref = outs
    blocks, normed_blocks, gain_blocks = scratch
    core, shard = spots[0], spots[1]
    rows = key_ref.shape[0]
    values = tokens_ref[...].astype(F32)
    inverse = lax.rsqrt(jnp.mean(values * values, axis=-1, keepdims=True) + EPSILON)
    inverse_ref[...] = inverse
    for z, block in enumerate(lane_blocks(values * inverse, shards)):
        blocks[z] = block
    sums = []
    for r in range(shards):
        at = shard ^ r
        if r == 0:
            pair = jnp.concatenate([gain_one[...], gain_two[...]], axis=0).astype(F32)
        else:
            pair = mine[r - 1][rows : rows + EXTRA_ROWS, :rows].astype(F32)[0:2, :]
        gain_blocks[at, 0:2, :] = pair
        normed = (blocks[at] * pair[0:1, :]).astype(BF16)
        normed_blocks[at] = normed
        left = key_ref[...] if r == 0 else mine[r - 1][:rows, :]
        right = value_ref[...] if r == 0 else other[r - 1][:rows, :]
        sums.append((dot_plain(normed, left), dot_plain(normed, right)))
    first = sum(s[0] for s in sums[1:])
    second = sum(s[1] for s in sums[1:])
    keys = jnp.where(core == 0, first, second) + sums[0][0]
    vals = jnp.where(core == 0, second, first) + sums[0][1]
    keys = rope_lanes(keys, cos_ref[...], sin_ref[...])
    kv_ref[...] = jnp.concatenate([keys, vals], axis=1).astype(BF16)
    normed_ref[...] = join_lanes(normed_blocks)
    gains_ref[...] = jnp.zeros_like(gains_ref)
    gains_ref[0:2, :] = jnp.concatenate([gain_blocks[z][0:2, :] for z in range(shards)], axis=1)


def attend(chunk, head, kv_ref, key_pos_ref, query_pos, stacked, state):
    def step(j, state):
        largest, total, weighted = state
        at = pl.ds(pl.multiple_of(j * chunk, chunk), chunk)
        keys = heads_of(kv_ref, head, 1, at)
        values = heads_of(kv_ref, KV_HEADS + head, 1, at)
        scores = dot_last(keys, stacked)
        scores = jnp.where(key_pos_ref[at, :] <= query_pos, scores, MASKED)
        new_largest = jnp.maximum(largest, jnp.max(scores, axis=0, keepdims=True))
        weights = jnp.exp(scores - new_largest)
        factor = jnp.exp(largest - new_largest)
        total = total * factor + jnp.sum(weights, axis=0, keepdims=True)
        weighted = weighted * factor + dot_first(values, weights.astype(BF16))
        return new_largest, total, weighted

    return lax.fori_loop(0, kv_ref.shape[0] // chunk, step, state)


def near_kernel(chunk, members, pieces, spots, *refs):
    ins, outs, scratch = split_refs(refs, 5 + members + pieces, 4, 2)
    normed_ref, key_pos_ref, query_pos_ref, cos_ref, sin_ref = ins[:5]
    weights, parts = split_refs(ins[5:], members, pieces)
    queries_ref, largest_ref, total_ref, weighted_ref = outs
    blocks, kv_ref = scratch
    dp = spots[2]
    stack_rows(kv_ref, parts)
    for j in range(members):
        blocks[dp ^ j] = dot_plain(normed_ref[...], weights[j][...])
    roped = rope_lanes(join_lanes(blocks), cos_ref[...], sin_ref[...]).astype(BF16)
    queries_ref[...] = roped * jnp.asarray(1.0 / math.sqrt(HEAD_DIM), BF16)
    columns = GROUPS * queries_ref.shape[0]
    query_pos = query_pos_ref[...]
    for head in range(KV_HEADS):
        stacked = heads_of(queries_ref, head * GROUPS, GROUPS)
        start = (
            jnp.full((1, columns), MASKED, F32),
            jnp.zeros((1, columns), F32),
            jnp.zeros((HEAD_DIM, columns), F32),
        )
        largest, total, weighted = attend(
            chunk, head, kv_ref, key_pos_ref, query_pos, stacked, start
        )
        largest_ref[head : head + 1, :] = largest
        total_ref[head : head + 1, :] = total
        weighted_ref[head] = weighted


def far_kernel(chunk, members, pieces, spots, *refs):
    ins, outs, scratch = split_refs(refs, 8 + members + pieces, 6, 2)
    (queries_ref, key_pos_ref, query_pos_ref, largest_ref, total_ref, weighted_ref, tokens_ref,
     gains_ref) = ins[:8]
    weights, parts = split_refs(ins[8:], members, pieces)
    attended_ref, turned_ref, log_ref, residual_ref, inverse_ref, normed_ref = outs
    blocks, kv_ref = scratch
    dp = spots[2]
    stack_rows(kv_ref, parts)
    rows = queries_ref.shape[0]
    query_pos = query_pos_ref[...]
    heads = []
    for head in range(KV_HEADS):
        stacked = heads_of(queries_ref, head * GROUPS, GROUPS)
        start = (largest_ref[head : head + 1, :], total_ref[head : head + 1, :], weighted_ref[head])
        largest, total, weighted = attend(
            chunk, head, kv_ref, key_pos_ref, query_pos, stacked, start
        )
        turned = weighted / total
        turned_ref[head] = turned
        log_ref[head : head + 1, :] = largest + jnp.log(total)
        straight = turned.T
        heads += [straight[g * rows : (g + 1) * rows, :] for g in range(GROUPS)]
    attended = jnp.concatenate(heads, axis=1).astype(BF16)
    attended_ref[...] = attended
    for j in range(members):
        blocks[dp ^ j] = dot_plain(attended, weights[j][...])
    residual = tokens_ref[...].astype(F32) + join_lanes(blocks)
    residual_ref[...] = residual
    normed, inverse = norm_rows(residual, gains_ref[1:2, :])
    inverse_ref[...] = inverse
    normed_ref[...] = normed.astype(BF16)


def unfold_down(pack_ref, down_ref, shards, part):
    piece = part // shards
    folds = (pack_ref.shape[0] // shards) // piece
    for z in range(shards):
        base = z * folds * piece
        down_ref[z * piece : (z + 1) * piece, :] = jnp.concatenate(
            [pack_ref[base + b * piece : base + (b + 1) * piece, 2 * part :] for b in range(folds)],
            axis=1,
        )


def feed_kernel(shards, pieces, spots, *refs):
    ins, outs, scratch = split_refs(refs, 1 + 2 * pieces, pieces + 2, 3)
    pack_ref = ins[0]
    normed_parts, cot_parts = split_refs(ins[1:], pieces, pieces)
    grads, (act_ref, both_ref) = outs[:pieces], outs[pieces:]
    normed_ref, cot_ref, down_ref = scratch
    part = pack_ref.shape[1] // 3
    rows = normed_parts[0].shape[0]
    stack_rows(normed_ref, normed_parts)
    stack_rows(cot_ref, cot_parts)
    unfold_down(pack_ref, down_ref, shards, part)
    gate_up = dot_plain(normed_ref[...], pack_ref[:, : 2 * part])
    gate, upward = gate_up[:, :part], gate_up[:, part:]
    act_grad = dot_last(cot_ref[...], down_ref[...])
    sigmoid_gate = jax.nn.sigmoid(gate)
    silu = gate * sigmoid_gate
    act_ref[...] = (silu * upward).astype(BF16)
    gate_grad = act_grad * upward * sigmoid_gate * (1.0 + gate * (1.0 - sigmoid_gate))
    both_ref[...] = jnp.concatenate([gate_grad, act_grad * silu], axis=1).astype(BF16)
    grad = dot_last(both_ref[...], pack_ref[:, : 2 * part])
    for i in range(pieces):
        grads[i][...] = grad[i * rows : (i + 1) * rows, :].astype(BF16)


def feed_weights_kernel(shards, pieces, spots, *refs):
    ins, outs, scratch = split_refs(refs, 5 + 2 * pieces, pieces + 1, 5)
    pack_ref, act_a, act_b, both_a, both_b = ins[:5]
    normed_parts, cot_parts = split_refs(ins[5:], pieces, pieces)
    results, grad_ref = outs[:pieces], outs[pieces]
    normed_ref, cot_ref, act_ref, both_ref, down_ref = scratch
    part = pack_ref.shape[1] // 3
    piece = part // shards
    rows = normed_parts[0].shape[0]
    stack_rows(normed_ref, normed_parts)
    stack_rows(cot_ref, cot_parts)
    stack_rows(act_ref, (act_a, act_b))
    stack_rows(both_ref, (both_a, both_b))
    unfold_down(pack_ref, down_ref, shards, part)
    grad_ref[:, : 2 * part] = dot_first(normed_ref[...], both_ref[...]).astype(BF16)
    down_grad = dot_first(act_ref[...], cot_ref[...]).astype(BF16)
    folds = (grad_ref.shape[0] // shards) // piece
    for z in range(shards):
        rows_of = down_grad[z * piece : (z + 1) * piece, :]
        for b, block in enumerate(lane_blocks(rows_of, folds)):
            base = (z * folds + b) * piece
            grad_ref[base : base + piece, 2 * part :] = block
    result = dot_plain(act_ref[...], down_ref[...])
    for i in range(pieces):
        results[i][...] = result[i * rows : (i + 1) * rows, :].astype(BF16)


def middle_kernel(members, spots, *refs):
    ins, outs, scratch = split_refs(refs, 9 + members, 4, 1)
    own_a, own_b, one_ref, two_ref, three_ref, residual_ref, inverse_ref, cot_ref, gains_ref = ins[:9]
    weights = ins[9:]
    residual_grad_ref, low_ref, attended_grad_ref, gain_grad_ref = outs
    (blocks,) = scratch
    dp = spots[2]
    grad = (own_a[...].astype(F32) + own_b[...].astype(F32)) + one_ref[...].astype(F32)
    grad = grad + two_ref[...].astype(F32) + three_ref[...].astype(F32)
    residual, inverse = residual_ref[...], inverse_ref[...]
    gain_grad_ref[...] = jnp.sum(grad * residual * inverse, axis=0, keepdims=True)
    residual_grad = cot_ref[...].astype(F32) + norm_back(grad, residual, inverse, gains_ref[1:2, :])
    residual_grad_ref[...] = residual_grad
    low = residual_grad.astype(BF16)
    low_ref[...] = low
    for i, block in enumerate(lane_blocks(low, members)):
        blocks[i] = block
    attended_grad_ref[...] = sum(
        dot_last(blocks[dp ^ j], weights[j][...]) for j in range(members)
    ).astype(BF16)


def halves_by_core(core, values):
    low, high = lane_blocks(values, 2)
    return jnp.where(core == 0, low, high), jnp.where(core == 0, high, low)


def output_grad_kernel(spots, attended_ref, low_ref, keep_ref, send_ref):
    keep, send = halves_by_core(spots[0], low_ref[...].astype(F32))
    attended = attended_ref[...]
    send_ref[...] = dot_first(attended, send.astype(BF16)).astype(BF16)
    keep_ref[...] = dot_first(attended, keep.astype(BF16)).astype(BF16)


def query_grad_kernel(members, spots, normed_ref, low_ref, *refs):
    weights, (keep_ref, send_ref, back_ref), (blocks,) = split_refs(refs, members, 3, 1)
    dp = spots[2]
    low = low_ref[...]
    keep, send = halves_by_core(spots[0], low.astype(F32))
    normed = normed_ref[...]
    send_ref[...] = dot_first(normed, send.astype(BF16)).astype(BF16)
    keep_ref[...] = dot_first(normed, keep.astype(BF16)).astype(BF16)
    for i, block in enumerate(lane_blocks(low, members)):
        blocks[i] = block
    back_ref[...] = sum(dot_last(blocks[dp ^ j], weights[j][...]) for j in range(members))


def back_kernel(chunk, pieces, first, last, spots, *refs):
    ins, outs, scratch = split_refs(refs, 9 + pieces, pieces + 1, 2)
    (queries_ref, key_pos_ref, query_pos_ref, cos_ref, sin_ref, turned_ref, log_ref, grad_ref,
     start_ref) = ins[:9]
    parts = ins[9:]
    query_grad_ref, kv_grads = outs[0], outs[1:]
    kv_ref, kv_grad_ref = scratch
    stack_rows(kv_ref, parts)
    rows = queries_ref.shape[0]
    columns = GROUPS * rows
    query_pos = query_pos_ref[...]
    heads = []
    for head in range(KV_HEADS):
        stacked = heads_of(queries_ref, head * GROUPS, GROUPS)
        upstream = heads_of(grad_ref, head * GROUPS, GROUPS)
        delta = jnp.sum(upstream.astype(F32).T * turned_ref[head], axis=0, keepdims=True)
        log_total = log_ref[head : head + 1, :]
        keys_at = head * HEAD_DIM
        values_at = (KV_HEADS + head) * HEAD_DIM

        def step(j, query_grad, head=head, stacked=stacked, upstream=upstream,
                 delta=delta, log_total=log_total, keys_at=keys_at, values_at=values_at):
            at = pl.ds(pl.multiple_of(j * chunk, chunk), chunk)
            keys = heads_of(kv_ref, head, 1, at)
            values = heads_of(kv_ref, KV_HEADS + head, 1, at)
            scores = dot_last(keys, stacked)
            scores = jnp.where(key_pos_ref[at, :] <= query_pos, scores, MASKED)
            weights = jnp.exp(scores - log_total)
            weight_grad = dot_last(values, upstream)
            score_grad = (weights * (weight_grad - delta)).astype(BF16)
            value_grad = dot_plain(weights.astype(BF16), upstream)
            key_grad = dot_plain(score_grad, stacked)
            kv_grad_ref[at, keys_at : keys_at + HEAD_DIM] = key_grad.astype(BF16)
            kv_grad_ref[at, values_at : values_at + HEAD_DIM] = value_grad.astype(BF16)
            return query_grad + dot_first(keys, score_grad)

        start = jnp.zeros((HEAD_DIM, columns), F32) if first else start_ref[head]
        query_grad = lax.fori_loop(0, kv_ref.shape[0] // chunk, step, start)
        if not last:
            query_grad_ref[head] = query_grad
        else:
            straight = query_grad.T * (1.0 / math.sqrt(HEAD_DIM))
            heads += [straight[g * rows : (g + 1) * rows, :] for g in range(GROUPS)]
    if last:
        query_grad_ref[...] = rope_lanes(
            jnp.concatenate(heads, axis=1), cos_ref[...], -sin_ref[...]
        ).astype(BF16)
    for i in range(pieces):
        kv_grads[i][...] = kv_grad_ref[i * rows : (i + 1) * rows, :]


def end_kernel(shards, spots, *refs):
    ins, outs, scratch = split_refs(refs, 12 + (shards + 1) + 2 * (shards - 1), 3, 1)
    (cos_ref, sin_ref, normed_ref, tokens_ref, inverse_ref, gains_ref, back_ref, residual_grad_ref,
     key_ref, value_ref, gain_two_ref, _) = ins[:12]
    sums, mine, other = split_refs(ins[12:], shards + 1, shards - 1, shards - 1)
    input_grad_ref, keep_ref, send_ref = outs
    (blocks,) = scratch
    core, shard = spots[0], spots[1]
    rows = key_ref.shape[0]
    width = key_ref.shape[1]
    total = sum(s[...].astype(F32) for s in sums)
    keys = rope_lanes(total[:, :width], cos_ref[...], -sin_ref[...])
    values = total[:, width:]
    keep = jnp.where(core == 0, keys, values).astype(BF16)
    send = jnp.where(core == 0, values, keys).astype(BF16)
    blocks[shard] = dot_last(keys.astype(BF16), key_ref[...]) + dot_last(
        values.astype(BF16), value_ref[...]
    )
    for r in range(1, shards):
        blocks[shard ^ r] = dot_last(keep, mine[r - 1][:rows, :]) + dot_last(
            send, other[r - 1][:rows, :]
        )
    normed_grad = back_ref[...] + join_lanes(blocks)
    inputs, inverse = tokens_ref[...].astype(F32), inverse_ref[...]
    gain_grad = jnp.sum(normed_grad * inputs * inverse, axis=0, keepdims=True)
    input_grad_ref[...] = residual_grad_ref[...] + norm_back(
        normed_grad, inputs, inverse, gains_ref[0:1, :]
    )
    normed = normed_ref[...]
    two = gain_two_ref[...]
    for out_ref, low, gain in (
        (send_ref, send, jnp.where(core == 0, two, gain_grad)),
        (keep_ref, keep, jnp.where(core == 0, gain_grad, two)),
    ):
        grad = dot_first(normed, low).astype(BF16)
        span = rows + EXTRA_ROWS
        for z, block in enumerate(lane_blocks(gain, shards)):
            out_ref[z * span : z * span + rows, :] = grad[z * rows : (z + 1) * rows, :]
            padded = jnp.concatenate([block, jnp.zeros((1, width - rows), F32)], axis=1)
            out_ref[z * span + rows : (z + 1) * span, :] = jnp.broadcast_to(
                padded, (EXTRA_ROWS, width)
            ).astype(BF16)


def spread_kernel(shards, members, spots, *refs):
    parts, outs, (blocks,) = split_refs(refs, members, 3, 1)
    gate_ref, up_ref, down_ref = outs
    member = spots[3]
    part = parts[0].shape[1] // 3
    piece = part // shards
    span = part // shards * members
    folds = parts[0].shape[0] // piece
    for i in range(members):
        at = member ^ i
        blocks[at] = parts[i][:, : 2 * part].astype(F32)
        down = parts[i][:, 2 * part :].astype(F32)
        down_ref[pl.ds(pl.multiple_of(at * piece, piece), piece), :] = jnp.concatenate(
            [down[b * piece : (b + 1) * piece, :] for b in range(folds)], axis=1
        )
    for which, out_ref in enumerate((gate_ref, up_ref)):
        for z in range(shards):
            at = which * part + z * piece
            out_ref[:, z * span : (z + 1) * span] = jnp.concatenate(
                [blocks[p, :, at : at + piece] for p in range(members)], axis=1
            )


def base_of(block_order, stored, block_length):
    which = stored // block_length
    count = block_order.shape[1]
    matches = (which[:, None] == jnp.arange(count, dtype=jnp.int32)[None, :]).astype(jnp.int32)
    return jnp.sum(block_order[0][None, :] * matches, axis=-1) * block_length + stored % block_length


def tables(positions):
    half_dim = HEAD_DIM // 2
    exponent = -(jnp.arange(half_dim, dtype=F32) * 2.0) / HEAD_DIM
    frequency = jnp.power(F32(ROPE_BASE), exponent)
    angles = positions.astype(F32)[:, None] * frequency
    cosine, sine = jnp.cos(angles), jnp.sin(angles)
    return (
        jnp.concatenate([cosine] * 4, axis=-1),
        jnp.concatenate([-sine, sine, -sine, sine], axis=-1),
    )


def after(x, other):
    return lax.optimization_barrier((x, other))[0]


def on_device(
    tokens,
    block_order,
    attention_gain,
    query_weight,
    key_weight,
    value_weight,
    output_weight,
    feedforward_gain,
    gate_weight,
    up_weight,
    down_weight,
    cotangent,
):
    tokens, cotangent = tokens[0], cotangent[0]
    rows, width = tokens.shape
    shards = lax.axis_size("fsdp")
    ctx_count = lax.axis_size("ctx")
    dp_count = lax.axis_size("dp")
    block_length = rows * shards * ctx_count // block_order.shape[1]
    shard = lax.axis_index("fsdp")
    ctx = lax.axis_index("ctx")
    dp = lax.axis_index("dp")
    core = dp & 1
    members = dp_count * 2
    weight_rows = query_weight.shape[0]
    query_width = HEADS * HEAD_DIM
    kv_width = KV_HEADS * HEAD_DIM
    hidden = gate_weight.shape[1]
    part = hidden // members
    spots = jnp.stack([core, shard, dp, dp * 2 + (ctx & 1)]).astype(jnp.int32)

    gain_one, gain_two = attention_gain[None, :], feedforward_gain[None, :]
    kv_pack = jnp.concatenate(
        [
            jnp.where(core == 0, key_weight, value_weight),
            jnp.pad(
                jnp.concatenate([gain_one, gain_two], axis=0),
                ((0, EXTRA_ROWS - 2), (0, kv_width - weight_rows)),
            ),
        ],
        axis=0,
    )
    kv_mine = [swap(kv_pack, "fsdp", r) for r in range(1, shards)]
    kv_other = [swap_core(piece) for piece in kv_mine]

    quarter = width // dp_count

    def spread_columns(weight):
        own = lax.all_gather(
            lax.dynamic_slice_in_dim(weight, dp * quarter, quarter, 1), "fsdp", axis=0, tiled=True
        )
        across = swap_plane(own, 2, 0)
        return [own, swap_core(own), across, swap_core(across)]

    query_parts = spread_columns(query_weight)

    offsets = jnp.arange(rows, dtype=jnp.int32)
    my_start = (ctx * shards + shard) * rows
    positions = base_of(block_order, my_start[None], block_length) + offsets
    cosine, sine = tables(positions)
    query_pos = jnp.concatenate([positions] * GROUPS)[None, :]
    starts = jnp.stack(
        [((ctx ^ d) * shards + (shard ^ r)) * rows for d in range(ctx_count) for r in range(shards)]
    )
    key_pos = (base_of(block_order, starts, block_length)[:, None] + offsets[None, :]).reshape(-1, 1)
    near_count = shards * rows
    near_pos, far_pos = key_pos[:near_count], key_pos[near_count:]
    far_count = far_pos.shape[0]

    (pack,) = call(
        functools.partial(pack_kernel, shards, members), spots,
        [gate_weight, up_weight, down_weight], [((weight_rows, 3 * part), BF16)],
        flops=4 * weight_rows * hidden * part // shards, name="pack_weights",
    )
    kv_own, normed_one, inverse_one, gains = call(
        functools.partial(begin_kernel, shards), spots,
        [tokens, gain_one, gain_two, key_weight, value_weight, cosine, sine, *kv_mine, *kv_other],
        [
            ((rows, 2 * kv_width), BF16), ((rows, width), BF16), ((rows, 1), F32), ((8, width), F32),
        ],
        scratch=[
            ((shards, rows, weight_rows), F32), ((shards, rows, weight_rows), BF16),
            ((shards, 8, weight_rows), F32),
        ],
        flops=4 * rows * width * kv_width, name="norm_keys_values",
    )
    near = [kv_own] + [swap(kv_own, "fsdp", r) for r in range(1, shards)]
    far = [swap(piece, "ctx", d) for d in range(1, ctx_count) for piece in near]

    output_parts = spread_columns(after(output_weight, kv_own))
    pack_all = lax.all_gather(after(pack, kv_own), "fsdp", axis=0, tiled=True)
    cot_a, cot_b = plane_pieces(after(cotangent, kv_own))

    chunk = rows * 2
    unit = 2 * HEADS * rows * near_count * HEAD_DIM
    stat = ((KV_HEADS, GROUPS * rows), F32)
    turned_shape = ((KV_HEADS, HEAD_DIM, GROUPS * rows), F32)
    queries, largest, total, weighted = call(
        functools.partial(near_kernel, chunk, dp_count, shards), spots,
        [normed_one, near_pos, query_pos, cosine, sine, *query_parts, *near],
        [((rows, query_width), BF16), stat, stat, turned_shape],
        scratch=[((dp_count, rows, quarter), F32), ((near_count, 2 * kv_width), BF16)],
        flops=8 * unit, name="attention_near",
    )
    attended, turned, log_total, residual, inverse_two, normed_two = call(
        functools.partial(far_kernel, chunk, dp_count, len(far)), spots,
        [
            queries, far_pos, query_pos, largest, total, weighted, tokens, gains,
            *output_parts, *far,
        ],
        [
            ((rows, query_width), BF16), turned_shape, stat, ((rows, width), F32),
            ((rows, 1), F32), ((rows, width), BF16),
        ],
        scratch=[((dp_count, rows, quarter), F32), ((far_count, 2 * kv_width), BF16)],
        flops=8 * unit * len(far) // shards, name="attention_far",
    )

    normed_a, normed_b = plane_pieces(normed_two)
    token_shape = ((rows, width), BF16)
    half = 4 * rows

    def feed(normed, cot):
        out = call(
            functools.partial(feed_kernel, shards, 4), spots, [pack_all, *normed, *cot],
            [token_shape] * 4 + [((half, part), BF16), ((half, 2 * part), BF16)],
            scratch=[((half, width), BF16), ((half, width), BF16), ((part, width), BF16)],
            flops=10 * half * width * part, name="feed_forward",
        )
        return out[:4], out[4], out[5]

    grad_b, act_b, both_b = feed(normed_b, cot_b)
    from_core = [swap_core(g) for g in grad_b]
    grad_a, act_a, both_a = feed(normed_a, cot_a)

    def send_chips(parts_a, parts_b):
        out = []
        for k, (a, b) in enumerate(CHIP_MASKS):
            both = (parts_a[k + 1].astype(F32) + parts_b[k + 1].astype(F32)).astype(BF16)
            out.append(swap_plane(both, a, b))
        return out

    grad_chips = send_chips(grad_a, from_core)
    out = call(
        functools.partial(feed_weights_kernel, shards, 8), spots,
        [pack_all, act_a, act_b, both_a, both_b, *normed_a, *normed_b, *cot_a, *cot_b],
        [token_shape] * 8 + [((width, 3 * part), BF16)],
        scratch=[
            ((2 * half, width), BF16), ((2 * half, width), BF16), ((2 * half, part), BF16),
            ((2 * half, 2 * part), BF16), ((part, width), BF16),
        ],
        flops=16 * half * width * part, name="feed_forward_weights",
    )
    result_a, result_b, pack_grad = out[:4], out[4:8], out[8]
    pack_share = sum_far(lax.psum_scatter(pack_grad, "fsdp", scatter_dimension=0, tiled=True))

    residual_grad, residual_low, attended_grad, second_gain_grad = call(
        functools.partial(middle_kernel, dp_count), spots,
        [
            grad_a[0], from_core[0], *grad_chips, residual, inverse_two, cotangent, gains,
            *output_parts,
        ],
        [((rows, width), F32), token_shape, ((rows, query_width), BF16), ((1, width), F32)],
        scratch=[((dp_count, rows, quarter), BF16)],
        flops=2 * rows * width * query_width, name="residual_back",
    )

    result_core = [swap_core(after(p, residual_low)) for p in result_b]
    result_chips = send_chips(result_a, result_core)
    result = residual + (
        (result_a[0].astype(F32) + result_core[0].astype(F32)) + result_chips[0].astype(F32)
        + (result_chips[1].astype(F32) + result_chips[2].astype(F32))
    )

    half_shape = ((width, width // 2), BF16)
    output_keep, output_send = call(
        output_grad_kernel, spots, [attended, residual_low], [half_shape, half_shape],
        flops=2 * rows * width * width, name="output_weight_grad",
    )

    def back(first, last, start, pos, pieces):
        count = pos.shape[0]
        shape = ((rows, query_width), BF16) if last else turned_shape
        out = call(
            functools.partial(back_kernel, chunk, len(pieces), first, last), spots,
            [
                queries, pos, query_pos, cosine, sine, turned, log_total, attended_grad, start,
                *pieces,
            ],
            [shape] + [((rows, 2 * kv_width), BF16)] * len(pieces),
            scratch=[((count, 2 * kv_width), BF16), ((count, 2 * kv_width), BF16)],
            flops=20 * unit * len(pieces) // shards,
            name="attention_back_near" if last else "attention_back_far",
        )
        return out[0], out[1:]

    query_partial, far_grads = turned, []
    for d in range(1, ctx_count):
        at = (d - 1) * shards
        query_partial, grads = back(
            d == 1, False, query_partial, far_pos[at * rows : (at + shards) * rows],
            far[at : at + shards],
        )
        far_grads += grads
    home = [
        [swap(far_grads[(d - 1) * shards + r], "ctx", d) for d in range(1, ctx_count)]
        for r in range(shards)
    ]
    query_low, near_grads = back(False, True, query_partial, near_pos, near)
    kv_sums = [
        near_grads[r].astype(F32) + sum(h.astype(F32) for h in home[r]) for r in range(shards)
    ]
    kv_arrived = [swap(kv_sums[r].astype(BF16), "fsdp", r) for r in range(1, shards)]

    def pieces_of(keep, arrived, span):
        out = []
        for r in range(shards):
            at = (shard ^ r) * span
            mine = lax.dynamic_slice_in_dim(keep, at, span, 0).astype(F32)
            theirs = lax.dynamic_slice_in_dim(arrived, at, span, 0).astype(F32)
            out.append((mine + theirs).astype(BF16))
        return out

    def sum_devices(keep, send, span):
        pieces = pieces_of(keep, swap_core(send), span)
        total = pieces[0].astype(F32)
        for r in range(1, shards):
            total = total + swap(pieces[r], "fsdp", r).astype(F32)
        own = total.astype(BF16)
        across, along, diagonal = [swap_plane(own, a, b) for a, b in CHIP_MASKS]
        total = (own.astype(F32) + across.astype(F32)) + (
            along.astype(F32) + diagonal.astype(F32)
        )
        low = sum_far(total.astype(BF16))
        away = swap_core(low)
        return (
            jnp.where(core == 0, low, away).astype(F32), jnp.where(core == 0, away, low).astype(F32)
        )

    output_weight_grad = jnp.concatenate(sum_devices(output_keep, output_send, weight_rows), axis=1)

    query_keep, query_send, query_back = call(
        functools.partial(query_grad_kernel, dp_count), spots,
        [normed_one, query_low, *query_parts],
        [half_shape, half_shape, ((rows, width), F32)],
        scratch=[((dp_count, rows, quarter), BF16)],
        flops=4 * rows * width * width, name="query_weight_grad",
    )
    query_weight_grad = jnp.concatenate(sum_devices(query_keep, query_send, weight_rows), axis=1)

    span = weight_rows + EXTRA_ROWS
    packed_shape = ((shards * span, kv_width), BF16)
    input_grad, kv_keep, kv_send = call(
        functools.partial(end_kernel, shards), spots,
        [
            cosine, sine, normed_one, tokens, inverse_one, gains, query_back, residual_grad,
            key_weight, value_weight, second_gain_grad, gain_one,
            near_grads[0], sum(h.astype(F32) for h in home[0]), *kv_arrived, *kv_mine, *kv_other,
        ],
        [((rows, width), F32), packed_shape, packed_shape],
        scratch=[((shards, rows, weight_rows), F32)],
        flops=8 * rows * width * kv_width, name="keys_values_back",
    )
    first, second = sum_devices(kv_keep, kv_send, span)

    share_a, share_b = plane_pieces(pack_share)
    share_by_mask = [None] * members
    for k, (a, b) in enumerate(((0, 0),) + CHIP_MASKS):
        share_by_mask[2 * a + b] = share_a[k]
        share_by_mask[2 * (a ^ 1) + b] = share_b[k]
    gate_weight_grad, up_weight_grad, down_weight_grad = call(
        functools.partial(spread_kernel, shards, members), spots, share_by_mask,
        [
            ((weight_rows, hidden), F32), ((weight_rows, hidden), F32),
            ((down_weight.shape[0], width), F32),
        ],
        scratch=[((members, weight_rows, 2 * part), F32)],
        name="feed_forward_out",
    )

    return (
        result[None],
        input_grad[None],
        first[weight_rows, :weight_rows],
        query_weight_grad,
        first[:weight_rows],
        second[:weight_rows],
        output_weight_grad,
        second[weight_rows, :weight_rows],
        gate_weight_grad,
        up_weight_grad,
        down_weight_grad,
    )


def solution(mesh):
    row = P("fsdp", None)
    token = P("dp", ("ctx", "fsdp"), None)
    return jax.shard_map(
        on_device,
        mesh=mesh,
        in_specs=(
            token, P("dp", None), P("fsdp"), row, row, row, row, P("fsdp"), row, row, row, token,
        ),
        out_specs=(
            token, token, P("fsdp"), row, row, row, row, P("fsdp"), row, row, row,
        ),
        check_vma=False,
    )
```

```python
import functools
import math

import jax
import jax.numpy as jnp
from jax import lax
from jax.experimental import pallas as pl
from jax.experimental.pallas import tpu as pltpu
from jax.sharding import PartitionSpec as P

HEADS = 15
KV_HEADS = 5
HEAD_DIM = 64
GROUPS = HEADS // KV_HEADS
LANES = 128

EPSILON = 1e-05
ROPE_BASE = 100000.0
MASKED = -1e30

F32 = jnp.float32
BF16 = jnp.bfloat16
VMEM_LIMIT = 56 * 1024 * 1024


def dot_plain(left, right):
    return jnp.dot(left, right, preferred_element_type=F32)


def dot_last(left, right):
    return lax.dot_general(left, right, (((1,), (1,)), ((), ())), preferred_element_type=F32)


def dot_first(left, right):
    return lax.dot_general(left, right, (((0,), (0,)), ((), ())), preferred_element_type=F32)


def swap(x, axis, mask):
    count = lax.axis_size(axis)
    return lax.ppermute(x, axis, [(i, i ^ mask) for i in range(count)])


def swap_plane(x, dp_mask, ctx_mask):
    ctx_count = lax.axis_size("ctx")
    pairs = []
    for d in range(lax.axis_size("dp")):
        for c in range(ctx_count):
            pairs.append((d * ctx_count + c, (d ^ dp_mask) * ctx_count + (c ^ ctx_mask)))
    return lax.ppermute(x, ("dp", "ctx"), pairs)


def swap_core(x):
    return swap_plane(x, 1, 0)


CHIP_MASKS = ((2, 0), (0, 1), (2, 1))


def plane_pieces(x):
    mine = [x] + [swap_plane(x, a, b) for a, b in CHIP_MASKS]
    return mine, [swap_core(piece) for piece in mine]


def sum_far(x):
    count = lax.axis_size("ctx")
    if count == 2:
        return x
    groups = [list(range(0, count, 2)), list(range(1, count, 2))]
    return lax.psum(x.astype(F32), "ctx", axis_index_groups=groups).astype(x.dtype)


def call(kernel, spots, args, out_shapes, scratch=(), flops=0, name=None):
    specs = [pl.BlockSpec(memory_space=pltpu.SMEM)]
    specs += [pl.BlockSpec(memory_space=pltpu.VMEM) for _ in args]
    outs = tuple(jax.ShapeDtypeStruct(s, d) for s, d in out_shapes)
    bytes_all = sum(a.size * a.dtype.itemsize for a in args) + sum(
        math.prod(s) * jnp.dtype(d).itemsize for s, d in out_shapes
    )
    return pl.pallas_call(
        kernel,
        out_shape=outs,
        in_specs=specs,
        out_specs=tuple(pl.BlockSpec(memory_space=pltpu.VMEM) for _ in outs),
        scratch_shapes=[pltpu.VMEM(s, d) for s, d in scratch],
        compiler_params=pltpu.CompilerParams(vmem_limit_bytes=VMEM_LIMIT),
        cost_estimate=pl.CostEstimate(flops=flops, bytes_accessed=bytes_all, transcendentals=0),
        name=name,
    )(spots, *args)


def split_refs(refs, *counts):
    out, at = [], 0
    for n in counts:
        out.append(refs[at : at + n])
        at += n
    assert at == len(refs)
    return out


def lane_blocks(values, count):
    size = values.shape[1] // count
    return [values[:, i * size : (i + 1) * size] for i in range(count)]


def join_lanes(ref):
    return jnp.concatenate([ref[i] for i in range(ref.shape[0])], axis=1)


def rope_lanes(values, cosine, sine):
    rows, width = values.shape
    lane = lax.broadcasted_iota(jnp.int32, (rows, LANES), 1)
    first_half = (lane % HEAD_DIM) < (HEAD_DIM // 2)
    out = []
    for start in range(0, width, LANES):
        piece = values[:, start : min(start + LANES, width)]
        size = piece.shape[1]
        if size < LANES:
            piece = jnp.concatenate([piece, jnp.zeros((rows, LANES - size), piece.dtype)], axis=1)
        ahead = pltpu.roll(piece, LANES - HEAD_DIM // 2, 1)
        behind = pltpu.roll(piece, HEAD_DIM // 2, 1)
        partner = jnp.where(first_half, ahead, behind)
        out.append((piece * cosine + partner * sine)[:, :size])
    return jnp.concatenate(out, axis=1)


def heads_of(ref, first, count, rows=None):
    out = []
    for h in range(first, first + count):
        start = (h * HEAD_DIM) // LANES * LANES
        stop = min(start + LANES, ref.shape[-1])
        pair = ref[:, start:stop] if rows is None else ref[rows, start:stop]
        at = h * HEAD_DIM - start
        out.append(pair[:, at : at + HEAD_DIM])
    return out[0] if count == 1 else jnp.concatenate(out, axis=0)


def stack_rows(scratch, pieces):
    rows = pieces[0].shape[0]
    for i, piece in enumerate(pieces):
        scratch[i * rows : (i + 1) * rows, :] = piece[...]


def norm_rows(values, gain):
    inverse = lax.rsqrt(jnp.mean(values * values, axis=-1, keepdims=True) + EPSILON)
    return (values * inverse * gain, inverse)


def norm_back(gradient, values, inverse, gain):
    scaled = gradient * gain
    inner_mean = jnp.mean(scaled * values, axis=-1, keepdims=True)
    return inverse * scaled - values * (inverse * inverse * inverse) * inner_mean


EXTRA_ROWS = 16


def pack_kernel(shards, members, spots, gate_ref, up_ref, down_ref, out_ref):
    member = spots[3]
    span = gate_ref.shape[1] // shards
    piece = span // members
    rows = gate_ref.shape[0]
    pick = (
        lax.broadcasted_iota(jnp.int32, (span, piece), 0)
        == lax.broadcasted_iota(jnp.int32, (span, piece), 1) + member * piece
    ).astype(BF16)
    out = []
    for ref in (gate_ref, up_ref):
        for z in range(shards):
            out.append(dot_plain(ref[:, z * span : (z + 1) * span], pick))
    down = dot_plain(down_ref[...], pick)
    out += [down[b : b + rows, :] for b in range(0, down_ref.shape[0], rows)]
    out_ref[...] = jnp.concatenate(out, axis=1).astype(BF16)


def quarter_kernel(members, spots, query_ref, output_ref, out_ref):
    size = query_ref.shape[1] // members
    for i in range(members):

        @pl.when(spots[2] == i)
        def _():
            out_ref[...] = jnp.concatenate(
                [ref[:, i * size : (i + 1) * size] for ref in (query_ref, output_ref)], axis=1
            )


def stack_kernel(spots, *refs):
    stack_rows(refs[-1], refs[:-1])


def begin_kernel(shards, spots, *refs):
    ins, outs, scratch = split_refs(refs, 7 + 2 * (shards - 1), 5, 3)
    tokens_ref, gain_one, gain_two, key_ref, value_ref, cos_ref, sin_ref = ins[:7]
    mine, other = split_refs(ins[7:], shards - 1, shards - 1)
    kv_ref, normed_ref, turned_ref, inverse_ref, gains_ref = outs
    blocks, normed_blocks, gain_blocks = scratch
    core, shard = spots[0], spots[1]
    width = key_ref.shape[0]
    values = tokens_ref[...].astype(F32)
    inverse = lax.rsqrt(jnp.mean(values * values, axis=-1, keepdims=True) + EPSILON)
    inverse_ref[...] = inverse
    for z, block in enumerate(lane_blocks(values * inverse, shards)):
        blocks[z] = block
    sums, order = [], []
    for r in range(shards):
        at = shard ^ r
        if r == 0:
            pair = jnp.concatenate([gain_one[...], gain_two[...]], axis=0).astype(F32)
        else:
            pair = mine[r - 1][width : width + EXTRA_ROWS, :].astype(F32)[0:2, :]
        gain_blocks[at, 0:2, :] = pair
        normed = (blocks[at] * pair[0:1, :]).astype(BF16)
        normed_blocks[at] = normed
        order.append(normed)
        left = key_ref[...] if r == 0 else mine[r - 1][:width, :]
        right = value_ref[...] if r == 0 else other[r - 1][:width, :]
        sums.append((dot_last(normed, left), dot_last(normed, right)))
    first = sum(s[0] for s in sums[1:])
    second = sum(s[1] for s in sums[1:])
    keys = jnp.where(core == 0, first, second) + sums[0][0]
    vals = jnp.where(core == 0, second, first) + sums[0][1]
    keys = rope_lanes(keys, cos_ref[...], sin_ref[...])
    kv_ref[...] = jnp.concatenate([keys, vals], axis=1).astype(BF16)
    normed_ref[...] = join_lanes(normed_blocks)
    turned_ref[...] = jnp.concatenate(order, axis=1)
    gains_ref[...] = jnp.zeros_like(gains_ref)
    gains_ref[0:2, :] = jnp.concatenate([gain_blocks[z][0:2, :] for z in range(shards)], axis=1)


def attend(chunk, head, kv_ref, key_pos_ref, query_pos, stacked, state):
    def step(j, state):
        largest, total, weighted = state
        at = pl.ds(pl.multiple_of(j * chunk, chunk), chunk)
        keys = heads_of(kv_ref, head, 1, at)
        values = heads_of(kv_ref, KV_HEADS + head, 1, at)
        scores = dot_last(keys, stacked)
        scores = jnp.where(key_pos_ref[at, :] <= query_pos, scores, MASKED)
        new_largest = jnp.maximum(largest, jnp.max(scores, axis=0, keepdims=True))
        weights = jnp.exp(scores - new_largest)
        factor = jnp.exp(largest - new_largest)
        total = total * factor + jnp.sum(weights, axis=0, keepdims=True)
        weighted = weighted * factor + dot_first(values, weights.astype(BF16))
        return new_largest, total, weighted

    return lax.fori_loop(0, kv_ref.shape[0] // chunk, step, state)


def near_kernel(chunk, members, pieces, spots, *refs):
    ins, outs, scratch = split_refs(refs, 6 + members + pieces, 4, 2)
    normed_ref, key_pos_ref, query_pos_ref, cos_ref, sin_ref, local_ref = ins[:6]
    weights, parts = split_refs(ins[6:], members, pieces)
    queries_ref, largest_ref, total_ref, weighted_ref = outs
    blocks, kv_ref = scratch
    dp = spots[2]
    stack_rows(kv_ref, parts)
    own = local_ref.shape[0]
    size = blocks.shape[-1]
    away = normed_ref[:, own:]
    for j in range(members):
        blocks[dp ^ j] = dot_plain(away, weights[j][:, :size])
    raw = join_lanes(blocks) + dot_plain(normed_ref[:, :own], local_ref[...])
    roped = rope_lanes(raw, cos_ref[...], sin_ref[...]).astype(BF16)
    queries_ref[...] = roped * jnp.asarray(1.0 / math.sqrt(HEAD_DIM), BF16)
    columns = GROUPS * queries_ref.shape[0]
    query_pos = query_pos_ref[...]
    for head in range(KV_HEADS):
        stacked = heads_of(queries_ref, head * GROUPS, GROUPS)
        start = (
            jnp.full((1, columns), MASKED, F32),
            jnp.zeros((1, columns), F32),
            jnp.zeros((HEAD_DIM, columns), F32),
        )
        largest, total, weighted = attend(
            chunk, head, kv_ref, key_pos_ref, query_pos, stacked, start
        )
        largest_ref[head : head + 1, :] = largest
        total_ref[head : head + 1, :] = total
        weighted_ref[head] = weighted


def far_kernel(chunk, shards, members, pieces, spots, *refs):
    ins, outs, scratch = split_refs(refs, 9 + members + pieces, 6, 3)
    (queries_ref, key_pos_ref, query_pos_ref, largest_ref, total_ref, weighted_ref, tokens_ref,
     gains_ref, local_ref) = ins[:9]
    weights, parts = split_refs(ins[9:], members, pieces)
    attended_ref, turned_ref, log_ref, residual_ref, inverse_ref, normed_ref = outs
    blocks, kv_ref, head_blocks = scratch
    shard, dp = spots[1], spots[2]
    stack_rows(kv_ref, parts)
    rows = queries_ref.shape[0]
    query_pos = query_pos_ref[...]
    heads = []
    for head in range(KV_HEADS):
        stacked = heads_of(queries_ref, head * GROUPS, GROUPS)
        start = (largest_ref[head : head + 1, :], total_ref[head : head + 1, :], weighted_ref[head])
        largest, total, weighted = attend(
            chunk, head, kv_ref, key_pos_ref, query_pos, stacked, start
        )
        turned = weighted / total
        turned_ref[head] = turned
        log_ref[head : head + 1, :] = largest + jnp.log(total)
        straight = turned.T
        heads += [straight[g * rows : (g + 1) * rows, :] for g in range(GROUPS)]
    attended = jnp.concatenate(heads, axis=1).astype(BF16)
    attended_ref[...] = attended
    for z, block in enumerate(lane_blocks(attended, shards)):
        head_blocks[z] = block
    away = jnp.concatenate([head_blocks[shard ^ r] for r in range(1, shards)], axis=1)
    size = blocks.shape[-1]
    for j in range(members):
        blocks[dp ^ j] = dot_plain(away, weights[j][:, size:])
    added = join_lanes(blocks) + dot_plain(head_blocks[shard], local_ref[...])
    residual = tokens_ref[...].astype(F32) + added
    residual_ref[...] = residual
    normed, inverse = norm_rows(residual, gains_ref[1:2, :])
    inverse_ref[...] = inverse
    normed_ref[...] = normed.astype(BF16)


def unfold_down(pack_ref, down_ref, shards, part):
    piece = part // shards
    rows = pack_ref.shape[0] // shards
    for b in range(down_ref.shape[0] // rows):
        at = 2 * part + b * piece
        down_ref[b * rows : (b + 1) * rows, :] = jnp.concatenate(
            [pack_ref[z * rows : (z + 1) * rows, at : at + piece] for z in range(shards)], axis=1
        )


def feed_kernel(shards, pieces, spots, *refs):
    ins, outs, scratch = split_refs(refs, 1 + 2 * pieces, 3, 3)
    pack_ref = ins[0]
    normed_parts, cot_parts = split_refs(ins[1:], pieces, pieces)
    grad_ref, act_ref, both_ref = outs
    normed_ref, cot_ref, down_ref = scratch
    part = pack_ref.shape[1] // 3
    stack_rows(normed_ref, normed_parts)
    stack_rows(cot_ref, cot_parts)
    unfold_down(pack_ref, down_ref, shards, part)
    gate_up = dot_plain(normed_ref[...], pack_ref[:, : 2 * part])
    gate, upward = gate_up[:, :part], gate_up[:, part:]
    act_grad = dot_plain(cot_ref[...], down_ref[...])
    sigmoid_gate = jax.nn.sigmoid(gate)
    silu = gate * sigmoid_gate
    act_ref[...] = (silu * upward).astype(BF16)
    gate_grad = act_grad * upward * sigmoid_gate * (1.0 + gate * (1.0 - sigmoid_gate))
    both_ref[...] = jnp.concatenate([gate_grad, act_grad * silu], axis=1).astype(BF16)
    grad_ref[...] = dot_last(both_ref[...], pack_ref[:, : 2 * part]).astype(BF16)


def feed_weights_kernel(shards, pieces, spots, *refs):
    ins, outs, scratch = split_refs(refs, 5 + 2 * pieces, 3, 5)
    pack_ref, act_a, act_b, both_a, both_b = ins[:5]
    normed_parts, cot_parts = split_refs(ins[5:], pieces, pieces)
    result_a, result_b, grad_ref = outs
    normed_ref, cot_ref, act_ref, both_ref, down_ref = scratch
    part = pack_ref.shape[1] // 3
    piece = part // shards
    rows = grad_ref.shape[0] // shards
    stack_rows(normed_ref, normed_parts)
    stack_rows(cot_ref, cot_parts)
    stack_rows(act_ref, (act_a, act_b))
    stack_rows(both_ref, (both_a, both_b))
    unfold_down(pack_ref, down_ref, shards, part)
    grad_ref[:, : 2 * part] = dot_first(normed_ref[...], both_ref[...]).astype(BF16)
    down_grad = dot_first(cot_ref[...], act_ref[...]).astype(BF16)
    folds = down_grad.shape[0] // rows
    for z in range(shards):
        at = z * piece
        grad_ref[z * rows : (z + 1) * rows, 2 * part :] = jnp.concatenate(
            [down_grad[b * rows : (b + 1) * rows, at : at + piece] for b in range(folds)], axis=1
        )
    result_a[...] = dot_last(act_a[...], down_ref[...]).astype(BF16)
    result_b[...] = dot_last(act_b[...], down_ref[...]).astype(BF16)


def middle_kernel(shards, members, spots, *refs):
    ins, outs, scratch = split_refs(refs, 10 + members, 4, 2)
    (own_a, own_b, one_ref, two_ref, three_ref, residual_ref, inverse_ref, cot_ref, gains_ref,
     local_ref) = ins[:10]
    weights = ins[10:]
    residual_grad_ref, low_ref, attended_grad_ref, gain_grad_ref = outs
    rows = cot_ref.shape[0]
    grad = (own_a[:rows, :].astype(F32) + own_b[:rows, :].astype(F32)) + one_ref[...].astype(F32)
    grad = grad + two_ref[...].astype(F32) + three_ref[...].astype(F32)
    residual, inverse = residual_ref[...], inverse_ref[...]
    gain_grad_ref[...] = jnp.sum(grad * residual * inverse, axis=0, keepdims=True)
    residual_grad = cot_ref[...].astype(F32) + norm_back(grad, residual, inverse, gains_ref[1:2, :])
    residual_grad_ref[...] = residual_grad
    low = residual_grad.astype(BF16)
    low_ref[...] = low
    attended_grad_ref[...] = back_through(
        shards, members, spots, low, weights, local_ref, scratch, 1
    ).astype(BF16)


def back_through(shards, members, spots, low, weights, local_ref, scratch, which):
    blocks, out_blocks = scratch
    shard, dp = spots[1], spots[2]
    for i, block in enumerate(lane_blocks(low, members)):
        blocks[i] = block
    size = blocks.shape[-1]
    at = slice(which * size, (which + 1) * size)
    away = sum(dot_last(blocks[dp ^ j], weights[j][:, at]) for j in range(members))
    out_blocks[shard] = dot_last(low, local_ref[...])
    for r, block in enumerate(lane_blocks(away, shards - 1)):
        out_blocks[shard ^ (r + 1)] = block
    return join_lanes(out_blocks)


def weight_grad_kernel(members, spots, left_ref, low_ref, keep_ref, send_ref, blocks):
    dp = spots[2]
    for i, block in enumerate(lane_blocks(low_ref[...], members)):
        blocks[i] = block
    left = left_ref[...]
    for j in range(members):
        out_ref = send_ref if j & 1 else keep_ref
        out_ref[j // 2] = dot_first(left, blocks[dp ^ j]).astype(BF16)


def join_kernel(members, spots, pair_ref, other_ref, out_ref, blocks):
    dp = spots[2]
    for j in range(members):
        ref = other_ref if j & 1 else pair_ref
        blocks[dp ^ j] = ref[j // 2]
    out_ref[...] = join_lanes(blocks).astype(F32)


def query_back_kernel(shards, members, spots, low_ref, local_ref, *refs):
    weights, (back_ref,), scratch = split_refs(refs, members, 1, 2)
    back_ref[...] = back_through(
        shards, members, spots, low_ref[...], weights, local_ref, scratch, 0
    )


def back_kernel(chunk, pieces, first, last, spots, *refs):
    ins, outs, scratch = split_refs(refs, 9 + pieces, (pieces if last else 2) + 1, 2)
    (queries_ref, key_pos_ref, query_pos_ref, cos_ref, sin_ref, turned_ref, log_ref, grad_ref,
     start_ref) = ins[:9]
    parts = ins[9:]
    query_grad_ref, kv_grads = outs[0], outs[1:]
    kv_ref, kv_grad_ref = scratch
    stack_rows(kv_ref, parts)
    rows = queries_ref.shape[0]
    columns = GROUPS * rows
    query_pos = query_pos_ref[...]
    heads = []
    for head in range(KV_HEADS):
        stacked = heads_of(queries_ref, head * GROUPS, GROUPS)
        upstream = heads_of(grad_ref, head * GROUPS, GROUPS)
        delta = jnp.sum(upstream.astype(F32).T * turned_ref[head], axis=0, keepdims=True)
        log_total = log_ref[head : head + 1, :]
        keys_at = head * HEAD_DIM
        values_at = (KV_HEADS + head) * HEAD_DIM

        def step(j, query_grad, head=head, stacked=stacked, upstream=upstream,
                 delta=delta, log_total=log_total, keys_at=keys_at, values_at=values_at):
            at = pl.ds(pl.multiple_of(j * chunk, chunk), chunk)
            keys = heads_of(kv_ref, head, 1, at)
            values = heads_of(kv_ref, KV_HEADS + head, 1, at)
            scores = dot_last(keys, stacked)
            scores = jnp.where(key_pos_ref[at, :] <= query_pos, scores, MASKED)
            weights = jnp.exp(scores - log_total)
            weight_grad = dot_last(values, upstream)
            score_grad = (weights * (weight_grad - delta)).astype(BF16)
            value_grad = dot_plain(weights.astype(BF16), upstream)
            key_grad = dot_plain(score_grad, stacked)
            kv_grad_ref[at, keys_at : keys_at + HEAD_DIM] = key_grad.astype(BF16)
            kv_grad_ref[at, values_at : values_at + HEAD_DIM] = value_grad.astype(BF16)
            return query_grad + dot_first(keys, score_grad)

        start = jnp.zeros((HEAD_DIM, columns), F32) if first else start_ref[head]
        query_grad = lax.fori_loop(0, kv_ref.shape[0] // chunk, step, start)
        if not last:
            query_grad_ref[head] = query_grad
        else:
            straight = query_grad.T * (1.0 / math.sqrt(HEAD_DIM))
            heads += [straight[g * rows : (g + 1) * rows, :] for g in range(GROUPS)]
    if last:
        query_grad_ref[...] = rope_lanes(
            jnp.concatenate(heads, axis=1), cos_ref[...], -sin_ref[...]
        ).astype(BF16)
    size = kv_ref.shape[0] // len(kv_grads)
    for i, ref in enumerate(kv_grads):
        ref[...] = kv_grad_ref[i * size : (i + 1) * size, :]


def end_kernel(shards, spots, *refs):
    ins, outs, scratch = split_refs(refs, 11 + (shards + 1) + 2 * (shards - 1), 3, 1)
    (cos_ref, sin_ref, normed_ref, tokens_ref, inverse_ref, gains_ref, back_ref, residual_grad_ref,
     key_ref, value_ref, gain_two_ref) = ins[:11]
    sums, mine, other = split_refs(ins[11:], shards + 1, shards - 1, shards - 1)
    input_grad_ref, keep_ref, send_ref = outs
    (blocks,) = scratch
    core, shard = spots[0], spots[1]
    width, span = key_ref.shape
    rows = tokens_ref.shape[0]
    total = sum(s[:rows, :].astype(F32) for s in sums)
    keys = rope_lanes(total[:, :width], cos_ref[...], -sin_ref[...])
    values = total[:, width:]
    keep = jnp.where(core == 0, keys, values).astype(BF16)
    send = jnp.where(core == 0, values, keys).astype(BF16)
    blocks[shard] = dot_plain(keys.astype(BF16), key_ref[...]) + dot_plain(
        values.astype(BF16), value_ref[...]
    )
    for r in range(1, shards):
        blocks[shard ^ r] = dot_plain(keep, mine[r - 1][:width, :]) + dot_plain(
            send, other[r - 1][:width, :]
        )
    normed_grad = back_ref[...] + join_lanes(blocks)
    inputs, inverse = tokens_ref[...].astype(F32), inverse_ref[...]
    gain_grad = jnp.sum(normed_grad * inputs * inverse, axis=0, keepdims=True)
    input_grad_ref[...] = residual_grad_ref[...] + norm_back(
        normed_grad, inputs, inverse, gains_ref[0:1, :]
    )
    normed = normed_ref[...]
    two = gain_two_ref[...]
    for out_ref, low, gain in (
        (send_ref, send, jnp.where(core == 0, two, gain_grad)),
        (keep_ref, keep, jnp.where(core == 0, gain_grad, two)),
    ):
        grad = dot_first(low, normed).astype(BF16)
        size = width + EXTRA_ROWS
        gains = lane_blocks(gain, shards)
        for z, block in enumerate(lane_blocks(grad, shards)):
            out_ref[z * size : z * size + width, :] = block
            out_ref[z * size + width : (z + 1) * size, :] = jnp.broadcast_to(
                gains[z], (EXTRA_ROWS, span)
            ).astype(BF16)


def spread_kernel(shards, members, spots, *refs):
    parts, outs, (blocks,) = split_refs(refs, members, 3, 1)
    gate_ref, up_ref, down_ref = outs
    member = spots[3]
    piece = parts[0].shape[1] // 3 // shards
    rows = parts[0].shape[0]
    span = piece * members
    for i in range(members):
        blocks[member ^ i] = parts[i][...]

    def block(k):
        at = k * piece
        return jnp.concatenate(
            [blocks[p, :, at : at + piece] for p in range(members)], axis=1
        ).astype(F32)

    for z in range(shards):
        gate_ref[:, z * span : (z + 1) * span] = block(z)
        up_ref[:, z * span : (z + 1) * span] = block(shards + z)
    for b in range(down_ref.shape[0] // rows):
        down_ref[b * rows : (b + 1) * rows, :] = block(2 * shards + b)


def base_of(block_order, stored, block_length):
    which = stored // block_length
    count = block_order.shape[1]
    matches = (which[:, None] == jnp.arange(count, dtype=jnp.int32)[None, :]).astype(jnp.int32)
    return jnp.sum(block_order[0][None, :] * matches, axis=-1) * block_length + stored % block_length


def tables(positions):
    half_dim = HEAD_DIM // 2
    exponent = -(jnp.arange(half_dim, dtype=F32) * 2.0) / HEAD_DIM
    frequency = jnp.power(F32(ROPE_BASE), exponent)
    angles = positions.astype(F32)[:, None] * frequency
    cosine, sine = jnp.cos(angles), jnp.sin(angles)
    return (
        jnp.concatenate([cosine] * 4, axis=-1),
        jnp.concatenate([-sine, sine, -sine, sine], axis=-1),
    )


def after(x, other):
    return lax.optimization_barrier((x, other))[0]


def on_device(
    tokens,
    block_order,
    attention_gain,
    query_weight,
    key_weight,
    value_weight,
    output_weight,
    feedforward_gain,
    gate_weight,
    up_weight,
    down_weight,
    cotangent,
):
    tokens, cotangent = tokens[0], cotangent[0]
    rows, width = tokens.shape
    shards = lax.axis_size("fsdp")
    ctx_count = lax.axis_size("ctx")
    dp_count = lax.axis_size("dp")
    block_length = rows * shards * ctx_count // block_order.shape[1]
    shard = lax.axis_index("fsdp")
    ctx = lax.axis_index("ctx")
    dp = lax.axis_index("dp")
    core = dp & 1
    members = dp_count * 2
    weight_rows = query_weight.shape[0]
    query_width = HEADS * HEAD_DIM
    kv_width = KV_HEADS * HEAD_DIM
    hidden = gate_weight.shape[1]
    part = hidden // members
    spots = jnp.stack([core, shard, dp, dp * 2 + (ctx & 1)]).astype(jnp.int32)

    gain_one, gain_two = attention_gain[None, :], feedforward_gain[None, :]
    key_turned, value_turned, down_turned = key_weight.T, value_weight.T, down_weight.T
    kv_pack = jnp.concatenate(
        [
            jnp.where(core == 0, key_turned, value_turned),
            jnp.pad(
                jnp.concatenate([gain_one, gain_two], axis=0), ((0, EXTRA_ROWS - 2), (0, 0))
            ),
        ],
        axis=0,
    )
    kv_mine = [swap(kv_pack, "fsdp", r) for r in range(1, shards)]
    kv_other = [swap_core(piece) for piece in kv_mine]

    quarter = width // dp_count
    (quarters,) = call(
        functools.partial(quarter_kernel, dp_count), spots,
        [after(query_weight, kv_pack), output_weight],
        [((weight_rows, 2 * quarter), BF16)], name="quarter_columns",
    )
    (stacked,) = call(
        stack_kernel, spots, [swap(quarters, "fsdp", r) for r in range(1, shards)],
        [(((shards - 1) * weight_rows, 2 * quarter), BF16)], name="stack_quarters",
    )
    across = swap_plane(stacked, 2, 0)
    stacks = [stacked, swap_core(stacked), across, swap_core(across)]

    offsets = jnp.arange(rows, dtype=jnp.int32)
    my_start = (ctx * shards + shard) * rows
    positions = base_of(block_order, my_start[None], block_length) + offsets
    cosine, sine = tables(positions)
    query_pos = jnp.concatenate([positions] * GROUPS)[None, :]
    starts = jnp.stack(
        [((ctx ^ d) * shards + (shard ^ r)) * rows for d in range(ctx_count) for r in range(shards)]
    )
    key_pos = (base_of(block_order, starts, block_length)[:, None] + offsets[None, :]).reshape(-1, 1)
    near_count = shards * rows
    near_pos, far_pos = key_pos[:near_count], key_pos[near_count:]
    far_count = far_pos.shape[0]

    (pack,) = call(
        functools.partial(pack_kernel, shards, members), spots,
        [gate_weight, up_weight, down_turned], [((weight_rows, 3 * part), BF16)],
        flops=4 * weight_rows * hidden * part // shards, name="pack_weights",
    )
    kv_own, normed_one, normed_turned, inverse_one, gains = call(
        functools.partial(begin_kernel, shards), spots,
        [
            tokens, gain_one, gain_two, key_turned, value_turned, cosine, sine, *kv_mine, *kv_other,
        ],
        [
            ((rows, 2 * kv_width), BF16), ((rows, width), BF16), ((rows, width), BF16),
            ((rows, 1), F32), ((8, width), F32),
        ],
        scratch=[
            ((shards, rows, weight_rows), F32), ((shards, rows, weight_rows), BF16),
            ((shards, 8, weight_rows), F32),
        ],
        flops=4 * rows * width * kv_width, name="norm_keys_values",
    )
    near = [kv_own] + [swap(kv_own, "fsdp", r) for r in range(1, shards)]
    far = [swap(piece, "ctx", d) for d in range(1, ctx_count) for piece in near]

    pack_all = lax.all_gather(after(pack, near[-1]), "fsdp", axis=0, tiled=True)
    cot_a, cot_b = plane_pieces(after(cotangent, near[-1]))

    chunk = rows * 2
    unit = 2 * HEADS * rows * near_count * HEAD_DIM
    stat = ((KV_HEADS, GROUPS * rows), F32)
    turned_shape = ((KV_HEADS, HEAD_DIM, GROUPS * rows), F32)
    queries, largest, total, weighted = call(
        functools.partial(near_kernel, chunk, dp_count, shards), spots,
        [normed_turned, near_pos, query_pos, cosine, sine, query_weight, *stacks, *near],
        [((rows, query_width), BF16), stat, stat, turned_shape],
        scratch=[((dp_count, rows, quarter), F32), ((near_count, 2 * kv_width), BF16)],
        flops=8 * unit, name="attention_near",
    )
    attended, turned, log_total, residual, inverse_two, normed_two = call(
        functools.partial(far_kernel, chunk, shards, dp_count, len(far)), spots,
        [
            queries, far_pos, query_pos, largest, total, weighted, tokens, gains,
            output_weight, *stacks, *far,
        ],
        [
            ((rows, query_width), BF16), turned_shape, stat, ((rows, width), F32),
            ((rows, 1), F32), ((rows, width), BF16),
        ],
        scratch=[
            ((dp_count, rows, quarter), F32), ((far_count, 2 * kv_width), BF16),
            ((shards, rows, weight_rows), BF16),
        ],
        flops=8 * unit * len(far) // shards, name="attention_far",
    )

    normed_a, normed_b = plane_pieces(normed_two)
    token_shape = ((rows, width), BF16)
    half = 4 * rows
    half_shape = ((half, width), BF16)

    def feed(normed, cot):
        return call(
            functools.partial(feed_kernel, shards, 4), spots, [pack_all, *normed, *cot],
            [half_shape, ((half, part), BF16), ((half, 2 * part), BF16)],
            scratch=[((half, width), BF16), ((half, width), BF16), ((width, part), BF16)],
            flops=10 * half * width * part, name="feed_forward",
        )

    grad_b, act_b, both_b = feed(normed_b, cot_b)
    from_core = swap_core(grad_b)
    grad_a, act_a, both_a = feed(normed_a, cot_a)

    def chip_sums(parts_a, parts_b):
        return [
            (parts_a[k * rows : (k + 1) * rows].astype(F32)
             + parts_b[k * rows : (k + 1) * rows].astype(F32)).astype(BF16)
            for k in range(1, 4)
        ]

    def send_chips(sums):
        return [swap_plane(x, a, b) for x, (a, b) in zip(sums, CHIP_MASKS)]

    grad_chips = send_chips(chip_sums(grad_a, from_core))
    result_a, result_b, pack_grad = call(
        functools.partial(feed_weights_kernel, shards, 8), spots,
        [pack_all, act_a, act_b, both_a, both_b, *normed_a, *normed_b, *cot_a, *cot_b],
        [half_shape, half_shape, ((width, 3 * part), BF16)],
        scratch=[
            ((2 * half, width), BF16), ((2 * half, width), BF16), ((2 * half, part), BF16),
            ((2 * half, 2 * part), BF16), ((width, part), BF16),
        ],
        flops=16 * half * width * part, name="feed_forward_weights",
    )
    pack_share = sum_far(lax.psum_scatter(pack_grad, "fsdp", scatter_dimension=0, tiled=True))

    residual_grad, residual_low, attended_grad, second_gain_grad = call(
        functools.partial(middle_kernel, shards, dp_count), spots,
        [
            grad_a, from_core, *grad_chips, residual, inverse_two, cotangent, gains, output_weight,
            *stacks,
        ],
        [((rows, width), F32), token_shape, ((rows, query_width), BF16), ((1, width), F32)],
        scratch=[((dp_count, rows, quarter), BF16), ((shards, rows, weight_rows), F32)],
        flops=2 * rows * width * query_width, name="residual_back",
    )

    result_core = swap_core(result_b)
    result_sums = chip_sums(after(result_a, residual_low), result_core)
    result_chips = send_chips(result_sums)
    result = residual + (
        (result_a[:rows].astype(F32) + result_core[:rows].astype(F32))
        + result_chips[0].astype(F32)
        + (result_chips[1].astype(F32) + result_chips[2].astype(F32))
    )

    def weight_grad(left, low, name):
        pair = ((2, width, quarter), BF16)
        return call(
            functools.partial(weight_grad_kernel, dp_count), spots, [left, low], [pair, pair],
            scratch=[((dp_count, rows, quarter), BF16)],
            flops=2 * rows * width * width, name=name,
        )

    def sum_quarters(keep, send):
        away = swap_core(send)
        sent = (keep[1].astype(F32) + away[1].astype(F32)).astype(BF16)
        across = swap_plane(sent, 2, 0)
        pieces = []
        for r in range(shards):
            at = (shard ^ r) * weight_rows
            parts = [
                lax.dynamic_slice_in_dim(x, at, weight_rows, 0).astype(F32)
                for x in (keep[0], away[0], across)
            ]
            pieces.append((parts[0] + parts[1] + parts[2]).astype(BF16))
        total = pieces[0].astype(F32)
        for r in range(1, shards):
            total = total + swap(pieces[r], "fsdp", r).astype(F32)
        own = total.astype(BF16)
        own = sum_far((own.astype(F32) + swap_plane(own, 0, 1).astype(F32)).astype(BF16))
        pair = jnp.stack([own, swap_plane(own, 2, 0)])
        (out,) = call(
            functools.partial(join_kernel, dp_count), spots, [pair, swap_core(pair)],
            [((weight_rows, width), F32)], scratch=[((dp_count, weight_rows, quarter), BF16)],
            name="join_columns",
        )
        return out

    output_keep, output_send = weight_grad(attended, residual_low, "output_weight_grad")
    attended_grad, _, _ = lax.optimization_barrier((attended_grad, output_send, result_sums[2]))

    def back(first, last, start, pos, pieces):
        count = pos.shape[0]
        shape = ((rows, query_width), BF16) if last else turned_shape
        out = call(
            functools.partial(back_kernel, chunk, len(pieces), first, last), spots,
            [
                queries, pos, query_pos, cosine, sine, turned, log_total, attended_grad, start,
                *pieces,
            ],
            [shape]
            + (
                [((rows, 2 * kv_width), BF16)] * len(pieces) if last
                else [((count // 2, 2 * kv_width), BF16)] * 2
            ),
            scratch=[((count, 2 * kv_width), BF16), ((count, 2 * kv_width), BF16)],
            flops=20 * unit * len(pieces) // shards,
            name="attention_back_near" if last else "attention_back_far",
        )
        return out[0], out[1:]

    query_partial, far_grads = turned, []
    for d in range(1, ctx_count):
        at = (d - 1) * shards
        query_partial, grads = back(
            d == 1, False, query_partial, far_pos[at * rows : (at + shards) * rows],
            far[at : at + shards],
        )
        far_grads.append([swap(g, "ctx", d) for g in (grads[1], grads[0])][::-1])
    query_low, near_grads = back(False, True, query_partial, near_pos, near)
    pack_share, *near_grads = lax.optimization_barrier((pack_share, *near_grads))

    def home(r):
        at = (r % 2) * rows
        return sum(pair[r // 2][at : at + rows].astype(F32) for pair in far_grads)

    kv_arrived = {
        r: swap((near_grads[r].astype(F32) + home(r)).astype(BF16), "fsdp", r)
        for r in reversed(range(1, shards))
    }
    share_a, share_b = plane_pieces(pack_share)

    def pieces_of(keep, arrived, span):
        out = []
        for r in range(shards):
            at = (shard ^ r) * span
            mine = lax.dynamic_slice_in_dim(keep, at, span, 0).astype(F32)
            theirs = lax.dynamic_slice_in_dim(arrived, at, span, 0).astype(F32)
            out.append((mine + theirs).astype(BF16))
        return out

    def sum_devices(keep, send, span):
        pieces = pieces_of(keep, swap_core(send), span)
        total = pieces[0].astype(F32)
        for r in range(1, shards):
            total = total + swap(pieces[r], "fsdp", r).astype(F32)
        own = total.astype(BF16)
        across, along, diagonal = [swap_plane(own, a, b) for a, b in CHIP_MASKS]
        total = (own.astype(F32) + across.astype(F32)) + (
            along.astype(F32) + diagonal.astype(F32)
        )
        low = sum_far(total.astype(BF16))
        away = swap_core(low)
        return (
            jnp.where(core == 0, low, away).astype(F32), jnp.where(core == 0, away, low).astype(F32)
        )

    query_keep, query_send = weight_grad(normed_one, query_low, "query_weight_grad")
    (query_back,) = call(
        functools.partial(query_back_kernel, shards, dp_count), spots,
        [query_low, query_weight, *stacks], [((rows, width), F32)],
        scratch=[((dp_count, rows, quarter), BF16), ((shards, rows, weight_rows), F32)],
        flops=2 * rows * width * width, name="query_back",
    )
    output_weight_grad = sum_quarters(output_keep, output_send)
    query_weight_grad = sum_quarters(query_keep, query_send)

    span = kv_width + EXTRA_ROWS
    packed_shape = ((shards * span, weight_rows), BF16)
    home_own = far_grads[0][0] if ctx_count == 2 else home(0)
    input_grad, kv_keep, kv_send = call(
        functools.partial(end_kernel, shards), spots,
        [
            cosine, sine, normed_one, tokens, inverse_one, gains, query_back, residual_grad,
            key_turned, value_turned, second_gain_grad, near_grads[0], home_own,
            *[kv_arrived[r] for r in range(1, shards)], *kv_mine, *kv_other,
        ],
        [((rows, width), F32), packed_shape, packed_shape],
        scratch=[((shards, rows, weight_rows), F32)],
        flops=8 * rows * width * kv_width, name="keys_values_back",
    )
    first, second = sum_devices(kv_keep, kv_send, span)

    share_by_mask = [None] * members
    for k, (a, b) in enumerate(((0, 0),) + CHIP_MASKS):
        share_by_mask[2 * a + b] = share_a[k]
        share_by_mask[2 * (a ^ 1) + b] = share_b[k]
    gate_weight_grad, up_weight_grad, down_weight_grad = call(
        functools.partial(spread_kernel, shards, members), spots, share_by_mask,
        [
            ((weight_rows, hidden), F32), ((weight_rows, hidden), F32),
            ((width, down_weight.shape[0]), F32),
        ],
        scratch=[((members, weight_rows, 3 * part), BF16)],
        name="feed_forward_out",
    )

    return (
        result[None],
        input_grad[None],
        first[kv_width],
        query_weight_grad,
        first[:kv_width].T,
        second[:kv_width].T,
        output_weight_grad,
        second[kv_width],
        gate_weight_grad,
        up_weight_grad,
        down_weight_grad.T,
    )


def solution(mesh):
    row = P("fsdp", None)
    token = P("dp", ("ctx", "fsdp"), None)
    return jax.shard_map(
        on_device,
        mesh=mesh,
        in_specs=(
            token, P("dp", None), P("fsdp"), row, row, row, row, P("fsdp"), row, row, row, token,
        ),
        out_specs=(
            token, token, P("fsdp"), row, row, row, row, P("fsdp"), row, row, row,
        ),
        check_vma=False,
    )
```

```python
import functools
import math

import jax
import jax.numpy as jnp
from jax import lax
from jax.experimental import pallas as pl
from jax.experimental.pallas import tpu as pltpu
from jax.sharding import PartitionSpec as P

HEADS = 15
KV_HEADS = 5
HEAD_DIM = 64
GROUPS = HEADS // KV_HEADS
LANES = 128

EPSILON = 1e-05
ROPE_BASE = 100000.0
MASKED = -1e30

F32 = jnp.float32
BF16 = jnp.bfloat16
VMEM_LIMIT = 56 * 1024 * 1024
FLOPS_PER_US = 1150 * 10**6
MEASURED_US = {
    "pack_weights": 4,
    "norm_keys_values": 4,
    "attention_near": 12,
    "attention_far": 14,
    "feed_forward": 8,
    "feed_forward_weights": 12,
    "residual_back": 6,
    "attention_back_far": 13,
    "attention_back_near": 14,
    "query_output_weight_grads": 7,
    "query_back": 4,
    "keys_values_back": 6,
    "feed_forward_out": 7,
}


def dot_plain(left, right):
    return jnp.dot(left, right, preferred_element_type=F32)


def dot_last(left, right):
    return lax.dot_general(left, right, (((1,), (1,)), ((), ())), preferred_element_type=F32)


def dot_first(left, right):
    return lax.dot_general(left, right, (((0,), (0,)), ((), ())), preferred_element_type=F32)


def swap(x, axis, mask):
    count = lax.axis_size(axis)
    return lax.ppermute(x, axis, [(i, i ^ mask) for i in range(count)])


def swap_plane(x, dp_mask, ctx_mask):
    ctx_count = lax.axis_size("ctx")
    pairs = []
    for d in range(lax.axis_size("dp")):
        for c in range(ctx_count):
            pairs.append((d * ctx_count + c, (d ^ dp_mask) * ctx_count + (c ^ ctx_mask)))
    return lax.ppermute(x, ("dp", "ctx"), pairs)


def swap_core(x):
    return swap_plane(x, 1, 0)


CHIP_MASKS = ((0, 1), (2, 0), (2, 1))


def plane_pieces(x):
    mine = [x] + [swap_plane(x, a, b) for a, b in CHIP_MASKS]
    return mine, [swap_core(piece) for piece in mine]


def sum_far(x):
    count = lax.axis_size("ctx")
    if count == 2:
        return x
    groups = [list(range(0, count, 2)), list(range(1, count, 2))]
    return lax.psum(x.astype(F32), "ctx", axis_index_groups=groups).astype(x.dtype)


def call(kernel, spots, args, out_shapes, scratch=(), name=None):
    specs = [pl.BlockSpec(memory_space=pltpu.SMEM)]
    specs += [pl.BlockSpec(memory_space=pltpu.VMEM) for _ in args]
    outs = tuple(jax.ShapeDtypeStruct(s, d) for s, d in out_shapes)
    return pl.pallas_call(
        kernel,
        out_shape=outs,
        in_specs=specs,
        out_specs=tuple(pl.BlockSpec(memory_space=pltpu.VMEM) for _ in outs),
        scratch_shapes=[pltpu.VMEM(s, d) for s, d in scratch],
        compiler_params=pltpu.CompilerParams(vmem_limit_bytes=VMEM_LIMIT),
        cost_estimate=pl.CostEstimate(
            flops=MEASURED_US.get(name, 2) * FLOPS_PER_US, bytes_accessed=0, transcendentals=0
        ),
        name=name,
    )(spots, *args)


def split_refs(refs, *counts):
    out, at = [], 0
    for n in counts:
        out.append(refs[at : at + n])
        at += n
    assert at == len(refs)
    return out


def lane_blocks(values, count):
    size = values.shape[1] // count
    return [values[:, i * size : (i + 1) * size] for i in range(count)]


def join_lanes(ref):
    return jnp.concatenate([ref[i] for i in range(ref.shape[0])], axis=1)


def rope_lanes(values, cosine, sine):
    rows, width = values.shape
    lane = lax.broadcasted_iota(jnp.int32, (rows, LANES), 1)
    first_half = (lane % HEAD_DIM) < (HEAD_DIM // 2)
    out = []
    for start in range(0, width, LANES):
        piece = values[:, start : min(start + LANES, width)]
        size = piece.shape[1]
        if size < LANES:
            piece = jnp.concatenate([piece, jnp.zeros((rows, LANES - size), piece.dtype)], axis=1)
        ahead = pltpu.roll(piece, LANES - HEAD_DIM // 2, 1)
        behind = pltpu.roll(piece, HEAD_DIM // 2, 1)
        partner = jnp.where(first_half, ahead, behind)
        out.append((piece * cosine + partner * sine)[:, :size])
    return jnp.concatenate(out, axis=1)


def heads_of(ref, first, count, rows=None):
    out = []
    for h in range(first, first + count):
        start = (h * HEAD_DIM) // LANES * LANES
        stop = min(start + LANES, ref.shape[-1])
        pair = ref[:, start:stop] if rows is None else ref[rows, start:stop]
        at = h * HEAD_DIM - start
        out.append(pair[:, at : at + HEAD_DIM])
    return out[0] if count == 1 else jnp.concatenate(out, axis=0)


def stack_rows(scratch, pieces):
    rows = pieces[0].shape[0]
    for i, piece in enumerate(pieces):
        scratch[i * rows : (i + 1) * rows, :] = piece[...]


def unstack_rows(out_ref, values):
    count, rows = out_ref.shape[:2]
    for i in range(count):
        out_ref[i] = values[i * rows : (i + 1) * rows, :].astype(out_ref.dtype)


def norm_rows(values, gain):
    inverse = lax.rsqrt(jnp.mean(values * values, axis=-1, keepdims=True) + EPSILON)
    return (values * inverse * gain, inverse)


def norm_back(gradient, values, inverse, gain):
    scaled = gradient * gain
    inner_mean = jnp.mean(scaled * values, axis=-1, keepdims=True)
    return inverse * scaled - values * (inverse * inverse * inverse) * inner_mean


EXTRA_ROWS = 16


def pack_kernel(shards, members, spots, gate_ref, up_ref, down_ref, out_ref):
    member = spots[3]
    span = gate_ref.shape[1] // shards
    piece = span // members
    rows = gate_ref.shape[0]
    pick = (
        lax.broadcasted_iota(jnp.int32, (span, piece), 0)
        == lax.broadcasted_iota(jnp.int32, (span, piece), 1) + member * piece
    ).astype(BF16)
    out = []
    for ref in (gate_ref, up_ref):
        for z in range(shards):
            out.append(dot_plain(ref[:, z * span : (z + 1) * span], pick))
    down = dot_plain(down_ref[...], pick)
    out += [down[b : b + rows, :] for b in range(0, down_ref.shape[0], rows)]
    out_ref[...] = jnp.concatenate(out, axis=1).astype(BF16)


def quarter_kernel(members, spots, query_ref, output_ref, out_ref):
    size = query_ref.shape[1] // members
    for i in range(members):

        @pl.when(spots[2] == i)
        def _():
            out_ref[...] = jnp.concatenate(
                [ref[:, i * size : (i + 1) * size] for ref in (query_ref, output_ref)], axis=1
            )


def stack_kernel(spots, *refs):
    stack_rows(refs[-1], refs[:-1])


def begin_kernel(shards, spots, *refs):
    ins, outs, scratch = split_refs(refs, 7 + 2 * (shards - 1), 5, 3)
    tokens_ref, gain_one, gain_two, key_ref, value_ref, cos_ref, sin_ref = ins[:7]
    mine, other = split_refs(ins[7:], shards - 1, shards - 1)
    kv_ref, normed_ref, turned_ref, inverse_ref, gains_ref = outs
    blocks, normed_blocks, gain_blocks = scratch
    core, shard = spots[0], spots[1]
    width = key_ref.shape[0]
    values = tokens_ref[...].astype(F32)
    inverse = lax.rsqrt(jnp.mean(values * values, axis=-1, keepdims=True) + EPSILON)
    inverse_ref[...] = inverse
    for z, block in enumerate(lane_blocks(values * inverse, shards)):
        blocks[z] = block
    sums, order = [], []
    for r in range(shards):
        at = shard ^ r
        if r == 0:
            pair = jnp.concatenate([gain_one[...], gain_two[...]], axis=0).astype(F32)
        else:
            pair = mine[r - 1][width : width + EXTRA_ROWS, :].astype(F32)[0:2, :]
        gain_blocks[at, 0:2, :] = pair
        normed = (blocks[at] * pair[0:1, :]).astype(BF16)
        normed_blocks[at] = normed
        order.append(normed)
        left = key_ref[...] if r == 0 else mine[r - 1][:width, :]
        right = value_ref[...] if r == 0 else other[r - 1][:width, :]
        sums.append((dot_last(normed, left), dot_last(normed, right)))
    first = sum(s[0] for s in sums[1:])
    second = sum(s[1] for s in sums[1:])
    keys = jnp.where(core == 0, first, second) + sums[0][0]
    vals = jnp.where(core == 0, second, first) + sums[0][1]
    keys = rope_lanes(keys, cos_ref[...], sin_ref[...])
    kv_ref[...] = jnp.concatenate([keys, vals], axis=1).astype(BF16)
    normed_ref[...] = join_lanes(normed_blocks)
    turned_ref[...] = jnp.concatenate(order, axis=1)
    gains_ref[...] = jnp.zeros_like(gains_ref)
    gains_ref[0:2, :] = jnp.concatenate([gain_blocks[z][0:2, :] for z in range(shards)], axis=1)


def attend(chunk, head, kv_ref, key_pos_ref, query_pos, stacked, state):
    def step(j, state):
        largest, total, weighted = state
        at = pl.ds(pl.multiple_of(j * chunk, chunk), chunk)
        keys = heads_of(kv_ref, head, 1, at)
        values = heads_of(kv_ref, KV_HEADS + head, 1, at)
        scores = dot_last(keys, stacked)
        scores = jnp.where(key_pos_ref[at, :] <= query_pos, scores, MASKED)
        new_largest = jnp.maximum(largest, jnp.max(scores, axis=0, keepdims=True))
        weights = jnp.exp(scores - new_largest)
        factor = jnp.exp(largest - new_largest)
        total = total * factor + jnp.sum(weights, axis=0, keepdims=True)
        weighted = weighted * factor + dot_first(values, weights.astype(BF16))
        return new_largest, total, weighted

    return lax.fori_loop(0, kv_ref.shape[0] // chunk, step, state)


def near_kernel(chunk, members, pieces, spots, *refs):
    ins, outs, scratch = split_refs(refs, 6 + members + pieces, 4, 2)
    normed_ref, key_pos_ref, query_pos_ref, cos_ref, sin_ref, local_ref = ins[:6]
    weights, parts = split_refs(ins[6:], members, pieces)
    queries_ref, largest_ref, total_ref, weighted_ref = outs
    blocks, kv_ref = scratch
    dp = spots[2]
    stack_rows(kv_ref, parts)
    own = local_ref.shape[0]
    size = blocks.shape[-1]
    away = normed_ref[:, own:]
    for j in range(members):
        blocks[dp ^ j] = dot_plain(away, weights[j][:, :size])
    raw = join_lanes(blocks) + dot_plain(normed_ref[:, :own], local_ref[...])
    roped = rope_lanes(raw, cos_ref[...], sin_ref[...]).astype(BF16)
    queries_ref[...] = roped * jnp.asarray(1.0 / math.sqrt(HEAD_DIM), BF16)
    columns = GROUPS * queries_ref.shape[0]
    query_pos = query_pos_ref[...]
    for head in range(KV_HEADS):
        stacked = heads_of(queries_ref, head * GROUPS, GROUPS)
        start = (
            jnp.full((1, columns), MASKED, F32),
            jnp.zeros((1, columns), F32),
            jnp.zeros((HEAD_DIM, columns), F32),
        )
        largest, total, weighted = attend(
            chunk, head, kv_ref, key_pos_ref, query_pos, stacked, start
        )
        largest_ref[head : head + 1, :] = largest
        total_ref[head : head + 1, :] = total
        weighted_ref[head] = weighted


def far_kernel(chunk, shards, members, pieces, spots, *refs):
    ins, outs, scratch = split_refs(refs, 9 + members + pieces, 6, 3)
    (queries_ref, key_pos_ref, query_pos_ref, largest_ref, total_ref, weighted_ref, tokens_ref,
     gains_ref, local_ref) = ins[:9]
    weights, parts = split_refs(ins[9:], members, pieces)
    attended_ref, turned_ref, log_ref, residual_ref, inverse_ref, normed_ref = outs
    blocks, kv_ref, head_blocks = scratch
    shard, dp = spots[1], spots[2]
    stack_rows(kv_ref, parts)
    rows = queries_ref.shape[0]
    query_pos = query_pos_ref[...]
    heads = []
    for head in range(KV_HEADS):
        stacked = heads_of(queries_ref, head * GROUPS, GROUPS)
        start = (largest_ref[head : head + 1, :], total_ref[head : head + 1, :], weighted_ref[head])
        largest, total, weighted = attend(
            chunk, head, kv_ref, key_pos_ref, query_pos, stacked, start
        )
        turned = weighted / total
        turned_ref[head] = turned
        log_ref[head : head + 1, :] = largest + jnp.log(total)
        straight = turned.T
        heads += [straight[g * rows : (g + 1) * rows, :] for g in range(GROUPS)]
    attended = jnp.concatenate(heads, axis=1).astype(BF16)
    attended_ref[...] = attended
    for z, block in enumerate(lane_blocks(attended, shards)):
        head_blocks[z] = block
    away = jnp.concatenate([head_blocks[shard ^ r] for r in range(1, shards)], axis=1)
    size = blocks.shape[-1]
    for j in range(members):
        blocks[dp ^ j] = dot_plain(away, weights[j][:, size:])
    added = join_lanes(blocks) + dot_plain(head_blocks[shard], local_ref[...])
    residual = tokens_ref[...].astype(F32) + added
    residual_ref[...] = residual
    normed, inverse = norm_rows(residual, gains_ref[1:2, :])
    inverse_ref[...] = inverse
    normed_ref[...] = normed.astype(BF16)


def unfold_down(pack_ref, down_ref, shards, part):
    piece = part // shards
    rows = pack_ref.shape[0] // shards
    for b in range(down_ref.shape[0] // rows):
        at = 2 * part + b * piece
        down_ref[b * rows : (b + 1) * rows, :] = jnp.concatenate(
            [pack_ref[z * rows : (z + 1) * rows, at : at + piece] for z in range(shards)], axis=1
        )


def feed_kernel(shards, masks, spots, *refs):
    ins, outs, scratch = split_refs(refs, 2 + len(masks), 3, 3)
    pack_ref, cot_all, normed_parts = ins[0], ins[1], ins[2:]
    cot_parts = [cot_all[spots[3] ^ mask] for mask in masks]
    grad_ref, act_ref, both_ref = outs
    normed_ref, cot_ref, down_ref = scratch
    part = pack_ref.shape[1] // 3
    stack_rows(normed_ref, normed_parts)
    stack_rows(cot_ref, cot_parts)
    unfold_down(pack_ref, down_ref, shards, part)
    gate_up = dot_plain(normed_ref[...], pack_ref[:, : 2 * part])
    gate, upward = gate_up[:, :part], gate_up[:, part:]
    act_grad = dot_plain(cot_ref[...], down_ref[...])
    sigmoid_gate = jax.nn.sigmoid(gate)
    silu = gate * sigmoid_gate
    act_ref[...] = (silu * upward).astype(BF16)
    gate_grad = act_grad * upward * sigmoid_gate * (1.0 + gate * (1.0 - sigmoid_gate))
    both_ref[...] = jnp.concatenate([gate_grad, act_grad * silu], axis=1).astype(BF16)
    unstack_rows(grad_ref, dot_last(both_ref[...], pack_ref[:, : 2 * part]))


def feed_weights_kernel(shards, masks, spots, *refs):
    ins, outs, scratch = split_refs(refs, 6 + len(masks), 3, 5)
    pack_ref, act_a, act_b, both_a, both_b, cot_all = ins[:6]
    normed_parts = ins[6:]
    cot_parts = [cot_all[spots[3] ^ mask] for mask in masks]
    result_a, result_b, grad_ref = outs
    normed_ref, cot_ref, act_ref, both_ref, down_ref = scratch
    part = pack_ref.shape[1] // 3
    piece = part // shards
    rows = grad_ref.shape[0] // shards
    stack_rows(normed_ref, normed_parts)
    stack_rows(cot_ref, cot_parts)
    stack_rows(act_ref, (act_a, act_b))
    stack_rows(both_ref, (both_a, both_b))
    unfold_down(pack_ref, down_ref, shards, part)
    grad_ref[:, : 2 * part] = dot_first(normed_ref[...], both_ref[...]).astype(BF16)
    down_grad = dot_first(cot_ref[...], act_ref[...]).astype(BF16)
    folds = down_grad.shape[0] // rows
    for z in range(shards):
        at = z * piece
        grad_ref[z * rows : (z + 1) * rows, 2 * part :] = jnp.concatenate(
            [down_grad[b * rows : (b + 1) * rows, at : at + piece] for b in range(folds)], axis=1
        )
    unstack_rows(result_a, dot_last(act_a[...], down_ref[...]))
    unstack_rows(result_b, dot_last(act_b[...], down_ref[...]))


def middle_kernel(shards, members, spots, *refs):
    ins, outs, scratch = split_refs(refs, 10 + members, 4, 2)
    (own_a, own_b, one_ref, two_ref, three_ref, residual_ref, inverse_ref, cot_ref, gains_ref,
     local_ref) = ins[:10]
    weights = ins[10:]
    residual_grad_ref, low_ref, attended_grad_ref, gain_grad_ref = outs
    rows = cot_ref.shape[0]
    grad = (own_a[0].astype(F32) + own_b[0].astype(F32)) + one_ref[...].astype(F32)
    grad = grad + two_ref[...].astype(F32) + three_ref[...].astype(F32)
    residual, inverse = residual_ref[...], inverse_ref[...]
    gain_grad_ref[...] = jnp.sum(grad * residual * inverse, axis=0, keepdims=True)
    residual_grad = cot_ref[...].astype(F32) + norm_back(grad, residual, inverse, gains_ref[1:2, :])
    residual_grad_ref[...] = residual_grad
    low = residual_grad.astype(BF16)
    low_ref[...] = low
    attended_grad_ref[...] = back_through(
        shards, members, spots, low, weights, local_ref, scratch, 1
    ).astype(BF16)


def back_through(shards, members, spots, low, weights, local_ref, scratch, which):
    blocks, out_blocks = scratch
    shard, dp = spots[1], spots[2]
    for i, block in enumerate(lane_blocks(low, members)):
        blocks[i] = block
    size = blocks.shape[-1]
    at = slice(which * size, (which + 1) * size)
    away = sum(dot_last(blocks[dp ^ j], weights[j][:, at]) for j in range(members))
    out_blocks[shard] = dot_last(low, local_ref[...])
    for r, block in enumerate(lane_blocks(away, shards - 1)):
        out_blocks[shard ^ (r + 1)] = block
    return join_lanes(out_blocks)


def weight_grads_kernel(members, spots, *refs):
    lefts, lows, (keep_ref, send_ref, blocks) = refs[0:4:2], refs[1:4:2], refs[4:]
    dp = spots[2]
    for k, (left_ref, low_ref) in enumerate(zip(lefts, lows)):
        for i, block in enumerate(lane_blocks(low_ref[...], members)):
            blocks[k * members + i] = block
    for j in (1, 3, 0, 2):
        out_ref = send_ref if j & 1 else keep_ref
        out_ref[j // 2] = jnp.concatenate(
            [
                dot_first(left_ref[...], blocks[k * members + (dp ^ j)])
                for k, left_ref in enumerate(lefts)
            ],
            axis=1,
        ).astype(BF16)


def join_kernel(members, spots, own_ref, across_ref, core_ref, core_across_ref, *refs):
    outs, blocks = refs[:2], refs[2]
    dp = spots[2]
    for j, ref in enumerate((own_ref, core_ref, across_ref, core_across_ref)):
        blocks[dp ^ j] = ref[...]
    size = blocks.shape[-1] // 2
    for k, out_ref in enumerate(outs):
        out_ref[...] = jnp.concatenate(
            [blocks[i][:, k * size : (k + 1) * size] for i in range(members)], axis=1
        ).astype(F32)


def query_back_kernel(shards, members, spots, low_ref, local_ref, *refs):
    weights, (back_ref,), scratch = split_refs(refs, members, 1, 2)
    back_ref[...] = back_through(
        shards, members, spots, low_ref[...], weights, local_ref, scratch, 0
    )


def back_kernel(chunk, pieces, first, last, spots, *refs):
    ins, outs, scratch = split_refs(refs, 9 + pieces, (pieces if last else 1) + 1, 2)
    (queries_ref, key_pos_ref, query_pos_ref, cos_ref, sin_ref, turned_ref, log_ref, grad_ref,
     start_ref) = ins[:9]
    parts = ins[9:]
    query_grad_ref, kv_grads = outs[0], outs[1:]
    kv_ref, kv_grad_ref = scratch
    stack_rows(kv_ref, parts)
    rows = queries_ref.shape[0]
    columns = GROUPS * rows
    query_pos = query_pos_ref[...]
    heads = []
    for head in range(KV_HEADS):
        stacked = heads_of(queries_ref, head * GROUPS, GROUPS)
        upstream = heads_of(grad_ref, head * GROUPS, GROUPS)
        delta = jnp.sum(upstream.astype(F32).T * turned_ref[head], axis=0, keepdims=True)
        log_total = log_ref[head : head + 1, :]
        keys_at = head * HEAD_DIM
        values_at = (KV_HEADS + head) * HEAD_DIM

        def step(j, query_grad, head=head, stacked=stacked, upstream=upstream,
                 delta=delta, log_total=log_total, keys_at=keys_at, values_at=values_at):
            at = pl.ds(pl.multiple_of(j * chunk, chunk), chunk)
            keys = heads_of(kv_ref, head, 1, at)
            values = heads_of(kv_ref, KV_HEADS + head, 1, at)
            scores = dot_last(keys, stacked)
            scores = jnp.where(key_pos_ref[at, :] <= query_pos, scores, MASKED)
            weights = jnp.exp(scores - log_total)
            weight_grad = dot_last(values, upstream)
            score_grad = (weights * (weight_grad - delta)).astype(BF16)
            value_grad = dot_plain(weights.astype(BF16), upstream)
            key_grad = dot_plain(score_grad, stacked)
            kv_grad_ref[at, keys_at : keys_at + HEAD_DIM] = key_grad.astype(BF16)
            kv_grad_ref[at, values_at : values_at + HEAD_DIM] = value_grad.astype(BF16)
            return query_grad + dot_first(keys, score_grad)

        start = jnp.zeros((HEAD_DIM, columns), F32) if first else start_ref[head]
        query_grad = lax.fori_loop(0, kv_ref.shape[0] // chunk, step, start)
        if not last:
            query_grad_ref[head] = query_grad
        else:
            straight = query_grad.T * (1.0 / math.sqrt(HEAD_DIM))
            heads += [straight[g * rows : (g + 1) * rows, :] for g in range(GROUPS)]
    if last:
        query_grad_ref[...] = rope_lanes(
            jnp.concatenate(heads, axis=1), cos_ref[...], -sin_ref[...]
        ).astype(BF16)
    if last:
        for i in range(pieces):
            kv_grads[i][...] = kv_grad_ref[i * rows : (i + 1) * rows, :]
    else:
        unstack_rows(kv_grads[0], kv_grad_ref[...])


def end_kernel(shards, spots, *refs):
    ins, outs, scratch = split_refs(refs, 11 + (shards + 1) + 2 * (shards - 1), 3, 1)
    (cos_ref, sin_ref, normed_ref, tokens_ref, inverse_ref, gains_ref, back_ref, residual_grad_ref,
     key_ref, value_ref, gain_two_ref) = ins[:11]
    sums, mine, other = split_refs(ins[11:], shards + 1, shards - 1, shards - 1)
    input_grad_ref, keep_ref, send_ref = outs
    (blocks,) = scratch
    core, shard = spots[0], spots[1]
    width, span = key_ref.shape
    rows = tokens_ref.shape[0]
    total = sums[0][...].astype(F32) + sums[1][0].astype(F32)
    total = total + sum(s[...].astype(F32) for s in sums[2:])
    keys = rope_lanes(total[:, :width], cos_ref[...], -sin_ref[...])
    values = total[:, width:]
    keep = jnp.where(core == 0, keys, values).astype(BF16)
    send = jnp.where(core == 0, values, keys).astype(BF16)
    blocks[shard] = dot_plain(keys.astype(BF16), key_ref[...]) + dot_plain(
        values.astype(BF16), value_ref[...]
    )
    for r in range(1, shards):
        blocks[shard ^ r] = dot_plain(keep, mine[r - 1][:width, :]) + dot_plain(
            send, other[r - 1][:width, :]
        )
    normed_grad = back_ref[...] + join_lanes(blocks)
    inputs, inverse = tokens_ref[...].astype(F32), inverse_ref[...]
    gain_grad = jnp.sum(normed_grad * inputs * inverse, axis=0, keepdims=True)
    input_grad_ref[...] = residual_grad_ref[...] + norm_back(
        normed_grad, inputs, inverse, gains_ref[0:1, :]
    )
    normed = normed_ref[...]
    two = gain_two_ref[...]
    for out_ref, low, gain in (
        (send_ref, send, jnp.where(core == 0, two, gain_grad)),
        (keep_ref, keep, jnp.where(core == 0, gain_grad, two)),
    ):
        grad = dot_first(low, normed).astype(BF16)
        gains = lane_blocks(gain, shards)
        for z, block in enumerate(lane_blocks(grad, shards)):
            out_ref[z, :width, :] = block
            out_ref[z, width:, :] = jnp.broadcast_to(
                gains[z], (EXTRA_ROWS, span)
            ).astype(BF16)


def spread_kernel(shards, members, spots, *refs):
    parts, outs, (blocks,) = split_refs(refs, members, 3, 1)
    gate_ref, up_ref, down_ref = outs
    member = spots[3]
    piece = parts[0].shape[1] // 3 // shards
    rows = parts[0].shape[0]
    span = piece * members
    for i in range(members):
        blocks[member ^ i] = parts[i][...]

    def block(k):
        at = k * piece
        return jnp.concatenate(
            [blocks[p, :, at : at + piece] for p in range(members)], axis=1
        ).astype(F32)

    for z in range(shards):
        gate_ref[:, z * span : (z + 1) * span] = block(z)
        up_ref[:, z * span : (z + 1) * span] = block(shards + z)
    for b in range(down_ref.shape[0] // rows):
        down_ref[b * rows : (b + 1) * rows, :] = block(2 * shards + b)


def base_of(block_order, stored, block_length):
    which = stored // block_length
    count = block_order.shape[1]
    matches = (which[:, None] == jnp.arange(count, dtype=jnp.int32)[None, :]).astype(jnp.int32)
    return jnp.sum(block_order[0][None, :] * matches, axis=-1) * block_length + stored % block_length


def tables(positions):
    half_dim = HEAD_DIM // 2
    exponent = -(jnp.arange(half_dim, dtype=F32) * 2.0) / HEAD_DIM
    frequency = jnp.power(F32(ROPE_BASE), exponent)
    angles = positions.astype(F32)[:, None] * frequency
    cosine, sine = jnp.cos(angles), jnp.sin(angles)
    return (
        jnp.concatenate([cosine] * 4, axis=-1),
        jnp.concatenate([-sine, sine, -sine, sine], axis=-1),
    )


def after(x, other):
    return lax.optimization_barrier((x, other))[0]


def on_device(
    tokens,
    block_order,
    attention_gain,
    query_weight,
    key_weight,
    value_weight,
    output_weight,
    feedforward_gain,
    gate_weight,
    up_weight,
    down_weight,
    cotangent,
):
    tokens, cotangent = tokens[0], cotangent[0]
    rows, width = tokens.shape
    shards = lax.axis_size("fsdp")
    ctx_count = lax.axis_size("ctx")
    dp_count = lax.axis_size("dp")
    block_length = rows * shards * ctx_count // block_order.shape[1]
    shard = lax.axis_index("fsdp")
    ctx = lax.axis_index("ctx")
    dp = lax.axis_index("dp")
    core = dp & 1
    members = dp_count * 2
    weight_rows = query_weight.shape[0]
    query_width = HEADS * HEAD_DIM
    kv_width = KV_HEADS * HEAD_DIM
    hidden = gate_weight.shape[1]
    part = hidden // members
    spots = jnp.stack([core, shard, dp, dp * 2 + (ctx & 1)]).astype(jnp.int32)

    gain_one, gain_two = attention_gain[None, :], feedforward_gain[None, :]
    key_turned, value_turned, down_turned = key_weight.T, value_weight.T, down_weight.T
    kv_pack = jnp.concatenate(
        [
            jnp.where(core == 0, key_turned, value_turned),
            jnp.pad(
                jnp.concatenate([gain_one, gain_two], axis=0), ((0, EXTRA_ROWS - 2), (0, 0))
            ),
        ],
        axis=0,
    )
    kv_mine = [swap(kv_pack, "fsdp", r) for r in range(1, shards)]
    kv_other = [swap_core(piece) for piece in kv_mine]

    quarter = width // dp_count
    (quarters,) = call(
        functools.partial(quarter_kernel, dp_count), spots,
        [after(query_weight, kv_pack), output_weight],
        [((weight_rows, 2 * quarter), BF16)], name="quarter_columns",
    )
    quarter_pieces = [swap(quarters, "fsdp", r) for r in range(1, shards)]

    group_axes = ("dp", "ctx")
    extra = {}
    if ctx_count > 2:
        extra["axis_index_groups"] = [
            [d * ctx_count + c for d in range(dp_count) for c in (first, first + 1)]
            for first in range(0, ctx_count, 2)
        ]
    cot_all = lax.all_gather(cotangent, group_axes, axis=0, tiled=False, **extra)

    offsets = jnp.arange(rows, dtype=jnp.int32)
    my_start = (ctx * shards + shard) * rows
    positions = base_of(block_order, my_start[None], block_length) + offsets
    cosine, sine = tables(positions)
    query_pos = jnp.concatenate([positions] * GROUPS)[None, :]
    starts = jnp.stack(
        [((ctx ^ d) * shards + (shard ^ r)) * rows for d in range(ctx_count) for r in range(shards)]
    )
    key_pos = (base_of(block_order, starts, block_length)[:, None] + offsets[None, :]).reshape(-1, 1)
    near_count = shards * rows
    near_pos, far_pos = key_pos[:near_count], key_pos[near_count:]
    far_count = far_pos.shape[0]

    (pack,) = call(
        functools.partial(pack_kernel, shards, members), spots,
        [gate_weight, up_weight, down_turned], [((weight_rows, 3 * part), BF16)],
        name="pack_weights",
    )
    kv_own, normed_one, normed_turned, inverse_one, gains = call(
        functools.partial(begin_kernel, shards), spots,
        [
            lax.optimization_barrier((tokens, quarters, pack))[0], gain_one, gain_two, key_turned, value_turned, cosine, sine,
            *kv_mine, *kv_other,
        ],
        [
            ((rows, 2 * kv_width), BF16), ((rows, width), BF16), ((rows, width), BF16),
            ((rows, 1), F32), ((8, width), F32),
        ],
        scratch=[
            ((shards, rows, weight_rows), F32), ((shards, rows, weight_rows), BF16),
            ((shards, 8, weight_rows), F32),
        ],
        name="norm_keys_values",
    )
    (stacked,) = call(
        stack_kernel, spots, lax.optimization_barrier((kv_own, *quarter_pieces))[1:],
        [(((shards - 1) * weight_rows, 2 * quarter), BF16)], name="stack_quarters",
    )
    near = [kv_own] + [swap(kv_own, "fsdp", r) for r in range(1, shards)]
    across, *near = lax.optimization_barrier((swap_plane(stacked, 2, 0), *near))
    stacks = [stacked, swap_core(stacked), across, swap_core(across)]
    far = [swap(piece, "ctx", d) for d in range(1, ctx_count) for piece in near]

    pack, cot_all, _ = lax.optimization_barrier((pack, cot_all, near[-1]))
    pack_all = lax.all_gather(pack, "fsdp", axis=0, tiled=True)

    chunk = rows * 2
    unit = 2 * HEADS * rows * near_count * HEAD_DIM
    stat = ((KV_HEADS, GROUPS * rows), F32)
    turned_shape = ((KV_HEADS, HEAD_DIM, GROUPS * rows), F32)
    queries, largest, total, weighted = call(
        functools.partial(near_kernel, chunk, dp_count, shards), spots,
        [normed_turned, near_pos, query_pos, cosine, sine, query_weight, *stacks, *near],
        [((rows, query_width), BF16), stat, stat, turned_shape],
        scratch=[((dp_count, rows, quarter), F32), ((near_count, 2 * kv_width), BF16)],
        name="attention_near",
    )
    attended, turned, log_total, residual, inverse_two, normed_two = call(
        functools.partial(far_kernel, chunk, shards, dp_count, len(far)), spots,
        [
            queries, far_pos, query_pos, largest, total, weighted, tokens, gains,
            output_weight, *stacks, *far,
        ],
        [
            ((rows, query_width), BF16), turned_shape, stat, ((rows, width), F32),
            ((rows, 1), F32), ((rows, width), BF16),
        ],
        scratch=[
            ((dp_count, rows, quarter), F32), ((far_count, 2 * kv_width), BF16),
            ((shards, rows, weight_rows), BF16),
        ],
        name="attention_far",
    )

    normed_a, normed_b = plane_pieces(normed_two)
    token_shape = ((rows, width), BF16)
    half = 4 * rows
    half_shape = ((4, rows, width), BF16)

    masks = [2 * a + b for a, b in ((0, 0),) + CHIP_MASKS]
    core_masks = [mask ^ 2 for mask in masks]

    def feed(normed, masks):
        return call(
            functools.partial(feed_kernel, shards, masks), spots, [pack_all, cot_all, *normed],
            [half_shape, ((half, part), BF16), ((half, 2 * part), BF16)],
            scratch=[((half, width), BF16), ((half, width), BF16), ((width, part), BF16)],
        name="feed_forward",
        )

    grad_b, act_b, both_b = feed(normed_b, core_masks)
    from_core = swap_core(grad_b)
    grad_a, act_a, both_a = feed(normed_a, masks)

    def chip_sums(parts_a, parts_b):
        return [
            (parts_a[k].astype(F32) + parts_b[k].astype(F32)).astype(BF16)
            for k in range(1, 4)
        ]

    def send_chips(sums):
        return [swap_plane(x, a, b) for x, (a, b) in zip(sums, CHIP_MASKS)]

    grad_sums = chip_sums(grad_a, from_core)
    grad_chips = send_chips(grad_sums)
    act_a, *_ = lax.optimization_barrier((act_a, *grad_sums))
    result_a, result_b, pack_grad = call(
        functools.partial(feed_weights_kernel, shards, masks + core_masks), spots,
        [pack_all, act_a, act_b, both_a, both_b, cot_all, *normed_a, *normed_b],
        [half_shape, half_shape, ((width, 3 * part), BF16)],
        scratch=[
            ((2 * half, width), BF16), ((2 * half, width), BF16), ((2 * half, part), BF16),
            ((2 * half, 2 * part), BF16), ((width, part), BF16),
        ],
        name="feed_forward_weights",
    )
    pack_share = sum_far(lax.psum_scatter(pack_grad, "fsdp", scatter_dimension=0, tiled=True))

    pack_grad, *grad_chips = lax.optimization_barrier((pack_grad, *grad_chips))
    residual_grad, residual_low, attended_grad, second_gain_grad = call(
        functools.partial(middle_kernel, shards, dp_count), spots,
        [
            grad_a, from_core, *grad_chips, residual, inverse_two, cotangent, gains, output_weight,
            *stacks,
        ],
        [((rows, width), F32), token_shape, ((rows, query_width), BF16), ((1, width), F32)],
        scratch=[((dp_count, rows, quarter), BF16), ((shards, rows, weight_rows), F32)],
        name="residual_back",
    )

    result_core = swap_core(after(result_b, residual_low))
    attended_grad, result_a = lax.optimization_barrier((attended_grad, result_a))

    def sum_x(keep, away):
        sent = (keep[1].astype(F32) + away[1].astype(F32)).astype(BF16)
        return sent, (keep[0], away[0], swap_plane(sent, 2, 0))

    def pieces_z(terms):
        out = []
        for r in range(shards):
            at = (shard ^ r) * weight_rows
            parts = [
                lax.dynamic_slice_in_dim(x, at, weight_rows, 0).astype(F32) for x in terms
            ]
            out.append((parts[0] + parts[1] + parts[2]).astype(BF16))
        return out

    def sum_z(pieces):
        total = pieces[0].astype(F32)
        for r in range(1, shards):
            total = total + swap(pieces[r], "fsdp", r).astype(F32)
        return total.astype(BF16)

    def sum_y(own):
        return sum_far((own.astype(F32) + swap_plane(own, 0, 1).astype(F32)).astype(BF16))

    def finish_quarters(own):
        across = swap_plane(own, 2, 0)
        return call(
            functools.partial(join_kernel, dp_count), spots,
            [own, across, swap_core(own), swap_core(across)],
            [((weight_rows, width), F32)] * 2,
            scratch=[((dp_count, weight_rows, 2 * quarter), BF16)], name="join_columns",
        )

    def sum_chips(own):
        for a, b in ((2, 0), (0, 1)):
            own = (own.astype(F32) + swap_plane(own, a, b).astype(F32)).astype(BF16)
        return sum_far(own)

    def back(first, last, start, pos, pieces):
        count = pos.shape[0]
        shape = ((rows, query_width), BF16) if last else turned_shape
        out = call(
            functools.partial(back_kernel, chunk, len(pieces), first, last), spots,
            [
                queries, pos, query_pos, cosine, sine, turned, log_total, attended_grad, start,
                *pieces,
            ],
            [shape]
            + (
                [((rows, 2 * kv_width), BF16)] * len(pieces) if last
                else [((shards, rows, 2 * kv_width), BF16)]
            ),
            scratch=[((count, 2 * kv_width), BF16), ((count, 2 * kv_width), BF16)],
            name="attention_back_near" if last else "attention_back_far",
        )
        return out[0], out[1:]

    query_partial, far_grads = turned, []
    for d in range(1, ctx_count):
        at = (d - 1) * shards
        query_partial, grads = back(
            d == 1, False, query_partial, far_pos[at * rows : (at + shards) * rows],
            far[at : at + shards],
        )
        far_grads.append(swap(grads[0], "ctx", d))
    result_sent = (result_a[2:].astype(F32) + result_core[2:].astype(F32)).astype(BF16)
    query_partial, result_sent = lax.optimization_barrier((query_partial, result_sent))
    result_across = swap_plane(result_sent, 2, 0)
    query_low, near_grads = back(False, True, query_partial, near_pos, near)
    query_low, pack_share = lax.optimization_barrier((query_low, pack_share))
    result_across = after(result_across, query_low)
    result_own, result_along = [
        (result_a[k].astype(F32) + result_core[k].astype(F32)) + result_across[k].astype(F32)
        for k in (0, 1)
    ]
    result_along = result_along.astype(BF16)
    share_across = swap_plane(pack_share, 2, 0)
    query_low, result_along, far_grads[-1] = lax.optimization_barrier(
        (query_low, result_along, far_grads[-1])
    )

    def home(r):
        return sum(grads[r].astype(F32) for grads in far_grads)

    kv_arrived = {
        r: swap((near_grads[r].astype(F32) + home(r)).astype(BF16), "fsdp", r)
        for r in reversed(range(1, shards))
    }
    share_own, share_across, _ = lax.optimization_barrier(
        (pack_share, share_across, far_grads[-1])
    )
    share_a = [share_own, swap_plane(share_own, 0, 1), share_across, swap_plane(share_across, 0, 1)]

    pair_shape = ((2, width, 2 * quarter), BF16)
    weights_keep, weights_send = call(
        functools.partial(weight_grads_kernel, dp_count), spots,
        [attended, residual_low, normed_one, query_low], [pair_shape, pair_shape],
        scratch=[((2 * dp_count, rows, quarter), BF16)], name="query_output_weight_grads",
    )
    weights_away = swap_core(weights_send)
    query_turn = after(query_low, weights_send)
    (query_back,) = call(
        functools.partial(query_back_kernel, shards, dp_count), spots,
        [query_turn, query_weight, *stacks], [((rows, width), F32)],
        scratch=[((dp_count, rows, quarter), BF16), ((shards, rows, weight_rows), F32)],
        name="query_back",
    )
    _, weights_terms = sum_x(weights_keep, weights_away)
    weights_pieces = pieces_z(weights_terms)
    query_back, *weights_pieces = lax.optimization_barrier((query_back, *weights_pieces))
    span = kv_width + EXTRA_ROWS
    packed_shape = ((shards, span, weight_rows), BF16)
    home_all = far_grads[0]
    if ctx_count > 2:
        home_all = sum(grads.astype(F32) for grads in far_grads)
    input_grad, kv_keep, kv_send = call(
        functools.partial(end_kernel, shards), spots,
        [
            cosine, sine, normed_one, tokens, inverse_one, gains, query_back, residual_grad,
            key_turned, value_turned, second_gain_grad, near_grads[0], home_all,
            *[kv_arrived[r] for r in range(1, shards)], *kv_mine, *kv_other,
        ],
        [((rows, width), F32), packed_shape, packed_shape],
        scratch=[((shards, rows, weight_rows), F32)],
        name="keys_values_back",
    )
    kv_away = swap_core(kv_send)
    pieces = [
        (lax.dynamic_index_in_dim(kv_keep, shard ^ r, 0, keepdims=False).astype(F32)
         + lax.dynamic_index_in_dim(kv_away, shard ^ r, 0, keepdims=False).astype(F32)).astype(BF16)
        for r in range(shards)
    ]
    share_b = [swap_core(piece) for piece in share_a]
    kv_share = pieces[0].astype(F32)
    for r in range(1, shards):
        kv_share = kv_share + swap(pieces[r], "fsdp", r).astype(F32)
    kv_share = kv_share.astype(BF16)

    share_by_mask = [None] * members
    for k, (a, b) in enumerate(((0, 0),) + CHIP_MASKS):
        share_by_mask[2 * a + b] = share_a[k]
        share_by_mask[2 * (a ^ 1) + b] = share_b[k]
    gate_weight_grad, up_weight_grad, down_weight_grad = call(
        functools.partial(spread_kernel, shards, members), spots, share_by_mask,
        [
            ((weight_rows, hidden), F32), ((weight_rows, hidden), F32),
            ((width, down_weight.shape[0]), F32),
        ],
        scratch=[((members, weight_rows, 3 * part), BF16)],
        name="feed_forward_out",
    )
    weights_own = sum_y(sum_z(weights_pieces))
    kv_share, weights_own, result_along, *big = lax.optimization_barrier(
        (kv_share, weights_own, result_along, gate_weight_grad, up_weight_grad, down_weight_grad)
    )
    gate_weight_grad, up_weight_grad, down_weight_grad = big
    result = residual + (result_own + swap_plane(result_along, 0, 1).astype(F32))
    output_weight_grad, query_weight_grad = finish_quarters(weights_own)
    low = sum_chips(kv_share)
    away = swap_core(low)
    first = jnp.where(core == 0, low, away).astype(F32)
    second = jnp.where(core == 0, away, low).astype(F32)

    return (
        result[None],
        input_grad[None],
        first[kv_width],
        query_weight_grad,
        first[:kv_width].T,
        second[:kv_width].T,
        output_weight_grad,
        second[kv_width],
        gate_weight_grad,
        up_weight_grad,
        down_weight_grad.T,
    )


def solution(mesh):
    row = P("fsdp", None)
    token = P("dp", ("ctx", "fsdp"), None)
    return jax.shard_map(
        on_device,
        mesh=mesh,
        in_specs=(
            token, P("dp", None), P("fsdp"), row, row, row, row, P("fsdp"), row, row, row, token,
        ),
        out_specs=(
            token, token, P("fsdp"), row, row, row, row, P("fsdp"), row, row, row,
        ),
        check_vma=False,
    )
```

```python
import functools
import math

import jax
import jax.numpy as jnp
from jax import lax
from jax.experimental import pallas as pl
from jax.experimental.pallas import tpu as pltpu
from jax.sharding import PartitionSpec as P

HEADS = 15
KV_HEADS = 5
HEAD_DIM = 64
GROUPS = HEADS // KV_HEADS
LANES = 128

EPSILON = 1e-05
ROPE_BASE = 100000.0
MASKED = -1e30

F32 = jnp.float32
BF16 = jnp.bfloat16
VMEM_LIMIT = 56 * 1024 * 1024
FLOPS_PER_US = 1150 * 10**6
MEASURED_US = {
    "pack_weights": 4,
    "norm_keys_values": 4,
    "attention_near": 12,
    "attention_far": 14,
    "feed_forward": 8,
    "feed_forward_weights": 12,
    "residual_back": 6,
    "attention_back_far": 13,
    "attention_back_near": 14,
    "query_output_weight_grads": 0,
    "query_back": 0,
    "stack_quarters": 0,
    "quarter_columns": 0,
    "keys_values_back": 6,
    "feed_forward_out": 7,
}


def dot_plain(left, right):
    return jnp.dot(left, right, preferred_element_type=F32)


def dot_last(left, right):
    return lax.dot_general(left, right, (((1,), (1,)), ((), ())), preferred_element_type=F32)


def dot_first(left, right):
    return lax.dot_general(left, right, (((0,), (0,)), ((), ())), preferred_element_type=F32)


def swap(x, axis, mask):
    count = lax.axis_size(axis)
    return lax.ppermute(x, axis, [(i, i ^ mask) for i in range(count)])


def swap_plane(x, dp_mask, ctx_mask):
    ctx_count = lax.axis_size("ctx")
    pairs = []
    for d in range(lax.axis_size("dp")):
        for c in range(ctx_count):
            pairs.append((d * ctx_count + c, (d ^ dp_mask) * ctx_count + (c ^ ctx_mask)))
    return lax.ppermute(x, ("dp", "ctx"), pairs)


def swaps_fsdp(x):
    pieces = {0: x}
    for r in range(1, lax.axis_size("fsdp")):
        top = 1 << (r.bit_length() - 1)
        pieces[r] = swap(pieces[r - top], "fsdp", top)
    return [pieces[r] for r in range(1, lax.axis_size("fsdp"))]


def swap_core(x):
    return swap_plane(x, 1, 0)


CHIP_MASKS = ((0, 1), (2, 0), (2, 1))


def plane_pieces(x):
    mine = [x] + [swap_plane(x, a, b) for a, b in CHIP_MASKS]
    return mine, [swap_core(piece) for piece in mine]


def sum_far(x):
    count = lax.axis_size("ctx")
    if count == 2:
        return x
    groups = [list(range(0, count, 2)), list(range(1, count, 2))]
    return lax.psum(x.astype(F32), "ctx", axis_index_groups=groups).astype(x.dtype)


def call(kernel, spots, args, out_shapes, scratch=(), name=None):
    specs = [pl.BlockSpec(memory_space=pltpu.SMEM)]
    specs += [pl.BlockSpec(memory_space=pltpu.VMEM) for _ in args]
    outs = tuple(jax.ShapeDtypeStruct(s, d) for s, d in out_shapes)
    return pl.pallas_call(
        kernel,
        out_shape=outs,
        in_specs=specs,
        out_specs=tuple(pl.BlockSpec(memory_space=pltpu.VMEM) for _ in outs),
        scratch_shapes=[pltpu.VMEM(s, d) for s, d in scratch],
        compiler_params=pltpu.CompilerParams(vmem_limit_bytes=VMEM_LIMIT),
        cost_estimate=pl.CostEstimate(
            flops=MEASURED_US.get(name, 2) * FLOPS_PER_US, bytes_accessed=0, transcendentals=0
        ),
        name=name,
    )(spots, *args)


def split_refs(refs, *counts):
    out, at = [], 0
    for n in counts:
        out.append(refs[at : at + n])
        at += n
    assert at == len(refs)
    return out


def lane_blocks(values, count):
    size = values.shape[1] // count
    return [values[:, i * size : (i + 1) * size] for i in range(count)]


def join_lanes(ref):
    return jnp.concatenate([ref[i] for i in range(ref.shape[0])], axis=1)


def rope_lanes(values, cosine, sine):
    rows, width = values.shape
    lane = lax.broadcasted_iota(jnp.int32, (rows, LANES), 1)
    first_half = (lane % HEAD_DIM) < (HEAD_DIM // 2)
    out = []
    for start in range(0, width, LANES):
        piece = values[:, start : min(start + LANES, width)]
        size = piece.shape[1]
        if size < LANES:
            piece = jnp.concatenate([piece, jnp.zeros((rows, LANES - size), piece.dtype)], axis=1)
        ahead = pltpu.roll(piece, LANES - HEAD_DIM // 2, 1)
        behind = pltpu.roll(piece, HEAD_DIM // 2, 1)
        partner = jnp.where(first_half, ahead, behind)
        out.append((piece * cosine + partner * sine)[:, :size])
    return jnp.concatenate(out, axis=1)


def heads_of(ref, first, count, rows=None):
    out = []
    for h in range(first, first + count):
        start = (h * HEAD_DIM) // LANES * LANES
        stop = min(start + LANES, ref.shape[-1])
        pair = ref[:, start:stop] if rows is None else ref[rows, start:stop]
        at = h * HEAD_DIM - start
        out.append(pair[:, at : at + HEAD_DIM])
    return out[0] if count == 1 else jnp.concatenate(out, axis=0)


def stack_rows(scratch, pieces):
    rows = pieces[0].shape[0]
    for i, piece in enumerate(pieces):
        scratch[i * rows : (i + 1) * rows, :] = piece[...]


def unstack_rows(out_ref, values):
    count, rows = out_ref.shape[:2]
    for i in range(count):
        out_ref[i] = values[i * rows : (i + 1) * rows, :].astype(out_ref.dtype)


def norm_rows(values, gain):
    inverse = lax.rsqrt(jnp.mean(values * values, axis=-1, keepdims=True) + EPSILON)
    return (values * inverse * gain, inverse)


def norm_back(gradient, values, inverse, gain):
    scaled = gradient * gain
    inner_mean = jnp.mean(scaled * values, axis=-1, keepdims=True)
    return inverse * scaled - values * (inverse * inverse * inverse) * inner_mean


EXTRA_ROWS = 16


def pack_kernel(shards, members, spots, gate_ref, up_ref, down_ref, out_ref):
    member = spots[3]
    span = gate_ref.shape[1] // shards
    piece = span // members
    rows = gate_ref.shape[0]
    pick = (
        lax.broadcasted_iota(jnp.int32, (span, piece), 0)
        == lax.broadcasted_iota(jnp.int32, (span, piece), 1) + member * piece
    ).astype(BF16)
    out = []
    for ref in (gate_ref, up_ref):
        for z in range(shards):
            out.append(dot_plain(ref[:, z * span : (z + 1) * span], pick))
    down = dot_plain(down_ref[...], pick)
    out += [down[b : b + rows, :] for b in range(0, down_ref.shape[0], rows)]
    out_ref[...] = jnp.concatenate(out, axis=1).astype(BF16)


def quarter_kernel(members, spots, query_ref, output_ref, out_ref):
    size = query_ref.shape[1] // members
    for i in range(members):

        @pl.when(spots[2] == i)
        def _():
            out_ref[...] = jnp.concatenate(
                [ref[:, i * size : (i + 1) * size] for ref in (query_ref, output_ref)], axis=1
            )


def stack_kernel(spots, *refs):
    stack_rows(refs[-1], refs[:-1])


def begin_kernel(shards, spots, *refs):
    ins, outs, scratch = split_refs(refs, 7 + 2 * (shards - 1), 5, 3)
    tokens_ref, gain_one, gain_two, key_ref, value_ref, cos_ref, sin_ref = ins[:7]
    mine, other = split_refs(ins[7:], shards - 1, shards - 1)
    kv_ref, normed_ref, turned_ref, inverse_ref, gains_ref = outs
    blocks, normed_blocks, gain_blocks = scratch
    core, shard = spots[0], spots[1]
    width = key_ref.shape[0]
    values = tokens_ref[...].astype(F32)
    inverse = lax.rsqrt(jnp.mean(values * values, axis=-1, keepdims=True) + EPSILON)
    inverse_ref[...] = inverse
    for z, block in enumerate(lane_blocks(values * inverse, shards)):
        blocks[z] = block
    sums, order = [], []
    for r in range(shards):
        at = shard ^ r
        if r == 0:
            pair = jnp.concatenate([gain_one[...], gain_two[...]], axis=0).astype(F32)
        else:
            pair = mine[r - 1][width : width + EXTRA_ROWS, :].astype(F32)[0:2, :]
        gain_blocks[at, 0:2, :] = pair
        normed = (blocks[at] * pair[0:1, :]).astype(BF16)
        normed_blocks[at] = normed
        order.append(normed)
        left = key_ref[...] if r == 0 else mine[r - 1][:width, :]
        right = value_ref[...] if r == 0 else other[r - 1][:width, :]
        sums.append((dot_last(normed, left), dot_last(normed, right)))
    first = sum(s[0] for s in sums[1:])
    second = sum(s[1] for s in sums[1:])
    keys = jnp.where(core == 0, first, second) + sums[0][0]
    vals = jnp.where(core == 0, second, first) + sums[0][1]
    keys = rope_lanes(keys, cos_ref[...], sin_ref[...])
    kv_ref[...] = jnp.concatenate([keys, vals], axis=1).astype(BF16)
    normed_ref[...] = join_lanes(normed_blocks)
    turned_ref[...] = jnp.concatenate(order, axis=1)
    gains_ref[...] = jnp.zeros_like(gains_ref)
    gains_ref[0:2, :] = jnp.concatenate([gain_blocks[z][0:2, :] for z in range(shards)], axis=1)


def attend(chunk, head, kv_ref, key_pos_ref, query_pos, stacked, state):
    def step(j, state):
        largest, total, weighted = state
        at = pl.ds(pl.multiple_of(j * chunk, chunk), chunk)
        keys = heads_of(kv_ref, head, 1, at)
        values = heads_of(kv_ref, KV_HEADS + head, 1, at)
        scores = dot_last(keys, stacked)
        scores = jnp.where(key_pos_ref[at, :] <= query_pos, scores, MASKED)
        new_largest = jnp.maximum(largest, jnp.max(scores, axis=0, keepdims=True))
        weights = jnp.exp(scores - new_largest)
        factor = jnp.exp(largest - new_largest)
        total = total * factor + jnp.sum(weights, axis=0, keepdims=True)
        weighted = weighted * factor + dot_first(values, weights.astype(BF16))
        return new_largest, total, weighted

    return lax.fori_loop(0, kv_ref.shape[0] // chunk, step, state)


def near_kernel(chunk, members, pieces, spots, *refs):
    ins, outs, scratch = split_refs(refs, 6 + members + pieces, 4, 2)
    normed_ref, key_pos_ref, query_pos_ref, cos_ref, sin_ref, local_ref = ins[:6]
    weights, parts = split_refs(ins[6:], members, pieces)
    queries_ref, largest_ref, total_ref, weighted_ref = outs
    blocks, kv_ref = scratch
    dp = spots[2]
    stack_rows(kv_ref, parts)
    own = local_ref.shape[0]
    size = blocks.shape[-1]
    away = normed_ref[:, own:]
    for j in range(members):
        blocks[dp ^ j] = dot_plain(away, weights[j][:, :size])
    raw = join_lanes(blocks) + dot_plain(normed_ref[:, :own], local_ref[...])
    roped = rope_lanes(raw, cos_ref[...], sin_ref[...]).astype(BF16)
    queries_ref[...] = roped * jnp.asarray(1.0 / math.sqrt(HEAD_DIM), BF16)
    columns = GROUPS * queries_ref.shape[0]
    query_pos = query_pos_ref[...]
    for head in range(KV_HEADS):
        stacked = heads_of(queries_ref, head * GROUPS, GROUPS)
        start = (
            jnp.full((1, columns), MASKED, F32),
            jnp.zeros((1, columns), F32),
            jnp.zeros((HEAD_DIM, columns), F32),
        )
        largest, total, weighted = attend(
            chunk, head, kv_ref, key_pos_ref, query_pos, stacked, start
        )
        largest_ref[head : head + 1, :] = largest
        total_ref[head : head + 1, :] = total
        weighted_ref[head] = weighted


def far_kernel(chunk, shards, members, pieces, spots, *refs):
    ins, outs, scratch = split_refs(refs, 9 + members + pieces, 6, 3)
    (queries_ref, key_pos_ref, query_pos_ref, largest_ref, total_ref, weighted_ref, tokens_ref,
     gains_ref, local_ref) = ins[:9]
    weights, parts = split_refs(ins[9:], members, pieces)
    attended_ref, turned_ref, log_ref, residual_ref, inverse_ref, normed_ref = outs
    blocks, kv_ref, head_blocks = scratch
    shard, dp = spots[1], spots[2]
    stack_rows(kv_ref, parts)
    rows = queries_ref.shape[0]
    query_pos = query_pos_ref[...]
    heads = []
    for head in range(KV_HEADS):
        stacked = heads_of(queries_ref, head * GROUPS, GROUPS)
        start = (largest_ref[head : head + 1, :], total_ref[head : head + 1, :], weighted_ref[head])
        largest, total, weighted = attend(
            chunk, head, kv_ref, key_pos_ref, query_pos, stacked, start
        )
        turned = weighted / total
        turned_ref[head] = turned
        log_ref[head : head + 1, :] = largest + jnp.log(total)
        straight = turned.T
        heads += [straight[g * rows : (g + 1) * rows, :] for g in range(GROUPS)]
    attended = jnp.concatenate(heads, axis=1).astype(BF16)
    attended_ref[...] = attended
    for z, block in enumerate(lane_blocks(attended, shards)):
        head_blocks[z] = block
    away = jnp.concatenate([head_blocks[shard ^ r] for r in range(1, shards)], axis=1)
    size = blocks.shape[-1]
    for j in range(members):
        blocks[dp ^ j] = dot_plain(away, weights[j][:, size:])
    added = join_lanes(blocks) + dot_plain(head_blocks[shard], local_ref[...])
    residual = tokens_ref[...].astype(F32) + added
    residual_ref[...] = residual
    normed, inverse = norm_rows(residual, gains_ref[1:2, :])
    inverse_ref[...] = inverse
    normed_ref[...] = normed.astype(BF16)


def unfold_down(pack_ref, down_ref, shards, part):
    piece = part // shards
    rows = pack_ref.shape[0] // shards
    for b in range(down_ref.shape[0] // rows):
        at = 2 * part + b * piece
        down_ref[b * rows : (b + 1) * rows, :] = jnp.concatenate(
            [pack_ref[z * rows : (z + 1) * rows, at : at + piece] for z in range(shards)], axis=1
        )


def feed_kernel(shards, masks, spots, *refs):
    ins, outs, scratch = split_refs(refs, 2 + len(masks), 3, 3)
    pack_ref, cot_all, normed_parts = ins[0], ins[1], ins[2:]
    cot_parts = [cot_all[spots[3] ^ mask] for mask in masks]
    grad_ref, act_ref, both_ref = outs
    normed_ref, cot_ref, down_ref = scratch
    part = pack_ref.shape[1] // 3
    stack_rows(normed_ref, normed_parts)
    stack_rows(cot_ref, cot_parts)
    unfold_down(pack_ref, down_ref, shards, part)
    gate_up = dot_plain(normed_ref[...], pack_ref[:, : 2 * part])
    gate, upward = gate_up[:, :part], gate_up[:, part:]
    act_grad = dot_plain(cot_ref[...], down_ref[...])
    sigmoid_gate = jax.nn.sigmoid(gate)
    silu = gate * sigmoid_gate
    act_ref[...] = (silu * upward).astype(BF16)
    gate_grad = act_grad * upward * sigmoid_gate * (1.0 + gate * (1.0 - sigmoid_gate))
    both_ref[...] = jnp.concatenate([gate_grad, act_grad * silu], axis=1).astype(BF16)
    unstack_rows(grad_ref, dot_last(both_ref[...], pack_ref[:, : 2 * part]))


def feed_weights_kernel(shards, masks, spots, *refs):
    ins, outs, scratch = split_refs(refs, 6 + len(masks), 3, 5)
    pack_ref, act_a, act_b, both_a, both_b, cot_all = ins[:6]
    normed_parts = ins[6:]
    cot_parts = [cot_all[spots[3] ^ mask] for mask in masks]
    result_a, result_b, grad_ref = outs
    normed_ref, cot_ref, act_ref, both_ref, down_ref = scratch
    part = pack_ref.shape[1] // 3
    piece = part // shards
    rows = grad_ref.shape[0] // shards
    stack_rows(normed_ref, normed_parts)
    stack_rows(cot_ref, cot_parts)
    stack_rows(act_ref, (act_a, act_b))
    stack_rows(both_ref, (both_a, both_b))
    unfold_down(pack_ref, down_ref, shards, part)
    grad_ref[:, : 2 * part] = dot_first(normed_ref[...], both_ref[...]).astype(BF16)
    down_grad = dot_first(cot_ref[...], act_ref[...]).astype(BF16)
    folds = down_grad.shape[0] // rows
    for z in range(shards):
        at = z * piece
        grad_ref[z * rows : (z + 1) * rows, 2 * part :] = jnp.concatenate(
            [down_grad[b * rows : (b + 1) * rows, at : at + piece] for b in range(folds)], axis=1
        )
    unstack_rows(result_a, dot_last(act_a[...], down_ref[...]))
    unstack_rows(result_b, dot_last(act_b[...], down_ref[...]))


def middle_kernel(shards, members, spots, *refs):
    ins, outs, scratch = split_refs(refs, 10 + members, 4, 2)
    (own_a, own_b, one_ref, two_ref, three_ref, residual_ref, inverse_ref, cot_ref, gains_ref,
     local_ref) = ins[:10]
    weights = ins[10:]
    residual_grad_ref, low_ref, attended_grad_ref, gain_grad_ref = outs
    rows = cot_ref.shape[0]
    grad = (own_a[0].astype(F32) + own_b[0].astype(F32)) + one_ref[...].astype(F32)
    grad = grad + two_ref[...].astype(F32) + three_ref[...].astype(F32)
    residual, inverse = residual_ref[...], inverse_ref[...]
    gain_grad_ref[...] = jnp.sum(grad * residual * inverse, axis=0, keepdims=True)
    residual_grad = cot_ref[...].astype(F32) + norm_back(grad, residual, inverse, gains_ref[1:2, :])
    residual_grad_ref[...] = residual_grad
    low = residual_grad.astype(BF16)
    low_ref[...] = low
    attended_grad_ref[...] = back_through(
        shards, members, spots, low, weights, local_ref, scratch, 1
    ).astype(BF16)


def back_through(shards, members, spots, low, weights, local_ref, scratch, which):
    blocks, out_blocks = scratch
    shard, dp = spots[1], spots[2]
    for i, block in enumerate(lane_blocks(low, members)):
        blocks[i] = block
    size = blocks.shape[-1]
    at = slice(which * size, (which + 1) * size)
    away = sum(dot_last(blocks[dp ^ j], weights[j][:, at]) for j in range(members))
    out_blocks[shard] = dot_last(low, local_ref[...])
    for r, block in enumerate(lane_blocks(away, shards - 1)):
        out_blocks[shard ^ (r + 1)] = block
    return join_lanes(out_blocks)


def weight_grads_kernel(members, spots, *refs):
    lefts, lows, (keep_ref, send_ref, blocks) = refs[0:4:2], refs[1:4:2], refs[4:]
    dp = spots[2]
    for k, (left_ref, low_ref) in enumerate(zip(lefts, lows)):
        for i, block in enumerate(lane_blocks(low_ref[...], members)):
            blocks[k * members + i] = block
    for j in (1, 3, 0, 2):
        out_ref = send_ref if j & 1 else keep_ref
        out_ref[j // 2] = jnp.concatenate(
            [
                dot_first(left_ref[...], blocks[k * members + (dp ^ j)])
                for k, left_ref in enumerate(lefts)
            ],
            axis=1,
        ).astype(BF16)


def join_kernel(members, spots, own_ref, across_ref, core_ref, core_across_ref, *refs):
    outs, blocks = refs[:2], refs[2]
    dp = spots[2]
    for j, ref in enumerate((own_ref, core_ref, across_ref, core_across_ref)):
        blocks[dp ^ j] = ref[...]
    size = blocks.shape[-1] // 2
    for k, out_ref in enumerate(outs):
        out_ref[...] = jnp.concatenate(
            [blocks[i][:, k * size : (k + 1) * size] for i in range(members)], axis=1
        ).astype(F32)


def query_back_kernel(shards, members, spots, low_ref, local_ref, *refs):
    weights, (back_ref,), scratch = split_refs(refs, members, 1, 2)
    back_ref[...] = back_through(
        shards, members, spots, low_ref[...], weights, local_ref, scratch, 0
    )


def back_kernel(chunk, pieces, first, last, spots, *refs):
    ins, outs, scratch = split_refs(refs, 9 + pieces, (pieces if last else 1) + 1, 2)
    (queries_ref, key_pos_ref, query_pos_ref, cos_ref, sin_ref, turned_ref, log_ref, grad_ref,
     start_ref) = ins[:9]
    parts = ins[9:]
    query_grad_ref, kv_grads = outs[0], outs[1:]
    kv_ref, kv_grad_ref = scratch
    stack_rows(kv_ref, parts)
    rows = queries_ref.shape[0]
    columns = GROUPS * rows
    query_pos = query_pos_ref[...]
    heads = []
    for head in range(KV_HEADS):
        stacked = heads_of(queries_ref, head * GROUPS, GROUPS)
        upstream = heads_of(grad_ref, head * GROUPS, GROUPS)
        delta = jnp.sum(upstream.astype(F32).T * turned_ref[head], axis=0, keepdims=True)
        log_total = log_ref[head : head + 1, :]
        keys_at = head * HEAD_DIM
        values_at = (KV_HEADS + head) * HEAD_DIM

        def step(j, query_grad, head=head, stacked=stacked, upstream=upstream,
                 delta=delta, log_total=log_total, keys_at=keys_at, values_at=values_at):
            at = pl.ds(pl.multiple_of(j * chunk, chunk), chunk)
            keys = heads_of(kv_ref, head, 1, at)
            values = heads_of(kv_ref, KV_HEADS + head, 1, at)
            scores = dot_last(keys, stacked)
            scores = jnp.where(key_pos_ref[at, :] <= query_pos, scores, MASKED)
            weights = jnp.exp(scores - log_total)
            weight_grad = dot_last(values, upstream)
            score_grad = (weights * (weight_grad - delta)).astype(BF16)
            value_grad = dot_plain(weights.astype(BF16), upstream)
            key_grad = dot_plain(score_grad, stacked)
            kv_grad_ref[at, keys_at : keys_at + HEAD_DIM] = key_grad.astype(BF16)
            kv_grad_ref[at, values_at : values_at + HEAD_DIM] = value_grad.astype(BF16)
            return query_grad + dot_first(keys, score_grad)

        start = jnp.zeros((HEAD_DIM, columns), F32) if first else start_ref[head]
        query_grad = lax.fori_loop(0, kv_ref.shape[0] // chunk, step, start)
        if not last:
            query_grad_ref[head] = query_grad
        else:
            straight = query_grad.T * (1.0 / math.sqrt(HEAD_DIM))
            heads += [straight[g * rows : (g + 1) * rows, :] for g in range(GROUPS)]
    if last:
        query_grad_ref[...] = rope_lanes(
            jnp.concatenate(heads, axis=1), cos_ref[...], -sin_ref[...]
        ).astype(BF16)
    if last:
        for i in range(pieces):
            kv_grads[i][...] = kv_grad_ref[i * rows : (i + 1) * rows, :]
    else:
        unstack_rows(kv_grads[0], kv_grad_ref[...])


def end_kernel(shards, spots, *refs):
    ins, outs, scratch = split_refs(refs, 11 + (shards + 1) + 2 * (shards - 1), 3, 1)
    (cos_ref, sin_ref, normed_ref, tokens_ref, inverse_ref, gains_ref, back_ref, residual_grad_ref,
     key_ref, value_ref, gain_two_ref) = ins[:11]
    sums, mine, other = split_refs(ins[11:], shards + 1, shards - 1, shards - 1)
    input_grad_ref, keep_ref, send_ref = outs
    (blocks,) = scratch
    core, shard = spots[0], spots[1]
    width, span = key_ref.shape
    rows = tokens_ref.shape[0]
    total = sums[0][...].astype(F32) + sums[1][0].astype(F32)
    total = total + sum(s[...].astype(F32) for s in sums[2:])
    keys = rope_lanes(total[:, :width], cos_ref[...], -sin_ref[...])
    values = total[:, width:]
    keep = jnp.where(core == 0, keys, values).astype(BF16)
    send = jnp.where(core == 0, values, keys).astype(BF16)
    blocks[shard] = dot_plain(keys.astype(BF16), key_ref[...]) + dot_plain(
        values.astype(BF16), value_ref[...]
    )
    for r in range(1, shards):
        blocks[shard ^ r] = dot_plain(keep, mine[r - 1][:width, :]) + dot_plain(
            send, other[r - 1][:width, :]
        )
    normed_grad = back_ref[...] + join_lanes(blocks)
    inputs, inverse = tokens_ref[...].astype(F32), inverse_ref[...]
    gain_grad = jnp.sum(normed_grad * inputs * inverse, axis=0, keepdims=True)
    input_grad_ref[...] = residual_grad_ref[...] + norm_back(
        normed_grad, inputs, inverse, gains_ref[0:1, :]
    )
    normed = normed_ref[...]
    two = gain_two_ref[...]
    for out_ref, low, gain in (
        (send_ref, send, jnp.where(core == 0, two, gain_grad)),
        (keep_ref, keep, jnp.where(core == 0, gain_grad, two)),
    ):
        grad = dot_first(low, normed).astype(BF16)
        gains = lane_blocks(gain, shards)
        for z, block in enumerate(lane_blocks(grad, shards)):
            out_ref[z, :width, :] = block
            out_ref[z, width:, :] = jnp.broadcast_to(
                gains[z], (EXTRA_ROWS, span)
            ).astype(BF16)


def spread_kernel(shards, members, spots, *refs):
    parts, outs, (blocks,) = split_refs(refs, members, 3, 1)
    gate_ref, up_ref, down_ref = outs
    member = spots[3]
    piece = parts[0].shape[1] // 3 // shards
    rows = parts[0].shape[0]
    span = piece * members
    for i in range(members):
        blocks[member ^ i] = parts[i][...]

    def block(k):
        at = k * piece
        return jnp.concatenate(
            [blocks[p, :, at : at + piece] for p in range(members)], axis=1
        ).astype(F32)

    for z in range(shards):
        gate_ref[:, z * span : (z + 1) * span] = block(z)
        up_ref[:, z * span : (z + 1) * span] = block(shards + z)
    for b in range(down_ref.shape[0] // rows):
        down_ref[b * rows : (b + 1) * rows, :] = block(2 * shards + b)


def base_of(block_order, stored, block_length):
    which = stored // block_length
    count = block_order.shape[1]
    matches = (which[:, None] == jnp.arange(count, dtype=jnp.int32)[None, :]).astype(jnp.int32)
    return jnp.sum(block_order[0][None, :] * matches, axis=-1) * block_length + stored % block_length


def tables(positions):
    half_dim = HEAD_DIM // 2
    exponent = -(jnp.arange(half_dim, dtype=F32) * 2.0) / HEAD_DIM
    frequency = jnp.power(F32(ROPE_BASE), exponent)
    angles = positions.astype(F32)[:, None] * frequency
    cosine, sine = jnp.cos(angles), jnp.sin(angles)
    return (
        jnp.concatenate([cosine] * 4, axis=-1),
        jnp.concatenate([-sine, sine, -sine, sine], axis=-1),
    )


def after(x, other):
    return lax.optimization_barrier((x, other))[0]


def on_device(
    tokens,
    block_order,
    attention_gain,
    query_weight,
    key_weight,
    value_weight,
    output_weight,
    feedforward_gain,
    gate_weight,
    up_weight,
    down_weight,
    cotangent,
):
    tokens, cotangent = tokens[0], cotangent[0]
    rows, width = tokens.shape
    shards = lax.axis_size("fsdp")
    ctx_count = lax.axis_size("ctx")
    dp_count = lax.axis_size("dp")
    block_length = rows * shards * ctx_count // block_order.shape[1]
    shard = lax.axis_index("fsdp")
    ctx = lax.axis_index("ctx")
    dp = lax.axis_index("dp")
    core = dp & 1
    members = dp_count * 2
    weight_rows = query_weight.shape[0]
    query_width = HEADS * HEAD_DIM
    kv_width = KV_HEADS * HEAD_DIM
    hidden = gate_weight.shape[1]
    part = hidden // members
    spots = jnp.stack([core, shard, dp, dp * 2 + (ctx & 1)]).astype(jnp.int32)

    gain_one, gain_two = attention_gain[None, :], feedforward_gain[None, :]
    key_turned, value_turned, down_turned = key_weight.T, value_weight.T, down_weight.T
    kv_pack = jnp.concatenate(
        [
            jnp.where(core == 0, key_turned, value_turned),
            jnp.pad(
                jnp.concatenate([gain_one, gain_two], axis=0), ((0, EXTRA_ROWS - 2), (0, 0))
            ),
        ],
        axis=0,
    )
    kv_mine = swaps_fsdp(kv_pack)
    kv_other = [swap_core(piece) for piece in kv_mine]

    quarter = width // dp_count
    (quarters,) = call(
        functools.partial(quarter_kernel, dp_count), spots,
        [after(query_weight, kv_pack), output_weight],
        [((weight_rows, 2 * quarter), BF16)], name="quarter_columns",
    )
    quarter_pieces = swaps_fsdp(quarters)

    group_axes = ("dp", "ctx")
    extra = {}
    if ctx_count > 2:
        extra["axis_index_groups"] = [
            [d * ctx_count + c for d in range(dp_count) for c in (first, first + 1)]
            for first in range(0, ctx_count, 2)
        ]
    cot_all = lax.all_gather(cotangent, group_axes, axis=0, tiled=False, **extra)

    offsets = jnp.arange(rows, dtype=jnp.int32)
    my_start = (ctx * shards + shard) * rows
    positions = base_of(block_order, my_start[None], block_length) + offsets
    cosine, sine = tables(positions)
    query_pos = jnp.concatenate([positions] * GROUPS)[None, :]
    starts = jnp.stack(
        [((ctx ^ d) * shards + (shard ^ r)) * rows for d in range(ctx_count) for r in range(shards)]
    )
    key_pos = (base_of(block_order, starts, block_length)[:, None] + offsets[None, :]).reshape(-1, 1)
    near_count = shards * rows
    near_pos, far_pos = key_pos[:near_count], key_pos[near_count:]
    far_count = far_pos.shape[0]

    (pack,) = call(
        functools.partial(pack_kernel, shards, members), spots,
        [gate_weight, up_weight, down_turned], [((weight_rows, 3 * part), BF16)],
        name="pack_weights",
    )
    kv_own, normed_one, normed_turned, inverse_one, gains = call(
        functools.partial(begin_kernel, shards), spots,
        [
            lax.optimization_barrier((tokens, quarters, pack))[0], gain_one, gain_two, key_turned, value_turned, cosine, sine,
            *kv_mine, *kv_other,
        ],
        [
            ((rows, 2 * kv_width), BF16), ((rows, width), BF16), ((rows, width), BF16),
            ((rows, 1), F32), ((8, width), F32),
        ],
        scratch=[
            ((shards, rows, weight_rows), F32), ((shards, rows, weight_rows), BF16),
            ((shards, 8, weight_rows), F32),
        ],
        name="norm_keys_values",
    )
    near = [kv_own] + swaps_fsdp(kv_own)
    quarter_pieces = lax.optimization_barrier((kv_own, *quarter_pieces))[1:]
    (stacked,) = call(
        stack_kernel, spots, quarter_pieces,
        [(((shards - 1) * weight_rows, 2 * quarter), BF16)], name="stack_quarters",
    )
    across, *near = lax.optimization_barrier((swap_plane(stacked, 2, 0), *near))
    stacks = [stacked, swap_core(stacked), across, swap_core(across)]
    far = [swap(piece, "ctx", d) for d in range(1, ctx_count) for piece in near]

    pack, cot_all, _ = lax.optimization_barrier((pack, cot_all, near[-1]))
    pack_all = lax.all_gather(pack, "fsdp", axis=0, tiled=True)

    chunk = rows * 2
    unit = 2 * HEADS * rows * near_count * HEAD_DIM
    stat = ((KV_HEADS, GROUPS * rows), F32)
    turned_shape = ((KV_HEADS, HEAD_DIM, GROUPS * rows), F32)
    queries, largest, total, weighted = call(
        functools.partial(near_kernel, chunk, dp_count, shards), spots,
        [normed_turned, near_pos, query_pos, cosine, sine, query_weight, *stacks, *near],
        [((rows, query_width), BF16), stat, stat, turned_shape],
        scratch=[((dp_count, rows, quarter), F32), ((near_count, 2 * kv_width), BF16)],
        name="attention_near",
    )
    attended, turned, log_total, residual, inverse_two, normed_two = call(
        functools.partial(far_kernel, chunk, shards, dp_count, len(far)), spots,
        [
            queries, far_pos, query_pos, largest, total, weighted, tokens, gains,
            output_weight, *stacks, *far,
        ],
        [
            ((rows, query_width), BF16), turned_shape, stat, ((rows, width), F32),
            ((rows, 1), F32), ((rows, width), BF16),
        ],
        scratch=[
            ((dp_count, rows, quarter), F32), ((far_count, 2 * kv_width), BF16),
            ((shards, rows, weight_rows), BF16),
        ],
        name="attention_far",
    )

    normed_a, normed_b = plane_pieces(normed_two)
    token_shape = ((rows, width), BF16)
    half = 4 * rows
    half_shape = ((4, rows, width), BF16)

    masks = [2 * a + b for a, b in ((0, 0),) + CHIP_MASKS]
    core_masks = [mask ^ 2 for mask in masks]

    def feed(normed, masks):
        return call(
            functools.partial(feed_kernel, shards, masks), spots, [pack_all, cot_all, *normed],
            [half_shape, ((half, part), BF16), ((half, 2 * part), BF16)],
            scratch=[((half, width), BF16), ((half, width), BF16), ((width, part), BF16)],
        name="feed_forward",
        )

    grad_b, act_b, both_b = feed(normed_b, core_masks)
    from_core = swap_core(grad_b)
    grad_a, act_a, both_a = feed(normed_a, masks)

    def chip_sums(parts_a, parts_b):
        return [
            (parts_a[k].astype(F32) + parts_b[k].astype(F32)).astype(BF16)
            for k in range(1, 4)
        ]

    def send_chips(sums):
        return [swap_plane(x, a, b) for x, (a, b) in zip(sums, CHIP_MASKS)]

    grad_sums = chip_sums(grad_a, from_core)
    grad_chips = send_chips(grad_sums)
    act_a, *_ = lax.optimization_barrier((act_a, *grad_sums))
    result_a, result_b, pack_grad = call(
        functools.partial(feed_weights_kernel, shards, masks + core_masks), spots,
        [pack_all, act_a, act_b, both_a, both_b, cot_all, *normed_a, *normed_b],
        [half_shape, half_shape, ((width, 3 * part), BF16)],
        scratch=[
            ((2 * half, width), BF16), ((2 * half, width), BF16), ((2 * half, part), BF16),
            ((2 * half, 2 * part), BF16), ((width, part), BF16),
        ],
        name="feed_forward_weights",
    )
    pack_share = sum_far(lax.psum_scatter(pack_grad, "fsdp", scatter_dimension=0, tiled=True))

    pack_grad, *grad_chips = lax.optimization_barrier((pack_grad, *grad_chips))
    residual_grad, residual_low, attended_grad, second_gain_grad = call(
        functools.partial(middle_kernel, shards, dp_count), spots,
        [
            grad_a, from_core, *grad_chips, residual, inverse_two, cotangent, gains, output_weight,
            *stacks,
        ],
        [((rows, width), F32), token_shape, ((rows, query_width), BF16), ((1, width), F32)],
        scratch=[((dp_count, rows, quarter), BF16), ((shards, rows, weight_rows), F32)],
        name="residual_back",
    )

    result_core = swap_core(after(result_b, residual_low))
    attended_grad, result_a = lax.optimization_barrier((attended_grad, result_a))

    def sum_x(keep, away):
        sent = (keep[1].astype(F32) + away[1].astype(F32)).astype(BF16)
        return sent, (keep[0], away[0], swap_plane(sent, 2, 0))

    def pieces_z(terms):
        out = []
        for r in range(shards):
            at = (shard ^ r) * weight_rows
            parts = [
                lax.dynamic_slice_in_dim(x, at, weight_rows, 0).astype(F32) for x in terms
            ]
            out.append((parts[0] + parts[1] + parts[2]).astype(BF16))
        return out

    def sum_z(pieces):
        arrived = {r: swap(pieces[r], "fsdp", r) for r in reversed(range(1, shards))}
        return sum(
            (arrived[r].astype(F32) for r in range(1, shards)), pieces[0].astype(F32)
        ).astype(BF16)

    def relay_z(terms):
        span = shards
        pieces = {r: piece.astype(F32) for r, piece in enumerate(pieces_z(terms))}
        while span > 1:
            span //= 2
            sent = jnp.stack([pieces[r].astype(BF16) for r in range(span, 2 * span)])
            arrived = swap(sent, "fsdp", span)
            pieces = {r: pieces[r] + arrived[r].astype(F32) for r in range(span)}
        return pieces[0].astype(BF16)

    def sum_y(own):
        return sum_far((own.astype(F32) + swap_plane(own, 0, 1).astype(F32)).astype(BF16))

    def finish_quarters(own):
        across = swap_plane(own, 2, 0)
        return call(
            functools.partial(join_kernel, dp_count), spots,
            [own, across, swap_core(own), swap_core(across)],
            [((weight_rows, width), F32)] * 2,
            scratch=[((dp_count, weight_rows, 2 * quarter), BF16)], name="join_columns",
        )

    def sum_chips(own):
        for a, b in ((2, 0), (0, 1)):
            own = (own.astype(F32) + swap_plane(own, a, b).astype(F32)).astype(BF16)
        return sum_far(own)

    def back(first, last, start, pos, pieces):
        count = pos.shape[0]
        shape = ((rows, query_width), BF16) if last else turned_shape
        out = call(
            functools.partial(back_kernel, chunk, len(pieces), first, last), spots,
            [
                queries, pos, query_pos, cosine, sine, turned, log_total, attended_grad, start,
                *pieces,
            ],
            [shape]
            + (
                [((rows, 2 * kv_width), BF16)] * len(pieces) if last
                else [((shards, rows, 2 * kv_width), BF16)]
            ),
            scratch=[((count, 2 * kv_width), BF16), ((count, 2 * kv_width), BF16)],
            name="attention_back_near" if last else "attention_back_far",
        )
        return out[0], out[1:]

    query_partial, far_grads = turned, []
    for d in range(1, ctx_count):
        at = (d - 1) * shards
        query_partial, grads = back(
            d == 1, False, query_partial, far_pos[at * rows : (at + shards) * rows],
            far[at : at + shards],
        )
        far_grads.append(swap(grads[0], "ctx", d))
    result_sent = (result_a[2:].astype(F32) + result_core[2:].astype(F32)).astype(BF16)
    query_partial, result_sent = lax.optimization_barrier((query_partial, result_sent))
    result_across = swap_plane(result_sent, 2, 0)
    query_low, near_grads = back(False, True, query_partial, near_pos, near)
    pair_shape = ((2, width, 2 * quarter), BF16)
    weights_keep, weights_send = call(
        functools.partial(weight_grads_kernel, dp_count), spots,
        [attended, residual_low, normed_one, query_low], [pair_shape, pair_shape],
        scratch=[((2 * dp_count, rows, quarter), BF16)], name="query_output_weight_grads",
    )
    weights_send, pack_share, result_across, far_grads[-1] = lax.optimization_barrier(
        (weights_send, pack_share, result_across, far_grads[-1])
    )

    def home(r):
        return sum(grads[r].astype(F32) for grads in far_grads)

    kv_sums = {
        r: (near_grads[r].astype(F32) + home(r)).astype(BF16) for r in range(1, shards)
    }
    kv_arrived = {r: swap(kv_sums[r], "fsdp", r) for r in reversed(range(1, shards))}
    query_low, result_across, *_ = lax.optimization_barrier(
        (query_low, result_across, *kv_sums.values())
    )
    result_own, result_along = [
        (result_a[k].astype(F32) + result_core[k].astype(F32)) + result_across[k].astype(F32)
        for k in (0, 1)
    ]
    result_along = result_along.astype(BF16)

    weights_away = swap_core(weights_send)
    query_turn = query_low
    (query_back,) = call(
        functools.partial(query_back_kernel, shards, dp_count), spots,
        [query_turn, query_weight, *stacks], [((rows, width), F32)],
        scratch=[((dp_count, rows, quarter), BF16), ((shards, rows, weight_rows), F32)],
        name="query_back",
    )
    weights_sent, weights_terms = sum_x(weights_keep, weights_away)
    query_back, weights_sent = lax.optimization_barrier((query_back, weights_sent))
    span = kv_width + EXTRA_ROWS
    packed_shape = ((shards, span, weight_rows), BF16)
    home_all = far_grads[0]
    if ctx_count > 2:
        home_all = sum(grads.astype(F32) for grads in far_grads)
    input_grad, kv_keep, kv_send = call(
        functools.partial(end_kernel, shards), spots,
        [
            cosine, sine, normed_one, tokens, inverse_one, gains, query_back, residual_grad,
            key_turned, value_turned, second_gain_grad, near_grads[0], home_all,
            *[kv_arrived[r] for r in range(1, shards)], *kv_mine, *kv_other,
        ],
        [((rows, width), F32), packed_shape, packed_shape],
        scratch=[((shards, rows, weight_rows), F32)],
        name="keys_values_back",
    )
    pack_share = after(pack_share, kv_send)
    share_across = swap_plane(pack_share, 2, 0)
    share_along = swap_plane(pack_share, 0, 1)
    kv_away = swap_core(kv_send)
    pieces = [
        (lax.dynamic_index_in_dim(kv_keep, shard ^ r, 0, keepdims=False).astype(F32)
         + lax.dynamic_index_in_dim(kv_away, shard ^ r, 0, keepdims=False).astype(F32)).astype(BF16)
        for r in range(shards)
    ]
    weights_terms, *pieces = lax.optimization_barrier((weights_terms, *pieces))
    kv_share = sum_z(pieces)
    kv_share, share_across, share_along = lax.optimization_barrier(
        (kv_share, share_across, share_along)
    )
    share_a = [pack_share, share_along, share_across, swap_plane(share_across, 0, 1)]
    share_b = [swap_core(piece) for piece in share_a]

    share_by_mask = [None] * members
    for k, (a, b) in enumerate(((0, 0),) + CHIP_MASKS):
        share_by_mask[2 * a + b] = share_a[k]
        share_by_mask[2 * (a ^ 1) + b] = share_b[k]
    gate_weight_grad, up_weight_grad, down_weight_grad = call(
        functools.partial(spread_kernel, shards, members), spots, share_by_mask,
        [
            ((weight_rows, hidden), F32), ((weight_rows, hidden), F32),
            ((width, down_weight.shape[0]), F32),
        ],
        scratch=[((members, weight_rows, 3 * part), BF16)],
        name="feed_forward_out",
    )
    kv_share, result_along = lax.optimization_barrier((kv_share, result_along))
    weights_own = sum_y(relay_z(weights_terms))
    result = residual + (result_own + swap_plane(result_along, 0, 1).astype(F32))
    output_weight_grad, query_weight_grad = finish_quarters(weights_own)
    low = sum_chips(kv_share)
    away = swap_core(low)
    first = jnp.where(core == 0, low, away).astype(F32)
    second = jnp.where(core == 0, away, low).astype(F32)

    return (
        result[None],
        input_grad[None],
        first[kv_width],
        query_weight_grad,
        first[:kv_width].T,
        second[:kv_width].T,
        output_weight_grad,
        second[kv_width],
        gate_weight_grad,
        up_weight_grad,
        down_weight_grad.T,
    )


def solution(mesh):
    row = P("fsdp", None)
    token = P("dp", ("ctx", "fsdp"), None)
    return jax.shard_map(
        on_device,
        mesh=mesh,
        in_specs=(
            token, P("dp", None), P("fsdp"), row, row, row, row, P("fsdp"), row, row, row, token,
        ),
        out_specs=(
            token, token, P("fsdp"), row, row, row, row, P("fsdp"), row, row, row,
        ),
        check_vma=False,
    )
```

```python
import functools
import math

import jax
import jax.numpy as jnp
from jax import lax
from jax.experimental import pallas as pl
from jax.experimental.pallas import tpu as pltpu
from jax.sharding import PartitionSpec as P

HEADS = 15
KV_HEADS = 5
HEAD_DIM = 64
GROUPS = HEADS // KV_HEADS
LANES = 128

EPSILON = 1e-05
ROPE_BASE = 100000.0
MASKED = -1e30

F32 = jnp.float32
BF16 = jnp.bfloat16
VMEM_LIMIT = 56 * 1024 * 1024
FLOPS_PER_US = 1150 * 10**6
MEASURED_US = {
    "pack_weights": 4,
    "norm_keys_values": 4,
    "attention_near": 12,
    "attention_far": 14,
    "feed_forward": 8,
    "feed_forward_weights": 12,
    "residual_back": 6,
    "attention_back_far": 13,
    "attention_back_near": 14,
    "query_output_weight_grads": 0,
    "query_back": 0,
    "stack_quarters": 0,
    "quarter_columns": 0,
    "keys_values_back": 6,
    "feed_forward_out": 7,
}


def dot_plain(left, right):
    return jnp.dot(left, right, preferred_element_type=F32)


def dot_last(left, right):
    return lax.dot_general(left, right, (((1,), (1,)), ((), ())), preferred_element_type=F32)


def dot_first(left, right):
    return lax.dot_general(left, right, (((0,), (0,)), ((), ())), preferred_element_type=F32)


def swap(x, axis, mask):
    count = lax.axis_size(axis)
    return lax.ppermute(x, axis, [(i, i ^ mask) for i in range(count)])


def swap_plane(x, dp_mask, ctx_mask):
    ctx_count = lax.axis_size("ctx")
    pairs = []
    for d in range(lax.axis_size("dp")):
        for c in range(ctx_count):
            pairs.append((d * ctx_count + c, (d ^ dp_mask) * ctx_count + (c ^ ctx_mask)))
    return lax.ppermute(x, ("dp", "ctx"), pairs)


def swaps_fsdp(x):
    pieces = {0: x}
    for r in range(1, lax.axis_size("fsdp")):
        top = 1 << (r.bit_length() - 1)
        pieces[r] = swap(pieces[r - top], "fsdp", top)
    return [pieces[r] for r in range(1, lax.axis_size("fsdp"))]


def direct_fsdp(x):
    return [swap(x, "fsdp", r) for r in range(1, lax.axis_size("fsdp"))]


def swap_core(x):
    return swap_plane(x, 1, 0)


CHIP_MASKS = ((0, 1), (2, 0), (2, 1))


def plane_pieces(x):
    mine = [x] + [swap_plane(x, a, b) for a, b in CHIP_MASKS]
    return mine, [swap_core(piece) for piece in mine]


def sum_far(x):
    count = lax.axis_size("ctx")
    if count == 2:
        return x
    groups = [list(range(0, count, 2)), list(range(1, count, 2))]
    return lax.psum(x.astype(F32), "ctx", axis_index_groups=groups).astype(x.dtype)


def call(kernel, spots, args, out_shapes, scratch=(), name=None):
    specs = [pl.BlockSpec(memory_space=pltpu.SMEM)]
    specs += [pl.BlockSpec(memory_space=pltpu.VMEM) for _ in args]
    outs = tuple(jax.ShapeDtypeStruct(s, d) for s, d in out_shapes)
    return pl.pallas_call(
        kernel,
        out_shape=outs,
        in_specs=specs,
        out_specs=tuple(pl.BlockSpec(memory_space=pltpu.VMEM) for _ in outs),
        scratch_shapes=[pltpu.VMEM(s, d) for s, d in scratch],
        compiler_params=pltpu.CompilerParams(vmem_limit_bytes=VMEM_LIMIT),
        cost_estimate=pl.CostEstimate(
            flops=MEASURED_US.get(name, 2) * FLOPS_PER_US, bytes_accessed=0, transcendentals=0
        ),
        name=name,
    )(spots, *args)


def split_refs(refs, *counts):
    out, at = [], 0
    for n in counts:
        out.append(refs[at : at + n])
        at += n
    assert at == len(refs)
    return out


def lane_blocks(values, count):
    size = values.shape[1] // count
    return [values[:, i * size : (i + 1) * size] for i in range(count)]


def join_lanes(ref):
    return jnp.concatenate([ref[i] for i in range(ref.shape[0])], axis=1)


def rope_lanes(values, cosine, sine):
    rows, width = values.shape
    lane = lax.broadcasted_iota(jnp.int32, (rows, LANES), 1)
    first_half = (lane % HEAD_DIM) < (HEAD_DIM // 2)
    out = []
    for start in range(0, width, LANES):
        piece = values[:, start : min(start + LANES, width)]
        size = piece.shape[1]
        if size < LANES:
            piece = jnp.concatenate([piece, jnp.zeros((rows, LANES - size), piece.dtype)], axis=1)
        ahead = pltpu.roll(piece, LANES - HEAD_DIM // 2, 1)
        behind = pltpu.roll(piece, HEAD_DIM // 2, 1)
        partner = jnp.where(first_half, ahead, behind)
        out.append((piece * cosine + partner * sine)[:, :size])
    return jnp.concatenate(out, axis=1)


def heads_of(ref, first, count, rows=None):
    out = []
    for h in range(first, first + count):
        start = (h * HEAD_DIM) // LANES * LANES
        stop = min(start + LANES, ref.shape[-1])
        pair = ref[:, start:stop] if rows is None else ref[rows, start:stop]
        at = h * HEAD_DIM - start
        out.append(pair[:, at : at + HEAD_DIM])
    return out[0] if count == 1 else jnp.concatenate(out, axis=0)


def stack_rows(scratch, pieces):
    rows = pieces[0].shape[0]
    for i, piece in enumerate(pieces):
        scratch[i * rows : (i + 1) * rows, :] = piece[...]


def unstack_rows(out_ref, values):
    count, rows = out_ref.shape[:2]
    for i in range(count):
        out_ref[i] = values[i * rows : (i + 1) * rows, :].astype(out_ref.dtype)


def norm_rows(values, gain):
    inverse = lax.rsqrt(jnp.mean(values * values, axis=-1, keepdims=True) + EPSILON)
    return (values * inverse * gain, inverse)


def norm_back(gradient, values, inverse, gain):
    scaled = gradient * gain
    inner_mean = jnp.mean(scaled * values, axis=-1, keepdims=True)
    return inverse * scaled - values * (inverse * inverse * inverse) * inner_mean


EXTRA_ROWS = 16


def pack_kernel(shards, members, spots, gate_ref, up_ref, down_ref, out_ref):
    member = spots[3]
    span = gate_ref.shape[1] // shards
    piece = span // members
    rows = gate_ref.shape[0]
    pick = (
        lax.broadcasted_iota(jnp.int32, (span, piece), 0)
        == lax.broadcasted_iota(jnp.int32, (span, piece), 1) + member * piece
    ).astype(BF16)
    out = []
    for ref in (gate_ref, up_ref):
        for z in range(shards):
            out.append(dot_plain(ref[:, z * span : (z + 1) * span], pick))
    down = dot_plain(down_ref[...], pick)
    out += [down[b : b + rows, :] for b in range(0, down_ref.shape[0], rows)]
    out_ref[...] = jnp.concatenate(out, axis=1).astype(BF16)


def quarter_kernel(members, spots, query_ref, output_ref, out_ref):
    size = query_ref.shape[1] // members
    for i in range(members):

        @pl.when(spots[2] == i)
        def _():
            out_ref[...] = jnp.concatenate(
                [ref[:, i * size : (i + 1) * size] for ref in (query_ref, output_ref)], axis=1
            )


def stack_kernel(spots, *refs):
    stack_rows(refs[-1], refs[:-1])


def begin_kernel(shards, spots, *refs):
    ins, outs, scratch = split_refs(refs, 7 + 2 * (shards - 1), 5, 3)
    tokens_ref, gain_one, gain_two, key_ref, value_ref, cos_ref, sin_ref = ins[:7]
    mine, other = split_refs(ins[7:], shards - 1, shards - 1)
    kv_ref, normed_ref, turned_ref, inverse_ref, gains_ref = outs
    blocks, normed_blocks, gain_blocks = scratch
    core, shard = spots[0], spots[1]
    width = key_ref.shape[0]
    values = tokens_ref[...].astype(F32)
    inverse = lax.rsqrt(jnp.mean(values * values, axis=-1, keepdims=True) + EPSILON)
    inverse_ref[...] = inverse
    for z, block in enumerate(lane_blocks(values * inverse, shards)):
        blocks[z] = block
    sums, order = [], []
    for r in range(shards):
        at = shard ^ r
        if r == 0:
            pair = jnp.concatenate([gain_one[...], gain_two[...]], axis=0).astype(F32)
        else:
            pair = mine[r - 1][width : width + EXTRA_ROWS, :].astype(F32)[0:2, :]
        gain_blocks[at, 0:2, :] = pair
        normed = (blocks[at] * pair[0:1, :]).astype(BF16)
        normed_blocks[at] = normed
        order.append(normed)
        left = key_ref[...] if r == 0 else mine[r - 1][:width, :]
        right = value_ref[...] if r == 0 else other[r - 1][:width, :]
        sums.append((dot_last(normed, left), dot_last(normed, right)))
    first = sum(s[0] for s in sums[1:])
    second = sum(s[1] for s in sums[1:])
    keys = jnp.where(core == 0, first, second) + sums[0][0]
    vals = jnp.where(core == 0, second, first) + sums[0][1]
    keys = rope_lanes(keys, cos_ref[...], sin_ref[...])
    kv_ref[...] = jnp.concatenate([keys, vals], axis=1).astype(BF16)
    normed_ref[...] = join_lanes(normed_blocks)
    turned_ref[...] = jnp.concatenate(order, axis=1)
    gains_ref[...] = jnp.zeros_like(gains_ref)
    gains_ref[0:2, :] = jnp.concatenate([gain_blocks[z][0:2, :] for z in range(shards)], axis=1)


def attend(chunk, head, kv_ref, key_pos_ref, query_pos, stacked, state):
    def step(j, state):
        largest, total, weighted = state
        at = pl.ds(pl.multiple_of(j * chunk, chunk), chunk)
        keys = heads_of(kv_ref, head, 1, at)
        values = heads_of(kv_ref, KV_HEADS + head, 1, at)
        scores = dot_last(keys, stacked)
        scores = jnp.where(key_pos_ref[at, :] <= query_pos, scores, MASKED)
        new_largest = jnp.maximum(largest, jnp.max(scores, axis=0, keepdims=True))
        weights = jnp.exp(scores - new_largest)
        factor = jnp.exp(largest - new_largest)
        total = total * factor + jnp.sum(weights, axis=0, keepdims=True)
        weighted = weighted * factor + dot_first(values, weights.astype(BF16))
        return new_largest, total, weighted

    return lax.fori_loop(0, kv_ref.shape[0] // chunk, step, state)


def near_kernel(chunk, members, pieces, spots, *refs):
    ins, outs, scratch = split_refs(refs, 6 + members + pieces, 4, 2)
    normed_ref, key_pos_ref, query_pos_ref, cos_ref, sin_ref, local_ref = ins[:6]
    weights, parts = split_refs(ins[6:], members, pieces)
    queries_ref, largest_ref, total_ref, weighted_ref = outs
    blocks, kv_ref = scratch
    dp = spots[2]
    stack_rows(kv_ref, parts)
    own = local_ref.shape[0]
    size = blocks.shape[-1]
    away = normed_ref[:, own:]
    for j in range(members):
        blocks[dp ^ j] = dot_plain(away, weights[j][:, :size])
    raw = join_lanes(blocks) + dot_plain(normed_ref[:, :own], local_ref[...])
    roped = rope_lanes(raw, cos_ref[...], sin_ref[...]).astype(BF16)
    queries_ref[...] = roped * jnp.asarray(1.0 / math.sqrt(HEAD_DIM), BF16)
    columns = GROUPS * queries_ref.shape[0]
    query_pos = query_pos_ref[...]
    for head in range(KV_HEADS):
        stacked = heads_of(queries_ref, head * GROUPS, GROUPS)
        start = (
            jnp.full((1, columns), MASKED, F32),
            jnp.zeros((1, columns), F32),
            jnp.zeros((HEAD_DIM, columns), F32),
        )
        largest, total, weighted = attend(
            chunk, head, kv_ref, key_pos_ref, query_pos, stacked, start
        )
        largest_ref[head : head + 1, :] = largest
        total_ref[head : head + 1, :] = total
        weighted_ref[head] = weighted


def far_kernel(chunk, shards, members, pieces, spots, *refs):
    ins, outs, scratch = split_refs(refs, 9 + members + pieces, 6, 3)
    (queries_ref, key_pos_ref, query_pos_ref, largest_ref, total_ref, weighted_ref, tokens_ref,
     gains_ref, local_ref) = ins[:9]
    weights, parts = split_refs(ins[9:], members, pieces)
    attended_ref, turned_ref, log_ref, residual_ref, inverse_ref, normed_ref = outs
    blocks, kv_ref, head_blocks = scratch
    shard, dp = spots[1], spots[2]
    stack_rows(kv_ref, parts)
    rows = queries_ref.shape[0]
    query_pos = query_pos_ref[...]
    heads = []
    for head in range(KV_HEADS):
        stacked = heads_of(queries_ref, head * GROUPS, GROUPS)
        start = (largest_ref[head : head + 1, :], total_ref[head : head + 1, :], weighted_ref[head])
        largest, total, weighted = attend(
            chunk, head, kv_ref, key_pos_ref, query_pos, stacked, start
        )
        turned = weighted / total
        turned_ref[head] = turned
        log_ref[head : head + 1, :] = largest + jnp.log(total)
        straight = turned.T
        heads += [straight[g * rows : (g + 1) * rows, :] for g in range(GROUPS)]
    attended = jnp.concatenate(heads, axis=1).astype(BF16)
    attended_ref[...] = attended
    for z, block in enumerate(lane_blocks(attended, shards)):
        head_blocks[z] = block
    away = jnp.concatenate([head_blocks[shard ^ r] for r in range(1, shards)], axis=1)
    size = blocks.shape[-1]
    for j in range(members):
        blocks[dp ^ j] = dot_plain(away, weights[j][:, size:])
    added = join_lanes(blocks) + dot_plain(head_blocks[shard], local_ref[...])
    residual = tokens_ref[...].astype(F32) + added
    residual_ref[...] = residual
    normed, inverse = norm_rows(residual, gains_ref[1:2, :])
    inverse_ref[...] = inverse
    normed_ref[...] = normed.astype(BF16)


def unfold_down(pack_ref, down_ref, shards, part):
    piece = part // shards
    rows = pack_ref.shape[0] // shards
    for b in range(down_ref.shape[0] // rows):
        at = 2 * part + b * piece
        down_ref[b * rows : (b + 1) * rows, :] = jnp.concatenate(
            [pack_ref[z * rows : (z + 1) * rows, at : at + piece] for z in range(shards)], axis=1
        )


def feed_kernel(shards, masks, spots, *refs):
    ins, outs, scratch = split_refs(refs, 2 + len(masks), 3, 3)
    pack_ref, cot_all, normed_parts = ins[0], ins[1], ins[2:]
    cot_parts = [cot_all[spots[3] ^ mask] for mask in masks]
    grad_ref, act_ref, both_ref = outs
    normed_ref, cot_ref, down_ref = scratch
    part = pack_ref.shape[1] // 3
    stack_rows(normed_ref, normed_parts)
    stack_rows(cot_ref, cot_parts)
    unfold_down(pack_ref, down_ref, shards, part)
    gate_up = dot_plain(normed_ref[...], pack_ref[:, : 2 * part])
    gate, upward = gate_up[:, :part], gate_up[:, part:]
    act_grad = dot_plain(cot_ref[...], down_ref[...])
    sigmoid_gate = jax.nn.sigmoid(gate)
    silu = gate * sigmoid_gate
    act_ref[...] = (silu * upward).astype(BF16)
    gate_grad = act_grad * upward * sigmoid_gate * (1.0 + gate * (1.0 - sigmoid_gate))
    both_ref[...] = jnp.concatenate([gate_grad, act_grad * silu], axis=1).astype(BF16)
    unstack_rows(grad_ref, dot_last(both_ref[...], pack_ref[:, : 2 * part]))


def feed_weights_kernel(shards, masks, spots, *refs):
    ins, outs, scratch = split_refs(refs, 6 + len(masks), 3, 5)
    pack_ref, act_a, act_b, both_a, both_b, cot_all = ins[:6]
    normed_parts = ins[6:]
    cot_parts = [cot_all[spots[3] ^ mask] for mask in masks]
    result_a, result_b, grad_ref = outs
    normed_ref, cot_ref, act_ref, both_ref, down_ref = scratch
    part = pack_ref.shape[1] // 3
    piece = part // shards
    rows = grad_ref.shape[0] // shards
    stack_rows(normed_ref, normed_parts)
    stack_rows(cot_ref, cot_parts)
    stack_rows(act_ref, (act_a, act_b))
    stack_rows(both_ref, (both_a, both_b))
    unfold_down(pack_ref, down_ref, shards, part)
    grad_ref[:, : 2 * part] = dot_first(normed_ref[...], both_ref[...]).astype(BF16)
    down_grad = dot_first(cot_ref[...], act_ref[...]).astype(BF16)
    folds = down_grad.shape[0] // rows
    for z in range(shards):
        at = z * piece
        grad_ref[z * rows : (z + 1) * rows, 2 * part :] = jnp.concatenate(
            [down_grad[b * rows : (b + 1) * rows, at : at + piece] for b in range(folds)], axis=1
        )
    unstack_rows(result_a, dot_last(act_a[...], down_ref[...]))
    unstack_rows(result_b, dot_last(act_b[...], down_ref[...]))


def middle_kernel(shards, members, spots, *refs):
    ins, outs, scratch = split_refs(refs, 10 + members, 4, 2)
    (own_a, own_b, one_ref, two_ref, three_ref, residual_ref, inverse_ref, cot_ref, gains_ref,
     local_ref) = ins[:10]
    weights = ins[10:]
    residual_grad_ref, low_ref, attended_grad_ref, gain_grad_ref = outs
    rows = cot_ref.shape[0]
    grad = (own_a[0].astype(F32) + own_b[0].astype(F32)) + one_ref[...].astype(F32)
    grad = grad + two_ref[...].astype(F32) + three_ref[...].astype(F32)
    residual, inverse = residual_ref[...], inverse_ref[...]
    gain_grad_ref[...] = jnp.sum(grad * residual * inverse, axis=0, keepdims=True)
    residual_grad = cot_ref[...].astype(F32) + norm_back(grad, residual, inverse, gains_ref[1:2, :])
    residual_grad_ref[...] = residual_grad
    low = residual_grad.astype(BF16)
    low_ref[...] = low
    attended_grad_ref[...] = back_through(
        shards, members, spots, low, weights, local_ref, scratch, 1
    ).astype(BF16)


def back_through(shards, members, spots, low, weights, local_ref, scratch, which):
    blocks, out_blocks = scratch
    shard, dp = spots[1], spots[2]
    for i, block in enumerate(lane_blocks(low, members)):
        blocks[i] = block
    size = blocks.shape[-1]
    at = slice(which * size, (which + 1) * size)
    away = sum(dot_last(blocks[dp ^ j], weights[j][:, at]) for j in range(members))
    out_blocks[shard] = dot_last(low, local_ref[...])
    for r, block in enumerate(lane_blocks(away, shards - 1)):
        out_blocks[shard ^ (r + 1)] = block
    return join_lanes(out_blocks)


def weight_grads_kernel(members, spots, *refs):
    lefts, lows, (keep_ref, send_ref, blocks) = refs[0:4:2], refs[1:4:2], refs[4:]
    dp = spots[2]
    for k, (left_ref, low_ref) in enumerate(zip(lefts, lows)):
        for i, block in enumerate(lane_blocks(low_ref[...], members)):
            blocks[k * members + i] = block
    for j in (1, 3, 0, 2):
        out_ref = send_ref if j & 1 else keep_ref
        out_ref[j // 2] = jnp.concatenate(
            [
                dot_first(left_ref[...], blocks[k * members + (dp ^ j)])
                for k, left_ref in enumerate(lefts)
            ],
            axis=1,
        ).astype(BF16)


def join_kernel(members, spots, own_ref, across_ref, core_ref, core_across_ref, *refs):
    outs, blocks = refs[:2], refs[2]
    dp = spots[2]
    for j, ref in enumerate((own_ref, core_ref, across_ref, core_across_ref)):
        blocks[dp ^ j] = ref[...]
    size = blocks.shape[-1] // 2
    for k, out_ref in enumerate(outs):
        out_ref[...] = jnp.concatenate(
            [blocks[i][:, k * size : (k + 1) * size] for i in range(members)], axis=1
        ).astype(F32)


def query_back_kernel(shards, members, spots, low_ref, local_ref, *refs):
    weights, (back_ref,), scratch = split_refs(refs, members, 1, 2)
    back_ref[...] = back_through(
        shards, members, spots, low_ref[...], weights, local_ref, scratch, 0
    )


def back_kernel(chunk, pieces, first, last, spots, *refs):
    ins, outs, scratch = split_refs(refs, 9 + pieces, (pieces if last else 1) + 1, 2)
    (queries_ref, key_pos_ref, query_pos_ref, cos_ref, sin_ref, turned_ref, log_ref, grad_ref,
     start_ref) = ins[:9]
    parts = ins[9:]
    query_grad_ref, kv_grads = outs[0], outs[1:]
    kv_ref, kv_grad_ref = scratch
    stack_rows(kv_ref, parts)
    rows = queries_ref.shape[0]
    columns = GROUPS * rows
    query_pos = query_pos_ref[...]
    heads = []
    for head in range(KV_HEADS):
        stacked = heads_of(queries_ref, head * GROUPS, GROUPS)
        upstream = heads_of(grad_ref, head * GROUPS, GROUPS)
        delta = jnp.sum(upstream.astype(F32).T * turned_ref[head], axis=0, keepdims=True)
        log_total = log_ref[head : head + 1, :]
        keys_at = head * HEAD_DIM
        values_at = (KV_HEADS + head) * HEAD_DIM

        def step(j, query_grad, head=head, stacked=stacked, upstream=upstream,
                 delta=delta, log_total=log_total, keys_at=keys_at, values_at=values_at):
            at = pl.ds(pl.multiple_of(j * chunk, chunk), chunk)
            keys = heads_of(kv_ref, head, 1, at)
            values = heads_of(kv_ref, KV_HEADS + head, 1, at)
            scores = dot_last(keys, stacked)
            scores = jnp.where(key_pos_ref[at, :] <= query_pos, scores, MASKED)
            weights = jnp.exp(scores - log_total)
            weight_grad = dot_last(values, upstream)
            score_grad = (weights * (weight_grad - delta)).astype(BF16)
            value_grad = dot_plain(weights.astype(BF16), upstream)
            key_grad = dot_plain(score_grad, stacked)
            kv_grad_ref[at, keys_at : keys_at + HEAD_DIM] = key_grad.astype(BF16)
            kv_grad_ref[at, values_at : values_at + HEAD_DIM] = value_grad.astype(BF16)
            return query_grad + dot_first(keys, score_grad)

        start = jnp.zeros((HEAD_DIM, columns), F32) if first else start_ref[head]
        query_grad = lax.fori_loop(0, kv_ref.shape[0] // chunk, step, start)
        if not last:
            query_grad_ref[head] = query_grad
        else:
            straight = query_grad.T * (1.0 / math.sqrt(HEAD_DIM))
            heads += [straight[g * rows : (g + 1) * rows, :] for g in range(GROUPS)]
    if last:
        query_grad_ref[...] = rope_lanes(
            jnp.concatenate(heads, axis=1), cos_ref[...], -sin_ref[...]
        ).astype(BF16)
    if last:
        for i in range(pieces):
            kv_grads[i][...] = kv_grad_ref[i * rows : (i + 1) * rows, :]
    else:
        unstack_rows(kv_grads[0], kv_grad_ref[...])


def end_kernel(shards, spots, *refs):
    ins, outs, scratch = split_refs(refs, 11 + (shards + 1) + 2 * (shards - 1), 3, 1)
    (cos_ref, sin_ref, normed_ref, tokens_ref, inverse_ref, gains_ref, back_ref, residual_grad_ref,
     key_ref, value_ref, gain_two_ref) = ins[:11]
    sums, mine, other = split_refs(ins[11:], shards + 1, shards - 1, shards - 1)
    input_grad_ref, keep_ref, send_ref = outs
    (blocks,) = scratch
    core, shard = spots[0], spots[1]
    width, span = key_ref.shape
    rows = tokens_ref.shape[0]
    total = sums[0][...].astype(F32) + sums[1][0].astype(F32)
    total = total + sum(s[...].astype(F32) for s in sums[2:])
    keys = rope_lanes(total[:, :width], cos_ref[...], -sin_ref[...])
    values = total[:, width:]
    keep = jnp.where(core == 0, keys, values).astype(BF16)
    send = jnp.where(core == 0, values, keys).astype(BF16)
    blocks[shard] = dot_plain(keys.astype(BF16), key_ref[...]) + dot_plain(
        values.astype(BF16), value_ref[...]
    )
    for r in range(1, shards):
        blocks[shard ^ r] = dot_plain(keep, mine[r - 1][:width, :]) + dot_plain(
            send, other[r - 1][:width, :]
        )
    normed_grad = back_ref[...] + join_lanes(blocks)
    inputs, inverse = tokens_ref[...].astype(F32), inverse_ref[...]
    gain_grad = jnp.sum(normed_grad * inputs * inverse, axis=0, keepdims=True)
    input_grad_ref[...] = residual_grad_ref[...] + norm_back(
        normed_grad, inputs, inverse, gains_ref[0:1, :]
    )
    normed = normed_ref[...]
    two = gain_two_ref[...]
    for out_ref, low, gain in (
        (send_ref, send, jnp.where(core == 0, two, gain_grad)),
        (keep_ref, keep, jnp.where(core == 0, gain_grad, two)),
    ):
        grad = dot_first(low, normed).astype(BF16)
        gains = lane_blocks(gain, shards)
        for z, block in enumerate(lane_blocks(grad, shards)):
            out_ref[z, :width, :] = block
            out_ref[z, width:, :] = jnp.broadcast_to(
                gains[z], (EXTRA_ROWS, span)
            ).astype(BF16)


def spread_kernel(shards, members, spots, *refs):
    parts, outs, (blocks,) = split_refs(refs, members, 3, 1)
    gate_ref, up_ref, down_ref = outs
    member = spots[3]
    piece = parts[0].shape[1] // 3 // shards
    rows = parts[0].shape[0]
    span = piece * members
    for i in range(members):
        blocks[member ^ i] = parts[i][...]

    def block(k):
        at = k * piece
        return jnp.concatenate(
            [blocks[p, :, at : at + piece] for p in range(members)], axis=1
        ).astype(F32)

    for z in range(shards):
        gate_ref[:, z * span : (z + 1) * span] = block(z)
        up_ref[:, z * span : (z + 1) * span] = block(shards + z)
    for b in range(down_ref.shape[0] // rows):
        down_ref[b * rows : (b + 1) * rows, :] = block(2 * shards + b)


def base_of(block_order, stored, block_length):
    which = stored // block_length
    count = block_order.shape[1]
    matches = (which[:, None] == jnp.arange(count, dtype=jnp.int32)[None, :]).astype(jnp.int32)
    return jnp.sum(block_order[0][None, :] * matches, axis=-1) * block_length + stored % block_length


def tables(positions):
    half_dim = HEAD_DIM // 2
    exponent = -(jnp.arange(half_dim, dtype=F32) * 2.0) / HEAD_DIM
    frequency = jnp.power(F32(ROPE_BASE), exponent)
    angles = positions.astype(F32)[:, None] * frequency
    cosine, sine = jnp.cos(angles), jnp.sin(angles)
    return (
        jnp.concatenate([cosine] * 4, axis=-1),
        jnp.concatenate([-sine, sine, -sine, sine], axis=-1),
    )


def after(x, other):
    return lax.optimization_barrier((x, other))[0]


def on_device(
    tokens,
    block_order,
    attention_gain,
    query_weight,
    key_weight,
    value_weight,
    output_weight,
    feedforward_gain,
    gate_weight,
    up_weight,
    down_weight,
    cotangent,
):
    tokens, cotangent = tokens[0], cotangent[0]
    rows, width = tokens.shape
    shards = lax.axis_size("fsdp")
    ctx_count = lax.axis_size("ctx")
    dp_count = lax.axis_size("dp")
    block_length = rows * shards * ctx_count // block_order.shape[1]
    shard = lax.axis_index("fsdp")
    ctx = lax.axis_index("ctx")
    dp = lax.axis_index("dp")
    core = dp & 1
    members = dp_count * 2
    weight_rows = query_weight.shape[0]
    query_width = HEADS * HEAD_DIM
    kv_width = KV_HEADS * HEAD_DIM
    hidden = gate_weight.shape[1]
    part = hidden // members
    spots = jnp.stack([core, shard, dp, dp * 2 + (ctx & 1)]).astype(jnp.int32)

    gain_one, gain_two = attention_gain[None, :], feedforward_gain[None, :]
    key_turned, value_turned, down_turned = key_weight.T, value_weight.T, down_weight.T
    kv_pack = jnp.concatenate(
        [
            jnp.where(core == 0, key_turned, value_turned),
            jnp.pad(
                jnp.concatenate([gain_one, gain_two], axis=0), ((0, EXTRA_ROWS - 2), (0, 0))
            ),
        ],
        axis=0,
    )
    kv_mine = direct_fsdp(kv_pack)

    quarter = width // dp_count
    (quarters,) = call(
        functools.partial(quarter_kernel, dp_count), spots,
        [after(query_weight, kv_pack), output_weight],
        [((weight_rows, 2 * quarter), BF16)], name="quarter_columns",
    )
    quarter_pieces = swaps_fsdp(quarters)
    quarter_pieces[0], *kv_mine = lax.optimization_barrier((quarter_pieces[0], *kv_mine))
    kv_other = [swap_core(piece) for piece in kv_mine]

    group_axes = ("dp", "ctx")
    extra = {}
    if ctx_count > 2:
        extra["axis_index_groups"] = [
            [d * ctx_count + c for d in range(dp_count) for c in (first, first + 1)]
            for first in range(0, ctx_count, 2)
        ]
    cot_all = lax.all_gather(cotangent, group_axes, axis=0, tiled=False, **extra)

    offsets = jnp.arange(rows, dtype=jnp.int32)
    my_start = (ctx * shards + shard) * rows
    positions = base_of(block_order, my_start[None], block_length) + offsets
    cosine, sine = tables(positions)
    query_pos = jnp.concatenate([positions] * GROUPS)[None, :]
    starts = jnp.stack(
        [((ctx ^ d) * shards + (shard ^ r)) * rows for d in range(ctx_count) for r in range(shards)]
    )
    key_pos = (base_of(block_order, starts, block_length)[:, None] + offsets[None, :]).reshape(-1, 1)
    near_count = shards * rows
    near_pos, far_pos = key_pos[:near_count], key_pos[near_count:]
    far_count = far_pos.shape[0]

    (pack,) = call(
        functools.partial(pack_kernel, shards, members), spots,
        [gate_weight, up_weight, down_turned], [((weight_rows, 3 * part), BF16)],
        name="pack_weights",
    )
    kv_own, normed_one, normed_turned, inverse_one, gains = call(
        functools.partial(begin_kernel, shards), spots,
        [
            lax.optimization_barrier((tokens, quarter_pieces[1], pack))[0], gain_one, gain_two, key_turned, value_turned, cosine, sine,
            *kv_mine, *kv_other,
        ],
        [
            ((rows, 2 * kv_width), BF16), ((rows, width), BF16), ((rows, width), BF16),
            ((rows, 1), F32), ((8, width), F32),
        ],
        scratch=[
            ((shards, rows, weight_rows), F32), ((shards, rows, weight_rows), BF16),
            ((shards, 8, weight_rows), F32),
        ],
        name="norm_keys_values",
    )
    near = [kv_own] + direct_fsdp(kv_own)
    near[1], *quarter_pieces = lax.optimization_barrier((near[1], *quarter_pieces))
    (stacked,) = call(
        stack_kernel, spots, quarter_pieces,
        [(((shards - 1) * weight_rows, 2 * quarter), BF16)], name="stack_quarters",
    )
    across, *near = lax.optimization_barrier((swap_plane(stacked, 2, 0), *near))
    stacks = [stacked, swap_core(stacked), across, swap_core(across)]
    far = [swap(piece, "ctx", d) for d in range(1, ctx_count) for piece in near]

    pack, cot_all, _ = lax.optimization_barrier((pack, cot_all, near[-1]))
    pack_all = lax.all_gather(pack, "fsdp", axis=0, tiled=True)

    normed_turned, far[0], far[1] = lax.optimization_barrier((normed_turned, far[0], far[1]))

    chunk = rows * 2
    unit = 2 * HEADS * rows * near_count * HEAD_DIM
    stat = ((KV_HEADS, GROUPS * rows), F32)
    turned_shape = ((KV_HEADS, HEAD_DIM, GROUPS * rows), F32)
    queries, largest, total, weighted = call(
        functools.partial(near_kernel, chunk, dp_count, shards), spots,
        [normed_turned, near_pos, query_pos, cosine, sine, query_weight, *stacks, *near],
        [((rows, query_width), BF16), stat, stat, turned_shape],
        scratch=[((dp_count, rows, quarter), F32), ((near_count, 2 * kv_width), BF16)],
        name="attention_near",
    )
    attended, turned, log_total, residual, inverse_two, normed_two = call(
        functools.partial(far_kernel, chunk, shards, dp_count, len(far)), spots,
        [
            queries, far_pos, query_pos, largest, total, weighted, tokens, gains,
            output_weight, *stacks, *far,
        ],
        [
            ((rows, query_width), BF16), turned_shape, stat, ((rows, width), F32),
            ((rows, 1), F32), ((rows, width), BF16),
        ],
        scratch=[
            ((dp_count, rows, quarter), F32), ((far_count, 2 * kv_width), BF16),
            ((shards, rows, weight_rows), BF16),
        ],
        name="attention_far",
    )

    normed_a, normed_b = plane_pieces(normed_two)
    token_shape = ((rows, width), BF16)
    half = 4 * rows
    half_shape = ((4, rows, width), BF16)

    masks = [2 * a + b for a, b in ((0, 0),) + CHIP_MASKS]
    core_masks = [mask ^ 2 for mask in masks]

    def feed(normed, masks):
        return call(
            functools.partial(feed_kernel, shards, masks), spots, [pack_all, cot_all, *normed],
            [half_shape, ((half, part), BF16), ((half, 2 * part), BF16)],
            scratch=[((half, width), BF16), ((half, width), BF16), ((width, part), BF16)],
        name="feed_forward",
        )

    grad_b, act_b, both_b = feed(normed_b, core_masks)
    from_core = swap_core(grad_b)
    grad_a, act_a, both_a = feed(normed_a, masks)

    def chip_sums(parts_a, parts_b):
        return [
            (parts_a[k].astype(F32) + parts_b[k].astype(F32)).astype(BF16)
            for k in range(1, 4)
        ]

    def send_chips(sums):
        return [swap_plane(x, a, b) for x, (a, b) in zip(sums, CHIP_MASKS)]

    grad_sums = chip_sums(grad_a, from_core)
    grad_chips = send_chips(grad_sums)
    act_a, *_ = lax.optimization_barrier((act_a, *grad_sums))
    result_a, result_b, pack_grad = call(
        functools.partial(feed_weights_kernel, shards, masks + core_masks), spots,
        [pack_all, act_a, act_b, both_a, both_b, cot_all, *normed_a, *normed_b],
        [half_shape, half_shape, ((width, 3 * part), BF16)],
        scratch=[
            ((2 * half, width), BF16), ((2 * half, width), BF16), ((2 * half, part), BF16),
            ((2 * half, 2 * part), BF16), ((width, part), BF16),
        ],
        name="feed_forward_weights",
    )
    pack_share = sum_far(lax.psum_scatter(pack_grad, "fsdp", scatter_dimension=0, tiled=True))

    pack_grad, *grad_chips = lax.optimization_barrier((pack_grad, *grad_chips))
    residual_grad, residual_low, attended_grad, second_gain_grad = call(
        functools.partial(middle_kernel, shards, dp_count), spots,
        [
            grad_a, from_core, *grad_chips, residual, inverse_two, cotangent, gains, output_weight,
            *stacks,
        ],
        [((rows, width), F32), token_shape, ((rows, query_width), BF16), ((1, width), F32)],
        scratch=[((dp_count, rows, quarter), BF16), ((shards, rows, weight_rows), F32)],
        name="residual_back",
    )

    result_core = swap_core(after(result_b, residual_low))
    attended_grad, result_a = lax.optimization_barrier((attended_grad, result_a))

    def sum_x(keep, away):
        sent = (keep[1].astype(F32) + away[1].astype(F32)).astype(BF16)
        return sent, (keep[0], away[0], swap_plane(sent, 2, 0))

    def pieces_z(terms):
        out = []
        for r in range(shards):
            at = (shard ^ r) * weight_rows
            parts = [
                lax.dynamic_slice_in_dim(x, at, weight_rows, 0).astype(F32) for x in terms
            ]
            out.append((parts[0] + parts[1] + parts[2]).astype(BF16))
        return out

    def sum_z(pieces):
        arrived = {r: swap(pieces[r], "fsdp", r) for r in reversed(range(1, shards))}
        return sum(
            (arrived[r].astype(F32) for r in range(1, shards)), pieces[0].astype(F32)
        ).astype(BF16)

    def relay_z(terms):
        span = shards
        pieces = {r: piece.astype(F32) for r, piece in enumerate(pieces_z(terms))}
        while span > 1:
            span //= 2
            sent = jnp.stack([pieces[r].astype(BF16) for r in range(span, 2 * span)])
            arrived = swap(sent, "fsdp", span)
            pieces = {r: pieces[r] + arrived[r].astype(F32) for r in range(span)}
        return pieces[0].astype(BF16)

    def sum_y(own):
        return sum_far((own.astype(F32) + swap_plane(own, 0, 1).astype(F32)).astype(BF16))

    def finish_quarters(own):
        across = swap_plane(own, 2, 0)
        return call(
            functools.partial(join_kernel, dp_count), spots,
            [own, across, swap_core(own), swap_core(across)],
            [((weight_rows, width), F32)] * 2,
            scratch=[((dp_count, weight_rows, 2 * quarter), BF16)], name="join_columns",
        )

    def sum_chips(own):
        for a, b in ((2, 0), (0, 1)):
            own = (own.astype(F32) + swap_plane(own, a, b).astype(F32)).astype(BF16)
        return sum_far(own)

    def back(first, last, start, pos, pieces):
        count = pos.shape[0]
        shape = ((rows, query_width), BF16) if last else turned_shape
        out = call(
            functools.partial(back_kernel, chunk, len(pieces), first, last), spots,
            [
                queries, pos, query_pos, cosine, sine, turned, log_total, attended_grad, start,
                *pieces,
            ],
            [shape]
            + (
                [((rows, 2 * kv_width), BF16)] * len(pieces) if last
                else [((shards, rows, 2 * kv_width), BF16)]
            ),
            scratch=[((count, 2 * kv_width), BF16), ((count, 2 * kv_width), BF16)],
            name="attention_back_near" if last else "attention_back_far",
        )
        return out[0], out[1:]

    query_partial, far_grads = turned, []
    for d in range(1, ctx_count):
        at = (d - 1) * shards
        query_partial, grads = back(
            d == 1, False, query_partial, far_pos[at * rows : (at + shards) * rows],
            far[at : at + shards],
        )
        far_grads.append(swap(grads[0], "ctx", d))
    result_sent = (result_a[2:].astype(F32) + result_core[2:].astype(F32)).astype(BF16)
    query_partial, result_sent = lax.optimization_barrier((query_partial, result_sent))
    result_across = swap_plane(result_sent, 2, 0)
    query_low, near_grads = back(False, True, query_partial, near_pos, near)
    query_low, result_across = lax.optimization_barrier((query_low, result_across))
    result_own, result_along = [
        (result_a[k].astype(F32) + result_core[k].astype(F32)) + result_across[k].astype(F32)
        for k in (0, 1)
    ]
    result_along = swap_plane(result_along.astype(BF16), 0, 1)
    pair_shape = ((2, width, 2 * quarter), BF16)
    weights_keep, weights_send = call(
        functools.partial(weight_grads_kernel, dp_count), spots,
        [attended, residual_low, normed_one, query_low], [pair_shape, pair_shape],
        scratch=[((2 * dp_count, rows, quarter), BF16)], name="query_output_weight_grads",
    )
    pack_share, query_low = lax.optimization_barrier((pack_share, query_low))
    share_across = swap_plane(pack_share, 2, 0)
    weights_send, far_grads[-1] = lax.optimization_barrier((weights_send, far_grads[-1]))

    def home(r):
        return sum(grads[r].astype(F32) for grads in far_grads)

    kv_sums = {
        r: (near_grads[r].astype(F32) + home(r)).astype(BF16) for r in range(1, shards)
    }
    kv_arrived = {r: swap(kv_sums[r], "fsdp", r) for r in reversed(range(1, shards))}
    query_low, *_ = lax.optimization_barrier((query_low, *kv_sums.values()))

    weights_away = swap_core(weights_send)
    weights_sent, weights_terms = sum_x(weights_keep, weights_away)
    query_turn = after(query_low, weights_sent)
    (query_back,) = call(
        functools.partial(query_back_kernel, shards, dp_count), spots,
        [query_turn, query_weight, *stacks], [((rows, width), F32)],
        scratch=[((dp_count, rows, quarter), BF16), ((shards, rows, weight_rows), F32)],
        name="query_back",
    )
    query_back, share_across = lax.optimization_barrier((query_back, share_across))
    share_a = [
        pack_share, swap_plane(pack_share, 0, 1), share_across, swap_plane(share_across, 0, 1)
    ]
    span = kv_width + EXTRA_ROWS
    packed_shape = ((shards, span, weight_rows), BF16)
    home_all = far_grads[0]
    if ctx_count > 2:
        home_all = sum(grads.astype(F32) for grads in far_grads)
    input_grad, kv_keep, kv_send = call(
        functools.partial(end_kernel, shards), spots,
        [
            cosine, sine, normed_one, tokens, inverse_one, gains, query_back, residual_grad,
            key_turned, value_turned, second_gain_grad, near_grads[0], home_all,
            *[kv_arrived[r] for r in range(1, shards)], *kv_mine, *kv_other,
        ],
        [((rows, width), F32), packed_shape, packed_shape],
        scratch=[((shards, rows, weight_rows), F32)],
        name="keys_values_back",
    )
    kv_away = swap_core(kv_send)
    pieces = [
        (lax.dynamic_index_in_dim(kv_keep, shard ^ r, 0, keepdims=False).astype(F32)
         + lax.dynamic_index_in_dim(kv_away, shard ^ r, 0, keepdims=False).astype(F32)).astype(BF16)
        for r in range(shards)
    ]
    weights_terms, result_along, *pieces = lax.optimization_barrier(
        (weights_terms, result_along, *pieces)
    )
    kv_share = sum_z(pieces)
    kv_share, *share_a = lax.optimization_barrier((kv_share, *share_a))
    share_b = [swap_core(piece) for piece in share_a]

    share_by_mask = [None] * members
    for k, (a, b) in enumerate(((0, 0),) + CHIP_MASKS):
        share_by_mask[2 * a + b] = share_a[k]
        share_by_mask[2 * (a ^ 1) + b] = share_b[k]
    gate_weight_grad, up_weight_grad, down_weight_grad = call(
        functools.partial(spread_kernel, shards, members), spots, share_by_mask,
        [
            ((weight_rows, hidden), F32), ((weight_rows, hidden), F32),
            ((width, down_weight.shape[0]), F32),
        ],
        scratch=[((members, weight_rows, 3 * part), BF16)],
        name="feed_forward_out",
    )
    weights_own = sum_y(relay_z(weights_terms))
    result = residual + (result_own + result_along.astype(F32))
    output_weight_grad, query_weight_grad = finish_quarters(weights_own)
    low = sum_chips(kv_share)
    away = swap_core(low)
    first = jnp.where(core == 0, low, away).astype(F32)
    second = jnp.where(core == 0, away, low).astype(F32)

    return (
        result[None],
        input_grad[None],
        first[kv_width],
        query_weight_grad,
        first[:kv_width].T,
        second[:kv_width].T,
        output_weight_grad,
        second[kv_width],
        gate_weight_grad,
        up_weight_grad,
        down_weight_grad.T,
    )


def solution(mesh):
    row = P("fsdp", None)
    token = P("dp", ("ctx", "fsdp"), None)
    return jax.shard_map(
        on_device,
        mesh=mesh,
        in_specs=(
            token, P("dp", None), P("fsdp"), row, row, row, row, P("fsdp"), row, row, row, token,
        ),
        out_specs=(
            token, token, P("fsdp"), row, row, row, row, P("fsdp"), row, row, row,
        ),
        check_vma=False,
    )
```

```python
import functools
import math

import jax
import jax.numpy as jnp
from jax import lax
from jax.experimental import pallas as pl
from jax.experimental.pallas import tpu as pltpu
from jax.sharding import PartitionSpec as P

HEADS = 15
KV_HEADS = 5
HEAD_DIM = 64
GROUPS = HEADS // KV_HEADS
LANES = 128

EPSILON = 1e-05
ROPE_BASE = 100000.0
MASKED = -1e30

F32 = jnp.float32
BF16 = jnp.bfloat16
VMEM_LIMIT = 56 * 1024 * 1024
FLOPS_PER_US = 1150 * 10**6
MEASURED_US = {
    "pack_weights": 4,
    "norm_keys_values": 4,
    "attention_near": 12,
    "attention_far": 12,
    "feed_forward": 8,
    "feed_forward_weights": 12,
    "residual_back": 6,
    "attention_back_far": 13,
    "attention_back_near": 14,
    "query_output_weight_grads": 0,
    "query_back": 0,
    "stack_quarters": 0,
    "quarter_columns": 0,
    "keys_values_back": 6,
    "feed_forward_out": 7,
}


def dot_plain(left, right):
    return jnp.dot(left, right, preferred_element_type=F32)


def dot_last(left, right):
    return lax.dot_general(left, right, (((1,), (1,)), ((), ())), preferred_element_type=F32)


def dot_first(left, right):
    return lax.dot_general(left, right, (((0,), (0,)), ((), ())), preferred_element_type=F32)


def swap(x, axis, mask):
    count = lax.axis_size(axis)
    return lax.ppermute(x, axis, [(i, i ^ mask) for i in range(count)])


def swap_plane(x, dp_mask, ctx_mask):
    ctx_count = lax.axis_size("ctx")
    pairs = []
    for d in range(lax.axis_size("dp")):
        for c in range(ctx_count):
            pairs.append((d * ctx_count + c, (d ^ dp_mask) * ctx_count + (c ^ ctx_mask)))
    return lax.ppermute(x, ("dp", "ctx"), pairs)


def swaps_fsdp(x):
    pieces = {0: x}
    for r in range(1, lax.axis_size("fsdp")):
        top = 1 << (r.bit_length() - 1)
        pieces[r] = swap(pieces[r - top], "fsdp", top)
    return [pieces[r] for r in range(1, lax.axis_size("fsdp"))]


def direct_fsdp(x):
    return [swap(x, "fsdp", r) for r in range(1, lax.axis_size("fsdp"))]


def swap_core(x):
    return swap_plane(x, 1, 0)


CHIP_MASKS = ((0, 1), (2, 0), (2, 1))


def plane_pieces(x):
    mine = [x] + [swap_plane(x, a, b) for a, b in CHIP_MASKS]
    return mine, [swap_core(piece) for piece in mine]


def sum_far(x):
    count = lax.axis_size("ctx")
    if count == 2:
        return x
    groups = [list(range(0, count, 2)), list(range(1, count, 2))]
    return lax.psum(x.astype(F32), "ctx", axis_index_groups=groups).astype(x.dtype)


def call(kernel, spots, args, out_shapes, scratch=(), name=None):
    specs = [pl.BlockSpec(memory_space=pltpu.SMEM)]
    specs += [pl.BlockSpec(memory_space=pltpu.VMEM) for _ in args]
    outs = tuple(jax.ShapeDtypeStruct(s, d) for s, d in out_shapes)
    return pl.pallas_call(
        kernel,
        out_shape=outs,
        in_specs=specs,
        out_specs=tuple(pl.BlockSpec(memory_space=pltpu.VMEM) for _ in outs),
        scratch_shapes=[pltpu.VMEM(s, d) for s, d in scratch],
        compiler_params=pltpu.CompilerParams(vmem_limit_bytes=VMEM_LIMIT),
        cost_estimate=pl.CostEstimate(
            flops=MEASURED_US.get(name, 2) * FLOPS_PER_US, bytes_accessed=0, transcendentals=0
        ),
        name=name,
    )(spots, *args)


def split_refs(refs, *counts):
    out, at = [], 0
    for n in counts:
        out.append(refs[at : at + n])
        at += n
    assert at == len(refs)
    return out


def lane_blocks(values, count):
    size = values.shape[1] // count
    return [values[:, i * size : (i + 1) * size] for i in range(count)]


def join_lanes(ref):
    return jnp.concatenate([ref[i] for i in range(ref.shape[0])], axis=1)


def rope_lanes(values, cosine, sine):
    rows, width = values.shape
    lane = lax.broadcasted_iota(jnp.int32, (rows, LANES), 1)
    first_half = (lane % HEAD_DIM) < (HEAD_DIM // 2)
    out = []
    for start in range(0, width, LANES):
        piece = values[:, start : min(start + LANES, width)]
        size = piece.shape[1]
        if size < LANES:
            piece = jnp.concatenate([piece, jnp.zeros((rows, LANES - size), piece.dtype)], axis=1)
        ahead = pltpu.roll(piece, LANES - HEAD_DIM // 2, 1)
        behind = pltpu.roll(piece, HEAD_DIM // 2, 1)
        partner = jnp.where(first_half, ahead, behind)
        out.append((piece * cosine + partner * sine)[:, :size])
    return jnp.concatenate(out, axis=1)


def heads_of(ref, first, count, rows=None):
    out = []
    for h in range(first, first + count):
        start = (h * HEAD_DIM) // LANES * LANES
        stop = min(start + LANES, ref.shape[-1])
        pair = ref[:, start:stop] if rows is None else ref[rows, start:stop]
        at = h * HEAD_DIM - start
        out.append(pair[:, at : at + HEAD_DIM])
    return out[0] if count == 1 else jnp.concatenate(out, axis=0)


def stack_rows(scratch, pieces):
    at = 0
    for piece in pieces:
        scratch[at : at + piece.shape[0], :] = piece[...]
        at += piece.shape[0]


def unstack_rows(out_ref, values):
    count, rows = out_ref.shape[:2]
    for i in range(count):
        out_ref[i] = values[i * rows : (i + 1) * rows, :].astype(out_ref.dtype)


def norm_rows(values, gain):
    inverse = lax.rsqrt(jnp.mean(values * values, axis=-1, keepdims=True) + EPSILON)
    return (values * inverse * gain, inverse)


def norm_back(gradient, values, inverse, gain):
    scaled = gradient * gain
    inner_mean = jnp.mean(scaled * values, axis=-1, keepdims=True)
    return inverse * scaled - values * (inverse * inverse * inverse) * inner_mean


EXTRA_ROWS = 16


def pack_kernel(shards, members, spots, gate_ref, up_ref, down_ref, out_ref):
    member = spots[3]
    span = gate_ref.shape[1] // shards
    piece = span // members
    rows = gate_ref.shape[0]
    pick = (
        lax.broadcasted_iota(jnp.int32, (span, piece), 0)
        == lax.broadcasted_iota(jnp.int32, (span, piece), 1) + member * piece
    ).astype(BF16)
    out = []
    for ref in (gate_ref, up_ref):
        for z in range(shards):
            out.append(dot_plain(ref[:, z * span : (z + 1) * span], pick))
    down = dot_plain(down_ref[...], pick)
    out += [down[b : b + rows, :] for b in range(0, down_ref.shape[0], rows)]
    out_ref[...] = jnp.concatenate(out, axis=1).astype(BF16)


def quarter_kernel(members, spots, query_ref, output_ref, *outs):
    size = query_ref.shape[1] // members
    for i in range(members):

        @pl.when(spots[2] == i)
        def _():
            for ref, out_ref in zip((query_ref, output_ref), outs):
                out_ref[...] = ref[:, i * size : (i + 1) * size]


def stack_kernel(spots, *refs):
    stack_rows(refs[-1], refs[:-1])


def begin_kernel(shards, spots, *refs):
    ins, outs, scratch = split_refs(refs, 7 + 2 * (shards - 1), 5, 3)
    tokens_ref, gain_one, gain_two, key_ref, value_ref, cos_ref, sin_ref = ins[:7]
    mine, other = split_refs(ins[7:], shards - 1, shards - 1)
    kv_ref, normed_ref, turned_ref, inverse_ref, gains_ref = outs
    blocks, normed_blocks, gain_blocks = scratch
    core, shard = spots[0], spots[1]
    width = key_ref.shape[0]
    values = tokens_ref[...].astype(F32)
    inverse = lax.rsqrt(jnp.mean(values * values, axis=-1, keepdims=True) + EPSILON)
    inverse_ref[...] = inverse
    for z, block in enumerate(lane_blocks(values * inverse, shards)):
        blocks[z] = block
    sums, order = [], []
    for r in range(shards):
        at = shard ^ r
        if r == 0:
            pair = jnp.concatenate([gain_one[...], gain_two[...]], axis=0).astype(F32)
        else:
            pair = mine[r - 1][width : width + EXTRA_ROWS, :].astype(F32)[0:2, :]
        gain_blocks[at, 0:2, :] = pair
        normed = (blocks[at] * pair[0:1, :]).astype(BF16)
        normed_blocks[at] = normed
        order.append(normed)
        left = key_ref[...] if r == 0 else mine[r - 1][:width, :]
        right = value_ref[...] if r == 0 else other[r - 1][:width, :]
        sums.append((dot_last(normed, left), dot_last(normed, right)))
    first = sum(s[0] for s in sums[1:])
    second = sum(s[1] for s in sums[1:])
    keys = jnp.where(core == 0, first, second) + sums[0][0]
    vals = jnp.where(core == 0, second, first) + sums[0][1]
    keys = rope_lanes(keys, cos_ref[...], sin_ref[...])
    kv_ref[...] = jnp.concatenate([keys, vals], axis=1).astype(BF16)
    normed_ref[...] = join_lanes(normed_blocks)
    turned_ref[...] = jnp.concatenate(order, axis=1)
    gains_ref[...] = jnp.zeros_like(gains_ref)
    gains_ref[0:2, :] = jnp.concatenate([gain_blocks[z][0:2, :] for z in range(shards)], axis=1)


def attend(chunk, head, kv_ref, key_pos_ref, query_pos, stacked, state):
    def step(j, state):
        largest, total, weighted = state
        at = pl.ds(pl.multiple_of(j * chunk, chunk), chunk)
        keys = heads_of(kv_ref, head, 1, at)
        values = heads_of(kv_ref, KV_HEADS + head, 1, at)
        scores = dot_last(keys, stacked)
        scores = jnp.where(key_pos_ref[at, :] <= query_pos, scores, MASKED)
        new_largest = jnp.maximum(largest, jnp.max(scores, axis=0, keepdims=True))
        weights = jnp.exp(scores - new_largest)
        factor = jnp.exp(largest - new_largest)
        total = total * factor + jnp.sum(weights, axis=0, keepdims=True)
        weighted = weighted * factor + dot_first(values, weights.astype(BF16))
        return new_largest, total, weighted

    return lax.fori_loop(0, kv_ref.shape[0] // chunk, step, state)


def near_kernel(chunk, members, pieces, spots, *refs):
    ins, outs, scratch = split_refs(refs, 6 + members + pieces, 4, 2)
    normed_ref, key_pos_ref, query_pos_ref, cos_ref, sin_ref, local_ref = ins[:6]
    weights, parts = split_refs(ins[6:], members, pieces)
    queries_ref, largest_ref, total_ref, weighted_ref = outs
    blocks, kv_ref = scratch
    dp = spots[2]
    stack_rows(kv_ref, parts)
    own = local_ref.shape[0]
    away = normed_ref[:, own:]
    for j in range(members):
        blocks[dp ^ j] = dot_plain(away, weights[j][...])
    raw = join_lanes(blocks) + dot_plain(normed_ref[:, :own], local_ref[...])
    roped = rope_lanes(raw, cos_ref[...], sin_ref[...]).astype(BF16)
    queries_ref[...] = roped * jnp.asarray(1.0 / math.sqrt(HEAD_DIM), BF16)
    columns = GROUPS * queries_ref.shape[0]
    query_pos = query_pos_ref[...]
    for head in range(KV_HEADS):
        stacked = heads_of(queries_ref, head * GROUPS, GROUPS)
        start = (
            jnp.full((1, columns), MASKED, F32),
            jnp.zeros((1, columns), F32),
            jnp.zeros((HEAD_DIM, columns), F32),
        )
        largest, total, weighted = attend(
            chunk, head, kv_ref, key_pos_ref, query_pos, stacked, start
        )
        largest_ref[head : head + 1, :] = largest
        total_ref[head : head + 1, :] = total
        weighted_ref[head] = weighted


def far_kernel(chunk, pieces, spots, *refs):
    ins, outs, (kv_ref,) = split_refs(refs, 6 + pieces, 3, 1)
    queries_ref, key_pos_ref, query_pos_ref, largest_ref, total_ref, weighted_ref = ins[:6]
    parts = ins[6:]
    attended_ref, turned_ref, log_ref = outs
    stack_rows(kv_ref, parts)
    rows = queries_ref.shape[0]
    query_pos = query_pos_ref[...]
    heads = []
    for head in range(KV_HEADS):
        stacked = heads_of(queries_ref, head * GROUPS, GROUPS)
        start = (largest_ref[head : head + 1, :], total_ref[head : head + 1, :], weighted_ref[head])
        largest, total, weighted = attend(
            chunk, head, kv_ref, key_pos_ref, query_pos, stacked, start
        )
        turned = weighted / total
        turned_ref[head] = turned
        log_ref[head : head + 1, :] = largest + jnp.log(total)
        straight = turned.T
        heads += [straight[g * rows : (g + 1) * rows, :] for g in range(GROUPS)]
    attended_ref[...] = jnp.concatenate(heads, axis=1).astype(BF16)


def project_kernel(shards, members, spots, *refs):
    ins, outs, (blocks, head_blocks) = split_refs(refs, 4 + members, 3, 2)
    attended_ref, tokens_ref, gains_ref, local_ref = ins[:4]
    weights = ins[4:]
    residual_ref, inverse_ref, normed_ref = outs
    shard, dp = spots[1], spots[2]
    for z, block in enumerate(lane_blocks(attended_ref[...], shards)):
        head_blocks[z] = block
    away = jnp.concatenate([head_blocks[shard ^ r] for r in range(1, shards)], axis=1)
    for j in range(members):
        blocks[dp ^ j] = dot_plain(away, weights[j][...])
    added = join_lanes(blocks) + dot_plain(head_blocks[shard], local_ref[...])
    residual = tokens_ref[...].astype(F32) + added
    residual_ref[...] = residual
    normed, inverse = norm_rows(residual, gains_ref[1:2, :])
    inverse_ref[...] = inverse
    normed_ref[...] = normed.astype(BF16)


def unfold_down(pack_ref, down_ref, shards, part):
    piece = part // shards
    rows = pack_ref.shape[0] // shards
    for b in range(down_ref.shape[0] // rows):
        at = 2 * part + b * piece
        down_ref[b * rows : (b + 1) * rows, :] = jnp.concatenate(
            [pack_ref[z * rows : (z + 1) * rows, at : at + piece] for z in range(shards)], axis=1
        )


def feed_kernel(shards, masks, spots, *refs):
    ins, outs, scratch = split_refs(refs, 2 + len(masks), 3, 3)
    pack_ref, cot_all, normed_parts = ins[0], ins[1], ins[2:]
    cot_parts = [cot_all[spots[3] ^ mask] for mask in masks]
    grad_ref, act_ref, both_ref = outs
    normed_ref, cot_ref, down_ref = scratch
    part = pack_ref.shape[1] // 3
    stack_rows(normed_ref, normed_parts)
    stack_rows(cot_ref, cot_parts)
    unfold_down(pack_ref, down_ref, shards, part)
    gate_up = dot_plain(normed_ref[...], pack_ref[:, : 2 * part])
    gate, upward = gate_up[:, :part], gate_up[:, part:]
    act_grad = dot_plain(cot_ref[...], down_ref[...])
    sigmoid_gate = jax.nn.sigmoid(gate)
    silu = gate * sigmoid_gate
    act_ref[...] = (silu * upward).astype(BF16)
    gate_grad = act_grad * upward * sigmoid_gate * (1.0 + gate * (1.0 - sigmoid_gate))
    both_ref[...] = jnp.concatenate([gate_grad, act_grad * silu], axis=1).astype(BF16)
    unstack_rows(grad_ref, dot_last(both_ref[...], pack_ref[:, : 2 * part]))


def feed_weights_kernel(shards, masks, spots, *refs):
    ins, outs, scratch = split_refs(refs, 6 + len(masks), 3, 5)
    pack_ref, act_a, act_b, both_a, both_b, cot_all = ins[:6]
    normed_parts = ins[6:]
    cot_parts = [cot_all[spots[3] ^ mask] for mask in masks]
    result_a, result_b, grad_ref = outs
    normed_ref, cot_ref, act_ref, both_ref, down_ref = scratch
    part = pack_ref.shape[1] // 3
    piece = part // shards
    rows = grad_ref.shape[0] // shards
    stack_rows(normed_ref, normed_parts)
    stack_rows(cot_ref, cot_parts)
    stack_rows(act_ref, (act_a, act_b))
    stack_rows(both_ref, (both_a, both_b))
    unfold_down(pack_ref, down_ref, shards, part)
    grad_ref[:, : 2 * part] = dot_first(normed_ref[...], both_ref[...]).astype(BF16)
    down_grad = dot_first(cot_ref[...], act_ref[...]).astype(BF16)
    folds = down_grad.shape[0] // rows
    for z in range(shards):
        at = z * piece
        grad_ref[z * rows : (z + 1) * rows, 2 * part :] = jnp.concatenate(
            [down_grad[b * rows : (b + 1) * rows, at : at + piece] for b in range(folds)], axis=1
        )
    unstack_rows(result_a, dot_last(act_a[...], down_ref[...]))
    unstack_rows(result_b, dot_last(act_b[...], down_ref[...]))


def middle_kernel(shards, members, spots, *refs):
    ins, outs, scratch = split_refs(refs, 10 + members, 4, 2)
    (own_a, own_b, one_ref, two_ref, three_ref, residual_ref, inverse_ref, cot_ref, gains_ref,
     local_ref) = ins[:10]
    weights = ins[10:]
    residual_grad_ref, low_ref, attended_grad_ref, gain_grad_ref = outs
    rows = cot_ref.shape[0]
    grad = (own_a[0].astype(F32) + own_b[0].astype(F32)) + one_ref[...].astype(F32)
    grad = grad + two_ref[...].astype(F32) + three_ref[...].astype(F32)
    residual, inverse = residual_ref[...], inverse_ref[...]
    gain_grad_ref[...] = jnp.sum(grad * residual * inverse, axis=0, keepdims=True)
    residual_grad = cot_ref[...].astype(F32) + norm_back(grad, residual, inverse, gains_ref[1:2, :])
    residual_grad_ref[...] = residual_grad
    low = residual_grad.astype(BF16)
    low_ref[...] = low
    attended_grad_ref[...] = back_through(
        shards, members, spots, low, weights, local_ref, scratch
    ).astype(BF16)


def back_through(shards, members, spots, low, weights, local_ref, scratch):
    blocks, out_blocks = scratch
    shard, dp = spots[1], spots[2]
    for i, block in enumerate(lane_blocks(low, members)):
        blocks[i] = block
    away = sum(dot_last(blocks[dp ^ j], weights[j][...]) for j in range(members))
    out_blocks[shard] = dot_last(low, local_ref[...])
    for r, block in enumerate(lane_blocks(away, shards - 1)):
        out_blocks[shard ^ (r + 1)] = block
    return join_lanes(out_blocks)


def weight_grads_kernel(members, spots, *refs):
    lefts, lows, (keep_ref, send_ref, blocks) = refs[0:4:2], refs[1:4:2], refs[4:]
    dp = spots[2]
    for k, (left_ref, low_ref) in enumerate(zip(lefts, lows)):
        for i, block in enumerate(lane_blocks(low_ref[...], members)):
            blocks[k * members + i] = block
    for j in (1, 3, 0, 2):
        out_ref = send_ref if j & 1 else keep_ref
        out_ref[j // 2] = jnp.concatenate(
            [
                dot_first(left_ref[...], blocks[k * members + (dp ^ j)])
                for k, left_ref in enumerate(lefts)
            ],
            axis=1,
        ).astype(BF16)


def join_kernel(members, spots, own_ref, across_ref, core_ref, core_across_ref, *refs):
    outs, blocks = refs[:2], refs[2]
    dp = spots[2]
    for j, ref in enumerate((own_ref, core_ref, across_ref, core_across_ref)):
        blocks[dp ^ j] = ref[...]
    size = blocks.shape[-1] // 2
    for k, out_ref in enumerate(outs):
        out_ref[...] = jnp.concatenate(
            [blocks[i][:, k * size : (k + 1) * size] for i in range(members)], axis=1
        ).astype(F32)


def query_back_kernel(shards, members, spots, low_ref, local_ref, *refs):
    weights, (back_ref,), scratch = split_refs(refs, members, 1, 2)
    back_ref[...] = back_through(
        shards, members, spots, low_ref[...], weights, local_ref, scratch
    )


def back_kernel(chunk, pieces, first, last, spots, *refs):
    ins, outs, scratch = split_refs(refs, 9 + pieces, (pieces if last else 1) + 1, 2)
    (queries_ref, key_pos_ref, query_pos_ref, cos_ref, sin_ref, turned_ref, log_ref, grad_ref,
     start_ref) = ins[:9]
    parts = ins[9:]
    query_grad_ref, kv_grads = outs[0], outs[1:]
    kv_ref, kv_grad_ref = scratch
    stack_rows(kv_ref, parts)
    rows = queries_ref.shape[0]
    columns = GROUPS * rows
    query_pos = query_pos_ref[...]
    heads = []
    for head in range(KV_HEADS):
        stacked = heads_of(queries_ref, head * GROUPS, GROUPS)
        upstream = heads_of(grad_ref, head * GROUPS, GROUPS)
        delta = jnp.sum(upstream.astype(F32).T * turned_ref[head], axis=0, keepdims=True)
        log_total = log_ref[head : head + 1, :]
        keys_at = head * HEAD_DIM
        values_at = (KV_HEADS + head) * HEAD_DIM

        def step(j, query_grad, head=head, stacked=stacked, upstream=upstream,
                 delta=delta, log_total=log_total, keys_at=keys_at, values_at=values_at):
            at = pl.ds(pl.multiple_of(j * chunk, chunk), chunk)
            keys = heads_of(kv_ref, head, 1, at)
            values = heads_of(kv_ref, KV_HEADS + head, 1, at)
            scores = dot_last(keys, stacked)
            scores = jnp.where(key_pos_ref[at, :] <= query_pos, scores, MASKED)
            weights = jnp.exp(scores - log_total)
            weight_grad = dot_last(values, upstream)
            score_grad = (weights * (weight_grad - delta)).astype(BF16)
            value_grad = dot_plain(weights.astype(BF16), upstream)
            key_grad = dot_plain(score_grad, stacked)
            kv_grad_ref[at, keys_at : keys_at + HEAD_DIM] = key_grad.astype(BF16)
            kv_grad_ref[at, values_at : values_at + HEAD_DIM] = value_grad.astype(BF16)
            return query_grad + dot_first(keys, score_grad)

        start = jnp.zeros((HEAD_DIM, columns), F32) if first else start_ref[head]
        query_grad = lax.fori_loop(0, kv_ref.shape[0] // chunk, step, start)
        if not last:
            query_grad_ref[head] = query_grad
        else:
            straight = query_grad.T * (1.0 / math.sqrt(HEAD_DIM))
            heads += [straight[g * rows : (g + 1) * rows, :] for g in range(GROUPS)]
    if last:
        query_grad_ref[...] = rope_lanes(
            jnp.concatenate(heads, axis=1), cos_ref[...], -sin_ref[...]
        ).astype(BF16)
    if last:
        for i in range(pieces):
            kv_grads[i][...] = kv_grad_ref[i * rows : (i + 1) * rows, :]
    else:
        unstack_rows(kv_grads[0], kv_grad_ref[...])


def end_kernel(shards, spots, *refs):
    ins, outs, scratch = split_refs(refs, 11 + (shards + 1) + 2 * (shards - 1), 3, 1)
    (cos_ref, sin_ref, normed_ref, tokens_ref, inverse_ref, gains_ref, back_ref, residual_grad_ref,
     key_ref, value_ref, gain_two_ref) = ins[:11]
    sums, mine, other = split_refs(ins[11:], shards + 1, shards - 1, shards - 1)
    input_grad_ref, keep_ref, send_ref = outs
    (blocks,) = scratch
    core, shard = spots[0], spots[1]
    width, span = key_ref.shape
    rows = tokens_ref.shape[0]
    total = sums[0][...].astype(F32) + sums[1][0].astype(F32)
    total = total + sum(s[...].astype(F32) for s in sums[2:])
    keys = rope_lanes(total[:, :width], cos_ref[...], -sin_ref[...])
    values = total[:, width:]
    keep = jnp.where(core == 0, keys, values).astype(BF16)
    send = jnp.where(core == 0, values, keys).astype(BF16)
    blocks[shard] = dot_plain(keys.astype(BF16), key_ref[...]) + dot_plain(
        values.astype(BF16), value_ref[...]
    )
    for r in range(1, shards):
        blocks[shard ^ r] = dot_plain(keep, mine[r - 1][:width, :]) + dot_plain(
            send, other[r - 1][:width, :]
        )
    normed_grad = back_ref[...] + join_lanes(blocks)
    inputs, inverse = tokens_ref[...].astype(F32), inverse_ref[...]
    gain_grad = jnp.sum(normed_grad * inputs * inverse, axis=0, keepdims=True)
    input_grad_ref[...] = residual_grad_ref[...] + norm_back(
        normed_grad, inputs, inverse, gains_ref[0:1, :]
    )
    normed = normed_ref[...]
    two = gain_two_ref[...]
    for out_ref, low, gain in (
        (send_ref, send, jnp.where(core == 0, two, gain_grad)),
        (keep_ref, keep, jnp.where(core == 0, gain_grad, two)),
    ):
        grad = dot_first(low, normed).astype(BF16)
        gains = lane_blocks(gain, shards)
        for z, block in enumerate(lane_blocks(grad, shards)):
            out_ref[z, :width, :] = block
            out_ref[z, width:, :] = jnp.broadcast_to(
                gains[z], (EXTRA_ROWS, span)
            ).astype(BF16)


def spread_kernel(shards, members, spots, *refs):
    parts, outs, (blocks,) = split_refs(refs, members, 3, 1)
    gate_ref, up_ref, down_ref = outs
    member = spots[3]
    piece = parts[0].shape[1] // 3 // shards
    rows = parts[0].shape[0]
    span = piece * members
    for i in range(members):
        blocks[member ^ i] = parts[i][...]

    def block(k):
        at = k * piece
        return jnp.concatenate(
            [blocks[p, :, at : at + piece] for p in range(members)], axis=1
        ).astype(F32)

    for z in range(shards):
        gate_ref[:, z * span : (z + 1) * span] = block(z)
        up_ref[:, z * span : (z + 1) * span] = block(shards + z)
    for b in range(down_ref.shape[0] // rows):
        down_ref[b * rows : (b + 1) * rows, :] = block(2 * shards + b)


def base_of(block_order, stored, block_length):
    which = stored // block_length
    count = block_order.shape[1]
    matches = (which[:, None] == jnp.arange(count, dtype=jnp.int32)[None, :]).astype(jnp.int32)
    return jnp.sum(block_order[0][None, :] * matches, axis=-1) * block_length + stored % block_length


def tables(positions):
    half_dim = HEAD_DIM // 2
    exponent = -(jnp.arange(half_dim, dtype=F32) * 2.0) / HEAD_DIM
    frequency = jnp.power(F32(ROPE_BASE), exponent)
    angles = positions.astype(F32)[:, None] * frequency
    cosine, sine = jnp.cos(angles), jnp.sin(angles)
    return (
        jnp.concatenate([cosine] * 4, axis=-1),
        jnp.concatenate([-sine, sine, -sine, sine], axis=-1),
    )


def after(x, other):
    return lax.optimization_barrier((x, other))[0]


def on_device(
    tokens,
    block_order,
    attention_gain,
    query_weight,
    key_weight,
    value_weight,
    output_weight,
    feedforward_gain,
    gate_weight,
    up_weight,
    down_weight,
    cotangent,
):
    tokens, cotangent = tokens[0], cotangent[0]
    rows, width = tokens.shape
    shards = lax.axis_size("fsdp")
    ctx_count = lax.axis_size("ctx")
    dp_count = lax.axis_size("dp")
    block_length = rows * shards * ctx_count // block_order.shape[1]
    shard = lax.axis_index("fsdp")
    ctx = lax.axis_index("ctx")
    dp = lax.axis_index("dp")
    core = dp & 1
    members = dp_count * 2
    weight_rows = query_weight.shape[0]
    query_width = HEADS * HEAD_DIM
    kv_width = KV_HEADS * HEAD_DIM
    hidden = gate_weight.shape[1]
    part = hidden // members
    spots = jnp.stack([core, shard, dp, dp * 2 + (ctx & 1)]).astype(jnp.int32)

    gain_one, gain_two = attention_gain[None, :], feedforward_gain[None, :]
    key_turned, value_turned, down_turned = key_weight.T, value_weight.T, down_weight.T
    kv_pack = jnp.concatenate(
        [
            jnp.where(core == 0, key_turned, value_turned),
            jnp.pad(
                jnp.concatenate([gain_one, gain_two], axis=0), ((0, EXTRA_ROWS - 2), (0, 0))
            ),
        ],
        axis=0,
    )
    kv_mine = direct_fsdp(kv_pack)

    quarter = width // dp_count
    query_quarter, output_quarter = call(
        functools.partial(quarter_kernel, dp_count), spots,
        [after(query_weight, kv_pack), output_weight],
        [((weight_rows, quarter), BF16)] * 2, name="quarter_columns",
    )
    query_pieces = direct_fsdp(query_quarter)
    kv_other = [swap_core(piece) for piece in kv_mine]

    def stack(pieces):
        (stacked,) = call(
            stack_kernel, spots, pieces, [(((shards - 1) * weight_rows, quarter), BF16)],
            name="stack_quarters",
        )
        return stacked, swap_plane(stacked, 2, 0)

    def four(stacked, across):
        return [stacked, swap_core(stacked), across, swap_core(across)]

    group_axes = ("dp", "ctx")
    extra = {}
    if ctx_count > 2:
        extra["axis_index_groups"] = [
            [d * ctx_count + c for d in range(dp_count) for c in (first, first + 1)]
            for first in range(0, ctx_count, 2)
        ]
    cot_all = lax.all_gather(cotangent, group_axes, axis=0, tiled=False, **extra)

    offsets = jnp.arange(rows, dtype=jnp.int32)
    my_start = (ctx * shards + shard) * rows
    positions = base_of(block_order, my_start[None], block_length) + offsets
    cosine, sine = tables(positions)
    query_pos = jnp.concatenate([positions] * GROUPS)[None, :]
    starts = jnp.stack(
        [((ctx ^ d) * shards + (shard ^ r)) * rows for d in range(ctx_count) for r in range(shards)]
    )
    key_pos = (base_of(block_order, starts, block_length)[:, None] + offsets[None, :]).reshape(-1, 1)
    near_count = shards * rows
    near_pos, far_pos = key_pos[:near_count], key_pos[near_count:]
    far_count = far_pos.shape[0]

    (pack,) = call(
        functools.partial(pack_kernel, shards, members), spots,
        [gate_weight, up_weight, down_turned], [((weight_rows, 3 * part), BF16)],
        name="pack_weights",
    )
    kv_own, normed_one, normed_turned, inverse_one, gains = call(
        functools.partial(begin_kernel, shards), spots,
        [
            lax.optimization_barrier((tokens, query_quarter, pack))[0], gain_one, gain_two, key_turned, value_turned, cosine, sine,
            *kv_mine, *kv_other,
        ],
        [
            ((rows, 2 * kv_width), BF16), ((rows, width), BF16), ((rows, width), BF16),
            ((rows, 1), F32), ((8, width), F32),
        ],
        scratch=[
            ((shards, rows, weight_rows), F32), ((shards, rows, weight_rows), BF16),
            ((shards, 8, weight_rows), F32),
        ],
        name="norm_keys_values",
    )
    near = [kv_own] + direct_fsdp(kv_own)
    query_pieces = lax.optimization_barrier((kv_own, *query_pieces))[1:]
    stacked, across = stack(query_pieces)
    across, *near = lax.optimization_barrier((across, *near))
    query_stacks = four(stacked, across)
    output_quarter, near[-1] = lax.optimization_barrier((output_quarter, near[-1]))
    output_pieces = direct_fsdp(output_quarter)
    (near_all,) = call(
        stack_kernel, spots, near, [((near_count, 2 * kv_width), BF16)],
        name="stack_keys_values",
    )
    far = [swap(near_all, "ctx", d) for d in range(1, ctx_count)]

    pack, cot_all, _ = lax.optimization_barrier((pack, cot_all, near[-1]))
    pack_all = lax.all_gather(pack, "fsdp", axis=0, tiled=True)


    chunk = rows * 2
    unit = 2 * HEADS * rows * near_count * HEAD_DIM
    stat = ((KV_HEADS, GROUPS * rows), F32)
    turned_shape = ((KV_HEADS, HEAD_DIM, GROUPS * rows), F32)
    queries, largest, total, weighted = call(
        functools.partial(near_kernel, chunk, dp_count, shards), spots,
        [normed_turned, near_pos, query_pos, cosine, sine, query_weight, *query_stacks, *near],
        [((rows, query_width), BF16), stat, stat, turned_shape],
        scratch=[((dp_count, rows, quarter), F32), ((near_count, 2 * kv_width), BF16)],
        name="attention_near",
    )
    attended, turned, log_total = call(
        functools.partial(far_kernel, chunk, len(far)), spots,
        [queries, far_pos, query_pos, largest, total, weighted, *far],
        [((rows, query_width), BF16), turned_shape, stat],
        scratch=[((far_count, 2 * kv_width), BF16)], name="attention_far",
    )
    output_pieces = lax.optimization_barrier((queries, *output_pieces))[1:]
    output_stacks = four(*stack(output_pieces))
    residual, inverse_two, normed_two = call(
        functools.partial(project_kernel, shards, dp_count), spots,
        [attended, tokens, gains, output_weight, *output_stacks],
        [((rows, width), F32), ((rows, 1), F32), ((rows, width), BF16)],
        scratch=[((dp_count, rows, quarter), F32), ((shards, rows, weight_rows), BF16)],
        name="project_residual",
    )

    normed_a, normed_b = plane_pieces(normed_two)
    token_shape = ((rows, width), BF16)
    half = 4 * rows
    half_shape = ((4, rows, width), BF16)

    masks = [2 * a + b for a, b in ((0, 0),) + CHIP_MASKS]
    core_masks = [mask ^ 2 for mask in masks]

    def feed(normed, masks):
        return call(
            functools.partial(feed_kernel, shards, masks), spots, [pack_all, cot_all, *normed],
            [half_shape, ((half, part), BF16), ((half, 2 * part), BF16)],
            scratch=[((half, width), BF16), ((half, width), BF16), ((width, part), BF16)],
        name="feed_forward",
        )

    grad_b, act_b, both_b = feed(normed_b, core_masks)
    from_core = swap_core(grad_b)
    grad_a, act_a, both_a = feed(normed_a, masks)

    def chip_sums(parts_a, parts_b):
        return [
            (parts_a[k].astype(F32) + parts_b[k].astype(F32)).astype(BF16)
            for k in range(1, 4)
        ]

    def send_chips(sums):
        return [swap_plane(x, a, b) for x, (a, b) in zip(sums, CHIP_MASKS)]

    grad_sums = chip_sums(grad_a, from_core)
    grad_chips = send_chips(grad_sums)
    act_a, *_ = lax.optimization_barrier((act_a, *grad_sums))
    result_a, result_b, pack_grad = call(
        functools.partial(feed_weights_kernel, shards, masks + core_masks), spots,
        [pack_all, act_a, act_b, both_a, both_b, cot_all, *normed_a, *normed_b],
        [half_shape, half_shape, ((width, 3 * part), BF16)],
        scratch=[
            ((2 * half, width), BF16), ((2 * half, width), BF16), ((2 * half, part), BF16),
            ((2 * half, 2 * part), BF16), ((width, part), BF16),
        ],
        name="feed_forward_weights",
    )
    pack_share = sum_far(lax.psum_scatter(pack_grad, "fsdp", scatter_dimension=0, tiled=True))

    pack_grad, *grad_chips = lax.optimization_barrier((pack_grad, *grad_chips))
    residual_grad, residual_low, attended_grad, second_gain_grad = call(
        functools.partial(middle_kernel, shards, dp_count), spots,
        [
            grad_a, from_core, *grad_chips, residual, inverse_two, cotangent, gains, output_weight,
            *output_stacks,
        ],
        [((rows, width), F32), token_shape, ((rows, query_width), BF16), ((1, width), F32)],
        scratch=[((dp_count, rows, quarter), BF16), ((shards, rows, weight_rows), F32)],
        name="residual_back",
    )

    result_core = swap_core(after(result_b, residual_low))
    attended_grad, result_a = lax.optimization_barrier((attended_grad, result_a))

    def sum_x(keep, away):
        sent = (keep[1].astype(F32) + away[1].astype(F32)).astype(BF16)
        return sent, (keep[0], away[0], swap_plane(sent, 2, 0))

    def pieces_z(terms):
        out = []
        for r in range(shards):
            at = (shard ^ r) * weight_rows
            parts = [
                lax.dynamic_slice_in_dim(x, at, weight_rows, 0).astype(F32) for x in terms
            ]
            out.append((parts[0] + parts[1] + parts[2]).astype(BF16))
        return out

    def sum_z(pieces):
        arrived = {r: swap(pieces[r], "fsdp", r) for r in reversed(range(1, shards))}
        return sum(
            (arrived[r].astype(F32) for r in range(1, shards)), pieces[0].astype(F32)
        ).astype(BF16)

    def halve_z(pieces, span):
        sent = jnp.stack([piece.astype(BF16) for piece in pieces[span:]])
        arrived = swap(sent, "fsdp", span)
        return [pieces[r].astype(F32) + arrived[r].astype(F32) for r in range(span)]

    def sum_swap(own, dp_mask, ctx_mask):
        return (own.astype(F32) + swap_plane(own, dp_mask, ctx_mask).astype(F32)).astype(BF16)

    def sum_y(own):
        return sum_far(sum_swap(own, 0, 1))

    def finish_quarters(own):
        across = swap_plane(own, 2, 0)
        return call(
            functools.partial(join_kernel, dp_count), spots,
            [own, across, swap_core(own), swap_core(across)],
            [((weight_rows, width), F32)] * 2,
            scratch=[((dp_count, weight_rows, 2 * quarter), BF16)], name="join_columns",
        )

    def back(first, last, start, pos, pieces):
        count = pos.shape[0]
        shape = ((rows, query_width), BF16) if last else turned_shape
        out = call(
            functools.partial(back_kernel, chunk, len(pieces), first, last), spots,
            [
                queries, pos, query_pos, cosine, sine, turned, log_total, attended_grad, start,
                *pieces,
            ],
            [shape]
            + (
                [((rows, 2 * kv_width), BF16)] * len(pieces) if last
                else [((shards, rows, 2 * kv_width), BF16)]
            ),
            scratch=[((count, 2 * kv_width), BF16), ((count, 2 * kv_width), BF16)],
            name="attention_back_near" if last else "attention_back_far",
        )
        return out[0], out[1:]

    query_partial, far_grads = turned, []
    for d in range(1, ctx_count):
        at = (d - 1) * near_count
        query_partial, grads = back(
            d == 1, False, query_partial, far_pos[at : at + near_count], far[d - 1 : d]
        )
        far_grads.append(swap(grads[0], "ctx", d))
    result_sent = (result_a[2:].astype(F32) + result_core[2:].astype(F32)).astype(BF16)
    query_partial, result_sent = lax.optimization_barrier((query_partial, result_sent))
    result_across = swap_plane(result_sent, 2, 0)
    query_low, near_grads = back(False, True, query_partial, near_pos, near)
    pair_shape = ((2, width, 2 * quarter), BF16)
    weights_keep, weights_send = call(
        functools.partial(weight_grads_kernel, dp_count), spots,
        [attended, residual_low, normed_one, query_low], [pair_shape, pair_shape],
        scratch=[((2 * dp_count, rows, quarter), BF16)], name="query_output_weight_grads",
    )
    weights_send, far_grads[-1], result_across = lax.optimization_barrier(
        (weights_send, far_grads[-1], result_across)
    )
    result_own, result_along = [
        (result_a[k].astype(F32) + result_core[k].astype(F32)) + result_across[k].astype(F32)
        for k in (0, 1)
    ]
    result_along = swap_plane(result_along.astype(BF16), 0, 1)

    def home(r):
        return sum(grads[r].astype(F32) for grads in far_grads)

    kv_sums = {
        r: (near_grads[r].astype(F32) + home(r)).astype(BF16) for r in range(1, shards)
    }
    kv_arrived = {r: swap(kv_sums[r], "fsdp", r) for r in reversed(range(1, shards))}
    query_low, pack_share, *_ = lax.optimization_barrier(
        (query_low, pack_share, *kv_sums.values())
    )
    share_across = swap_plane(pack_share, 2, 0)

    weights_away = swap_core(weights_send)
    weights_sent, weights_terms = sum_x(weights_keep, weights_away)
    query_turn = after(query_low, weights_sent)
    (query_back,) = call(
        functools.partial(query_back_kernel, shards, dp_count), spots,
        [query_turn, query_weight, *query_stacks], [((rows, width), F32)],
        scratch=[((dp_count, rows, quarter), BF16), ((shards, rows, weight_rows), F32)],
        name="query_back",
    )
    share_along = swap_plane(pack_share, 0, 1)
    share_diagonal = swap_plane(share_across, 0, 1)
    span = kv_width + EXTRA_ROWS
    packed_shape = ((shards, span, weight_rows), BF16)
    home_all = far_grads[0]
    if ctx_count > 2:
        home_all = sum(grads.astype(F32) for grads in far_grads)
    input_grad, kv_keep, kv_send = call(
        functools.partial(end_kernel, shards), spots,
        [
            cosine, sine, normed_one, tokens, inverse_one, gains, query_back, residual_grad,
            key_turned, value_turned, second_gain_grad, near_grads[0], home_all,
            *[kv_arrived[r] for r in range(1, shards)], *kv_mine, *kv_other,
        ],
        [((rows, width), F32), packed_shape, packed_shape],
        scratch=[((shards, rows, weight_rows), F32)],
        name="keys_values_back",
    )
    kv_away = swap_core(kv_send)
    kv_keep, *weights_terms = lax.optimization_barrier((kv_keep, *weights_terms))
    weights_pieces = pieces_z(weights_terms)
    pieces = [
        (lax.dynamic_index_in_dim(kv_keep, shard ^ r, 0, keepdims=False).astype(F32)
         + lax.dynamic_index_in_dim(kv_away, shard ^ r, 0, keepdims=False).astype(F32)).astype(BF16)
        for r in range(shards)
    ]
    weights_pieces, *pieces = lax.optimization_barrier((weights_pieces, *pieces))
    kv_share = sum_z(pieces)
    weights_half = halve_z(weights_pieces, shards // 2)
    kv_share, weights_half, share_across = lax.optimization_barrier(
        (kv_share, weights_half, share_across)
    )
    kv_share = sum_swap(kv_share, 2, 0)
    kv_share, share_along, share_diagonal, result_along = lax.optimization_barrier(
        (kv_share, share_along, share_diagonal, result_along)
    )
    share_a = [pack_share, share_along, share_across, share_diagonal]
    share_b = [swap_core(piece) for piece in share_a]

    share_by_mask = [None] * members
    for k, (a, b) in enumerate(((0, 0),) + CHIP_MASKS):
        share_by_mask[2 * a + b] = share_a[k]
        share_by_mask[2 * (a ^ 1) + b] = share_b[k]
    gate_weight_grad, up_weight_grad, down_weight_grad = call(
        functools.partial(spread_kernel, shards, members), spots, share_by_mask,
        [
            ((weight_rows, hidden), F32), ((weight_rows, hidden), F32),
            ((width, down_weight.shape[0]), F32),
        ],
        scratch=[((members, weight_rows, 3 * part), BF16)],
        name="feed_forward_out",
    )
    span = shards // 2
    while span > 1:
        span //= 2
        weights_half = halve_z(weights_half, span)
    weights_own = sum_y(weights_half[0].astype(BF16))
    result = residual + (result_own + result_along.astype(F32))
    output_weight_grad, query_weight_grad = finish_quarters(weights_own)
    low = sum_far(sum_swap(kv_share, 0, 1))
    away = swap_core(low)
    first = jnp.where(core == 0, low, away).astype(F32)
    second = jnp.where(core == 0, away, low).astype(F32)

    return (
        result[None],
        input_grad[None],
        first[kv_width],
        query_weight_grad,
        first[:kv_width].T,
        second[:kv_width].T,
        output_weight_grad,
        second[kv_width],
        gate_weight_grad,
        up_weight_grad,
        down_weight_grad.T,
    )


def solution(mesh):
    row = P("fsdp", None)
    token = P("dp", ("ctx", "fsdp"), None)
    return jax.shard_map(
        on_device,
        mesh=mesh,
        in_specs=(
            token, P("dp", None), P("fsdp"), row, row, row, row, P("fsdp"), row, row, row, token,
        ),
        out_specs=(
            token, token, P("fsdp"), row, row, row, row, P("fsdp"), row, row, row,
        ),
        check_vma=False,
    )
```

```python
import functools
import math

import jax
import jax.numpy as jnp
from jax import lax
from jax.experimental import pallas as pl
from jax.experimental.pallas import tpu as pltpu
from jax.sharding import PartitionSpec as P

HEADS = 15
KV_HEADS = 5
HEAD_DIM = 64
GROUPS = HEADS // KV_HEADS
LANES = 128

EPSILON = 1e-05
ROPE_BASE = 100000.0
MASKED = -1e30

F32 = jnp.float32
BF16 = jnp.bfloat16
VMEM_LIMIT = 56 * 1024 * 1024
FLOPS_PER_US = 1150 * 10**6
MEASURED_US = {
    "pack_weights": 4,
    "norm_keys_values": 4,
    "attention_near": 12,
    "attention_far": 12,
    "feed_forward": 8,
    "feed_forward_weights": 12,
    "residual_back": 6,
    "attention_back_far": 13,
    "attention_back_near": 14,
    "query_output_weight_grads": 0,
    "query_back": 0,
    "stack_quarters": 0,
    "quarter_columns": 0,
    "keys_values_back": 6,
    "feed_forward_out": 7,
}


def dot_plain(left, right):
    return jnp.dot(left, right, preferred_element_type=F32)


def dot_last(left, right):
    return lax.dot_general(left, right, (((1,), (1,)), ((), ())), preferred_element_type=F32)


def dot_first(left, right):
    return lax.dot_general(left, right, (((0,), (0,)), ((), ())), preferred_element_type=F32)


def swap(x, axis, mask):
    count = lax.axis_size(axis)
    return lax.ppermute(x, axis, [(i, i ^ mask) for i in range(count)])


def swap_plane(x, dp_mask, ctx_mask):
    ctx_count = lax.axis_size("ctx")
    pairs = []
    for d in range(lax.axis_size("dp")):
        for c in range(ctx_count):
            pairs.append((d * ctx_count + c, (d ^ dp_mask) * ctx_count + (c ^ ctx_mask)))
    return lax.ppermute(x, ("dp", "ctx"), pairs)


def swaps_fsdp(x):
    pieces = {0: x}
    for r in range(1, lax.axis_size("fsdp")):
        top = 1 << (r.bit_length() - 1)
        pieces[r] = swap(pieces[r - top], "fsdp", top)
    return [pieces[r] for r in range(1, lax.axis_size("fsdp"))]


def direct_fsdp(x):
    return [swap(x, "fsdp", r) for r in range(1, lax.axis_size("fsdp"))]


def swap_core(x):
    return swap_plane(x, 1, 0)


CHIP_MASKS = ((0, 1), (2, 0), (2, 1))


def plane_pieces(x):
    mine = [x] + [swap_plane(x, a, b) for a, b in CHIP_MASKS]
    return mine, [swap_core(piece) for piece in mine]


def sum_far(x):
    count = lax.axis_size("ctx")
    if count == 2:
        return x
    groups = [list(range(0, count, 2)), list(range(1, count, 2))]
    return lax.psum(x.astype(F32), "ctx", axis_index_groups=groups).astype(x.dtype)


def call(kernel, spots, args, out_shapes, scratch=(), name=None):
    specs = [pl.BlockSpec(memory_space=pltpu.SMEM)]
    specs += [pl.BlockSpec(memory_space=pltpu.VMEM) for _ in args]
    outs = tuple(jax.ShapeDtypeStruct(s, d) for s, d in out_shapes)
    return pl.pallas_call(
        kernel,
        out_shape=outs,
        in_specs=specs,
        out_specs=tuple(pl.BlockSpec(memory_space=pltpu.VMEM) for _ in outs),
        scratch_shapes=[pltpu.VMEM(s, d) for s, d in scratch],
        compiler_params=pltpu.CompilerParams(vmem_limit_bytes=VMEM_LIMIT),
        cost_estimate=pl.CostEstimate(
            flops=MEASURED_US.get(name, 2) * FLOPS_PER_US, bytes_accessed=0, transcendentals=0
        ),
        name=name,
    )(spots, *args)


def split_refs(refs, *counts):
    out, at = [], 0
    for n in counts:
        out.append(refs[at : at + n])
        at += n
    assert at == len(refs)
    return out


def lane_blocks(values, count):
    size = values.shape[1] // count
    return [values[:, i * size : (i + 1) * size] for i in range(count)]


def join_lanes(ref):
    return jnp.concatenate([ref[i] for i in range(ref.shape[0])], axis=1)


def rope_lanes(values, cosine, sine):
    rows, width = values.shape
    lane = lax.broadcasted_iota(jnp.int32, (rows, LANES), 1)
    first_half = (lane % HEAD_DIM) < (HEAD_DIM // 2)
    out = []
    for start in range(0, width, LANES):
        piece = values[:, start : min(start + LANES, width)]
        size = piece.shape[1]
        if size < LANES:
            piece = jnp.concatenate([piece, jnp.zeros((rows, LANES - size), piece.dtype)], axis=1)
        ahead = pltpu.roll(piece, LANES - HEAD_DIM // 2, 1)
        behind = pltpu.roll(piece, HEAD_DIM // 2, 1)
        partner = jnp.where(first_half, ahead, behind)
        out.append((piece * cosine + partner * sine)[:, :size])
    return jnp.concatenate(out, axis=1)


def heads_of(ref, first, count, rows=None):
    out = []
    for h in range(first, first + count):
        start = (h * HEAD_DIM) // LANES * LANES
        stop = min(start + LANES, ref.shape[-1])
        pair = ref[:, start:stop] if rows is None else ref[rows, start:stop]
        at = h * HEAD_DIM - start
        out.append(pair[:, at : at + HEAD_DIM])
    return out[0] if count == 1 else jnp.concatenate(out, axis=0)


def stack_rows(scratch, pieces):
    at = 0
    for piece in pieces:
        scratch[at : at + piece.shape[0], :] = piece[...]
        at += piece.shape[0]


def unstack_rows(out_ref, values):
    count, rows = out_ref.shape[:2]
    for i in range(count):
        out_ref[i] = values[i * rows : (i + 1) * rows, :].astype(out_ref.dtype)


def norm_rows(values, gain):
    inverse = lax.rsqrt(jnp.mean(values * values, axis=-1, keepdims=True) + EPSILON)
    return (values * inverse * gain, inverse)


def norm_back(gradient, values, inverse, gain):
    scaled = gradient * gain
    inner_mean = jnp.mean(scaled * values, axis=-1, keepdims=True)
    return inverse * scaled - values * (inverse * inverse * inverse) * inner_mean


EXTRA_ROWS = 16


def pack_kernel(shards, members, spots, gate_ref, up_ref, down_ref, out_ref):
    member = spots[3]
    span = gate_ref.shape[1] // shards
    piece = span // members
    rows = gate_ref.shape[0]
    pick = (
        lax.broadcasted_iota(jnp.int32, (span, piece), 0)
        == lax.broadcasted_iota(jnp.int32, (span, piece), 1) + member * piece
    ).astype(BF16)
    out = []
    for ref in (gate_ref, up_ref):
        for z in range(shards):
            out.append(dot_plain(ref[:, z * span : (z + 1) * span], pick))
    down = dot_plain(down_ref[...], pick)
    out += [down[b : b + rows, :] for b in range(0, down_ref.shape[0], rows)]
    out_ref[...] = jnp.concatenate(out, axis=1).astype(BF16)


def quarter_kernel(members, spots, query_ref, output_ref, *outs):
    size = query_ref.shape[1] // members
    for i in range(members):

        @pl.when(spots[2] == i)
        def _():
            for ref, out_ref in zip((query_ref, output_ref), outs):
                out_ref[...] = ref[:, i * size : (i + 1) * size]


def stack_kernel(spots, *refs):
    stack_rows(refs[-1], refs[:-1])


def begin_kernel(shards, spots, *refs):
    ins, outs, scratch = split_refs(refs, 7 + 2 * (shards - 1), 5, 3)
    tokens_ref, gain_one, gain_two, key_ref, value_ref, cos_ref, sin_ref = ins[:7]
    mine, other = split_refs(ins[7:], shards - 1, shards - 1)
    kv_ref, normed_ref, turned_ref, inverse_ref, gains_ref = outs
    blocks, normed_blocks, gain_blocks = scratch
    core, shard = spots[0], spots[1]
    width = key_ref.shape[0]
    values = tokens_ref[...].astype(F32)
    inverse = lax.rsqrt(jnp.mean(values * values, axis=-1, keepdims=True) + EPSILON)
    inverse_ref[...] = inverse
    for z, block in enumerate(lane_blocks(values * inverse, shards)):
        blocks[z] = block
    sums, order = [], []
    for r in range(shards):
        at = shard ^ r
        if r == 0:
            pair = jnp.concatenate([gain_one[...], gain_two[...]], axis=0).astype(F32)
        else:
            pair = mine[r - 1][width : width + EXTRA_ROWS, :].astype(F32)[0:2, :]
        gain_blocks[at, 0:2, :] = pair
        normed = (blocks[at] * pair[0:1, :]).astype(BF16)
        normed_blocks[at] = normed
        order.append(normed)
        left = key_ref[...] if r == 0 else mine[r - 1][:width, :]
        right = value_ref[...] if r == 0 else other[r - 1][:width, :]
        sums.append((dot_last(normed, left), dot_last(normed, right)))
    first = sum(s[0] for s in sums[1:])
    second = sum(s[1] for s in sums[1:])
    keys = jnp.where(core == 0, first, second) + sums[0][0]
    vals = jnp.where(core == 0, second, first) + sums[0][1]
    keys = rope_lanes(keys, cos_ref[...], sin_ref[...])
    kv_ref[...] = jnp.concatenate([keys, vals], axis=1).astype(BF16)
    normed_ref[...] = join_lanes(normed_blocks)
    turned_ref[...] = jnp.concatenate(order, axis=1)
    gains_ref[...] = jnp.zeros_like(gains_ref)
    gains_ref[0:2, :] = jnp.concatenate([gain_blocks[z][0:2, :] for z in range(shards)], axis=1)


def repeat(count, step, state):
    if count > 2:
        return lax.fori_loop(0, count, step, state)
    for j in range(count):
        state = step(j, state)
    return state


def rows_at(j, chunk):
    if isinstance(j, int):
        return slice(j * chunk, (j + 1) * chunk)
    return pl.ds(pl.multiple_of(j * chunk, chunk), chunk)


def attend(chunk, head, kv_ref, key_pos_ref, query_pos, stacked, state):
    def step(j, state):
        largest, total, weighted = state
        at = rows_at(j, chunk)
        keys = heads_of(kv_ref, head, 1, at)
        values = heads_of(kv_ref, KV_HEADS + head, 1, at)
        scores = dot_last(keys, stacked)
        scores = jnp.where(key_pos_ref[at, :] <= query_pos, scores, MASKED)
        new_largest = jnp.maximum(largest, jnp.max(scores, axis=0, keepdims=True))
        weights = jnp.exp(scores - new_largest)
        factor = jnp.exp(largest - new_largest)
        total = total * factor + jnp.sum(weights, axis=0, keepdims=True)
        weighted = weighted * factor + dot_first(values, weights.astype(BF16))
        return new_largest, total, weighted

    return repeat(kv_ref.shape[0] // chunk, step, state)


def near_kernel(chunk, members, pieces, spots, *refs):
    ins, outs, scratch = split_refs(refs, 6 + members + pieces, 4, 2)
    normed_ref, key_pos_ref, query_pos_ref, cos_ref, sin_ref, local_ref = ins[:6]
    weights, parts = split_refs(ins[6:], members, pieces)
    queries_ref, largest_ref, total_ref, weighted_ref = outs
    blocks, kv_ref = scratch
    dp = spots[2]
    stack_rows(kv_ref, parts)
    own = local_ref.shape[0]
    away = normed_ref[:, own:]
    for j in range(members):
        blocks[dp ^ j] = dot_plain(away, weights[j][...])
    raw = join_lanes(blocks) + dot_plain(normed_ref[:, :own], local_ref[...])
    roped = rope_lanes(raw, cos_ref[...], sin_ref[...]).astype(BF16)
    queries_ref[...] = roped * jnp.asarray(1.0 / math.sqrt(HEAD_DIM), BF16)
    columns = GROUPS * queries_ref.shape[0]
    query_pos = query_pos_ref[...]
    for head in range(KV_HEADS):
        stacked = heads_of(queries_ref, head * GROUPS, GROUPS)
        start = (
            jnp.full((1, columns), MASKED, F32),
            jnp.zeros((1, columns), F32),
            jnp.zeros((HEAD_DIM, columns), F32),
        )
        largest, total, weighted = attend(
            chunk, head, kv_ref, key_pos_ref, query_pos, stacked, start
        )
        largest_ref[head : head + 1, :] = largest
        total_ref[head : head + 1, :] = total
        weighted_ref[head] = weighted


def far_kernel(chunk, pieces, spots, *refs):
    ins, outs, (kv_ref,) = split_refs(refs, 6 + pieces, 3, 1)
    queries_ref, key_pos_ref, query_pos_ref, largest_ref, total_ref, weighted_ref = ins[:6]
    parts = ins[6:]
    attended_ref, turned_ref, log_ref = outs
    stack_rows(kv_ref, parts)
    rows = queries_ref.shape[0]
    query_pos = query_pos_ref[...]
    heads = []
    for head in range(KV_HEADS):
        stacked = heads_of(queries_ref, head * GROUPS, GROUPS)
        start = (largest_ref[head : head + 1, :], total_ref[head : head + 1, :], weighted_ref[head])
        largest, total, weighted = attend(
            chunk, head, kv_ref, key_pos_ref, query_pos, stacked, start
        )
        turned = weighted / total
        turned_ref[head] = turned
        log_ref[head : head + 1, :] = largest + jnp.log(total)
        straight = turned.T
        heads += [straight[g * rows : (g + 1) * rows, :] for g in range(GROUPS)]
    attended_ref[...] = jnp.concatenate(heads, axis=1).astype(BF16)


def project_kernel(shards, members, spots, *refs):
    ins, outs, (blocks, head_blocks) = split_refs(refs, 4 + members, 3, 2)
    attended_ref, tokens_ref, gains_ref, local_ref = ins[:4]
    weights = ins[4:]
    residual_ref, inverse_ref, normed_ref = outs
    shard, dp = spots[1], spots[2]
    for z, block in enumerate(lane_blocks(attended_ref[...], shards)):
        head_blocks[z] = block
    away = jnp.concatenate([head_blocks[shard ^ r] for r in range(1, shards)], axis=1)
    for j in range(members):
        blocks[dp ^ j] = dot_plain(away, weights[j][...])
    added = join_lanes(blocks) + dot_plain(head_blocks[shard], local_ref[...])
    residual = tokens_ref[...].astype(F32) + added
    residual_ref[...] = residual
    normed, inverse = norm_rows(residual, gains_ref[1:2, :])
    inverse_ref[...] = inverse
    normed_ref[...] = normed.astype(BF16)


def unfold_down(pack_ref, down_ref, shards, part):
    piece = part // shards
    rows = pack_ref.shape[0] // shards
    for b in range(down_ref.shape[0] // rows):
        at = 2 * part + b * piece
        down_ref[b * rows : (b + 1) * rows, :] = jnp.concatenate(
            [pack_ref[z * rows : (z + 1) * rows, at : at + piece] for z in range(shards)], axis=1
        )


def feed_kernel(shards, masks, spots, *refs):
    ins, outs, scratch = split_refs(refs, 2 + len(masks), 3, 3)
    pack_ref, cot_all, normed_parts = ins[0], ins[1], ins[2:]
    cot_parts = [cot_all[spots[3] ^ mask] for mask in masks]
    grad_ref, act_ref, both_ref = outs
    normed_ref, cot_ref, down_ref = scratch
    part = pack_ref.shape[1] // 3
    stack_rows(normed_ref, normed_parts)
    stack_rows(cot_ref, cot_parts)
    unfold_down(pack_ref, down_ref, shards, part)
    gate_up = dot_plain(normed_ref[...], pack_ref[:, : 2 * part])
    gate, upward = gate_up[:, :part], gate_up[:, part:]
    act_grad = dot_plain(cot_ref[...], down_ref[...])
    sigmoid_gate = jax.nn.sigmoid(gate)
    silu = gate * sigmoid_gate
    act_ref[...] = (silu * upward).astype(BF16)
    gate_grad = act_grad * upward * sigmoid_gate * (1.0 + gate * (1.0 - sigmoid_gate))
    both_ref[...] = jnp.concatenate([gate_grad, act_grad * silu], axis=1).astype(BF16)
    unstack_rows(grad_ref, dot_last(both_ref[...], pack_ref[:, : 2 * part]))


def feed_weights_kernel(shards, masks, spots, *refs):
    ins, outs, scratch = split_refs(refs, 6 + len(masks), 3, 5)
    pack_ref, act_a, act_b, both_a, both_b, cot_all = ins[:6]
    normed_parts = ins[6:]
    cot_parts = [cot_all[spots[3] ^ mask] for mask in masks]
    result_a, result_b, grad_ref = outs
    normed_ref, cot_ref, act_ref, both_ref, down_ref = scratch
    part = pack_ref.shape[1] // 3
    piece = part // shards
    rows = grad_ref.shape[0] // shards
    stack_rows(normed_ref, normed_parts)
    stack_rows(cot_ref, cot_parts)
    stack_rows(act_ref, (act_a, act_b))
    stack_rows(both_ref, (both_a, both_b))
    unfold_down(pack_ref, down_ref, shards, part)
    grad_ref[:, : 2 * part] = dot_first(normed_ref[...], both_ref[...]).astype(BF16)
    down_grad = dot_first(cot_ref[...], act_ref[...]).astype(BF16)
    folds = down_grad.shape[0] // rows
    for z in range(shards):
        at = z * piece
        grad_ref[z * rows : (z + 1) * rows, 2 * part :] = jnp.concatenate(
            [down_grad[b * rows : (b + 1) * rows, at : at + piece] for b in range(folds)], axis=1
        )
    unstack_rows(result_a, dot_last(act_a[...], down_ref[...]))
    unstack_rows(result_b, dot_last(act_b[...], down_ref[...]))


def middle_kernel(shards, members, spots, *refs):
    ins, outs, scratch = split_refs(refs, 10 + members, 4, 2)
    (own_a, own_b, one_ref, two_ref, three_ref, residual_ref, inverse_ref, cot_ref, gains_ref,
     local_ref) = ins[:10]
    weights = ins[10:]
    residual_grad_ref, low_ref, attended_grad_ref, gain_grad_ref = outs
    rows = cot_ref.shape[0]
    grad = (own_a[0].astype(F32) + own_b[0].astype(F32)) + one_ref[...].astype(F32)
    grad = grad + two_ref[...].astype(F32) + three_ref[...].astype(F32)
    residual, inverse = residual_ref[...], inverse_ref[...]
    gain_grad_ref[...] = jnp.sum(grad * residual * inverse, axis=0, keepdims=True)
    residual_grad = cot_ref[...].astype(F32) + norm_back(grad, residual, inverse, gains_ref[1:2, :])
    residual_grad_ref[...] = residual_grad
    low = residual_grad.astype(BF16)
    low_ref[...] = low
    attended_grad_ref[...] = back_through(
        shards, members, spots, low, weights, local_ref, scratch
    ).astype(BF16)


def back_through(shards, members, spots, low, weights, local_ref, scratch):
    blocks, out_blocks = scratch
    shard, dp = spots[1], spots[2]
    for i, block in enumerate(lane_blocks(low, members)):
        blocks[i] = block
    away = sum(dot_last(blocks[dp ^ j], weights[j][...]) for j in range(members))
    out_blocks[shard] = dot_last(low, local_ref[...])
    for r, block in enumerate(lane_blocks(away, shards - 1)):
        out_blocks[shard ^ (r + 1)] = block
    return join_lanes(out_blocks)


def weight_grads_kernel(members, spots, *refs):
    lefts, lows, (keep_ref, send_ref, blocks) = refs[0:4:2], refs[1:4:2], refs[4:]
    dp = spots[2]
    for k, (left_ref, low_ref) in enumerate(zip(lefts, lows)):
        for i, block in enumerate(lane_blocks(low_ref[...], members)):
            blocks[k * members + i] = block
    for j in (1, 3, 0, 2):
        out_ref = send_ref if j & 1 else keep_ref
        out_ref[j // 2] = jnp.concatenate(
            [
                dot_first(left_ref[...], blocks[k * members + (dp ^ j)])
                for k, left_ref in enumerate(lefts)
            ],
            axis=1,
        ).astype(BF16)


def join_kernel(members, spots, own_ref, across_ref, core_ref, core_across_ref, *refs):
    outs, blocks = refs[:2], refs[2]
    dp = spots[2]
    for j, ref in enumerate((own_ref, core_ref, across_ref, core_across_ref)):
        blocks[dp ^ j] = ref[...]
    size = blocks.shape[-1] // 2
    for k, out_ref in enumerate(outs):
        out_ref[...] = jnp.concatenate(
            [blocks[i][:, k * size : (k + 1) * size] for i in range(members)], axis=1
        ).astype(F32)


def query_back_kernel(shards, members, spots, low_ref, local_ref, *refs):
    weights, (back_ref,), scratch = split_refs(refs, members, 1, 2)
    back_ref[...] = back_through(
        shards, members, spots, low_ref[...], weights, local_ref, scratch
    )


def back_kernel(chunk, pieces, first, last, spots, *refs):
    ins, outs, scratch = split_refs(refs, 9 + pieces, (pieces if last else 1) + 1, 2)
    (queries_ref, key_pos_ref, query_pos_ref, cos_ref, sin_ref, turned_ref, log_ref, grad_ref,
     start_ref) = ins[:9]
    parts = ins[9:]
    query_grad_ref, kv_grads = outs[0], outs[1:]
    kv_ref, kv_grad_ref = scratch
    stack_rows(kv_ref, parts)
    rows = queries_ref.shape[0]
    columns = GROUPS * rows
    query_pos = query_pos_ref[...]
    heads = []
    for head in range(KV_HEADS):
        stacked = heads_of(queries_ref, head * GROUPS, GROUPS)
        upstream = heads_of(grad_ref, head * GROUPS, GROUPS)
        delta = jnp.sum(upstream.astype(F32).T * turned_ref[head], axis=0, keepdims=True)
        log_total = log_ref[head : head + 1, :]
        keys_at = head * HEAD_DIM
        values_at = (KV_HEADS + head) * HEAD_DIM

        def step(j, query_grad, head=head, stacked=stacked, upstream=upstream,
                 delta=delta, log_total=log_total, keys_at=keys_at, values_at=values_at):
            at = rows_at(j, chunk)
            keys = heads_of(kv_ref, head, 1, at)
            values = heads_of(kv_ref, KV_HEADS + head, 1, at)
            scores = dot_last(keys, stacked)
            scores = jnp.where(key_pos_ref[at, :] <= query_pos, scores, MASKED)
            weights = jnp.exp(scores - log_total)
            weight_grad = dot_last(values, upstream)
            score_grad = (weights * (weight_grad - delta)).astype(BF16)
            value_grad = dot_plain(weights.astype(BF16), upstream)
            key_grad = dot_plain(score_grad, stacked)
            kv_grad_ref[at, keys_at : keys_at + HEAD_DIM] = key_grad.astype(BF16)
            kv_grad_ref[at, values_at : values_at + HEAD_DIM] = value_grad.astype(BF16)
            return query_grad + dot_first(keys, score_grad)

        start = jnp.zeros((HEAD_DIM, columns), F32) if first else start_ref[head]
        query_grad = repeat(kv_ref.shape[0] // chunk, step, start)
        if not last:
            query_grad_ref[head] = query_grad
        else:
            straight = query_grad.T * (1.0 / math.sqrt(HEAD_DIM))
            heads += [straight[g * rows : (g + 1) * rows, :] for g in range(GROUPS)]
    if last:
        query_grad_ref[...] = rope_lanes(
            jnp.concatenate(heads, axis=1), cos_ref[...], -sin_ref[...]
        ).astype(BF16)
    if last:
        for i in range(pieces):
            kv_grads[i][...] = kv_grad_ref[i * rows : (i + 1) * rows, :]
    else:
        unstack_rows(kv_grads[0], kv_grad_ref[...])


def end_kernel(shards, spots, *refs):
    ins, outs, scratch = split_refs(refs, 11 + (shards + 1) + 2 * (shards - 1), 3, 1)
    (cos_ref, sin_ref, normed_ref, tokens_ref, inverse_ref, gains_ref, back_ref, residual_grad_ref,
     key_ref, value_ref, gain_two_ref) = ins[:11]
    sums, mine, other = split_refs(ins[11:], shards + 1, shards - 1, shards - 1)
    input_grad_ref, keep_ref, send_ref = outs
    (blocks,) = scratch
    core, shard = spots[0], spots[1]
    width, span = key_ref.shape
    rows = tokens_ref.shape[0]
    total = sums[0][...].astype(F32) + sums[1][0].astype(F32)
    total = total + sum(s[...].astype(F32) for s in sums[2:])
    keys = rope_lanes(total[:, :width], cos_ref[...], -sin_ref[...])
    values = total[:, width:]
    keep = jnp.where(core == 0, keys, values).astype(BF16)
    send = jnp.where(core == 0, values, keys).astype(BF16)
    blocks[shard] = dot_plain(keys.astype(BF16), key_ref[...]) + dot_plain(
        values.astype(BF16), value_ref[...]
    )
    for r in range(1, shards):
        blocks[shard ^ r] = dot_plain(keep, mine[r - 1][:width, :]) + dot_plain(
            send, other[r - 1][:width, :]
        )
    normed_grad = back_ref[...] + join_lanes(blocks)
    inputs, inverse = tokens_ref[...].astype(F32), inverse_ref[...]
    gain_grad = jnp.sum(normed_grad * inputs * inverse, axis=0, keepdims=True)
    input_grad_ref[...] = residual_grad_ref[...] + norm_back(
        normed_grad, inputs, inverse, gains_ref[0:1, :]
    )
    normed = normed_ref[...]
    two = gain_two_ref[...]
    for out_ref, low, gain in (
        (send_ref, send, jnp.where(core == 0, two, gain_grad)),
        (keep_ref, keep, jnp.where(core == 0, gain_grad, two)),
    ):
        grad = dot_first(low, normed).astype(BF16)
        gains = lane_blocks(gain, shards)
        for z, block in enumerate(lane_blocks(grad, shards)):
            out_ref[z, :width, :] = block
            out_ref[z, width:, :] = jnp.broadcast_to(
                gains[z], (EXTRA_ROWS, span)
            ).astype(BF16)


def spread_kernel(shards, members, spots, *refs):
    parts, outs, (blocks,) = split_refs(refs, members, 3, 1)
    gate_ref, up_ref, down_ref = outs
    member = spots[3]
    piece = parts[0].shape[1] // 3 // shards
    rows = parts[0].shape[0]
    span = piece * members
    for i in range(members):
        blocks[member ^ i] = parts[i][...]

    def block(k):
        at = k * piece
        return jnp.concatenate(
            [blocks[p, :, at : at + piece] for p in range(members)], axis=1
        ).astype(F32)

    for z in range(shards):
        gate_ref[:, z * span : (z + 1) * span] = block(z)
        up_ref[:, z * span : (z + 1) * span] = block(shards + z)
    for b in range(down_ref.shape[0] // rows):
        down_ref[b * rows : (b + 1) * rows, :] = block(2 * shards + b)


def base_of(block_order, stored, block_length):
    which = stored // block_length
    count = block_order.shape[1]
    matches = (which[:, None] == jnp.arange(count, dtype=jnp.int32)[None, :]).astype(jnp.int32)
    return jnp.sum(block_order[0][None, :] * matches, axis=-1) * block_length + stored % block_length


def tables(positions):
    half_dim = HEAD_DIM // 2
    exponent = -(jnp.arange(half_dim, dtype=F32) * 2.0) / HEAD_DIM
    frequency = jnp.power(F32(ROPE_BASE), exponent)
    angles = positions.astype(F32)[:, None] * frequency
    cosine, sine = jnp.cos(angles), jnp.sin(angles)
    return (
        jnp.concatenate([cosine] * 4, axis=-1),
        jnp.concatenate([-sine, sine, -sine, sine], axis=-1),
    )


def after(x, other):
    return lax.optimization_barrier((x, other))[0]


def on_device(
    tokens,
    block_order,
    attention_gain,
    query_weight,
    key_weight,
    value_weight,
    output_weight,
    feedforward_gain,
    gate_weight,
    up_weight,
    down_weight,
    cotangent,
):
    tokens, cotangent = tokens[0], cotangent[0]
    rows, width = tokens.shape
    shards = lax.axis_size("fsdp")
    ctx_count = lax.axis_size("ctx")
    dp_count = lax.axis_size("dp")
    block_length = rows * shards * ctx_count // block_order.shape[1]
    shard = lax.axis_index("fsdp")
    ctx = lax.axis_index("ctx")
    dp = lax.axis_index("dp")
    core = dp & 1
    members = dp_count * 2
    weight_rows = query_weight.shape[0]
    query_width = HEADS * HEAD_DIM
    kv_width = KV_HEADS * HEAD_DIM
    hidden = gate_weight.shape[1]
    part = hidden // members
    spots = jnp.stack([core, shard, dp, dp * 2 + (ctx & 1)]).astype(jnp.int32)

    gain_one, gain_two = attention_gain[None, :], feedforward_gain[None, :]
    key_turned, value_turned, down_turned = key_weight.T, value_weight.T, down_weight.T
    kv_pack = jnp.concatenate(
        [
            jnp.where(core == 0, key_turned, value_turned),
            jnp.pad(
                jnp.concatenate([gain_one, gain_two], axis=0), ((0, EXTRA_ROWS - 2), (0, 0))
            ),
        ],
        axis=0,
    )
    kv_mine = direct_fsdp(kv_pack)

    quarter = width // dp_count
    query_quarter, output_quarter = call(
        functools.partial(quarter_kernel, dp_count), spots,
        [after(query_weight, kv_pack), output_weight],
        [((weight_rows, quarter), BF16)] * 2, name="quarter_columns",
    )
    query_pieces = direct_fsdp(query_quarter)
    kv_other = [swap_core(piece) for piece in kv_mine]

    def stack(pieces):
        (stacked,) = call(
            stack_kernel, spots, pieces, [(((shards - 1) * weight_rows, quarter), BF16)],
            name="stack_quarters",
        )
        return stacked, swap_plane(stacked, 2, 0)

    def four(stacked, across):
        return [stacked, swap_core(stacked), across, swap_core(across)]

    group_axes = ("dp", "ctx")
    extra = {}
    if ctx_count > 2:
        extra["axis_index_groups"] = [
            [d * ctx_count + c for d in range(dp_count) for c in (first, first + 1)]
            for first in range(0, ctx_count, 2)
        ]
    cot_all = lax.all_gather(cotangent, group_axes, axis=0, tiled=False, **extra)

    offsets = jnp.arange(rows, dtype=jnp.int32)
    my_start = (ctx * shards + shard) * rows
    positions = base_of(block_order, my_start[None], block_length) + offsets
    cosine, sine = tables(positions)
    query_pos = jnp.concatenate([positions] * GROUPS)[None, :]
    starts = jnp.stack(
        [((ctx ^ d) * shards + (shard ^ r)) * rows for d in range(ctx_count) for r in range(shards)]
    )
    key_pos = (base_of(block_order, starts, block_length)[:, None] + offsets[None, :]).reshape(-1, 1)
    near_count = shards * rows
    near_pos, far_pos = key_pos[:near_count], key_pos[near_count:]
    far_count = far_pos.shape[0]

    (pack,) = call(
        functools.partial(pack_kernel, shards, members), spots,
        [gate_weight, up_weight, down_turned], [((weight_rows, 3 * part), BF16)],
        name="pack_weights",
    )
    kv_own, normed_one, normed_turned, inverse_one, gains = call(
        functools.partial(begin_kernel, shards), spots,
        [
            lax.optimization_barrier((tokens, query_quarter, pack))[0], gain_one, gain_two, key_turned, value_turned, cosine, sine,
            *kv_mine, *kv_other,
        ],
        [
            ((rows, 2 * kv_width), BF16), ((rows, width), BF16), ((rows, width), BF16),
            ((rows, 1), F32), ((8, width), F32),
        ],
        scratch=[
            ((shards, rows, weight_rows), F32), ((shards, rows, weight_rows), BF16),
            ((shards, 8, weight_rows), F32),
        ],
        name="norm_keys_values",
    )
    near = [kv_own] + direct_fsdp(kv_own)
    query_pieces = lax.optimization_barrier((kv_own, *query_pieces))[1:]
    stacked, across = stack(query_pieces)
    output_quarter = after(output_quarter, near[1])
    across, *near = lax.optimization_barrier((across, *near))
    query_stacks = four(stacked, across)
    output_pieces = direct_fsdp(output_quarter)
    (near_all,) = call(
        stack_kernel, spots, near, [((near_count, 2 * kv_width), BF16)],
        name="stack_keys_values",
    )
    far = [swap(near_all, "ctx", d) for d in range(1, ctx_count)]

    pack, cot_all, _ = lax.optimization_barrier((pack, cot_all, near[-1]))
    pack_all = lax.all_gather(pack, "fsdp", axis=0, tiled=True)


    chunk = rows * 2
    unit = 2 * HEADS * rows * near_count * HEAD_DIM
    stat = ((KV_HEADS, GROUPS * rows), F32)
    turned_shape = ((KV_HEADS, HEAD_DIM, GROUPS * rows), F32)
    queries, largest, total, weighted = call(
        functools.partial(near_kernel, chunk, dp_count, shards), spots,
        [normed_turned, near_pos, query_pos, cosine, sine, query_weight, *query_stacks, *near],
        [((rows, query_width), BF16), stat, stat, turned_shape],
        scratch=[((dp_count, rows, quarter), F32), ((near_count, 2 * kv_width), BF16)],
        name="attention_near",
    )
    attended, turned, log_total = call(
        functools.partial(far_kernel, chunk, len(far)), spots,
        [queries, far_pos, query_pos, largest, total, weighted, *far],
        [((rows, query_width), BF16), turned_shape, stat],
        scratch=[((far_count, 2 * kv_width), BF16)], name="attention_far",
    )
    output_pieces = lax.optimization_barrier((queries, *output_pieces))[1:]
    output_stacks = four(*stack(output_pieces))
    residual, inverse_two, normed_two = call(
        functools.partial(project_kernel, shards, dp_count), spots,
        [attended, tokens, gains, output_weight, *output_stacks],
        [((rows, width), F32), ((rows, 1), F32), ((rows, width), BF16)],
        scratch=[((dp_count, rows, quarter), F32), ((shards, rows, weight_rows), BF16)],
        name="project_residual",
    )

    normed_a, normed_b = plane_pieces(normed_two)
    token_shape = ((rows, width), BF16)
    half = 4 * rows
    half_shape = ((4, rows, width), BF16)

    masks = [2 * a + b for a, b in ((0, 0),) + CHIP_MASKS]
    core_masks = [mask ^ 2 for mask in masks]

    def feed(normed, masks):
        return call(
            functools.partial(feed_kernel, shards, masks), spots, [pack_all, cot_all, *normed],
            [half_shape, ((half, part), BF16), ((half, 2 * part), BF16)],
            scratch=[((half, width), BF16), ((half, width), BF16), ((width, part), BF16)],
        name="feed_forward",
        )

    grad_b, act_b, both_b = feed(normed_b, core_masks)
    from_core = swap_core(grad_b)
    grad_a, act_a, both_a = feed(normed_a, masks)

    def chip_sums(parts_a, parts_b):
        return [
            (parts_a[k].astype(F32) + parts_b[k].astype(F32)).astype(BF16)
            for k in range(1, 4)
        ]

    def send_chips(sums):
        return [swap_plane(x, a, b) for x, (a, b) in zip(sums, CHIP_MASKS)]

    grad_sums = chip_sums(grad_a, from_core)
    grad_chips = send_chips(grad_sums)
    act_a, *_ = lax.optimization_barrier((act_a, *grad_sums))
    result_a, result_b, pack_grad = call(
        functools.partial(feed_weights_kernel, shards, masks + core_masks), spots,
        [pack_all, act_a, act_b, both_a, both_b, cot_all, *normed_a, *normed_b],
        [half_shape, half_shape, ((width, 3 * part), BF16)],
        scratch=[
            ((2 * half, width), BF16), ((2 * half, width), BF16), ((2 * half, part), BF16),
            ((2 * half, 2 * part), BF16), ((width, part), BF16),
        ],
        name="feed_forward_weights",
    )
    pack_share = sum_far(lax.psum_scatter(pack_grad, "fsdp", scatter_dimension=0, tiled=True))

    pack_grad, *grad_chips = lax.optimization_barrier((pack_grad, *grad_chips))
    residual_grad, residual_low, attended_grad, second_gain_grad = call(
        functools.partial(middle_kernel, shards, dp_count), spots,
        [
            grad_a, from_core, *grad_chips, residual, inverse_two, cotangent, gains, output_weight,
            *output_stacks,
        ],
        [((rows, width), F32), token_shape, ((rows, query_width), BF16), ((1, width), F32)],
        scratch=[((dp_count, rows, quarter), BF16), ((shards, rows, weight_rows), F32)],
        name="residual_back",
    )

    result_core = swap_core(after(result_b, residual_low))
    attended_grad, result_a = lax.optimization_barrier((attended_grad, result_a))

    def sum_x(keep, away):
        sent = (keep[1].astype(F32) + away[1].astype(F32)).astype(BF16)
        return sent, (keep[0], away[0], swap_plane(sent, 2, 0))

    def pieces_z(terms):
        out = []
        for r in range(shards):
            at = (shard ^ r) * weight_rows
            parts = [
                lax.dynamic_slice_in_dim(x, at, weight_rows, 0).astype(F32) for x in terms
            ]
            out.append((parts[0] + parts[1] + parts[2]).astype(BF16))
        return out

    def sum_z(pieces):
        arrived = {r: swap(pieces[r], "fsdp", r) for r in reversed(range(1, shards))}
        return sum(
            (arrived[r].astype(F32) for r in range(1, shards)), pieces[0].astype(F32)
        ).astype(BF16)

    def halve_z(pieces, span):
        sent = jnp.stack([piece.astype(BF16) for piece in pieces[span:]])
        arrived = swap(sent, "fsdp", span)
        return [pieces[r].astype(F32) + arrived[r].astype(F32) for r in range(span)]

    def sum_swap(own, dp_mask, ctx_mask):
        return (own.astype(F32) + swap_plane(own, dp_mask, ctx_mask).astype(F32)).astype(BF16)

    def sum_y(own):
        return sum_far(sum_swap(own, 0, 1))

    def finish_quarters(own):
        across = swap_plane(own, 2, 0)
        return call(
            functools.partial(join_kernel, dp_count), spots,
            [own, across, swap_core(own), swap_core(across)],
            [((weight_rows, width), F32)] * 2,
            scratch=[((dp_count, weight_rows, 2 * quarter), BF16)], name="join_columns",
        )

    def back(first, last, start, pos, pieces):
        count = pos.shape[0]
        shape = ((rows, query_width), BF16) if last else turned_shape
        out = call(
            functools.partial(back_kernel, chunk, len(pieces), first, last), spots,
            [
                queries, pos, query_pos, cosine, sine, turned, log_total, attended_grad, start,
                *pieces,
            ],
            [shape]
            + (
                [((rows, 2 * kv_width), BF16)] * len(pieces) if last
                else [((shards, rows, 2 * kv_width), BF16)]
            ),
            scratch=[((count, 2 * kv_width), BF16), ((count, 2 * kv_width), BF16)],
            name="attention_back_near" if last else "attention_back_far",
        )
        return out[0], out[1:]

    query_partial, far_grads = turned, []
    for d in range(1, ctx_count):
        at = (d - 1) * near_count
        query_partial, grads = back(
            d == 1, False, query_partial, far_pos[at : at + near_count], far[d - 1 : d]
        )
        far_grads.append(swap(grads[0], "ctx", d))
    result_sent = (result_a[2:].astype(F32) + result_core[2:].astype(F32)).astype(BF16)
    query_partial, result_sent = lax.optimization_barrier((query_partial, result_sent))
    result_across = swap_plane(result_sent, 2, 0)
    query_low, near_grads = back(False, True, query_partial, near_pos, near)
    pair_shape = ((2, width, 2 * quarter), BF16)
    weights_keep, weights_send = call(
        functools.partial(weight_grads_kernel, dp_count), spots,
        [attended, residual_low, normed_one, query_low], [pair_shape, pair_shape],
        scratch=[((2 * dp_count, rows, quarter), BF16)], name="query_output_weight_grads",
    )
    weights_send, far_grads[-1], result_across = lax.optimization_barrier(
        (weights_send, far_grads[-1], result_across)
    )
    result_own, result_along = [
        (result_a[k].astype(F32) + result_core[k].astype(F32)) + result_across[k].astype(F32)
        for k in (0, 1)
    ]
    result_along = swap_plane(result_along.astype(BF16), 0, 1)

    def home(r):
        return sum(grads[r].astype(F32) for grads in far_grads)

    kv_sums = {
        r: (near_grads[r].astype(F32) + home(r)).astype(BF16) for r in range(1, shards)
    }
    kv_arrived = {r: swap(kv_sums[r], "fsdp", r) for r in reversed(range(1, shards))}
    query_low, pack_share, *_ = lax.optimization_barrier(
        (query_low, pack_share, *kv_sums.values())
    )

    weights_away = swap_core(weights_send)
    weights_sent, weights_terms = sum_x(weights_keep, weights_away)
    query_turn = after(query_low, weights_sent)
    (query_back,) = call(
        functools.partial(query_back_kernel, shards, dp_count), spots,
        [query_turn, query_weight, *query_stacks], [((rows, width), F32)],
        scratch=[((dp_count, rows, quarter), BF16), ((shards, rows, weight_rows), F32)],
        name="query_back",
    )
    query_back, share_along = lax.optimization_barrier(
        (query_back, swap_plane(pack_share, 0, 1))
    )
    share_across = swap_plane(after(pack_share, weights_sent), 2, 0)
    span = kv_width + EXTRA_ROWS
    packed_shape = ((shards, span, weight_rows), BF16)
    home_all = far_grads[0]
    if ctx_count > 2:
        home_all = sum(grads.astype(F32) for grads in far_grads)
    input_grad, kv_keep, kv_send = call(
        functools.partial(end_kernel, shards), spots,
        [
            cosine, sine, normed_one, tokens, inverse_one, gains, query_back, residual_grad,
            key_turned, value_turned, second_gain_grad, near_grads[0], home_all,
            *[kv_arrived[r] for r in range(1, shards)], *kv_mine, *kv_other,
        ],
        [((rows, width), F32), packed_shape, packed_shape],
        scratch=[((shards, rows, weight_rows), F32)],
        name="keys_values_back",
    )
    kv_away = swap_core(kv_send)
    kv_keep, *weights_terms = lax.optimization_barrier((kv_keep, *weights_terms))
    weights_pieces = pieces_z(weights_terms)
    pieces = [
        (lax.dynamic_index_in_dim(kv_keep, shard ^ r, 0, keepdims=False).astype(F32)
         + lax.dynamic_index_in_dim(kv_away, shard ^ r, 0, keepdims=False).astype(F32)).astype(BF16)
        for r in range(shards)
    ]
    weights_pieces, *pieces = lax.optimization_barrier((weights_pieces, *pieces))
    share_across = lax.optimization_barrier((share_across, *pieces))[0]
    share_a = [pack_share, share_along, share_across, swap_plane(share_across, 0, 1)]
    share_b = [swap_core(piece) for piece in share_a]
    kv_share = sum_z(pieces)
    weights_half = halve_z(weights_pieces, shards // 2)
    share_by_mask = [None] * members
    for k, (a, b) in enumerate(((0, 0),) + CHIP_MASKS):
        share_by_mask[2 * a + b] = share_a[k]
        share_by_mask[2 * (a ^ 1) + b] = share_b[k]
    gate_weight_grad, up_weight_grad, down_weight_grad = call(
        functools.partial(spread_kernel, shards, members), spots, share_by_mask,
        [
            ((weight_rows, hidden), F32), ((weight_rows, hidden), F32),
            ((width, down_weight.shape[0]), F32),
        ],
        scratch=[((members, weight_rows, 3 * part), BF16)],
        name="feed_forward_out",
    )
    kv_share, weights_half = lax.optimization_barrier((kv_share, weights_half))
    kv_share, result_along, *big = lax.optimization_barrier(
        (sum_swap(kv_share, 2, 0), result_along, gate_weight_grad, up_weight_grad,
         down_weight_grad)
    )
    gate_weight_grad, up_weight_grad, down_weight_grad = big
    span = shards // 2
    while span > 1:
        span //= 2
        weights_half = halve_z(weights_half, span)
    weights_own = sum_y(weights_half[0].astype(BF16))
    result = residual + (result_own + result_along.astype(F32))
    output_weight_grad, query_weight_grad = finish_quarters(weights_own)
    low = sum_far(sum_swap(kv_share, 0, 1))
    away = swap_core(low)
    first = jnp.where(core == 0, low, away).astype(F32)
    second = jnp.where(core == 0, away, low).astype(F32)

    return (
        result[None],
        input_grad[None],
        first[kv_width],
        query_weight_grad,
        first[:kv_width].T,
        second[:kv_width].T,
        output_weight_grad,
        second[kv_width],
        gate_weight_grad,
        up_weight_grad,
        down_weight_grad.T,
    )


def solution(mesh):
    row = P("fsdp", None)
    token = P("dp", ("ctx", "fsdp"), None)
    return jax.shard_map(
        on_device,
        mesh=mesh,
        in_specs=(
            token, P("dp", None), P("fsdp"), row, row, row, row, P("fsdp"), row, row, row, token,
        ),
        out_specs=(
            token, token, P("fsdp"), row, row, row, row, P("fsdp"), row, row, row,
        ),
        check_vma=False,
    )
```

```python
import functools
import math

import jax
import jax.numpy as jnp
from jax import lax
from jax.experimental import pallas as pl
from jax.experimental.pallas import tpu as pltpu
from jax.sharding import PartitionSpec as P

HEADS = 15
KV_HEADS = 5
HEAD_DIM = 64
GROUPS = HEADS // KV_HEADS
LANES = 128

EPSILON = 1e-05
ROPE_BASE = 100000.0
MASKED = -1e30

F32 = jnp.float32
BF16 = jnp.bfloat16
VMEM_LIMIT = 56 * 1024 * 1024
FLOPS_PER_US = 1150 * 10**6
MEASURED_US = {
    "pack_weights": 4,
    "norm_keys_values": 4,
    "attention_near": 12,
    "attention_far": 12,
    "feed_forward": 8,
    "feed_forward_weights": 12,
    "residual_back": 6,
    "attention_back_far": 13,
    "attention_back_near": 14,
    "output_weight_grad": 3,
    "query_weight_grad": 0,
    "query_back": 0,
    "stack_quarters": 0,
    "quarter_columns": 0,
    "keys_values_back": 6,
    "feed_forward_out": 7,
}


def dot_plain(left, right):
    return jnp.dot(left, right, preferred_element_type=F32)


def dot_last(left, right):
    return lax.dot_general(left, right, (((1,), (1,)), ((), ())), preferred_element_type=F32)


def dot_first(left, right):
    return lax.dot_general(left, right, (((0,), (0,)), ((), ())), preferred_element_type=F32)


def swap(x, axis, mask):
    count = lax.axis_size(axis)
    return lax.ppermute(x, axis, [(i, i ^ mask) for i in range(count)])


def swap_plane(x, dp_mask, ctx_mask):
    ctx_count = lax.axis_size("ctx")
    pairs = []
    for d in range(lax.axis_size("dp")):
        for c in range(ctx_count):
            pairs.append((d * ctx_count + c, (d ^ dp_mask) * ctx_count + (c ^ ctx_mask)))
    return lax.ppermute(x, ("dp", "ctx"), pairs)


def swaps_fsdp(x):
    pieces = {0: x}
    for r in range(1, lax.axis_size("fsdp")):
        top = 1 << (r.bit_length() - 1)
        pieces[r] = swap(pieces[r - top], "fsdp", top)
    return [pieces[r] for r in range(1, lax.axis_size("fsdp"))]


def direct_fsdp(x):
    return [swap(x, "fsdp", r) for r in range(1, lax.axis_size("fsdp"))]


def swap_core(x):
    return swap_plane(x, 1, 0)


CHIP_MASKS = ((0, 1), (2, 0), (2, 1))


def plane_pieces(x):
    mine = [x] + [swap_plane(x, a, b) for a, b in CHIP_MASKS]
    return mine, [swap_core(piece) for piece in mine]


def sum_far(x):
    count = lax.axis_size("ctx")
    if count == 2:
        return x
    groups = [list(range(0, count, 2)), list(range(1, count, 2))]
    return lax.psum(x.astype(F32), "ctx", axis_index_groups=groups).astype(x.dtype)


def call(kernel, spots, args, out_shapes, scratch=(), name=None):
    specs = [pl.BlockSpec(memory_space=pltpu.SMEM)]
    specs += [pl.BlockSpec(memory_space=pltpu.VMEM) for _ in args]
    outs = tuple(jax.ShapeDtypeStruct(s, d) for s, d in out_shapes)
    return pl.pallas_call(
        kernel,
        out_shape=outs,
        in_specs=specs,
        out_specs=tuple(pl.BlockSpec(memory_space=pltpu.VMEM) for _ in outs),
        scratch_shapes=[pltpu.VMEM(s, d) for s, d in scratch],
        compiler_params=pltpu.CompilerParams(vmem_limit_bytes=VMEM_LIMIT),
        cost_estimate=pl.CostEstimate(
            flops=MEASURED_US.get(name, 2) * FLOPS_PER_US, bytes_accessed=0, transcendentals=0
        ),
        name=name,
    )(spots, *args)


def split_refs(refs, *counts):
    out, at = [], 0
    for n in counts:
        out.append(refs[at : at + n])
        at += n
    assert at == len(refs)
    return out


def lane_blocks(values, count):
    size = values.shape[1] // count
    return [values[:, i * size : (i + 1) * size] for i in range(count)]


def join_lanes(ref):
    return jnp.concatenate([ref[i] for i in range(ref.shape[0])], axis=1)


def rope_lanes(values, cosine, sine):
    rows, width = values.shape
    lane = lax.broadcasted_iota(jnp.int32, (rows, LANES), 1)
    first_half = (lane % HEAD_DIM) < (HEAD_DIM // 2)
    out = []
    for start in range(0, width, LANES):
        piece = values[:, start : min(start + LANES, width)]
        size = piece.shape[1]
        if size < LANES:
            piece = jnp.concatenate([piece, jnp.zeros((rows, LANES - size), piece.dtype)], axis=1)
        ahead = pltpu.roll(piece, LANES - HEAD_DIM // 2, 1)
        behind = pltpu.roll(piece, HEAD_DIM // 2, 1)
        partner = jnp.where(first_half, ahead, behind)
        out.append((piece * cosine + partner * sine)[:, :size])
    return jnp.concatenate(out, axis=1)


def heads_of(ref, first, count, rows=None):
    out = []
    for h in range(first, first + count):
        start = (h * HEAD_DIM) // LANES * LANES
        stop = min(start + LANES, ref.shape[-1])
        pair = ref[:, start:stop] if rows is None else ref[rows, start:stop]
        at = h * HEAD_DIM - start
        out.append(pair[:, at : at + HEAD_DIM])
    return out[0] if count == 1 else jnp.concatenate(out, axis=0)


def stack_rows(scratch, pieces):
    at = 0
    for piece in pieces:
        scratch[at : at + piece.shape[0], :] = piece[...]
        at += piece.shape[0]


def unstack_rows(out_ref, values):
    count, rows = out_ref.shape[:2]
    for i in range(count):
        out_ref[i] = values[i * rows : (i + 1) * rows, :].astype(out_ref.dtype)


def norm_rows(values, gain):
    inverse = lax.rsqrt(jnp.mean(values * values, axis=-1, keepdims=True) + EPSILON)
    return (values * inverse * gain, inverse)


def norm_back(gradient, values, inverse, gain):
    scaled = gradient * gain
    inner_mean = jnp.mean(scaled * values, axis=-1, keepdims=True)
    return inverse * scaled - values * (inverse * inverse * inverse) * inner_mean


EXTRA_ROWS = 16


def pack_kernel(shards, members, spots, gate_ref, up_ref, down_ref, out_ref):
    member = spots[3]
    span = gate_ref.shape[1] // shards
    piece = span // members
    rows = gate_ref.shape[0]
    pick = (
        lax.broadcasted_iota(jnp.int32, (span, piece), 0)
        == lax.broadcasted_iota(jnp.int32, (span, piece), 1) + member * piece
    ).astype(BF16)
    out = []
    for ref in (gate_ref, up_ref):
        for z in range(shards):
            out.append(dot_plain(ref[:, z * span : (z + 1) * span], pick))
    down = dot_plain(down_ref[...], pick)
    out += [down[b : b + rows, :] for b in range(0, down_ref.shape[0], rows)]
    out_ref[...] = jnp.concatenate(out, axis=1).astype(BF16)


def quarter_kernel(members, spots, query_ref, output_ref, *outs):
    size = query_ref.shape[1] // members
    for i in range(members):

        @pl.when(spots[2] == i)
        def _():
            for ref, out_ref in zip((query_ref, output_ref), outs):
                out_ref[...] = ref[:, i * size : (i + 1) * size]


def stack_kernel(spots, *refs):
    stack_rows(refs[-1], refs[:-1])


def begin_kernel(shards, spots, *refs):
    ins, outs, scratch = split_refs(refs, 7 + 2 * (shards - 1), 5, 3)
    tokens_ref, gain_one, gain_two, key_ref, value_ref, cos_ref, sin_ref = ins[:7]
    mine, other = split_refs(ins[7:], shards - 1, shards - 1)
    kv_ref, normed_ref, turned_ref, inverse_ref, gains_ref = outs
    blocks, normed_blocks, gain_blocks = scratch
    core, shard = spots[0], spots[1]
    width = key_ref.shape[0]
    values = tokens_ref[...].astype(F32)
    inverse = lax.rsqrt(jnp.mean(values * values, axis=-1, keepdims=True) + EPSILON)
    inverse_ref[...] = inverse
    for z, block in enumerate(lane_blocks(values * inverse, shards)):
        blocks[z] = block
    sums, order = [], []
    for r in range(shards):
        at = shard ^ r
        if r == 0:
            pair = jnp.concatenate([gain_one[...], gain_two[...]], axis=0).astype(F32)
        else:
            pair = mine[r - 1][width : width + EXTRA_ROWS, :].astype(F32)[0:2, :]
        gain_blocks[at, 0:2, :] = pair
        normed = (blocks[at] * pair[0:1, :]).astype(BF16)
        normed_blocks[at] = normed
        order.append(normed)
        left = key_ref[...] if r == 0 else mine[r - 1][:width, :]
        right = value_ref[...] if r == 0 else other[r - 1][:width, :]
        sums.append((dot_last(normed, left), dot_last(normed, right)))
    first = sum(s[0] for s in sums[1:])
    second = sum(s[1] for s in sums[1:])
    keys = jnp.where(core == 0, first, second) + sums[0][0]
    vals = jnp.where(core == 0, second, first) + sums[0][1]
    keys = rope_lanes(keys, cos_ref[...], sin_ref[...])
    kv_ref[...] = jnp.concatenate([keys, vals], axis=1).astype(BF16)
    normed_ref[...] = join_lanes(normed_blocks)
    turned_ref[...] = jnp.concatenate(order, axis=1)
    gains_ref[...] = jnp.zeros_like(gains_ref)
    gains_ref[0:2, :] = jnp.concatenate([gain_blocks[z][0:2, :] for z in range(shards)], axis=1)


def repeat(count, step, state):
    if count > 2:
        return lax.fori_loop(0, count, step, state)
    for j in range(count):
        state = step(j, state)
    return state


def rows_at(j, chunk):
    if isinstance(j, int):
        return slice(j * chunk, (j + 1) * chunk)
    return pl.ds(pl.multiple_of(j * chunk, chunk), chunk)


def attend(chunk, head, kv_ref, key_pos_ref, query_pos, stacked, state):
    def step(j, state):
        largest, total, weighted = state
        at = rows_at(j, chunk)
        keys = heads_of(kv_ref, head, 1, at)
        values = heads_of(kv_ref, KV_HEADS + head, 1, at)
        scores = dot_last(keys, stacked)
        scores = jnp.where(key_pos_ref[at, :] <= query_pos, scores, MASKED)
        new_largest = jnp.maximum(largest, jnp.max(scores, axis=0, keepdims=True))
        weights = jnp.exp(scores - new_largest)
        factor = jnp.exp(largest - new_largest)
        total = total * factor + jnp.sum(weights, axis=0, keepdims=True)
        weighted = weighted * factor + dot_first(values, weights.astype(BF16))
        return new_largest, total, weighted

    return repeat(kv_ref.shape[0] // chunk, step, state)


def near_kernel(chunk, members, pieces, spots, *refs):
    ins, outs, scratch = split_refs(refs, 6 + members + pieces, 4, 2)
    normed_ref, key_pos_ref, query_pos_ref, cos_ref, sin_ref, local_ref = ins[:6]
    weights, parts = split_refs(ins[6:], members, pieces)
    queries_ref, largest_ref, total_ref, weighted_ref = outs
    blocks, kv_ref = scratch
    dp = spots[2]
    stack_rows(kv_ref, parts)
    own = local_ref.shape[0]
    away = normed_ref[:, own:]
    for j in range(members):
        blocks[dp ^ j] = dot_plain(away, weights[j][...])
    raw = join_lanes(blocks) + dot_plain(normed_ref[:, :own], local_ref[...])
    roped = rope_lanes(raw, cos_ref[...], sin_ref[...]).astype(BF16)
    queries_ref[...] = roped * jnp.asarray(1.0 / math.sqrt(HEAD_DIM), BF16)
    columns = GROUPS * queries_ref.shape[0]
    query_pos = query_pos_ref[...]
    for head in range(KV_HEADS):
        stacked = heads_of(queries_ref, head * GROUPS, GROUPS)
        start = (
            jnp.full((1, columns), MASKED, F32),
            jnp.zeros((1, columns), F32),
            jnp.zeros((HEAD_DIM, columns), F32),
        )
        largest, total, weighted = attend(
            chunk, head, kv_ref, key_pos_ref, query_pos, stacked, start
        )
        largest_ref[head : head + 1, :] = largest
        total_ref[head : head + 1, :] = total
        weighted_ref[head] = weighted


def far_kernel(chunk, pieces, spots, *refs):
    ins, outs, (kv_ref,) = split_refs(refs, 6 + pieces, 3, 1)
    queries_ref, key_pos_ref, query_pos_ref, largest_ref, total_ref, weighted_ref = ins[:6]
    parts = ins[6:]
    attended_ref, turned_ref, log_ref = outs
    stack_rows(kv_ref, parts)
    rows = queries_ref.shape[0]
    query_pos = query_pos_ref[...]
    heads = []
    for head in range(KV_HEADS):
        stacked = heads_of(queries_ref, head * GROUPS, GROUPS)
        start = (largest_ref[head : head + 1, :], total_ref[head : head + 1, :], weighted_ref[head])
        largest, total, weighted = attend(
            chunk, head, kv_ref, key_pos_ref, query_pos, stacked, start
        )
        turned = weighted / total
        turned_ref[head] = turned
        log_ref[head : head + 1, :] = largest + jnp.log(total)
        straight = turned.T
        heads += [straight[g * rows : (g + 1) * rows, :] for g in range(GROUPS)]
    attended_ref[...] = jnp.concatenate(heads, axis=1).astype(BF16)


def project_kernel(shards, members, spots, *refs):
    ins, outs, (blocks, head_blocks) = split_refs(refs, 4 + members, 3, 2)
    attended_ref, tokens_ref, gains_ref, local_ref = ins[:4]
    weights = ins[4:]
    residual_ref, inverse_ref, normed_ref = outs
    shard, dp = spots[1], spots[2]
    for z, block in enumerate(lane_blocks(attended_ref[...], shards)):
        head_blocks[z] = block
    away = jnp.concatenate([head_blocks[shard ^ r] for r in range(1, shards)], axis=1)
    for j in range(members):
        blocks[dp ^ j] = dot_plain(away, weights[j][...])
    added = join_lanes(blocks) + dot_plain(head_blocks[shard], local_ref[...])
    residual = tokens_ref[...].astype(F32) + added
    residual_ref[...] = residual
    normed, inverse = norm_rows(residual, gains_ref[1:2, :])
    inverse_ref[...] = inverse
    normed_ref[...] = normed.astype(BF16)


def unfold_down(pack_ref, down_ref, shards, part):
    piece = part // shards
    rows = pack_ref.shape[0] // shards
    for b in range(down_ref.shape[0] // rows):
        at = 2 * part + b * piece
        down_ref[b * rows : (b + 1) * rows, :] = jnp.concatenate(
            [pack_ref[z * rows : (z + 1) * rows, at : at + piece] for z in range(shards)], axis=1
        )


def feed_kernel(shards, masks, spots, *refs):
    ins, outs, scratch = split_refs(refs, 2 + len(masks), 3, 3)
    pack_ref, cot_all, normed_parts = ins[0], ins[1], ins[2:]
    cot_parts = [cot_all[spots[3] ^ mask] for mask in masks]
    grad_ref, act_ref, both_ref = outs
    normed_ref, cot_ref, down_ref = scratch
    part = pack_ref.shape[1] // 3
    stack_rows(normed_ref, normed_parts)
    stack_rows(cot_ref, cot_parts)
    unfold_down(pack_ref, down_ref, shards, part)
    gate_up = dot_plain(normed_ref[...], pack_ref[:, : 2 * part])
    gate, upward = gate_up[:, :part], gate_up[:, part:]
    act_grad = dot_plain(cot_ref[...], down_ref[...])
    sigmoid_gate = jax.nn.sigmoid(gate)
    silu = gate * sigmoid_gate
    act_ref[...] = (silu * upward).astype(BF16)
    gate_grad = act_grad * upward * sigmoid_gate * (1.0 + gate * (1.0 - sigmoid_gate))
    both_ref[...] = jnp.concatenate([gate_grad, act_grad * silu], axis=1).astype(BF16)
    unstack_rows(grad_ref, dot_last(both_ref[...], pack_ref[:, : 2 * part]))


def feed_weights_kernel(shards, masks, spots, *refs):
    ins, outs, scratch = split_refs(refs, 6 + len(masks), 3, 5)
    pack_ref, act_a, act_b, both_a, both_b, cot_all = ins[:6]
    normed_parts = ins[6:]
    cot_parts = [cot_all[spots[3] ^ mask] for mask in masks]
    result_a, result_b, grad_ref = outs
    normed_ref, cot_ref, act_ref, both_ref, down_ref = scratch
    part = pack_ref.shape[1] // 3
    piece = part // shards
    rows = grad_ref.shape[0] // shards
    stack_rows(normed_ref, normed_parts)
    stack_rows(cot_ref, cot_parts)
    stack_rows(act_ref, (act_a, act_b))
    stack_rows(both_ref, (both_a, both_b))
    unfold_down(pack_ref, down_ref, shards, part)
    grad_ref[:, : 2 * part] = dot_first(normed_ref[...], both_ref[...]).astype(BF16)
    down_grad = dot_first(cot_ref[...], act_ref[...]).astype(BF16)
    folds = down_grad.shape[0] // rows
    for z in range(shards):
        at = z * piece
        grad_ref[z * rows : (z + 1) * rows, 2 * part :] = jnp.concatenate(
            [down_grad[b * rows : (b + 1) * rows, at : at + piece] for b in range(folds)], axis=1
        )
    unstack_rows(result_a, dot_last(act_a[...], down_ref[...]))
    unstack_rows(result_b, dot_last(act_b[...], down_ref[...]))


def middle_kernel(shards, members, spots, *refs):
    ins, outs, scratch = split_refs(refs, 10 + members, 4, 2)
    (own_a, own_b, one_ref, two_ref, three_ref, residual_ref, inverse_ref, cot_ref, gains_ref,
     local_ref) = ins[:10]
    weights = ins[10:]
    residual_grad_ref, low_ref, attended_grad_ref, gain_grad_ref = outs
    rows = cot_ref.shape[0]
    grad = (own_a[0].astype(F32) + own_b[0].astype(F32)) + one_ref[...].astype(F32)
    grad = grad + two_ref[...].astype(F32) + three_ref[...].astype(F32)
    residual, inverse = residual_ref[...], inverse_ref[...]
    gain_grad_ref[...] = jnp.sum(grad * residual * inverse, axis=0, keepdims=True)
    residual_grad = cot_ref[...].astype(F32) + norm_back(grad, residual, inverse, gains_ref[1:2, :])
    residual_grad_ref[...] = residual_grad
    low = residual_grad.astype(BF16)
    low_ref[...] = low
    attended_grad_ref[...] = back_through(
        shards, members, spots, low, weights, local_ref, scratch
    ).astype(BF16)


def back_through(shards, members, spots, low, weights, local_ref, scratch):
    blocks, out_blocks = scratch
    shard, dp = spots[1], spots[2]
    for i, block in enumerate(lane_blocks(low, members)):
        blocks[i] = block
    away = sum(dot_last(blocks[dp ^ j], weights[j][...]) for j in range(members))
    out_blocks[shard] = dot_last(low, local_ref[...])
    for r, block in enumerate(lane_blocks(away, shards - 1)):
        out_blocks[shard ^ (r + 1)] = block
    return join_lanes(out_blocks)


def weight_grad_kernel(members, spots, left_ref, low_ref, keep_ref, send_ref, blocks):
    dp = spots[2]
    for i, block in enumerate(lane_blocks(low_ref[...], members)):
        blocks[i] = block
    for j in (1, 3, 0, 2):
        out_ref = send_ref if j & 1 else keep_ref
        out_ref[j // 2] = dot_first(left_ref[...], blocks[dp ^ j]).astype(BF16)


def join_kernel(members, spots, own_ref, across_ref, core_ref, core_across_ref, *refs):
    outs, blocks = refs[:2], refs[2]
    dp = spots[2]
    for j, ref in enumerate((own_ref, core_ref, across_ref, core_across_ref)):
        blocks[dp ^ j] = ref[...]
    size = blocks.shape[-1] // 2
    for k, out_ref in enumerate(outs):
        out_ref[...] = jnp.concatenate(
            [blocks[i][:, k * size : (k + 1) * size] for i in range(members)], axis=1
        ).astype(F32)


def query_back_kernel(shards, members, spots, low_ref, local_ref, *refs):
    weights, (back_ref,), scratch = split_refs(refs, members, 1, 2)
    back_ref[...] = back_through(
        shards, members, spots, low_ref[...], weights, local_ref, scratch
    )


def back_kernel(chunk, pieces, first, last, spots, *refs):
    ins, outs, scratch = split_refs(refs, 9 + pieces, (pieces if last else 1) + 1, 2)
    (queries_ref, key_pos_ref, query_pos_ref, cos_ref, sin_ref, turned_ref, log_ref, grad_ref,
     start_ref) = ins[:9]
    parts = ins[9:]
    query_grad_ref, kv_grads = outs[0], outs[1:]
    kv_ref, kv_grad_ref = scratch
    stack_rows(kv_ref, parts)
    rows = queries_ref.shape[0]
    columns = GROUPS * rows
    query_pos = query_pos_ref[...]
    heads = []
    for head in range(KV_HEADS):
        stacked = heads_of(queries_ref, head * GROUPS, GROUPS)
        upstream = heads_of(grad_ref, head * GROUPS, GROUPS)
        delta = jnp.sum(upstream.astype(F32).T * turned_ref[head], axis=0, keepdims=True)
        log_total = log_ref[head : head + 1, :]
        keys_at = head * HEAD_DIM
        values_at = (KV_HEADS + head) * HEAD_DIM

        def step(j, query_grad, head=head, stacked=stacked, upstream=upstream,
                 delta=delta, log_total=log_total, keys_at=keys_at, values_at=values_at):
            at = rows_at(j, chunk)
            keys = heads_of(kv_ref, head, 1, at)
            values = heads_of(kv_ref, KV_HEADS + head, 1, at)
            scores = dot_last(keys, stacked)
            scores = jnp.where(key_pos_ref[at, :] <= query_pos, scores, MASKED)
            weights = jnp.exp(scores - log_total)
            weight_grad = dot_last(values, upstream)
            score_grad = (weights * (weight_grad - delta)).astype(BF16)
            value_grad = dot_plain(weights.astype(BF16), upstream)
            key_grad = dot_plain(score_grad, stacked)
            kv_grad_ref[at, keys_at : keys_at + HEAD_DIM] = key_grad.astype(BF16)
            kv_grad_ref[at, values_at : values_at + HEAD_DIM] = value_grad.astype(BF16)
            return query_grad + dot_first(keys, score_grad)

        start = jnp.zeros((HEAD_DIM, columns), F32) if first else start_ref[head]
        query_grad = repeat(kv_ref.shape[0] // chunk, step, start)
        if not last:
            query_grad_ref[head] = query_grad
        else:
            straight = query_grad.T * (1.0 / math.sqrt(HEAD_DIM))
            heads += [straight[g * rows : (g + 1) * rows, :] for g in range(GROUPS)]
    if last:
        query_grad_ref[...] = rope_lanes(
            jnp.concatenate(heads, axis=1), cos_ref[...], -sin_ref[...]
        ).astype(BF16)
    if last:
        for i in range(pieces):
            kv_grads[i][...] = kv_grad_ref[i * rows : (i + 1) * rows, :]
    else:
        unstack_rows(kv_grads[0], kv_grad_ref[...])


def end_kernel(shards, spots, *refs):
    ins, outs, scratch = split_refs(refs, 11 + (shards + 1) + 2 * (shards - 1), 3, 1)
    (cos_ref, sin_ref, normed_ref, tokens_ref, inverse_ref, gains_ref, back_ref, residual_grad_ref,
     key_ref, value_ref, gain_two_ref) = ins[:11]
    sums, mine, other = split_refs(ins[11:], shards + 1, shards - 1, shards - 1)
    input_grad_ref, keep_ref, send_ref = outs
    (blocks,) = scratch
    core, shard = spots[0], spots[1]
    width, span = key_ref.shape
    rows = tokens_ref.shape[0]
    total = sums[0][...].astype(F32) + sums[1][0].astype(F32)
    total = total + sum(s[...].astype(F32) for s in sums[2:])
    keys = rope_lanes(total[:, :width], cos_ref[...], -sin_ref[...])
    values = total[:, width:]
    keep = jnp.where(core == 0, keys, values).astype(BF16)
    send = jnp.where(core == 0, values, keys).astype(BF16)
    blocks[shard] = dot_plain(keys.astype(BF16), key_ref[...]) + dot_plain(
        values.astype(BF16), value_ref[...]
    )
    for r in range(1, shards):
        blocks[shard ^ r] = dot_plain(keep, mine[r - 1][:width, :]) + dot_plain(
            send, other[r - 1][:width, :]
        )
    normed_grad = back_ref[...] + join_lanes(blocks)
    inputs, inverse = tokens_ref[...].astype(F32), inverse_ref[...]
    gain_grad = jnp.sum(normed_grad * inputs * inverse, axis=0, keepdims=True)
    input_grad_ref[...] = residual_grad_ref[...] + norm_back(
        normed_grad, inputs, inverse, gains_ref[0:1, :]
    )
    normed = normed_ref[...]
    two = gain_two_ref[...]
    for out_ref, low, gain in (
        (send_ref, send, jnp.where(core == 0, two, gain_grad)),
        (keep_ref, keep, jnp.where(core == 0, gain_grad, two)),
    ):
        grad = dot_first(low, normed).astype(BF16)
        gains = lane_blocks(gain, shards)
        for z, block in enumerate(lane_blocks(grad, shards)):
            out_ref[z, :width, :] = block
            out_ref[z, width:, :] = jnp.broadcast_to(
                gains[z], (EXTRA_ROWS, span)
            ).astype(BF16)


def spread_kernel(shards, members, spots, *refs):
    parts, outs, (blocks,) = split_refs(refs, members, 3, 1)
    gate_ref, up_ref, down_ref = outs
    member = spots[3]
    piece = parts[0].shape[1] // 3 // shards
    rows = parts[0].shape[0]
    span = piece * members
    for i in range(members):
        blocks[member ^ i] = parts[i][...]

    def block(k):
        at = k * piece
        return jnp.concatenate(
            [blocks[p, :, at : at + piece] for p in range(members)], axis=1
        ).astype(F32)

    for z in range(shards):
        gate_ref[:, z * span : (z + 1) * span] = block(z)
        up_ref[:, z * span : (z + 1) * span] = block(shards + z)
    for b in range(down_ref.shape[0] // rows):
        down_ref[b * rows : (b + 1) * rows, :] = block(2 * shards + b)


def base_of(block_order, stored, block_length):
    which = stored // block_length
    count = block_order.shape[1]
    matches = (which[:, None] == jnp.arange(count, dtype=jnp.int32)[None, :]).astype(jnp.int32)
    return jnp.sum(block_order[0][None, :] * matches, axis=-1) * block_length + stored % block_length


def tables(positions):
    half_dim = HEAD_DIM // 2
    exponent = -(jnp.arange(half_dim, dtype=F32) * 2.0) / HEAD_DIM
    frequency = jnp.power(F32(ROPE_BASE), exponent)
    angles = positions.astype(F32)[:, None] * frequency
    cosine, sine = jnp.cos(angles), jnp.sin(angles)
    return (
        jnp.concatenate([cosine] * 4, axis=-1),
        jnp.concatenate([-sine, sine, -sine, sine], axis=-1),
    )


def after(x, other):
    return lax.optimization_barrier((x, other))[0]


def on_device(
    tokens,
    block_order,
    attention_gain,
    query_weight,
    key_weight,
    value_weight,
    output_weight,
    feedforward_gain,
    gate_weight,
    up_weight,
    down_weight,
    cotangent,
):
    tokens, cotangent = tokens[0], cotangent[0]
    rows, width = tokens.shape
    shards = lax.axis_size("fsdp")
    ctx_count = lax.axis_size("ctx")
    dp_count = lax.axis_size("dp")
    block_length = rows * shards * ctx_count // block_order.shape[1]
    shard = lax.axis_index("fsdp")
    ctx = lax.axis_index("ctx")
    dp = lax.axis_index("dp")
    core = dp & 1
    members = dp_count * 2
    weight_rows = query_weight.shape[0]
    query_width = HEADS * HEAD_DIM
    kv_width = KV_HEADS * HEAD_DIM
    hidden = gate_weight.shape[1]
    part = hidden // members
    spots = jnp.stack([core, shard, dp, dp * 2 + (ctx & 1)]).astype(jnp.int32)

    gain_one, gain_two = attention_gain[None, :], feedforward_gain[None, :]
    key_turned, value_turned, down_turned = key_weight.T, value_weight.T, down_weight.T
    kv_pack = jnp.concatenate(
        [
            jnp.where(core == 0, key_turned, value_turned),
            jnp.pad(
                jnp.concatenate([gain_one, gain_two], axis=0), ((0, EXTRA_ROWS - 2), (0, 0))
            ),
        ],
        axis=0,
    )
    kv_mine = direct_fsdp(kv_pack)

    quarter = width // dp_count
    query_quarter, output_quarter = call(
        functools.partial(quarter_kernel, dp_count), spots,
        [after(query_weight, kv_pack), output_weight],
        [((weight_rows, quarter), BF16)] * 2, name="quarter_columns",
    )
    query_pieces = direct_fsdp(query_quarter)
    kv_other = [swap_core(piece) for piece in kv_mine]

    def stack(pieces):
        (stacked,) = call(
            stack_kernel, spots, pieces, [(((shards - 1) * weight_rows, quarter), BF16)],
            name="stack_quarters",
        )
        return stacked, swap_plane(stacked, 2, 0)

    def four(stacked, across):
        return [stacked, swap_core(stacked), across, swap_core(across)]

    group_axes = ("dp", "ctx")
    extra = {}
    if ctx_count > 2:
        extra["axis_index_groups"] = [
            [d * ctx_count + c for d in range(dp_count) for c in (first, first + 1)]
            for first in range(0, ctx_count, 2)
        ]
    cot_all = lax.all_gather(cotangent, group_axes, axis=0, tiled=False, **extra)

    offsets = jnp.arange(rows, dtype=jnp.int32)
    my_start = (ctx * shards + shard) * rows
    positions = base_of(block_order, my_start[None], block_length) + offsets
    cosine, sine = tables(positions)
    query_pos = jnp.concatenate([positions] * GROUPS)[None, :]
    starts = jnp.stack(
        [((ctx ^ d) * shards + (shard ^ r)) * rows for d in range(ctx_count) for r in range(shards)]
    )
    key_pos = (base_of(block_order, starts, block_length)[:, None] + offsets[None, :]).reshape(-1, 1)
    near_count = shards * rows
    near_pos, far_pos = key_pos[:near_count], key_pos[near_count:]
    far_count = far_pos.shape[0]

    (pack,) = call(
        functools.partial(pack_kernel, shards, members), spots,
        [gate_weight, up_weight, down_turned], [((weight_rows, 3 * part), BF16)],
        name="pack_weights",
    )
    kv_own, normed_one, normed_turned, inverse_one, gains = call(
        functools.partial(begin_kernel, shards), spots,
        [
            lax.optimization_barrier((tokens, query_quarter, pack))[0], gain_one, gain_two, key_turned, value_turned, cosine, sine,
            *kv_mine, *kv_other,
        ],
        [
            ((rows, 2 * kv_width), BF16), ((rows, width), BF16), ((rows, width), BF16),
            ((rows, 1), F32), ((8, width), F32),
        ],
        scratch=[
            ((shards, rows, weight_rows), F32), ((shards, rows, weight_rows), BF16),
            ((shards, 8, weight_rows), F32),
        ],
        name="norm_keys_values",
    )
    near = [kv_own] + direct_fsdp(kv_own)
    query_pieces = lax.optimization_barrier((kv_own, *query_pieces))[1:]
    stacked, across = stack(query_pieces)
    across, *near = lax.optimization_barrier((across, *near))
    query_stacks = four(stacked, across)
    (near_all,) = call(
        stack_kernel, spots, near, [((near_count, 2 * kv_width), BF16)],
        name="stack_keys_values",
    )
    far = [swap(near_all, "ctx", d) for d in range(1, ctx_count)]
    output_pieces = direct_fsdp(after(output_quarter, near_all))

    pack, cot_all, _ = lax.optimization_barrier((pack, cot_all, near[-1]))
    pack_all = lax.all_gather(pack, "fsdp", axis=0, tiled=True)


    chunk = rows * 2
    unit = 2 * HEADS * rows * near_count * HEAD_DIM
    stat = ((KV_HEADS, GROUPS * rows), F32)
    turned_shape = ((KV_HEADS, HEAD_DIM, GROUPS * rows), F32)
    queries, largest, total, weighted = call(
        functools.partial(near_kernel, chunk, dp_count, shards), spots,
        [normed_turned, near_pos, query_pos, cosine, sine, query_weight, *query_stacks, *near],
        [((rows, query_width), BF16), stat, stat, turned_shape],
        scratch=[((dp_count, rows, quarter), F32), ((near_count, 2 * kv_width), BF16)],
        name="attention_near",
    )
    attended, turned, log_total = call(
        functools.partial(far_kernel, chunk, len(far)), spots,
        [queries, far_pos, query_pos, largest, total, weighted, *far],
        [((rows, query_width), BF16), turned_shape, stat],
        scratch=[((far_count, 2 * kv_width), BF16)], name="attention_far",
    )
    output_pieces = lax.optimization_barrier((queries, *output_pieces))[1:]
    output_stacked, output_across = stack(output_pieces)
    attended, output_across = lax.optimization_barrier((attended, output_across))
    output_stacks = four(output_stacked, output_across)
    residual, inverse_two, normed_two = call(
        functools.partial(project_kernel, shards, dp_count), spots,
        [attended, tokens, gains, output_weight, *output_stacks],
        [((rows, width), F32), ((rows, 1), F32), ((rows, width), BF16)],
        scratch=[((dp_count, rows, quarter), F32), ((shards, rows, weight_rows), BF16)],
        name="project_residual",
    )

    normed_a, normed_b = plane_pieces(normed_two)
    token_shape = ((rows, width), BF16)
    half = 4 * rows
    half_shape = ((4, rows, width), BF16)

    masks = [2 * a + b for a, b in ((0, 0),) + CHIP_MASKS]
    core_masks = [mask ^ 2 for mask in masks]

    def feed(normed, masks):
        return call(
            functools.partial(feed_kernel, shards, masks), spots, [pack_all, cot_all, *normed],
            [half_shape, ((half, part), BF16), ((half, 2 * part), BF16)],
            scratch=[((half, width), BF16), ((half, width), BF16), ((width, part), BF16)],
        name="feed_forward",
        )

    grad_b, act_b, both_b = feed(normed_b, core_masks)
    from_core = swap_core(grad_b)
    grad_a, act_a, both_a = feed(normed_a, masks)

    def chip_sums(parts_a, parts_b):
        return [
            (parts_a[k].astype(F32) + parts_b[k].astype(F32)).astype(BF16)
            for k in range(1, 4)
        ]

    def send_chips(sums):
        return [swap_plane(x, a, b) for x, (a, b) in zip(sums, CHIP_MASKS)]

    grad_sums = chip_sums(grad_a, from_core)
    grad_chips = send_chips(grad_sums)
    act_a, *_ = lax.optimization_barrier((act_a, *grad_sums))
    result_a, result_b, pack_grad = call(
        functools.partial(feed_weights_kernel, shards, masks + core_masks), spots,
        [pack_all, act_a, act_b, both_a, both_b, cot_all, *normed_a, *normed_b],
        [half_shape, half_shape, ((width, 3 * part), BF16)],
        scratch=[
            ((2 * half, width), BF16), ((2 * half, width), BF16), ((2 * half, part), BF16),
            ((2 * half, 2 * part), BF16), ((width, part), BF16),
        ],
        name="feed_forward_weights",
    )
    pack_share = sum_far(lax.psum_scatter(pack_grad, "fsdp", scatter_dimension=0, tiled=True))

    pack_grad, result_b, *grad_chips = lax.optimization_barrier(
        (pack_grad, result_b, *grad_chips)
    )
    residual_grad, residual_low, attended_grad, second_gain_grad = call(
        functools.partial(middle_kernel, shards, dp_count), spots,
        [
            grad_a, from_core, *grad_chips, residual, inverse_two, cotangent, gains, output_weight,
            *output_stacks,
        ],
        [((rows, width), F32), token_shape, ((rows, query_width), BF16), ((1, width), F32)],
        scratch=[((dp_count, rows, quarter), BF16), ((shards, rows, weight_rows), F32)],
        name="residual_back",
    )

    result_core = swap_core(result_b)
    result_sent = (result_a[2:].astype(F32) + result_core[2:].astype(F32)).astype(BF16)

    def weight_grad(left, low, name):
        pair = ((2, width, quarter), BF16)
        return call(
            functools.partial(weight_grad_kernel, dp_count), spots, [left, low], [pair, pair],
            scratch=[((dp_count, rows, quarter), BF16)], name=name,
        )

    output_keep, output_send = weight_grad(attended, residual_low, "output_weight_grad")
    attended_grad, result_sent, output_send = lax.optimization_barrier(
        (attended_grad, result_sent, output_send)
    )

    def sum_x(keep, away):
        sent = (keep[1].astype(F32) + away[1].astype(F32)).astype(BF16)
        return sent, (keep[0], away[0], swap_plane(sent, 2, 0))

    def pieces_z(terms):
        out = []
        for r in range(shards):
            at = (shard ^ r) * weight_rows
            parts = [
                lax.dynamic_slice_in_dim(x, at, weight_rows, 0).astype(F32) for x in terms
            ]
            out.append((parts[0] + parts[1] + parts[2]).astype(BF16))
        return out

    def sum_z(pieces):
        arrived = {r: swap(pieces[r], "fsdp", r) for r in reversed(range(1, shards))}
        return sum(
            (arrived[r].astype(F32) for r in range(1, shards)), pieces[0].astype(F32)
        ).astype(BF16)

    def halve_z(pieces, span):
        sent = jnp.stack([piece.astype(BF16) for piece in pieces[span:]])
        arrived = swap(sent, "fsdp", span)
        return [pieces[r].astype(F32) + arrived[r].astype(F32) for r in range(span)]

    def sum_swap(own, dp_mask, ctx_mask):
        return (own.astype(F32) + swap_plane(own, dp_mask, ctx_mask).astype(F32)).astype(BF16)

    def sum_y(own):
        return sum_far(sum_swap(own, 0, 1))

    def finish_quarters(own):
        across = swap_plane(own, 2, 0)
        return call(
            functools.partial(join_kernel, dp_count), spots,
            [own, across, swap_core(own), swap_core(across)],
            [((weight_rows, width), F32)] * 2,
            scratch=[((dp_count, weight_rows, 2 * quarter), BF16)], name="join_columns",
        )

    def back(first, last, start, pos, pieces):
        count = pos.shape[0]
        shape = ((rows, query_width), BF16) if last else turned_shape
        out = call(
            functools.partial(back_kernel, chunk, len(pieces), first, last), spots,
            [
                queries, pos, query_pos, cosine, sine, turned, log_total, attended_grad, start,
                *pieces,
            ],
            [shape]
            + (
                [((rows, 2 * kv_width), BF16)] * len(pieces) if last
                else [((shards, rows, 2 * kv_width), BF16)]
            ),
            scratch=[((count, 2 * kv_width), BF16), ((count, 2 * kv_width), BF16)],
            name="attention_back_near" if last else "attention_back_far",
        )
        return out[0], out[1:]

    query_partial, far_grads = turned, []
    for d in range(1, ctx_count):
        at = (d - 1) * near_count
        query_partial, grads = back(
            d == 1, False, query_partial, far_pos[at : at + near_count], far[d - 1 : d]
        )
        far_grads.append(swap(grads[0], "ctx", d))
    output_sent, output_terms = sum_x(output_keep, swap_core(output_send))
    query_partial = after(query_partial, output_sent)
    result_across = swap_plane(result_sent, 2, 0)
    query_low, near_grads = back(False, True, query_partial, near_pos, near)
    query_low, result_across, *output_terms = lax.optimization_barrier(
        (query_low, result_across, *output_terms)
    )
    output_half_pieces = pieces_z(output_terms)
    query_low, *output_half_pieces = lax.optimization_barrier((query_low, *output_half_pieces))
    output_half = halve_z(output_half_pieces, shards // 2)
    weights_keep, weights_send = weight_grad(normed_one, query_low, "query_weight_grad")
    weights_send, pack_share, far_grads[-1], *output_half = lax.optimization_barrier(
        (weights_send, pack_share, far_grads[-1], *output_half)
    )
    def home(r):
        return sum(grads[r].astype(F32) for grads in far_grads)

    kv_sums = {
        r: (near_grads[r].astype(F32) + home(r)).astype(BF16) for r in range(1, shards)
    }
    kv_arrived = {r: swap(kv_sums[r], "fsdp", r) for r in reversed(range(1, shards))}
    query_low, weights_away, *_ = lax.optimization_barrier(
        (query_low, swap_core(weights_send), *kv_sums.values())
    )

    weights_sent, weights_terms = sum_x(weights_keep, weights_away)
    query_turn = after(query_low, weights_sent)
    (query_back,) = call(
        functools.partial(query_back_kernel, shards, dp_count), spots,
        [query_turn, query_weight, *query_stacks], [((rows, width), F32)],
        scratch=[((dp_count, rows, quarter), BF16), ((shards, rows, weight_rows), F32)],
        name="query_back",
    )
    weights_pieces = pieces_z(weights_terms)
    query_back, share_along, result_across, *weights_pieces = lax.optimization_barrier(
        (query_back, swap_plane(pack_share, 0, 1), result_across, *weights_pieces)
    )
    result_own, result_along = [
        (result_a[k].astype(F32) + result_core[k].astype(F32)) + result_across[k].astype(F32)
        for k in (0, 1)
    ]
    result_along = swap_plane(result_along.astype(BF16), 0, 1)
    share_across = swap_plane(after(pack_share, weights_sent), 2, 0)
    span = kv_width + EXTRA_ROWS
    packed_shape = ((shards, span, weight_rows), BF16)
    home_all = far_grads[0]
    if ctx_count > 2:
        home_all = sum(grads.astype(F32) for grads in far_grads)
    input_grad, kv_keep, kv_send = call(
        functools.partial(end_kernel, shards), spots,
        [
            cosine, sine, normed_one, tokens, inverse_one, gains, query_back, residual_grad,
            key_turned, value_turned, second_gain_grad, near_grads[0], home_all,
            *[kv_arrived[r] for r in range(1, shards)], *kv_mine, *kv_other,
        ],
        [((rows, width), F32), packed_shape, packed_shape],
        scratch=[((shards, rows, weight_rows), F32)],
        name="keys_values_back",
    )
    kv_away = swap_core(kv_send)
    pieces = [
        (lax.dynamic_index_in_dim(kv_keep, shard ^ r, 0, keepdims=False).astype(F32)
         + lax.dynamic_index_in_dim(kv_away, shard ^ r, 0, keepdims=False).astype(F32)).astype(BF16)
        for r in range(shards)
    ]
    share_across = lax.optimization_barrier((share_across, *pieces))[0]
    share_a = [pack_share, share_along, share_across, swap_plane(share_across, 0, 1)]
    share_b = [swap_core(piece) for piece in share_a]
    kv_share = sum_z(pieces)
    weights_half = [
        jnp.concatenate([left, right], axis=1)
        for left, right in zip(output_half, halve_z(weights_pieces, shards // 2))
    ]
    share_by_mask = [None] * members
    for k, (a, b) in enumerate(((0, 0),) + CHIP_MASKS):
        share_by_mask[2 * a + b] = share_a[k]
        share_by_mask[2 * (a ^ 1) + b] = share_b[k]
    gate_weight_grad, up_weight_grad, down_weight_grad = call(
        functools.partial(spread_kernel, shards, members), spots, share_by_mask,
        [
            ((weight_rows, hidden), F32), ((weight_rows, hidden), F32),
            ((width, down_weight.shape[0]), F32),
        ],
        scratch=[((members, weight_rows, 3 * part), BF16)],
        name="feed_forward_out",
    )
    kv_share, weights_half = lax.optimization_barrier((kv_share, weights_half))
    kv_share, result_along = lax.optimization_barrier((sum_swap(kv_share, 2, 0), result_along))
    span = shards // 2
    while span > 1:
        span //= 2
        weights_half = halve_z(weights_half, span)
    weights_own, *big = lax.optimization_barrier(
        (sum_y(weights_half[0].astype(BF16)), gate_weight_grad, up_weight_grad, down_weight_grad)
    )
    gate_weight_grad, up_weight_grad, down_weight_grad = big
    result = residual + (result_own + result_along.astype(F32))
    output_weight_grad, query_weight_grad = finish_quarters(weights_own)
    low = sum_far(sum_swap(kv_share, 0, 1))
    away = swap_core(low)
    first = jnp.where(core == 0, low, away).astype(F32)
    second = jnp.where(core == 0, away, low).astype(F32)

    return (
        result[None],
        input_grad[None],
        first[kv_width],
        query_weight_grad,
        first[:kv_width].T,
        second[:kv_width].T,
        output_weight_grad,
        second[kv_width],
        gate_weight_grad,
        up_weight_grad,
        down_weight_grad.T,
    )


def solution(mesh):
    row = P("fsdp", None)
    token = P("dp", ("ctx", "fsdp"), None)
    return jax.shard_map(
        on_device,
        mesh=mesh,
        in_specs=(
            token, P("dp", None), P("fsdp"), row, row, row, row, P("fsdp"), row, row, row, token,
        ),
        out_specs=(
            token, token, P("fsdp"), row, row, row, row, P("fsdp"), row, row, row,
        ),
        check_vma=False,
    )
```

```python
import functools
import math

import jax
import jax.numpy as jnp
from jax import lax
from jax.experimental import pallas as pl
from jax.experimental.pallas import tpu as pltpu
from jax.sharding import PartitionSpec as P

HEADS = 15
KV_HEADS = 5
HEAD_DIM = 64
GROUPS = HEADS // KV_HEADS
LANES = 128

EPSILON = 1e-05
ROPE_BASE = 100000.0
MASKED = -1e30

F32 = jnp.float32
BF16 = jnp.bfloat16
VMEM_LIMIT = 56 * 1024 * 1024
FLOPS_PER_US = 1150 * 10**6
MEASURED_US = {
    "pack_weights": 4,
    "norm_keys_values": 4,
    "attention_near": 12,
    "attention_far": 12,
    "feed_forward": 8,
    "feed_forward_weights": 12,
    "residual_back": 6,
    "attention_back_far": 13,
    "attention_back_near": 14,
    "query_output_weight_grads": 0,
    "query_back": 0,
    "stack_quarters": 0,
    "quarter_columns": 0,
    "keys_values_back": 6,
    "feed_forward_out": 7,
}


def dot_plain(left, right):
    return jnp.dot(left, right, preferred_element_type=F32)


def dot_last(left, right):
    return lax.dot_general(left, right, (((1,), (1,)), ((), ())), preferred_element_type=F32)


def dot_first(left, right):
    return lax.dot_general(left, right, (((0,), (0,)), ((), ())), preferred_element_type=F32)


def swap(x, axis, mask):
    count = lax.axis_size(axis)
    return lax.ppermute(x, axis, [(i, i ^ mask) for i in range(count)])


def swap_plane(x, dp_mask, ctx_mask):
    ctx_count = lax.axis_size("ctx")
    pairs = []
    for d in range(lax.axis_size("dp")):
        for c in range(ctx_count):
            pairs.append((d * ctx_count + c, (d ^ dp_mask) * ctx_count + (c ^ ctx_mask)))
    return lax.ppermute(x, ("dp", "ctx"), pairs)


def swaps_fsdp(x):
    pieces = {0: x}
    for r in range(1, lax.axis_size("fsdp")):
        top = 1 << (r.bit_length() - 1)
        pieces[r] = swap(pieces[r - top], "fsdp", top)
    return [pieces[r] for r in range(1, lax.axis_size("fsdp"))]


def direct_fsdp(x):
    return [swap(x, "fsdp", r) for r in range(1, lax.axis_size("fsdp"))]


def swap_core(x):
    return swap_plane(x, 1, 0)


CHIP_MASKS = ((0, 1), (2, 0), (2, 1))


def plane_pieces(x):
    mine = [x] + [swap_plane(x, a, b) for a, b in CHIP_MASKS]
    return mine, [swap_core(piece) for piece in mine]


def sum_far(x):
    count = lax.axis_size("ctx")
    if count == 2:
        return x
    groups = [list(range(0, count, 2)), list(range(1, count, 2))]
    return lax.psum(x.astype(F32), "ctx", axis_index_groups=groups).astype(x.dtype)


def call(kernel, spots, args, out_shapes, scratch=(), name=None):
    specs = [pl.BlockSpec(memory_space=pltpu.SMEM)]
    specs += [pl.BlockSpec(memory_space=pltpu.VMEM) for _ in args]
    outs = tuple(jax.ShapeDtypeStruct(s, d) for s, d in out_shapes)
    return pl.pallas_call(
        kernel,
        out_shape=outs,
        in_specs=specs,
        out_specs=tuple(pl.BlockSpec(memory_space=pltpu.VMEM) for _ in outs),
        scratch_shapes=[pltpu.VMEM(s, d) for s, d in scratch],
        compiler_params=pltpu.CompilerParams(vmem_limit_bytes=VMEM_LIMIT),
        cost_estimate=pl.CostEstimate(
            flops=MEASURED_US.get(name, 2) * FLOPS_PER_US, bytes_accessed=0, transcendentals=0
        ),
        name=name,
    )(spots, *args)


def split_refs(refs, *counts):
    out, at = [], 0
    for n in counts:
        out.append(refs[at : at + n])
        at += n
    assert at == len(refs)
    return out


def lane_blocks(values, count):
    size = values.shape[1] // count
    return [values[:, i * size : (i + 1) * size] for i in range(count)]


def join_lanes(ref):
    return jnp.concatenate([ref[i] for i in range(ref.shape[0])], axis=1)


def rope_lanes(values, cosine, sine):
    rows, width = values.shape
    lane = lax.broadcasted_iota(jnp.int32, (rows, LANES), 1)
    first_half = (lane % HEAD_DIM) < (HEAD_DIM // 2)
    out = []
    for start in range(0, width, LANES):
        piece = values[:, start : min(start + LANES, width)]
        size = piece.shape[1]
        if size < LANES:
            piece = jnp.concatenate([piece, jnp.zeros((rows, LANES - size), piece.dtype)], axis=1)
        ahead = pltpu.roll(piece, LANES - HEAD_DIM // 2, 1)
        behind = pltpu.roll(piece, HEAD_DIM // 2, 1)
        partner = jnp.where(first_half, ahead, behind)
        out.append((piece * cosine + partner * sine)[:, :size])
    return jnp.concatenate(out, axis=1)


def heads_of(ref, first, count, rows=None):
    out = []
    for h in range(first, first + count):
        start = (h * HEAD_DIM) // LANES * LANES
        stop = min(start + LANES, ref.shape[-1])
        pair = ref[:, start:stop] if rows is None else ref[rows, start:stop]
        at = h * HEAD_DIM - start
        out.append(pair[:, at : at + HEAD_DIM])
    return out[0] if count == 1 else jnp.concatenate(out, axis=0)


def stack_rows(scratch, pieces):
    at = 0
    for piece in pieces:
        scratch[at : at + piece.shape[0], :] = piece[...]
        at += piece.shape[0]


def unstack_rows(out_ref, values):
    count, rows = out_ref.shape[:2]
    for i in range(count):
        out_ref[i] = values[i * rows : (i + 1) * rows, :].astype(out_ref.dtype)


def norm_rows(values, gain):
    inverse = lax.rsqrt(jnp.mean(values * values, axis=-1, keepdims=True) + EPSILON)
    return (values * inverse * gain, inverse)


def norm_back(gradient, values, inverse, gain):
    scaled = gradient * gain
    inner_mean = jnp.mean(scaled * values, axis=-1, keepdims=True)
    return inverse * scaled - values * (inverse * inverse * inverse) * inner_mean


EXTRA_ROWS = 16


def pack_kernel(shards, members, spots, gate_ref, up_ref, down_ref, out_ref):
    member = spots[3]
    span = gate_ref.shape[1] // shards
    piece = span // members
    rows = gate_ref.shape[0]
    pick = (
        lax.broadcasted_iota(jnp.int32, (span, piece), 0)
        == lax.broadcasted_iota(jnp.int32, (span, piece), 1) + member * piece
    ).astype(BF16)
    out = []
    for ref in (gate_ref, up_ref):
        for z in range(shards):
            out.append(dot_plain(ref[:, z * span : (z + 1) * span], pick))
    down = dot_plain(down_ref[...], pick)
    out += [down[b : b + rows, :] for b in range(0, down_ref.shape[0], rows)]
    out_ref[...] = jnp.concatenate(out, axis=1).astype(BF16)


def quarter_kernel(members, spots, query_ref, output_ref, *outs):
    size = query_ref.shape[1] // members
    for i in range(members):

        @pl.when(spots[2] == i)
        def _():
            for ref, out_ref in zip((query_ref, output_ref), outs):
                out_ref[...] = ref[:, i * size : (i + 1) * size]


def stack_kernel(spots, *refs):
    stack_rows(refs[-1], refs[:-1])


def begin_kernel(shards, spots, *refs):
    ins, outs, scratch = split_refs(refs, 7 + 2 * (shards - 1), 5, 3)
    tokens_ref, gain_one, gain_two, key_ref, value_ref, cos_ref, sin_ref = ins[:7]
    mine, other = split_refs(ins[7:], shards - 1, shards - 1)
    kv_ref, normed_ref, turned_ref, inverse_ref, gains_ref = outs
    blocks, normed_blocks, gain_blocks = scratch
    core, shard = spots[0], spots[1]
    width = key_ref.shape[0]
    values = tokens_ref[...].astype(F32)
    inverse = lax.rsqrt(jnp.mean(values * values, axis=-1, keepdims=True) + EPSILON)
    inverse_ref[...] = inverse
    for z, block in enumerate(lane_blocks(values * inverse, shards)):
        blocks[z] = block
    sums, order = [], []
    for r in range(shards):
        at = shard ^ r
        if r == 0:
            pair = jnp.concatenate([gain_one[...], gain_two[...]], axis=0).astype(F32)
        else:
            pair = mine[r - 1][width : width + EXTRA_ROWS, :].astype(F32)[0:2, :]
        gain_blocks[at, 0:2, :] = pair
        normed = (blocks[at] * pair[0:1, :]).astype(BF16)
        normed_blocks[at] = normed
        order.append(normed)
        left = key_ref[...] if r == 0 else mine[r - 1][:width, :]
        right = value_ref[...] if r == 0 else other[r - 1][:width, :]
        sums.append((dot_last(normed, left), dot_last(normed, right)))
    first = sum(s[0] for s in sums[1:])
    second = sum(s[1] for s in sums[1:])
    keys = jnp.where(core == 0, first, second) + sums[0][0]
    vals = jnp.where(core == 0, second, first) + sums[0][1]
    keys = rope_lanes(keys, cos_ref[...], sin_ref[...])
    kv_ref[...] = jnp.concatenate([keys, vals], axis=1).astype(BF16)
    normed_ref[...] = join_lanes(normed_blocks)
    turned_ref[...] = jnp.concatenate(order, axis=1)
    gains_ref[...] = jnp.zeros_like(gains_ref)
    gains_ref[0:2, :] = jnp.concatenate([gain_blocks[z][0:2, :] for z in range(shards)], axis=1)


def repeat(count, step, state):
    if count > 2:
        return lax.fori_loop(0, count, step, state)
    for j in range(count):
        state = step(j, state)
    return state


def rows_at(j, chunk):
    if isinstance(j, int):
        return slice(j * chunk, (j + 1) * chunk)
    return pl.ds(pl.multiple_of(j * chunk, chunk), chunk)


def attend(chunk, head, kv_ref, key_pos_ref, query_pos, stacked, state):
    def step(j, state):
        largest, total, weighted = state
        at = rows_at(j, chunk)
        keys = heads_of(kv_ref, head, 1, at)
        values = heads_of(kv_ref, KV_HEADS + head, 1, at)
        scores = dot_last(keys, stacked)
        scores = jnp.where(key_pos_ref[at, :] <= query_pos, scores, MASKED)
        new_largest = jnp.maximum(largest, jnp.max(scores, axis=0, keepdims=True))
        weights = jnp.exp(scores - new_largest)
        factor = jnp.exp(largest - new_largest)
        total = total * factor + jnp.sum(weights, axis=0, keepdims=True)
        weighted = weighted * factor + dot_first(values, weights.astype(BF16))
        return new_largest, total, weighted

    return repeat(kv_ref.shape[0] // chunk, step, state)


def near_kernel(chunk, members, pieces, spots, *refs):
    ins, outs, scratch = split_refs(refs, 6 + members + pieces, 4, 2)
    normed_ref, key_pos_ref, query_pos_ref, cos_ref, sin_ref, local_ref = ins[:6]
    weights, parts = split_refs(ins[6:], members, pieces)
    queries_ref, largest_ref, total_ref, weighted_ref = outs
    blocks, kv_ref = scratch
    dp = spots[2]
    stack_rows(kv_ref, parts)
    own = local_ref.shape[0]
    away = normed_ref[:, own:]
    for j in range(members):
        blocks[dp ^ j] = dot_plain(away, weights[j][...])
    raw = join_lanes(blocks) + dot_plain(normed_ref[:, :own], local_ref[...])
    roped = rope_lanes(raw, cos_ref[...], sin_ref[...]).astype(BF16)
    queries_ref[...] = roped * jnp.asarray(1.0 / math.sqrt(HEAD_DIM), BF16)
    columns = GROUPS * queries_ref.shape[0]
    query_pos = query_pos_ref[...]
    for head in range(KV_HEADS):
        stacked = heads_of(queries_ref, head * GROUPS, GROUPS)
        start = (
            jnp.full((1, columns), MASKED, F32),
            jnp.zeros((1, columns), F32),
            jnp.zeros((HEAD_DIM, columns), F32),
        )
        largest, total, weighted = attend(
            chunk, head, kv_ref, key_pos_ref, query_pos, stacked, start
        )
        largest_ref[head : head + 1, :] = largest
        total_ref[head : head + 1, :] = total
        weighted_ref[head] = weighted


def far_kernel(chunk, pieces, spots, *refs):
    ins, outs, (kv_ref,) = split_refs(refs, 6 + pieces, 3, 1)
    queries_ref, key_pos_ref, query_pos_ref, largest_ref, total_ref, weighted_ref = ins[:6]
    parts = ins[6:]
    attended_ref, turned_ref, log_ref = outs
    stack_rows(kv_ref, parts)
    rows = queries_ref.shape[0]
    query_pos = query_pos_ref[...]
    heads = []
    for head in range(KV_HEADS):
        stacked = heads_of(queries_ref, head * GROUPS, GROUPS)
        start = (largest_ref[head : head + 1, :], total_ref[head : head + 1, :], weighted_ref[head])
        largest, total, weighted = attend(
            chunk, head, kv_ref, key_pos_ref, query_pos, stacked, start
        )
        turned = weighted / total
        turned_ref[head] = turned
        log_ref[head : head + 1, :] = largest + jnp.log(total)
        straight = turned.T
        heads += [straight[g * rows : (g + 1) * rows, :] for g in range(GROUPS)]
    attended_ref[...] = jnp.concatenate(heads, axis=1).astype(BF16)


def project_kernel(shards, members, spots, *refs):
    ins, outs, (blocks, head_blocks) = split_refs(refs, 4 + members, 3, 2)
    attended_ref, tokens_ref, gains_ref, local_ref = ins[:4]
    weights = ins[4:]
    residual_ref, inverse_ref, normed_ref = outs
    shard, dp = spots[1], spots[2]
    for z, block in enumerate(lane_blocks(attended_ref[...], shards)):
        head_blocks[z] = block
    away = jnp.concatenate([head_blocks[shard ^ r] for r in range(1, shards)], axis=1)
    for j in range(members):
        blocks[dp ^ j] = dot_plain(away, weights[j][...])
    added = join_lanes(blocks) + dot_plain(head_blocks[shard], local_ref[...])
    residual = tokens_ref[...].astype(F32) + added
    residual_ref[...] = residual
    normed, inverse = norm_rows(residual, gains_ref[1:2, :])
    inverse_ref[...] = inverse
    normed_ref[...] = normed.astype(BF16)


def unfold_down(pack_ref, down_ref, shards, part):
    piece = part // shards
    rows = pack_ref.shape[0] // shards
    for b in range(down_ref.shape[0] // rows):
        at = 2 * part + b * piece
        down_ref[b * rows : (b + 1) * rows, :] = jnp.concatenate(
            [pack_ref[z * rows : (z + 1) * rows, at : at + piece] for z in range(shards)], axis=1
        )


def feed_kernel(shards, masks, spots, *refs):
    ins, outs, scratch = split_refs(refs, 2 + len(masks), 3, 3)
    pack_ref, cot_all, normed_parts = ins[0], ins[1], ins[2:]
    cot_parts = [cot_all[spots[3] ^ mask] for mask in masks]
    grad_ref, act_ref, both_ref = outs
    normed_ref, cot_ref, down_ref = scratch
    part = pack_ref.shape[1] // 3
    stack_rows(normed_ref, normed_parts)
    stack_rows(cot_ref, cot_parts)
    unfold_down(pack_ref, down_ref, shards, part)
    gate_up = dot_plain(normed_ref[...], pack_ref[:, : 2 * part])
    gate, upward = gate_up[:, :part], gate_up[:, part:]
    act_grad = dot_plain(cot_ref[...], down_ref[...])
    sigmoid_gate = jax.nn.sigmoid(gate)
    silu = gate * sigmoid_gate
    act_ref[...] = (silu * upward).astype(BF16)
    gate_grad = act_grad * upward * sigmoid_gate * (1.0 + gate * (1.0 - sigmoid_gate))
    both_ref[...] = jnp.concatenate([gate_grad, act_grad * silu], axis=1).astype(BF16)
    unstack_rows(grad_ref, dot_last(both_ref[...], pack_ref[:, : 2 * part]))


def feed_weights_kernel(shards, masks, spots, *refs):
    ins, outs, scratch = split_refs(refs, 6 + len(masks), 3, 5)
    pack_ref, act_a, act_b, both_a, both_b, cot_all = ins[:6]
    normed_parts = ins[6:]
    cot_parts = [cot_all[spots[3] ^ mask] for mask in masks]
    result_a, result_b, grad_ref = outs
    normed_ref, cot_ref, act_ref, both_ref, down_ref = scratch
    part = pack_ref.shape[1] // 3
    piece = part // shards
    rows = grad_ref.shape[0] // shards
    stack_rows(normed_ref, normed_parts)
    stack_rows(cot_ref, cot_parts)
    stack_rows(act_ref, (act_a, act_b))
    stack_rows(both_ref, (both_a, both_b))
    unfold_down(pack_ref, down_ref, shards, part)
    grad_ref[:, : 2 * part] = dot_first(normed_ref[...], both_ref[...]).astype(BF16)
    down_grad = dot_first(cot_ref[...], act_ref[...]).astype(BF16)
    folds = down_grad.shape[0] // rows
    for z in range(shards):
        at = z * piece
        grad_ref[z * rows : (z + 1) * rows, 2 * part :] = jnp.concatenate(
            [down_grad[b * rows : (b + 1) * rows, at : at + piece] for b in range(folds)], axis=1
        )
    unstack_rows(result_a, dot_last(act_a[...], down_ref[...]))
    unstack_rows(result_b, dot_last(act_b[...], down_ref[...]))


def middle_kernel(shards, members, spots, *refs):
    ins, outs, scratch = split_refs(refs, 10 + members, 4, 2)
    (own_a, own_b, one_ref, two_ref, three_ref, residual_ref, inverse_ref, cot_ref, gains_ref,
     local_ref) = ins[:10]
    weights = ins[10:]
    residual_grad_ref, low_ref, attended_grad_ref, gain_grad_ref = outs
    rows = cot_ref.shape[0]
    grad = (own_a[0].astype(F32) + own_b[0].astype(F32)) + one_ref[...].astype(F32)
    grad = grad + two_ref[...].astype(F32) + three_ref[...].astype(F32)
    residual, inverse = residual_ref[...], inverse_ref[...]
    gain_grad_ref[...] = jnp.sum(grad * residual * inverse, axis=0, keepdims=True)
    residual_grad = cot_ref[...].astype(F32) + norm_back(grad, residual, inverse, gains_ref[1:2, :])
    residual_grad_ref[...] = residual_grad
    low = residual_grad.astype(BF16)
    low_ref[...] = low
    attended_grad_ref[...] = back_through(
        shards, members, spots, low, weights, local_ref, scratch
    ).astype(BF16)


def back_through(shards, members, spots, low, weights, local_ref, scratch):
    blocks, out_blocks = scratch
    shard, dp = spots[1], spots[2]
    for i, block in enumerate(lane_blocks(low, members)):
        blocks[i] = block
    away = sum(dot_last(blocks[dp ^ j], weights[j][...]) for j in range(members))
    out_blocks[shard] = dot_last(low, local_ref[...])
    for r, block in enumerate(lane_blocks(away, shards - 1)):
        out_blocks[shard ^ (r + 1)] = block
    return join_lanes(out_blocks)


def weight_grads_kernel(members, spots, *refs):
    lefts, lows, (keep_ref, send_ref, blocks) = refs[0:4:2], refs[1:4:2], refs[4:]
    dp = spots[2]
    for k, (left_ref, low_ref) in enumerate(zip(lefts, lows)):
        for i, block in enumerate(lane_blocks(low_ref[...], members)):
            blocks[k * members + i] = block
    for j in (1, 3, 0, 2):
        out_ref = send_ref if j & 1 else keep_ref
        out_ref[j // 2] = jnp.concatenate(
            [
                dot_first(left_ref[...], blocks[k * members + (dp ^ j)])
                for k, left_ref in enumerate(lefts)
            ],
            axis=1,
        ).astype(BF16)


def join_kernel(members, spots, own_ref, across_ref, core_ref, core_across_ref, *refs):
    outs, blocks = refs[:2], refs[2]
    dp = spots[2]
    for j, ref in enumerate((own_ref, core_ref, across_ref, core_across_ref)):
        blocks[dp ^ j] = ref[...]
    size = blocks.shape[-1] // 2
    for k, out_ref in enumerate(outs):
        out_ref[...] = jnp.concatenate(
            [blocks[i][:, k * size : (k + 1) * size] for i in range(members)], axis=1
        ).astype(F32)


def query_back_kernel(shards, members, spots, low_ref, local_ref, *refs):
    weights, (back_ref,), scratch = split_refs(refs, members, 1, 2)
    back_ref[...] = back_through(
        shards, members, spots, low_ref[...], weights, local_ref, scratch
    )


def back_kernel(chunk, pieces, first, last, spots, *refs):
    ins, outs, scratch = split_refs(refs, 9 + pieces, (pieces if last else 1) + 1, 2)
    (queries_ref, key_pos_ref, query_pos_ref, cos_ref, sin_ref, turned_ref, log_ref, grad_ref,
     start_ref) = ins[:9]
    parts = ins[9:]
    query_grad_ref, kv_grads = outs[0], outs[1:]
    kv_ref, kv_grad_ref = scratch
    stack_rows(kv_ref, parts)
    rows = queries_ref.shape[0]
    columns = GROUPS * rows
    query_pos = query_pos_ref[...]
    heads = []
    for head in range(KV_HEADS):
        stacked = heads_of(queries_ref, head * GROUPS, GROUPS)
        upstream = heads_of(grad_ref, head * GROUPS, GROUPS)
        delta = jnp.sum(upstream.astype(F32).T * turned_ref[head], axis=0, keepdims=True)
        log_total = log_ref[head : head + 1, :]
        keys_at = head * HEAD_DIM
        values_at = (KV_HEADS + head) * HEAD_DIM

        def step(j, query_grad, head=head, stacked=stacked, upstream=upstream,
                 delta=delta, log_total=log_total, keys_at=keys_at, values_at=values_at):
            at = rows_at(j, chunk)
            keys = heads_of(kv_ref, head, 1, at)
            values = heads_of(kv_ref, KV_HEADS + head, 1, at)
            scores = dot_last(keys, stacked)
            scores = jnp.where(key_pos_ref[at, :] <= query_pos, scores, MASKED)
            weights = jnp.exp(scores - log_total)
            weight_grad = dot_last(values, upstream)
            score_grad = (weights * (weight_grad - delta)).astype(BF16)
            value_grad = dot_plain(weights.astype(BF16), upstream)
            key_grad = dot_plain(score_grad, stacked)
            kv_grad_ref[at, keys_at : keys_at + HEAD_DIM] = key_grad.astype(BF16)
            kv_grad_ref[at, values_at : values_at + HEAD_DIM] = value_grad.astype(BF16)
            return query_grad + dot_first(keys, score_grad)

        start = jnp.zeros((HEAD_DIM, columns), F32) if first else start_ref[head]
        query_grad = repeat(kv_ref.shape[0] // chunk, step, start)
        if not last:
            query_grad_ref[head] = query_grad
        else:
            straight = query_grad.T * (1.0 / math.sqrt(HEAD_DIM))
            heads += [straight[g * rows : (g + 1) * rows, :] for g in range(GROUPS)]
    if last:
        query_grad_ref[...] = rope_lanes(
            jnp.concatenate(heads, axis=1), cos_ref[...], -sin_ref[...]
        ).astype(BF16)
    if last:
        for i in range(pieces):
            kv_grads[i][...] = kv_grad_ref[i * rows : (i + 1) * rows, :]
    else:
        unstack_rows(kv_grads[0], kv_grad_ref[...])


def end_kernel(shards, spots, *refs):
    ins, outs, scratch = split_refs(refs, 11 + (shards + 1) + 2 * (shards - 1), 3, 1)
    (cos_ref, sin_ref, normed_ref, tokens_ref, inverse_ref, gains_ref, back_ref, residual_grad_ref,
     key_ref, value_ref, gain_two_ref) = ins[:11]
    sums, mine, other = split_refs(ins[11:], shards + 1, shards - 1, shards - 1)
    input_grad_ref, keep_ref, send_ref = outs
    (blocks,) = scratch
    core, shard = spots[0], spots[1]
    width, span = key_ref.shape
    rows = tokens_ref.shape[0]
    total = sums[0][...].astype(F32) + sums[1][0].astype(F32)
    total = total + sum(s[...].astype(F32) for s in sums[2:])
    keys = rope_lanes(total[:, :width], cos_ref[...], -sin_ref[...])
    values = total[:, width:]
    keep = jnp.where(core == 0, keys, values).astype(BF16)
    send = jnp.where(core == 0, values, keys).astype(BF16)
    blocks[shard] = dot_plain(keys.astype(BF16), key_ref[...]) + dot_plain(
        values.astype(BF16), value_ref[...]
    )
    for r in range(1, shards):
        blocks[shard ^ r] = dot_plain(keep, mine[r - 1][:width, :]) + dot_plain(
            send, other[r - 1][:width, :]
        )
    normed_grad = back_ref[...] + join_lanes(blocks)
    inputs, inverse = tokens_ref[...].astype(F32), inverse_ref[...]
    gain_grad = jnp.sum(normed_grad * inputs * inverse, axis=0, keepdims=True)
    input_grad_ref[...] = residual_grad_ref[...] + norm_back(
        normed_grad, inputs, inverse, gains_ref[0:1, :]
    )
    normed = normed_ref[...]
    two = gain_two_ref[...]
    for out_ref, low, gain in (
        (send_ref, send, jnp.where(core == 0, two, gain_grad)),
        (keep_ref, keep, jnp.where(core == 0, gain_grad, two)),
    ):
        grad = dot_first(low, normed).astype(BF16)
        gains = lane_blocks(gain, shards)
        for z, block in enumerate(lane_blocks(grad, shards)):
            out_ref[z, :width, :] = block
            out_ref[z, width:, :] = jnp.broadcast_to(
                gains[z], (EXTRA_ROWS, span)
            ).astype(BF16)


def spread_kernel(shards, members, spots, *refs):
    parts, outs, (blocks,) = split_refs(refs, members, 3, 1)
    gate_ref, up_ref, down_ref = outs
    member = spots[3]
    piece = parts[0].shape[1] // 3 // shards
    rows = parts[0].shape[0]
    span = piece * members
    for i in range(members):
        blocks[member ^ i] = parts[i][...]

    def block(k):
        at = k * piece
        return jnp.concatenate(
            [blocks[p, :, at : at + piece] for p in range(members)], axis=1
        ).astype(F32)

    for z in range(shards):
        gate_ref[:, z * span : (z + 1) * span] = block(z)
        up_ref[:, z * span : (z + 1) * span] = block(shards + z)
    for b in range(down_ref.shape[0] // rows):
        down_ref[b * rows : (b + 1) * rows, :] = block(2 * shards + b)


def base_of(block_order, stored, block_length):
    which = stored // block_length
    count = block_order.shape[1]
    matches = (which[:, None] == jnp.arange(count, dtype=jnp.int32)[None, :]).astype(jnp.int32)
    return jnp.sum(block_order[0][None, :] * matches, axis=-1) * block_length + stored % block_length


def tables(positions):
    half_dim = HEAD_DIM // 2
    exponent = -(jnp.arange(half_dim, dtype=F32) * 2.0) / HEAD_DIM
    frequency = jnp.power(F32(ROPE_BASE), exponent)
    angles = positions.astype(F32)[:, None] * frequency
    cosine, sine = jnp.cos(angles), jnp.sin(angles)
    return (
        jnp.concatenate([cosine] * 4, axis=-1),
        jnp.concatenate([-sine, sine, -sine, sine], axis=-1),
    )


def after(x, other):
    return lax.optimization_barrier((x, other))[0]


def on_device(
    tokens,
    block_order,
    attention_gain,
    query_weight,
    key_weight,
    value_weight,
    output_weight,
    feedforward_gain,
    gate_weight,
    up_weight,
    down_weight,
    cotangent,
):
    tokens, cotangent = tokens[0], cotangent[0]
    rows, width = tokens.shape
    shards = lax.axis_size("fsdp")
    ctx_count = lax.axis_size("ctx")
    dp_count = lax.axis_size("dp")
    block_length = rows * shards * ctx_count // block_order.shape[1]
    shard = lax.axis_index("fsdp")
    ctx = lax.axis_index("ctx")
    dp = lax.axis_index("dp")
    core = dp & 1
    members = dp_count * 2
    weight_rows = query_weight.shape[0]
    query_width = HEADS * HEAD_DIM
    kv_width = KV_HEADS * HEAD_DIM
    hidden = gate_weight.shape[1]
    part = hidden // members
    spots = jnp.stack([core, shard, dp, dp * 2 + (ctx & 1)]).astype(jnp.int32)

    gain_one, gain_two = attention_gain[None, :], feedforward_gain[None, :]
    key_turned, value_turned, down_turned = key_weight.T, value_weight.T, down_weight.T
    kv_pack = jnp.concatenate(
        [
            jnp.where(core == 0, key_turned, value_turned),
            jnp.pad(
                jnp.concatenate([gain_one, gain_two], axis=0), ((0, EXTRA_ROWS - 2), (0, 0))
            ),
        ],
        axis=0,
    )
    kv_mine = direct_fsdp(kv_pack)

    quarter = width // dp_count
    query_quarter, output_quarter = call(
        functools.partial(quarter_kernel, dp_count), spots,
        [after(query_weight, kv_pack), output_weight],
        [((weight_rows, quarter), BF16)] * 2, name="quarter_columns",
    )
    query_pieces = direct_fsdp(query_quarter)
    kv_other = [swap_core(piece) for piece in kv_mine]

    def stack(pieces):
        (stacked,) = call(
            stack_kernel, spots, pieces, [(((shards - 1) * weight_rows, quarter), BF16)],
            name="stack_quarters",
        )
        return stacked, swap_plane(stacked, 2, 0)

    def four(stacked, across):
        return [stacked, swap_core(stacked), across, swap_core(across)]

    group_axes = ("dp", "ctx")
    extra = {}
    if ctx_count > 2:
        extra["axis_index_groups"] = [
            [d * ctx_count + c for d in range(dp_count) for c in (first, first + 1)]
            for first in range(0, ctx_count, 2)
        ]
    cot_all = lax.all_gather(cotangent, group_axes, axis=0, tiled=False, **extra)

    offsets = jnp.arange(rows, dtype=jnp.int32)
    my_start = (ctx * shards + shard) * rows
    positions = base_of(block_order, my_start[None], block_length) + offsets
    cosine, sine = tables(positions)
    query_pos = jnp.concatenate([positions] * GROUPS)[None, :]
    starts = jnp.stack(
        [((ctx ^ d) * shards + (shard ^ r)) * rows for d in range(ctx_count) for r in range(shards)]
    )
    key_pos = (base_of(block_order, starts, block_length)[:, None] + offsets[None, :]).reshape(-1, 1)
    near_count = shards * rows
    near_pos, far_pos = key_pos[:near_count], key_pos[near_count:]
    far_count = far_pos.shape[0]

    (pack,) = call(
        functools.partial(pack_kernel, shards, members), spots,
        [gate_weight, up_weight, down_turned], [((weight_rows, 3 * part), BF16)],
        name="pack_weights",
    )
    kv_own, normed_one, normed_turned, inverse_one, gains = call(
        functools.partial(begin_kernel, shards), spots,
        [
            lax.optimization_barrier((tokens, query_quarter, pack))[0], gain_one, gain_two, key_turned, value_turned, cosine, sine,
            *kv_mine, *kv_other,
        ],
        [
            ((rows, 2 * kv_width), BF16), ((rows, width), BF16), ((rows, width), BF16),
            ((rows, 1), F32), ((8, width), F32),
        ],
        scratch=[
            ((shards, rows, weight_rows), F32), ((shards, rows, weight_rows), BF16),
            ((shards, 8, weight_rows), F32),
        ],
        name="norm_keys_values",
    )
    near = [kv_own] + direct_fsdp(kv_own)
    query_pieces = lax.optimization_barrier((kv_own, *query_pieces))[1:]
    stacked, across = stack(query_pieces)
    across, *near = lax.optimization_barrier((across, *near))
    query_stacks = four(stacked, across)
    (near_all,) = call(
        stack_kernel, spots, near, [((near_count, 2 * kv_width), BF16)],
        name="stack_keys_values",
    )
    far = [swap(near_all, "ctx", d) for d in range(1, ctx_count)]
    output_pieces = direct_fsdp(after(output_quarter, near_all))

    pack, cot_all, _ = lax.optimization_barrier((pack, cot_all, near[-1]))
    pack_all = lax.all_gather(pack, "fsdp", axis=0, tiled=True)


    chunk = rows * 2
    unit = 2 * HEADS * rows * near_count * HEAD_DIM
    stat = ((KV_HEADS, GROUPS * rows), F32)
    turned_shape = ((KV_HEADS, HEAD_DIM, GROUPS * rows), F32)
    queries, largest, total, weighted = call(
        functools.partial(near_kernel, chunk, dp_count, shards), spots,
        [normed_turned, near_pos, query_pos, cosine, sine, query_weight, *query_stacks, *near],
        [((rows, query_width), BF16), stat, stat, turned_shape],
        scratch=[((dp_count, rows, quarter), F32), ((near_count, 2 * kv_width), BF16)],
        name="attention_near",
    )
    attended, turned, log_total = call(
        functools.partial(far_kernel, chunk, len(far)), spots,
        [queries, far_pos, query_pos, largest, total, weighted, *far],
        [((rows, query_width), BF16), turned_shape, stat],
        scratch=[((far_count, 2 * kv_width), BF16)], name="attention_far",
    )
    output_pieces = lax.optimization_barrier((queries, *output_pieces))[1:]
    output_stacked, output_across = stack(output_pieces)
    attended, output_across = lax.optimization_barrier((attended, output_across))
    output_stacks = four(output_stacked, output_across)
    residual, inverse_two, normed_two = call(
        functools.partial(project_kernel, shards, dp_count), spots,
        [attended, tokens, gains, output_weight, *output_stacks],
        [((rows, width), F32), ((rows, 1), F32), ((rows, width), BF16)],
        scratch=[((dp_count, rows, quarter), F32), ((shards, rows, weight_rows), BF16)],
        name="project_residual",
    )

    normed_a, normed_b = plane_pieces(normed_two)
    token_shape = ((rows, width), BF16)
    half = 4 * rows
    half_shape = ((4, rows, width), BF16)

    masks = [2 * a + b for a, b in ((0, 0),) + CHIP_MASKS]
    core_masks = [mask ^ 2 for mask in masks]

    def feed(normed, masks):
        return call(
            functools.partial(feed_kernel, shards, masks), spots, [pack_all, cot_all, *normed],
            [half_shape, ((half, part), BF16), ((half, 2 * part), BF16)],
            scratch=[((half, width), BF16), ((half, width), BF16), ((width, part), BF16)],
        name="feed_forward",
        )

    grad_b, act_b, both_b = feed(normed_b, core_masks)
    from_core = swap_core(grad_b)
    grad_a, act_a, both_a = feed(normed_a, masks)

    def chip_sums(parts_a, parts_b):
        return [
            (parts_a[k].astype(F32) + parts_b[k].astype(F32)).astype(BF16)
            for k in range(1, 4)
        ]

    def send_chips(sums):
        return [swap_plane(x, a, b) for x, (a, b) in zip(sums, CHIP_MASKS)]

    grad_sums = chip_sums(grad_a, from_core)
    grad_chips = send_chips(grad_sums)
    act_a, *_ = lax.optimization_barrier((act_a, *grad_sums))
    result_a, result_b, pack_grad = call(
        functools.partial(feed_weights_kernel, shards, masks + core_masks), spots,
        [pack_all, act_a, act_b, both_a, both_b, cot_all, *normed_a, *normed_b],
        [half_shape, half_shape, ((width, 3 * part), BF16)],
        scratch=[
            ((2 * half, width), BF16), ((2 * half, width), BF16), ((2 * half, part), BF16),
            ((2 * half, 2 * part), BF16), ((width, part), BF16),
        ],
        name="feed_forward_weights",
    )
    pack_share = sum_far(lax.psum_scatter(pack_grad, "fsdp", scatter_dimension=0, tiled=True))

    pack_grad, result_b, *grad_chips = lax.optimization_barrier(
        (pack_grad, result_b, *grad_chips)
    )
    residual_grad, residual_low, attended_grad, second_gain_grad = call(
        functools.partial(middle_kernel, shards, dp_count), spots,
        [
            grad_a, from_core, *grad_chips, residual, inverse_two, cotangent, gains, output_weight,
            *output_stacks,
        ],
        [((rows, width), F32), token_shape, ((rows, query_width), BF16), ((1, width), F32)],
        scratch=[((dp_count, rows, quarter), BF16), ((shards, rows, weight_rows), F32)],
        name="residual_back",
    )

    result_core = swap_core(result_b)
    attended_grad, result_a = lax.optimization_barrier((attended_grad, result_a))

    def sum_x(keep, away):
        sent = (keep[1].astype(F32) + away[1].astype(F32)).astype(BF16)
        return sent, (keep[0], away[0], swap_plane(sent, 2, 0))

    def pieces_z(terms):
        out = []
        for r in range(shards):
            at = (shard ^ r) * weight_rows
            parts = [
                lax.dynamic_slice_in_dim(x, at, weight_rows, 0).astype(F32) for x in terms
            ]
            out.append((parts[0] + parts[1] + parts[2]).astype(BF16))
        return out

    def sum_z(pieces):
        arrived = {r: swap(pieces[r], "fsdp", r) for r in reversed(range(1, shards))}
        return sum(
            (arrived[r].astype(F32) for r in range(1, shards)), pieces[0].astype(F32)
        ).astype(BF16)

    def halve_z(pieces, span):
        sent = jnp.stack([piece.astype(BF16) for piece in pieces[span:]])
        arrived = swap(sent, "fsdp", span)
        return [pieces[r].astype(F32) + arrived[r].astype(F32) for r in range(span)]

    def sum_swap(own, dp_mask, ctx_mask):
        return (own.astype(F32) + swap_plane(own, dp_mask, ctx_mask).astype(F32)).astype(BF16)

    def sum_y(own):
        return sum_far(sum_swap(own, 0, 1))

    def finish_quarters(own):
        across = swap_plane(own, 2, 0)
        return call(
            functools.partial(join_kernel, dp_count), spots,
            [own, across, swap_core(own), swap_core(across)],
            [((weight_rows, width), F32)] * 2,
            scratch=[((dp_count, weight_rows, 2 * quarter), BF16)], name="join_columns",
        )

    def back(first, last, start, pos, pieces):
        count = pos.shape[0]
        shape = ((rows, query_width), BF16) if last else turned_shape
        out = call(
            functools.partial(back_kernel, chunk, len(pieces), first, last), spots,
            [
                queries, pos, query_pos, cosine, sine, turned, log_total, attended_grad, start,
                *pieces,
            ],
            [shape]
            + (
                [((rows, 2 * kv_width), BF16)] * len(pieces) if last
                else [((shards, rows, 2 * kv_width), BF16)]
            ),
            scratch=[((count, 2 * kv_width), BF16), ((count, 2 * kv_width), BF16)],
            name="attention_back_near" if last else "attention_back_far",
        )
        return out[0], out[1:]

    query_partial, far_grads = turned, []
    for d in range(1, ctx_count):
        at = (d - 1) * near_count
        query_partial, grads = back(
            d == 1, False, query_partial, far_pos[at : at + near_count], far[d - 1 : d]
        )
        far_grads.append(swap(grads[0], "ctx", d))
    result_sent = (result_a[2:].astype(F32) + result_core[2:].astype(F32)).astype(BF16)
    query_partial, result_sent = lax.optimization_barrier((query_partial, result_sent))
    result_across = swap_plane(result_sent, 2, 0)
    query_low, near_grads = back(False, True, query_partial, near_pos, near)
    pair_shape = ((2, width, 2 * quarter), BF16)
    weights_keep, weights_send = call(
        functools.partial(weight_grads_kernel, dp_count), spots,
        [attended, residual_low, normed_one, query_low], [pair_shape, pair_shape],
        scratch=[((2 * dp_count, rows, quarter), BF16)], name="query_output_weight_grads",
    )
    weights_send, pack_share, far_grads[-1], result_across = lax.optimization_barrier(
        (weights_send, pack_share, far_grads[-1], result_across)
    )
    result_own, result_along = [
        (result_a[k].astype(F32) + result_core[k].astype(F32)) + result_across[k].astype(F32)
        for k in (0, 1)
    ]
    result_along = swap_plane(result_along.astype(BF16), 0, 1)

    def home(r):
        return sum(grads[r].astype(F32) for grads in far_grads)

    kv_sums = {
        r: (near_grads[r].astype(F32) + home(r)).astype(BF16) for r in range(1, shards)
    }
    kv_arrived = {r: swap(kv_sums[r], "fsdp", r) for r in reversed(range(1, shards))}
    query_low = lax.optimization_barrier((query_low, *kv_sums.values()))[0]

    weights_away = swap_core(weights_send)
    weights_sent, weights_terms = sum_x(weights_keep, weights_away)
    query_turn = after(query_low, weights_sent)
    (query_back,) = call(
        functools.partial(query_back_kernel, shards, dp_count), spots,
        [query_turn, query_weight, *query_stacks], [((rows, width), F32)],
        scratch=[((dp_count, rows, quarter), BF16), ((shards, rows, weight_rows), F32)],
        name="query_back",
    )
    query_back, share_along = lax.optimization_barrier(
        (query_back, swap_plane(pack_share, 0, 1))
    )
    share_across = swap_plane(after(pack_share, weights_sent), 2, 0)
    span = kv_width + EXTRA_ROWS
    packed_shape = ((shards, span, weight_rows), BF16)
    home_all = far_grads[0]
    if ctx_count > 2:
        home_all = sum(grads.astype(F32) for grads in far_grads)
    input_grad, kv_keep, kv_send = call(
        functools.partial(end_kernel, shards), spots,
        [
            cosine, sine, normed_one, tokens, inverse_one, gains, query_back, residual_grad,
            key_turned, value_turned, second_gain_grad, near_grads[0], home_all,
            *[kv_arrived[r] for r in range(1, shards)], *kv_mine, *kv_other,
        ],
        [((rows, width), F32), packed_shape, packed_shape],
        scratch=[((shards, rows, weight_rows), F32)],
        name="keys_values_back",
    )
    kv_away = swap_core(kv_send)
    kv_keep, *weights_terms = lax.optimization_barrier((kv_keep, *weights_terms))
    weights_pieces = pieces_z(weights_terms)
    pieces = [
        (lax.dynamic_index_in_dim(kv_keep, shard ^ r, 0, keepdims=False).astype(F32)
         + lax.dynamic_index_in_dim(kv_away, shard ^ r, 0, keepdims=False).astype(F32)).astype(BF16)
        for r in range(shards)
    ]
    weights_pieces, *pieces = lax.optimization_barrier((weights_pieces, *pieces))
    share_across = lax.optimization_barrier((share_across, *pieces))[0]
    share_a = [pack_share, share_along, share_across, swap_plane(share_across, 0, 1)]
    share_b = [swap_core(piece) for piece in share_a]
    kv_share = sum_z(pieces)
    weights_half = halve_z(weights_pieces, shards // 2)
    share_by_mask = [None] * members
    for k, (a, b) in enumerate(((0, 0),) + CHIP_MASKS):
        share_by_mask[2 * a + b] = share_a[k]
        share_by_mask[2 * (a ^ 1) + b] = share_b[k]
    gate_weight_grad, up_weight_grad, down_weight_grad = call(
        functools.partial(spread_kernel, shards, members), spots, share_by_mask,
        [
            ((weight_rows, hidden), F32), ((weight_rows, hidden), F32),
            ((width, down_weight.shape[0]), F32),
        ],
        scratch=[((members, weight_rows, 3 * part), BF16)],
        name="feed_forward_out",
    )
    kv_share, weights_half = lax.optimization_barrier((kv_share, weights_half))
    kv_share, result_along, *big = lax.optimization_barrier(
        (sum_swap(kv_share, 2, 0), result_along, gate_weight_grad, up_weight_grad,
         down_weight_grad)
    )
    gate_weight_grad, up_weight_grad, down_weight_grad = big
    span = shards // 2
    while span > 1:
        span //= 2
        weights_half = halve_z(weights_half, span)
    weights_own = sum_y(weights_half[0].astype(BF16))
    result = residual + (result_own + result_along.astype(F32))
    output_weight_grad, query_weight_grad = finish_quarters(weights_own)
    low = sum_far(sum_swap(kv_share, 0, 1))
    away = swap_core(low)
    first = jnp.where(core == 0, low, away).astype(F32)
    second = jnp.where(core == 0, away, low).astype(F32)

    return (
        result[None],
        input_grad[None],
        first[kv_width],
        query_weight_grad,
        first[:kv_width].T,
        second[:kv_width].T,
        output_weight_grad,
        second[kv_width],
        gate_weight_grad,
        up_weight_grad,
        down_weight_grad.T,
    )


def solution(mesh):
    row = P("fsdp", None)
    token = P("dp", ("ctx", "fsdp"), None)
    return jax.shard_map(
        on_device,
        mesh=mesh,
        in_specs=(
            token, P("dp", None), P("fsdp"), row, row, row, row, P("fsdp"), row, row, row, token,
        ),
        out_specs=(
            token, token, P("fsdp"), row, row, row, row, P("fsdp"), row, row, row,
        ),
        check_vma=False,
    )
```

```python
import functools
import math

import jax
import jax.numpy as jnp
from jax import lax
from jax.experimental import pallas as pl
from jax.experimental.pallas import tpu as pltpu
from jax.sharding import PartitionSpec as P

HEADS = 15
KV_HEADS = 5
HEAD_DIM = 64
GROUPS = HEADS // KV_HEADS
LANES = 128

EPSILON = 1e-05
ROPE_BASE = 100000.0
MASKED = -1e30

F32 = jnp.float32
BF16 = jnp.bfloat16
VMEM_LIMIT = 56 * 1024 * 1024
FLOPS_PER_US = 1150 * 10**6
MEASURED_US = {
    "pack_weights": 4,
    "norm_keys_values": 4,
    "attention_near": 12,
    "attention_far": 12,
    "feed_forward": 8,
    "feed_forward_weights": 12,
    "residual_back": 6,
    "attention_back_far": 13,
    "attention_back_near": 14,
    "query_output_weight_grads": 0,
    "query_back": 0,
    "stack_quarters": 0,
    "quarter_columns": 0,
    "keys_values_back": 6,
    "feed_forward_out": 7,
}


def dot_plain(left, right):
    return jnp.dot(left, right, preferred_element_type=F32)


def dot_last(left, right):
    return lax.dot_general(left, right, (((1,), (1,)), ((), ())), preferred_element_type=F32)


def dot_first(left, right):
    return lax.dot_general(left, right, (((0,), (0,)), ((), ())), preferred_element_type=F32)


def swap(x, axis, mask):
    count = lax.axis_size(axis)
    return lax.ppermute(x, axis, [(i, i ^ mask) for i in range(count)])


def swap_plane(x, dp_mask, ctx_mask):
    ctx_count = lax.axis_size("ctx")
    pairs = []
    for d in range(lax.axis_size("dp")):
        for c in range(ctx_count):
            pairs.append((d * ctx_count + c, (d ^ dp_mask) * ctx_count + (c ^ ctx_mask)))
    return lax.ppermute(x, ("dp", "ctx"), pairs)


def swaps_fsdp(x):
    pieces = {0: x}
    for r in range(1, lax.axis_size("fsdp")):
        top = 1 << (r.bit_length() - 1)
        pieces[r] = swap(pieces[r - top], "fsdp", top)
    return [pieces[r] for r in range(1, lax.axis_size("fsdp"))]


def direct_fsdp(x):
    return [swap(x, "fsdp", r) for r in range(1, lax.axis_size("fsdp"))]


def swap_core(x):
    return swap_plane(x, 1, 0)


CHIP_MASKS = ((0, 1), (2, 0), (2, 1))


def plane_pieces(x):
    mine = [x] + [swap_plane(x, a, b) for a, b in CHIP_MASKS]
    return mine, [swap_core(piece) for piece in mine]


def sum_far(x):
    count = lax.axis_size("ctx")
    if count == 2:
        return x
    groups = [list(range(0, count, 2)), list(range(1, count, 2))]
    return lax.psum(x.astype(F32), "ctx", axis_index_groups=groups).astype(x.dtype)


def call(kernel, spots, args, out_shapes, scratch=(), name=None):
    specs = [pl.BlockSpec(memory_space=pltpu.SMEM)]
    specs += [pl.BlockSpec(memory_space=pltpu.VMEM) for _ in args]
    outs = tuple(jax.ShapeDtypeStruct(s, d) for s, d in out_shapes)
    return pl.pallas_call(
        kernel,
        out_shape=outs,
        in_specs=specs,
        out_specs=tuple(pl.BlockSpec(memory_space=pltpu.VMEM) for _ in outs),
        scratch_shapes=[pltpu.VMEM(s, d) for s, d in scratch],
        compiler_params=pltpu.CompilerParams(vmem_limit_bytes=VMEM_LIMIT),
        cost_estimate=pl.CostEstimate(
            flops=MEASURED_US.get(name, 2) * FLOPS_PER_US, bytes_accessed=0, transcendentals=0
        ),
        name=name,
    )(spots, *args)


def split_refs(refs, *counts):
    out, at = [], 0
    for n in counts:
        out.append(refs[at : at + n])
        at += n
    assert at == len(refs)
    return out


def lane_blocks(values, count):
    size = values.shape[1] // count
    return [values[:, i * size : (i + 1) * size] for i in range(count)]


def join_lanes(ref):
    return jnp.concatenate([ref[i] for i in range(ref.shape[0])], axis=1)


def rope_lanes(values, cosine, sine):
    rows, width = values.shape
    lane = lax.broadcasted_iota(jnp.int32, (rows, LANES), 1)
    first_half = (lane % HEAD_DIM) < (HEAD_DIM // 2)
    out = []
    for start in range(0, width, LANES):
        piece = values[:, start : min(start + LANES, width)]
        size = piece.shape[1]
        if size < LANES:
            piece = jnp.concatenate([piece, jnp.zeros((rows, LANES - size), piece.dtype)], axis=1)
        ahead = pltpu.roll(piece, LANES - HEAD_DIM // 2, 1)
        behind = pltpu.roll(piece, HEAD_DIM // 2, 1)
        partner = jnp.where(first_half, ahead, behind)
        out.append((piece * cosine + partner * sine)[:, :size])
    return jnp.concatenate(out, axis=1)


def heads_of(ref, first, count, rows=None):
    out = []
    for h in range(first, first + count):
        start = (h * HEAD_DIM) // LANES * LANES
        stop = min(start + LANES, ref.shape[-1])
        pair = ref[:, start:stop] if rows is None else ref[rows, start:stop]
        at = h * HEAD_DIM - start
        out.append(pair[:, at : at + HEAD_DIM])
    return out[0] if count == 1 else jnp.concatenate(out, axis=0)


def stack_rows(scratch, pieces):
    at = 0
    for piece in pieces:
        scratch[at : at + piece.shape[0], :] = piece[...]
        at += piece.shape[0]


def unstack_rows(out_ref, values):
    count, rows = out_ref.shape[:2]
    for i in range(count):
        out_ref[i] = values[i * rows : (i + 1) * rows, :].astype(out_ref.dtype)


def norm_rows(values, gain):
    inverse = lax.rsqrt(jnp.mean(values * values, axis=-1, keepdims=True) + EPSILON)
    return (values * inverse * gain, inverse)


def norm_back(gradient, values, inverse, gain):
    scaled = gradient * gain
    inner_mean = jnp.mean(scaled * values, axis=-1, keepdims=True)
    return inverse * scaled - values * (inverse * inverse * inverse) * inner_mean


EXTRA_ROWS = 16


def pack_kernel(shards, members, spots, gate_ref, up_ref, down_ref, out_ref):
    member = spots[3]
    span = gate_ref.shape[1] // shards
    piece = span // members
    rows = gate_ref.shape[0]
    pick = (
        lax.broadcasted_iota(jnp.int32, (span, piece), 0)
        == lax.broadcasted_iota(jnp.int32, (span, piece), 1) + member * piece
    ).astype(BF16)
    out = []
    for ref in (gate_ref, up_ref):
        for z in range(shards):
            out.append(dot_plain(ref[:, z * span : (z + 1) * span], pick))
    down = dot_plain(down_ref[...], pick)
    out += [down[b : b + rows, :] for b in range(0, down_ref.shape[0], rows)]
    out_ref[...] = jnp.concatenate(out, axis=1).astype(BF16)


def quarter_kernel(members, spots, query_ref, output_ref, *outs):
    size = query_ref.shape[1] // members
    for i in range(members):

        @pl.when(spots[2] == i)
        def _():
            for ref, out_ref in zip((query_ref, output_ref), outs):
                out_ref[...] = ref[:, i * size : (i + 1) * size]


def stack_kernel(spots, *refs):
    stack_rows(refs[-1], refs[:-1])


def begin_kernel(shards, spots, *refs):
    ins, outs, scratch = split_refs(refs, 7 + 2 * (shards - 1), 5, 3)
    tokens_ref, gain_one, gain_two, key_ref, value_ref, cos_ref, sin_ref = ins[:7]
    mine, other = split_refs(ins[7:], shards - 1, shards - 1)
    kv_ref, normed_ref, turned_ref, inverse_ref, gains_ref = outs
    blocks, normed_blocks, gain_blocks = scratch
    core, shard = spots[0], spots[1]
    width = key_ref.shape[0]
    values = tokens_ref[...].astype(F32)
    inverse = lax.rsqrt(jnp.mean(values * values, axis=-1, keepdims=True) + EPSILON)
    inverse_ref[...] = inverse
    for z, block in enumerate(lane_blocks(values * inverse, shards)):
        blocks[z] = block
    sums, order = [], []
    for r in range(shards):
        at = shard ^ r
        if r == 0:
            pair = jnp.concatenate([gain_one[...], gain_two[...]], axis=0).astype(F32)
        else:
            pair = mine[r - 1][width : width + EXTRA_ROWS, :].astype(F32)[0:2, :]
        gain_blocks[at, 0:2, :] = pair
        normed = (blocks[at] * pair[0:1, :]).astype(BF16)
        normed_blocks[at] = normed
        order.append(normed)
        left = key_ref[...] if r == 0 else mine[r - 1][:width, :]
        right = value_ref[...] if r == 0 else other[r - 1][:width, :]
        sums.append((dot_last(normed, left), dot_last(normed, right)))
    first = sum(s[0] for s in sums[1:])
    second = sum(s[1] for s in sums[1:])
    keys = jnp.where(core == 0, first, second) + sums[0][0]
    vals = jnp.where(core == 0, second, first) + sums[0][1]
    keys = rope_lanes(keys, cos_ref[...], sin_ref[...])
    kv_ref[...] = jnp.concatenate([keys, vals], axis=1).astype(BF16)
    normed_ref[...] = join_lanes(normed_blocks)
    turned_ref[...] = jnp.concatenate(order, axis=1)
    gains_ref[...] = jnp.zeros_like(gains_ref)
    gains_ref[0:2, :] = jnp.concatenate([gain_blocks[z][0:2, :] for z in range(shards)], axis=1)


def repeat(count, step, state):
    if count > 2:
        return lax.fori_loop(0, count, step, state)
    for j in range(count):
        state = step(j, state)
    return state


def rows_at(j, chunk):
    if isinstance(j, int):
        return slice(j * chunk, (j + 1) * chunk)
    return pl.ds(pl.multiple_of(j * chunk, chunk), chunk)


def attend(chunk, head, kv_ref, key_pos_ref, query_pos, stacked, state):
    def step(j, state):
        largest, total, weighted = state
        at = rows_at(j, chunk)
        keys = heads_of(kv_ref, head, 1, at)
        values = heads_of(kv_ref, KV_HEADS + head, 1, at)
        scores = dot_last(keys, stacked)
        scores = jnp.where(key_pos_ref[at, :] <= query_pos, scores, MASKED)
        new_largest = jnp.maximum(largest, jnp.max(scores, axis=0, keepdims=True))
        weights = jnp.exp(scores - new_largest)
        factor = jnp.exp(largest - new_largest)
        total = total * factor + jnp.sum(weights, axis=0, keepdims=True)
        weighted = weighted * factor + dot_first(values, weights.astype(BF16))
        return new_largest, total, weighted

    return repeat(kv_ref.shape[0] // chunk, step, state)


def near_kernel(chunk, members, pieces, spots, *refs):
    ins, outs, scratch = split_refs(refs, 6 + members + pieces, 4, 2)
    normed_ref, key_pos_ref, query_pos_ref, cos_ref, sin_ref, local_ref = ins[:6]
    weights, parts = split_refs(ins[6:], members, pieces)
    queries_ref, largest_ref, total_ref, weighted_ref = outs
    blocks, kv_ref = scratch
    dp = spots[2]
    stack_rows(kv_ref, parts)
    own = local_ref.shape[0]
    away = normed_ref[:, own:]
    for j in range(members):
        blocks[dp ^ j] = dot_plain(away, weights[j][...])
    raw = join_lanes(blocks) + dot_plain(normed_ref[:, :own], local_ref[...])
    roped = rope_lanes(raw, cos_ref[...], sin_ref[...]).astype(BF16)
    queries_ref[...] = roped * jnp.asarray(1.0 / math.sqrt(HEAD_DIM), BF16)
    columns = GROUPS * queries_ref.shape[0]
    query_pos = query_pos_ref[...]
    for head in range(KV_HEADS):
        stacked = heads_of(queries_ref, head * GROUPS, GROUPS)
        start = (
            jnp.full((1, columns), MASKED, F32),
            jnp.zeros((1, columns), F32),
            jnp.zeros((HEAD_DIM, columns), F32),
        )
        largest, total, weighted = attend(
            chunk, head, kv_ref, key_pos_ref, query_pos, stacked, start
        )
        largest_ref[head : head + 1, :] = largest
        total_ref[head : head + 1, :] = total
        weighted_ref[head] = weighted


def far_kernel(chunk, pieces, spots, *refs):
    ins, outs, (kv_ref,) = split_refs(refs, 6 + pieces, 3, 1)
    queries_ref, key_pos_ref, query_pos_ref, largest_ref, total_ref, weighted_ref = ins[:6]
    parts = ins[6:]
    attended_ref, turned_ref, log_ref = outs
    stack_rows(kv_ref, parts)
    rows = queries_ref.shape[0]
    query_pos = query_pos_ref[...]
    heads = []
    for head in range(KV_HEADS):
        stacked = heads_of(queries_ref, head * GROUPS, GROUPS)
        start = (largest_ref[head : head + 1, :], total_ref[head : head + 1, :], weighted_ref[head])
        largest, total, weighted = attend(
            chunk, head, kv_ref, key_pos_ref, query_pos, stacked, start
        )
        turned = weighted / total
        turned_ref[head] = turned
        log_ref[head : head + 1, :] = largest + jnp.log(total)
        straight = turned.T
        heads += [straight[g * rows : (g + 1) * rows, :] for g in range(GROUPS)]
    attended_ref[...] = jnp.concatenate(heads, axis=1).astype(BF16)


def project_kernel(shards, members, spots, *refs):
    ins, outs, (blocks, head_blocks) = split_refs(refs, 4 + members, 3, 2)
    attended_ref, tokens_ref, gains_ref, local_ref = ins[:4]
    weights = ins[4:]
    residual_ref, inverse_ref, normed_ref = outs
    shard, dp = spots[1], spots[2]
    for z, block in enumerate(lane_blocks(attended_ref[...], shards)):
        head_blocks[z] = block
    away = jnp.concatenate([head_blocks[shard ^ r] for r in range(1, shards)], axis=1)
    for j in range(members):
        blocks[dp ^ j] = dot_plain(away, weights[j][...])
    added = join_lanes(blocks) + dot_plain(head_blocks[shard], local_ref[...])
    residual = tokens_ref[...].astype(F32) + added
    residual_ref[...] = residual
    normed, inverse = norm_rows(residual, gains_ref[1:2, :])
    inverse_ref[...] = inverse
    normed_ref[...] = normed.astype(BF16)


def unfold_down(pack_ref, down_ref, shards, part):
    piece = part // shards
    rows = pack_ref.shape[0] // shards
    for b in range(down_ref.shape[0] // rows):
        at = 2 * part + b * piece
        down_ref[b * rows : (b + 1) * rows, :] = jnp.concatenate(
            [pack_ref[z * rows : (z + 1) * rows, at : at + piece] for z in range(shards)], axis=1
        )


def feed_kernel(shards, masks, spots, *refs):
    ins, outs, scratch = split_refs(refs, 2 + len(masks), 3, 3)
    pack_ref, cot_all, normed_parts = ins[0], ins[1], ins[2:]
    cot_parts = [cot_all[spots[3] ^ mask] for mask in masks]
    grad_ref, act_ref, both_ref = outs
    normed_ref, cot_ref, down_ref = scratch
    part = pack_ref.shape[1] // 3
    stack_rows(normed_ref, normed_parts)
    stack_rows(cot_ref, cot_parts)
    unfold_down(pack_ref, down_ref, shards, part)
    gate_up = dot_plain(normed_ref[...], pack_ref[:, : 2 * part])
    gate, upward = gate_up[:, :part], gate_up[:, part:]
    act_grad = dot_plain(cot_ref[...], down_ref[...])
    sigmoid_gate = jax.nn.sigmoid(gate)
    silu = gate * sigmoid_gate
    act_ref[...] = (silu * upward).astype(BF16)
    gate_grad = act_grad * upward * sigmoid_gate * (1.0 + gate * (1.0 - sigmoid_gate))
    both_ref[...] = jnp.concatenate([gate_grad, act_grad * silu], axis=1).astype(BF16)
    unstack_rows(grad_ref, dot_last(both_ref[...], pack_ref[:, : 2 * part]))


def feed_weights_kernel(shards, masks, spots, *refs):
    ins, outs, scratch = split_refs(refs, 6 + len(masks), 3, 5)
    pack_ref, act_a, act_b, both_a, both_b, cot_all = ins[:6]
    normed_parts = ins[6:]
    cot_parts = [cot_all[spots[3] ^ mask] for mask in masks]
    result_a, result_b, grad_ref = outs
    normed_ref, cot_ref, act_ref, both_ref, down_ref = scratch
    part = pack_ref.shape[1] // 3
    piece = part // shards
    rows = grad_ref.shape[0] // shards
    stack_rows(normed_ref, normed_parts)
    stack_rows(cot_ref, cot_parts)
    stack_rows(act_ref, (act_a, act_b))
    stack_rows(both_ref, (both_a, both_b))
    unfold_down(pack_ref, down_ref, shards, part)
    grad_ref[:, : 2 * part] = dot_first(normed_ref[...], both_ref[...]).astype(BF16)
    down_grad = dot_first(cot_ref[...], act_ref[...]).astype(BF16)
    folds = down_grad.shape[0] // rows
    for z in range(shards):
        at = z * piece
        grad_ref[z * rows : (z + 1) * rows, 2 * part :] = jnp.concatenate(
            [down_grad[b * rows : (b + 1) * rows, at : at + piece] for b in range(folds)], axis=1
        )
    unstack_rows(result_a, dot_last(act_a[...], down_ref[...]))
    unstack_rows(result_b, dot_last(act_b[...], down_ref[...]))


def middle_kernel(shards, members, spots, *refs):
    ins, outs, scratch = split_refs(refs, 10 + members, 4, 2)
    (own_a, own_b, one_ref, two_ref, three_ref, residual_ref, inverse_ref, cot_ref, gains_ref,
     local_ref) = ins[:10]
    weights = ins[10:]
    residual_grad_ref, low_ref, attended_grad_ref, gain_grad_ref = outs
    rows = cot_ref.shape[0]
    grad = (own_a[0].astype(F32) + own_b[0].astype(F32)) + one_ref[...].astype(F32)
    grad = grad + two_ref[...].astype(F32) + three_ref[...].astype(F32)
    residual, inverse = residual_ref[...], inverse_ref[...]
    gain_grad_ref[...] = jnp.sum(grad * residual * inverse, axis=0, keepdims=True)
    residual_grad = cot_ref[...].astype(F32) + norm_back(grad, residual, inverse, gains_ref[1:2, :])
    residual_grad_ref[...] = residual_grad
    low = residual_grad.astype(BF16)
    low_ref[...] = low
    attended_grad_ref[...] = back_through(
        shards, members, spots, low, weights, local_ref, scratch
    ).astype(BF16)


def back_through(shards, members, spots, low, weights, local_ref, scratch):
    blocks, out_blocks = scratch
    shard, dp = spots[1], spots[2]
    for i, block in enumerate(lane_blocks(low, members)):
        blocks[i] = block
    away = sum(dot_last(blocks[dp ^ j], weights[j][...]) for j in range(members))
    out_blocks[shard] = dot_last(low, local_ref[...])
    for r, block in enumerate(lane_blocks(away, shards - 1)):
        out_blocks[shard ^ (r + 1)] = block
    return join_lanes(out_blocks)


def weight_grads_kernel(members, spots, *refs):
    lefts, lows, (keep_ref, send_ref, blocks) = refs[0:4:2], refs[1:4:2], refs[4:]
    dp = spots[2]
    for k, (left_ref, low_ref) in enumerate(zip(lefts, lows)):
        for i, block in enumerate(lane_blocks(low_ref[...], members)):
            blocks[k * members + i] = block
    for j in (1, 3, 0, 2):
        out_ref = send_ref if j & 1 else keep_ref
        out_ref[j // 2] = jnp.concatenate(
            [
                dot_first(left_ref[...], blocks[k * members + (dp ^ j)])
                for k, left_ref in enumerate(lefts)
            ],
            axis=1,
        ).astype(BF16)


def join_kernel(members, spots, own_ref, across_ref, core_ref, core_across_ref, *refs):
    outs, blocks = refs[:2], refs[2]
    dp = spots[2]
    for j, ref in enumerate((own_ref, core_ref, across_ref, core_across_ref)):
        blocks[dp ^ j] = ref[...]
    size = blocks.shape[-1] // 2
    for k, out_ref in enumerate(outs):
        out_ref[...] = jnp.concatenate(
            [blocks[i][:, k * size : (k + 1) * size] for i in range(members)], axis=1
        ).astype(F32)


def query_back_kernel(shards, members, spots, low_ref, local_ref, *refs):
    weights, (back_ref,), scratch = split_refs(refs, members, 1, 2)
    back_ref[...] = back_through(
        shards, members, spots, low_ref[...], weights, local_ref, scratch
    )


def back_kernel(chunk, pieces, first, last, spots, *refs):
    ins, outs, scratch = split_refs(refs, 9 + pieces, (pieces if last else 1) + 1, 2)
    (queries_ref, key_pos_ref, query_pos_ref, cos_ref, sin_ref, turned_ref, log_ref, grad_ref,
     start_ref) = ins[:9]
    parts = ins[9:]
    query_grad_ref, kv_grads = outs[0], outs[1:]
    kv_ref, kv_grad_ref = scratch
    stack_rows(kv_ref, parts)
    rows = queries_ref.shape[0]
    columns = GROUPS * rows
    query_pos = query_pos_ref[...]
    heads = []
    for head in range(KV_HEADS):
        stacked = heads_of(queries_ref, head * GROUPS, GROUPS)
        upstream = heads_of(grad_ref, head * GROUPS, GROUPS)
        delta = jnp.sum(upstream.astype(F32).T * turned_ref[head], axis=0, keepdims=True)
        log_total = log_ref[head : head + 1, :]
        keys_at = head * HEAD_DIM
        values_at = (KV_HEADS + head) * HEAD_DIM

        def step(j, query_grad, head=head, stacked=stacked, upstream=upstream,
                 delta=delta, log_total=log_total, keys_at=keys_at, values_at=values_at):
            at = rows_at(j, chunk)
            keys = heads_of(kv_ref, head, 1, at)
            values = heads_of(kv_ref, KV_HEADS + head, 1, at)
            scores = dot_last(keys, stacked)
            scores = jnp.where(key_pos_ref[at, :] <= query_pos, scores, MASKED)
            weights = jnp.exp(scores - log_total)
            weight_grad = dot_last(values, upstream)
            score_grad = (weights * (weight_grad - delta)).astype(BF16)
            value_grad = dot_plain(weights.astype(BF16), upstream)
            key_grad = dot_plain(score_grad, stacked)
            kv_grad_ref[at, keys_at : keys_at + HEAD_DIM] = key_grad.astype(BF16)
            kv_grad_ref[at, values_at : values_at + HEAD_DIM] = value_grad.astype(BF16)
            return query_grad + dot_first(keys, score_grad)

        start = jnp.zeros((HEAD_DIM, columns), F32) if first else start_ref[head]
        query_grad = repeat(kv_ref.shape[0] // chunk, step, start)
        if not last:
            query_grad_ref[head] = query_grad
        else:
            straight = query_grad.T * (1.0 / math.sqrt(HEAD_DIM))
            heads += [straight[g * rows : (g + 1) * rows, :] for g in range(GROUPS)]
    if last:
        query_grad_ref[...] = rope_lanes(
            jnp.concatenate(heads, axis=1), cos_ref[...], -sin_ref[...]
        ).astype(BF16)
    if last:
        for i in range(pieces):
            kv_grads[i][...] = kv_grad_ref[i * rows : (i + 1) * rows, :]
    else:
        unstack_rows(kv_grads[0], kv_grad_ref[...])


def end_kernel(shards, spots, *refs):
    ins, outs, scratch = split_refs(refs, 11 + (shards + 1) + 2 * (shards - 1), 3, 1)
    (cos_ref, sin_ref, normed_ref, tokens_ref, inverse_ref, gains_ref, back_ref, residual_grad_ref,
     key_ref, value_ref, gain_two_ref) = ins[:11]
    sums, mine, other = split_refs(ins[11:], shards + 1, shards - 1, shards - 1)
    input_grad_ref, keep_ref, send_ref = outs
    (blocks,) = scratch
    core, shard = spots[0], spots[1]
    width, span = key_ref.shape
    rows = tokens_ref.shape[0]
    total = sums[0][...].astype(F32) + sums[1][0].astype(F32)
    total = total + sum(s[...].astype(F32) for s in sums[2:])
    keys = rope_lanes(total[:, :width], cos_ref[...], -sin_ref[...])
    values = total[:, width:]
    keep = jnp.where(core == 0, keys, values).astype(BF16)
    send = jnp.where(core == 0, values, keys).astype(BF16)
    blocks[shard] = dot_plain(keys.astype(BF16), key_ref[...]) + dot_plain(
        values.astype(BF16), value_ref[...]
    )
    for r in range(1, shards):
        blocks[shard ^ r] = dot_plain(keep, mine[r - 1][:width, :]) + dot_plain(
            send, other[r - 1][:width, :]
        )
    normed_grad = back_ref[...] + join_lanes(blocks)
    inputs, inverse = tokens_ref[...].astype(F32), inverse_ref[...]
    gain_grad = jnp.sum(normed_grad * inputs * inverse, axis=0, keepdims=True)
    input_grad_ref[...] = residual_grad_ref[...] + norm_back(
        normed_grad, inputs, inverse, gains_ref[0:1, :]
    )
    normed = normed_ref[...]
    two = gain_two_ref[...]
    for out_ref, low, gain in (
        (send_ref, send, jnp.where(core == 0, two, gain_grad)),
        (keep_ref, keep, jnp.where(core == 0, gain_grad, two)),
    ):
        grad = dot_first(low, normed).astype(BF16)
        gains = lane_blocks(gain, shards)
        for z, block in enumerate(lane_blocks(grad, shards)):
            out_ref[z, :width, :] = block
            out_ref[z, width:, :] = jnp.broadcast_to(
                gains[z], (EXTRA_ROWS, span)
            ).astype(BF16)


def spread_kernel(shards, members, spots, *refs):
    parts, outs, (blocks,) = split_refs(refs, members, 3, 1)
    gate_ref, up_ref, down_ref = outs
    member = spots[3]
    piece = parts[0].shape[1] // 3 // shards
    rows = parts[0].shape[0]
    span = piece * members
    for i in range(members):
        blocks[member ^ i] = parts[i][...]

    def block(k):
        at = k * piece
        return jnp.concatenate(
            [blocks[p, :, at : at + piece] for p in range(members)], axis=1
        ).astype(F32)

    for z in range(shards):
        gate_ref[:, z * span : (z + 1) * span] = block(z)
        up_ref[:, z * span : (z + 1) * span] = block(shards + z)
    for b in range(down_ref.shape[0] // rows):
        down_ref[b * rows : (b + 1) * rows, :] = block(2 * shards + b)


def base_of(block_order, stored, block_length):
    which = stored // block_length
    count = block_order.shape[1]
    matches = (which[:, None] == jnp.arange(count, dtype=jnp.int32)[None, :]).astype(jnp.int32)
    return jnp.sum(block_order[0][None, :] * matches, axis=-1) * block_length + stored % block_length


def tables(positions):
    half_dim = HEAD_DIM // 2
    exponent = -(jnp.arange(half_dim, dtype=F32) * 2.0) / HEAD_DIM
    frequency = jnp.power(F32(ROPE_BASE), exponent)
    angles = positions.astype(F32)[:, None] * frequency
    cosine, sine = jnp.cos(angles), jnp.sin(angles)
    return (
        jnp.concatenate([cosine] * 4, axis=-1),
        jnp.concatenate([-sine, sine, -sine, sine], axis=-1),
    )


def after(x, other):
    return lax.optimization_barrier((x, other))[0]


def on_device(
    tokens,
    block_order,
    attention_gain,
    query_weight,
    key_weight,
    value_weight,
    output_weight,
    feedforward_gain,
    gate_weight,
    up_weight,
    down_weight,
    cotangent,
):
    tokens, cotangent = tokens[0], cotangent[0]
    rows, width = tokens.shape
    shards = lax.axis_size("fsdp")
    ctx_count = lax.axis_size("ctx")
    dp_count = lax.axis_size("dp")
    block_length = rows * shards * ctx_count // block_order.shape[1]
    shard = lax.axis_index("fsdp")
    ctx = lax.axis_index("ctx")
    dp = lax.axis_index("dp")
    core = dp & 1
    members = dp_count * 2
    weight_rows = query_weight.shape[0]
    query_width = HEADS * HEAD_DIM
    kv_width = KV_HEADS * HEAD_DIM
    hidden = gate_weight.shape[1]
    part = hidden // members
    spots = jnp.stack([core, shard, dp, dp * 2 + (ctx & 1)]).astype(jnp.int32)

    gain_one, gain_two = attention_gain[None, :], feedforward_gain[None, :]
    key_turned, value_turned, down_turned = key_weight.T, value_weight.T, down_weight.T
    kv_pack = jnp.concatenate(
        [
            jnp.where(core == 0, key_turned, value_turned),
            jnp.pad(
                jnp.concatenate([gain_one, gain_two], axis=0), ((0, EXTRA_ROWS - 2), (0, 0))
            ),
        ],
        axis=0,
    )
    kv_mine = direct_fsdp(kv_pack)

    quarter = width // dp_count
    query_quarter, output_quarter = call(
        functools.partial(quarter_kernel, dp_count), spots,
        [after(query_weight, kv_pack), output_weight],
        [((weight_rows, quarter), BF16)] * 2, name="quarter_columns",
    )
    query_pieces = direct_fsdp(query_quarter)
    kv_other = [swap_core(piece) for piece in kv_mine]

    def stack(pieces):
        (stacked,) = call(
            stack_kernel, spots, pieces, [(((shards - 1) * weight_rows, quarter), BF16)],
            name="stack_quarters",
        )
        return stacked, swap_plane(stacked, 2, 0)

    def four(stacked, across):
        return [stacked, swap_core(stacked), across, swap_core(across)]

    group_axes = ("dp", "ctx")
    extra = {}
    if ctx_count > 2:
        extra["axis_index_groups"] = [
            [d * ctx_count + c for d in range(dp_count) for c in (first, first + 1)]
            for first in range(0, ctx_count, 2)
        ]
    cot_all = lax.all_gather(cotangent, group_axes, axis=0, tiled=False, **extra)

    offsets = jnp.arange(rows, dtype=jnp.int32)
    my_start = (ctx * shards + shard) * rows
    positions = base_of(block_order, my_start[None], block_length) + offsets
    cosine, sine = tables(positions)
    query_pos = jnp.concatenate([positions] * GROUPS)[None, :]
    starts = jnp.stack(
        [((ctx ^ d) * shards + (shard ^ r)) * rows for d in range(ctx_count) for r in range(shards)]
    )
    key_pos = (base_of(block_order, starts, block_length)[:, None] + offsets[None, :]).reshape(-1, 1)
    near_count = shards * rows
    near_pos, far_pos = key_pos[:near_count], key_pos[near_count:]
    far_count = far_pos.shape[0]

    (pack,) = call(
        functools.partial(pack_kernel, shards, members), spots,
        [gate_weight, up_weight, down_turned], [((weight_rows, 3 * part), BF16)],
        name="pack_weights",
    )
    kv_own, normed_one, normed_turned, inverse_one, gains = call(
        functools.partial(begin_kernel, shards), spots,
        [
            lax.optimization_barrier((tokens, query_quarter, pack))[0], gain_one, gain_two, key_turned, value_turned, cosine, sine,
            *kv_mine, *kv_other,
        ],
        [
            ((rows, 2 * kv_width), BF16), ((rows, width), BF16), ((rows, width), BF16),
            ((rows, 1), F32), ((8, width), F32),
        ],
        scratch=[
            ((shards, rows, weight_rows), F32), ((shards, rows, weight_rows), BF16),
            ((shards, 8, weight_rows), F32),
        ],
        name="norm_keys_values",
    )
    near = [kv_own] + direct_fsdp(kv_own)
    query_pieces = lax.optimization_barrier((kv_own, *query_pieces))[1:]
    stacked, across = stack(query_pieces)
    across, *near = lax.optimization_barrier((across, *near))
    query_stacks = four(stacked, across)
    (near_all,) = call(
        stack_kernel, spots, near, [((near_count, 2 * kv_width), BF16)],
        name="stack_keys_values",
    )
    far = [swap(near_all, "ctx", d) for d in range(1, ctx_count)]
    output_pieces = direct_fsdp(after(output_quarter, near_all))

    pack, cot_all, _ = lax.optimization_barrier((pack, cot_all, near[-1]))
    pack_all = lax.all_gather(pack, "fsdp", axis=0, tiled=True)


    chunk = rows * 2
    unit = 2 * HEADS * rows * near_count * HEAD_DIM
    stat = ((KV_HEADS, GROUPS * rows), F32)
    turned_shape = ((KV_HEADS, HEAD_DIM, GROUPS * rows), F32)
    queries, largest, total, weighted = call(
        functools.partial(near_kernel, chunk, dp_count, shards), spots,
        [normed_turned, near_pos, query_pos, cosine, sine, query_weight, *query_stacks, *near],
        [((rows, query_width), BF16), stat, stat, turned_shape],
        scratch=[((dp_count, rows, quarter), F32), ((near_count, 2 * kv_width), BF16)],
        name="attention_near",
    )
    attended, turned, log_total = call(
        functools.partial(far_kernel, chunk, len(far)), spots,
        [queries, far_pos, query_pos, largest, total, weighted, *far],
        [((rows, query_width), BF16), turned_shape, stat],
        scratch=[((far_count, 2 * kv_width), BF16)], name="attention_far",
    )
    output_pieces = lax.optimization_barrier((queries, *output_pieces))[1:]
    output_stacked, output_across = stack(output_pieces)
    attended, output_across = lax.optimization_barrier((attended, output_across))
    output_stacks = four(output_stacked, output_across)
    residual, inverse_two, normed_two = call(
        functools.partial(project_kernel, shards, dp_count), spots,
        [attended, tokens, gains, output_weight, *output_stacks],
        [((rows, width), F32), ((rows, 1), F32), ((rows, width), BF16)],
        scratch=[((dp_count, rows, quarter), F32), ((shards, rows, weight_rows), BF16)],
        name="project_residual",
    )

    normed_a, normed_b = plane_pieces(normed_two)
    token_shape = ((rows, width), BF16)
    half = 4 * rows
    half_shape = ((4, rows, width), BF16)

    masks = [2 * a + b for a, b in ((0, 0),) + CHIP_MASKS]
    core_masks = [mask ^ 2 for mask in masks]

    def feed(normed, masks):
        return call(
            functools.partial(feed_kernel, shards, masks), spots, [pack_all, cot_all, *normed],
            [half_shape, ((half, part), BF16), ((half, 2 * part), BF16)],
            scratch=[((half, width), BF16), ((half, width), BF16), ((width, part), BF16)],
        name="feed_forward",
        )

    grad_b, act_b, both_b = feed(normed_b, core_masks)
    from_core = swap_core(grad_b)
    grad_a, act_a, both_a = feed(normed_a, masks)

    def chip_sums(parts_a, parts_b):
        return [
            (parts_a[k].astype(F32) + parts_b[k].astype(F32)).astype(BF16)
            for k in range(1, 4)
        ]

    def send_chips(sums):
        return [swap_plane(x, a, b) for x, (a, b) in zip(sums, CHIP_MASKS)]

    grad_sums = chip_sums(grad_a, from_core)
    grad_chips = send_chips(grad_sums)
    act_a, *_ = lax.optimization_barrier((act_a, *grad_sums))
    result_a, result_b, pack_grad = call(
        functools.partial(feed_weights_kernel, shards, masks + core_masks), spots,
        [pack_all, act_a, act_b, both_a, both_b, cot_all, *normed_a, *normed_b],
        [half_shape, half_shape, ((width, 3 * part), BF16)],
        scratch=[
            ((2 * half, width), BF16), ((2 * half, width), BF16), ((2 * half, part), BF16),
            ((2 * half, 2 * part), BF16), ((width, part), BF16),
        ],
        name="feed_forward_weights",
    )
    pack_share = sum_far(lax.psum_scatter(pack_grad, "fsdp", scatter_dimension=0, tiled=True))

    pack_grad, result_b, *grad_chips = lax.optimization_barrier(
        (pack_grad, result_b, *grad_chips)
    )
    residual_grad, residual_low, attended_grad, second_gain_grad = call(
        functools.partial(middle_kernel, shards, dp_count), spots,
        [
            grad_a, from_core, *grad_chips, residual, inverse_two, cotangent, gains, output_weight,
            *output_stacks,
        ],
        [((rows, width), F32), token_shape, ((rows, query_width), BF16), ((1, width), F32)],
        scratch=[((dp_count, rows, quarter), BF16), ((shards, rows, weight_rows), F32)],
        name="residual_back",
    )

    result_core = swap_core(result_b)
    attended_grad, result_a = lax.optimization_barrier((attended_grad, result_a))

    def sum_x(keep, away):
        sent = (keep[1].astype(F32) + away[1].astype(F32)).astype(BF16)
        return sent, (keep[0], away[0], swap_plane(sent, 2, 0))

    def pieces_z(terms):
        out = []
        for r in range(shards):
            at = (shard ^ r) * weight_rows
            parts = [
                lax.dynamic_slice_in_dim(x, at, weight_rows, 0).astype(F32) for x in terms
            ]
            out.append((parts[0] + parts[1] + parts[2]).astype(BF16))
        return out

    def sum_z(pieces):
        arrived = {r: swap(pieces[r], "fsdp", r) for r in reversed(range(1, shards))}
        return sum(
            (arrived[r].astype(F32) for r in range(1, shards)), pieces[0].astype(F32)
        ).astype(BF16)

    def halve_z(pieces, span):
        sent = jnp.stack([piece.astype(BF16) for piece in pieces[span:]])
        arrived = swap(sent, "fsdp", span)
        return [pieces[r].astype(F32) + arrived[r].astype(F32) for r in range(span)]

    def sum_swap(own, dp_mask, ctx_mask):
        return (own.astype(F32) + swap_plane(own, dp_mask, ctx_mask).astype(F32)).astype(BF16)

    def sum_y(own):
        return sum_far(sum_swap(own, 0, 1))

    def finish_quarters(own):
        across = swap_plane(own, 2, 0)
        return call(
            functools.partial(join_kernel, dp_count), spots,
            [own, across, swap_core(own), swap_core(across)],
            [((weight_rows, width), F32)] * 2,
            scratch=[((dp_count, weight_rows, 2 * quarter), BF16)], name="join_columns",
        )

    def back(first, last, start, pos, pieces):
        count = pos.shape[0]
        shape = ((rows, query_width), BF16) if last else turned_shape
        out = call(
            functools.partial(back_kernel, chunk, len(pieces), first, last), spots,
            [
                queries, pos, query_pos, cosine, sine, turned, log_total, attended_grad, start,
                *pieces,
            ],
            [shape]
            + (
                [((rows, 2 * kv_width), BF16)] * len(pieces) if last
                else [((shards, rows, 2 * kv_width), BF16)]
            ),
            scratch=[((count, 2 * kv_width), BF16), ((count, 2 * kv_width), BF16)],
            name="attention_back_near" if last else "attention_back_far",
        )
        return out[0], out[1:]

    query_partial, far_grads = turned, []
    for d in range(1, ctx_count):
        at = (d - 1) * near_count
        query_partial, grads = back(
            d == 1, False, query_partial, far_pos[at : at + near_count], far[d - 1 : d]
        )
        far_grads.append(swap(grads[0], "ctx", d))
    result_sent = (result_a[2:].astype(F32) + result_core[2:].astype(F32)).astype(BF16)
    query_partial, result_sent = lax.optimization_barrier((query_partial, result_sent))
    result_across = swap_plane(result_sent, 2, 0)
    query_low, near_grads = back(False, True, query_partial, near_pos, near)
    pair_shape = ((2, width, 2 * quarter), BF16)
    weights_keep, weights_send = call(
        functools.partial(weight_grads_kernel, dp_count), spots,
        [attended, residual_low, normed_one, query_low], [pair_shape, pair_shape],
        scratch=[((2 * dp_count, rows, quarter), BF16)], name="query_output_weight_grads",
    )
    weights_send, pack_share, far_grads[-1], result_across = lax.optimization_barrier(
        (weights_send, pack_share, far_grads[-1], result_across)
    )
    result_own, result_along = [
        (result_a[k].astype(F32) + result_core[k].astype(F32)) + result_across[k].astype(F32)
        for k in (0, 1)
    ]
    result_along = swap_plane(result_along.astype(BF16), 0, 1)

    def home(r):
        return sum(grads[r].astype(F32) for grads in far_grads)

    kv_sums = {
        r: (near_grads[r].astype(F32) + home(r)).astype(BF16) for r in range(1, shards)
    }
    kv_arrived = {r: swap(kv_sums[r], "fsdp", r) for r in reversed(range(1, shards))}
    query_low = lax.optimization_barrier((query_low, *kv_sums.values()))[0]

    weights_away = swap_core(weights_send)
    weights_sent, weights_terms = sum_x(weights_keep, weights_away)
    query_turn = after(query_low, weights_sent)
    (query_back,) = call(
        functools.partial(query_back_kernel, shards, dp_count), spots,
        [query_turn, query_weight, *query_stacks], [((rows, width), F32)],
        scratch=[((dp_count, rows, quarter), BF16), ((shards, rows, weight_rows), F32)],
        name="query_back",
    )
    query_back, share_along = lax.optimization_barrier(
        (query_back, swap_plane(pack_share, 0, 1))
    )
    share_across = swap_plane(after(pack_share, weights_sent), 2, 0)
    span = kv_width + EXTRA_ROWS
    packed_shape = ((shards, span, weight_rows), BF16)
    home_all = far_grads[0]
    if ctx_count > 2:
        home_all = sum(grads.astype(F32) for grads in far_grads)
    input_grad, kv_keep, kv_send = call(
        functools.partial(end_kernel, shards), spots,
        [
            cosine, sine, normed_one, tokens, inverse_one, gains, query_back, residual_grad,
            key_turned, value_turned, second_gain_grad, near_grads[0], home_all,
            *[kv_arrived[r] for r in range(1, shards)], *kv_mine, *kv_other,
        ],
        [((rows, width), F32), packed_shape, packed_shape],
        scratch=[((shards, rows, weight_rows), F32)],
        name="keys_values_back",
    )
    kv_away = swap_core(kv_send)
    kv_keep, *weights_terms = lax.optimization_barrier((kv_keep, *weights_terms))
    weights_pieces = pieces_z(weights_terms)
    pieces = [
        (lax.dynamic_index_in_dim(kv_keep, shard ^ r, 0, keepdims=False).astype(F32)
         + lax.dynamic_index_in_dim(kv_away, shard ^ r, 0, keepdims=False).astype(F32)).astype(BF16)
        for r in range(shards)
    ]
    weights_pieces, *pieces = lax.optimization_barrier((weights_pieces, *pieces))
    share_across = lax.optimization_barrier((share_across, *pieces))[0]
    share_a = [pack_share, share_along, share_across, swap_plane(share_across, 0, 1)]
    share_b = [swap_core(piece) for piece in share_a]
    kv_share = sum_z(pieces)
    weights_half = halve_z(weights_pieces, shards // 2)
    share_by_mask = [None] * members
    for k, (a, b) in enumerate(((0, 0),) + CHIP_MASKS):
        share_by_mask[2 * a + b] = share_a[k]
        share_by_mask[2 * (a ^ 1) + b] = share_b[k]
    gate_weight_grad, up_weight_grad, down_weight_grad = call(
        functools.partial(spread_kernel, shards, members), spots, share_by_mask,
        [
            ((weight_rows, hidden), F32), ((weight_rows, hidden), F32),
            ((width, down_weight.shape[0]), F32),
        ],
        scratch=[((members, weight_rows, 3 * part), BF16)],
        name="feed_forward_out",
    )
    kv_share, weights_half, result_along = lax.optimization_barrier(
        (kv_share, weights_half, result_along)
    )
    kv_share, result_along, *big = lax.optimization_barrier(
        (sum_swap(kv_share, 2, 0), result_along, gate_weight_grad, up_weight_grad,
         down_weight_grad)
    )
    gate_weight_grad, up_weight_grad, down_weight_grad = big
    span = shards // 2
    while span > 1:
        span //= 2
        weights_half = halve_z(weights_half, span)
    weights_own = sum_y(weights_half[0].astype(BF16))
    result = residual + (result_own + result_along.astype(F32))
    output_weight_grad, query_weight_grad = finish_quarters(weights_own)
    low = sum_far(sum_swap(kv_share, 0, 1))
    away = swap_core(low)
    first = jnp.where(core == 0, low, away).astype(F32)
    second = jnp.where(core == 0, away, low).astype(F32)

    return (
        result[None],
        input_grad[None],
        first[kv_width],
        query_weight_grad,
        first[:kv_width].T,
        second[:kv_width].T,
        output_weight_grad,
        second[kv_width],
        gate_weight_grad,
        up_weight_grad,
        down_weight_grad.T,
    )


def solution(mesh):
    row = P("fsdp", None)
    token = P("dp", ("ctx", "fsdp"), None)
    return jax.shard_map(
        on_device,
        mesh=mesh,
        in_specs=(
            token, P("dp", None), P("fsdp"), row, row, row, row, P("fsdp"), row, row, row, token,
        ),
        out_specs=(
            token, token, P("fsdp"), row, row, row, row, P("fsdp"), row, row, row,
        ),
        check_vma=False,
    )
```
